32 devices in a mesh: groups: 2 (over x), node: 16 (over z, y, core).
Axes of the slice: x: 2, y: 2, z: 4, core: 2. Of those that a mesh axis runs over, the one named last changes fastest.
Arguments:
- grid_in: bfloat16 [16384, 1024], P(('groups', 'node')), parts along dimension 0, may hold values from -6 to 6
- mesh_in: bfloat16 [4096, 1024], P(('groups', 'node')), parts along dimension 0, may hold values from -6 to 6
- own_src: int32 [32768], P(('groups', 'node')), parts along dimension 0, may hold values from 0 to 511, as said below
- own_dst: int32 [32768], P(('groups', 'node')), parts along dimension 0, may hold values from 0 to 127
- side_src: int32 [131072], P(('groups', 'node')), parts along dimension 0, may hold values from 0 to 511, as said below
- side_dst: int32 [131072], P(('groups', 'node')), parts along dimension 0, may hold values from 0 to 127
- side_count: int32 [64], P(('groups', 'node')), parts along dimension 0, may hold values from 0 to 2048, as said below
- far_src: int32 [2048], P(('groups', 'node')), parts along dimension 0, may hold values from 0 to 511
- far_dst: int32 [2048], P(('groups', 'node')), parts along dimension 0, may hold values from 0 to 127
- far_count: int32 [512], P(('groups', 'node')), parts along dimension 0, may hold values from 0 to 4, as said below
- window: int32 [2, 4096], P(None, ('groups', 'node')), parts along dimension 1, may hold values from 1 to 128, as said below
- cotangent: bfloat16 [4096, 1024], P(('groups', 'node')), parts along dimension 0, may hold values from -6 to 6
- w_edge: bfloat16 [1024, 1024], replicated, may hold values from -0.09375 to 0.09375
- w_qkv: bfloat16 [1024, 3072], replicated, may hold values from -4 to 4
- w_out: bfloat16 [1024, 1024], replicated, may hold values from -0.1875 to 0.1875
Outputs:
- mesh_out: bfloat16 [4096, 1024], P(('groups', 'node')), parts along dimension 0
- mesh_grad: bfloat16 [4096, 1024], P(('groups', 'node')), parts along dimension 0
The draws below stay inside these ranges and needn't reach their ends.
There are 2 independent parts, one for each index of `groups`. The reference program is written for one: setup_inputs(seed, part) draws one part's arguments, and reference() takes and returns one part's arrays. A program takes and returns all parts, laid end to end along the dimension named above; an argument that names none is the same for every part. Nothing has to cross between parts.
Inputs may be any that keep to these rules, and one draw needn't show every extreme that they name: `own_src`: each device's 1024 slots name every one of its 512 grid nodes exactly twice. `side_src`: slots toward the device before name grid nodes below 128; slots toward the device after name grid nodes from 384 on. `side_count`: the first device's count toward the device before it and the last device's count toward the device after it are 0, all others at least 512; one device sends 2048 live slots to both sides and receives 2048 from both. `far_count`: 0 where sender and receiver are the same or adjacent devices, at least 1 otherwise; one receiving device gets 4 live slots from every device not adjacent to it. `window`: both 1 and 128 occur in each row.
All inputs are finite; a program needn't handle non-finite values.
Results may differ from the reference program's by a relative error of at most 0.01.
Values may be sent and summed in bfloat16 or wider, within the bound.
No kernel may reach another device: no remote copies, remote signals or barrier semaphores. Data moves between devices by JAX's collectives and lax.ppermute only.
A program may use at most 128 MiB of HBM per device.

```python
import math
import jax
import jax.numpy as jnp
from jax import lax

CHANNELS = 1024
HEADS = 16
HEAD_DIM = 64
GRID_DEV = 512
MESH_DEV = 128
SIDE_CAP = 2048
FAR_CAP = 4
OWN_CAP = 1024
BAND = 128
WINDOW = 128
GRID = 8192
MESH = 2048
N_NODE = 16


def draw_own_src(key, part):
    key = jax.random.fold_in(key, 3)
    keys = jax.random.split(key, N_NODE * 2)
    orders = jax.vmap(lambda single: jax.random.permutation(single, GRID_DEV))(keys)
    return orders.reshape(N_NODE * OWN_CAP).astype(jnp.int32)


def draw_side_src(key, part):
    key = jax.random.fold_in(key, 4)
    offsets = jax.random.randint(key, (N_NODE, 2, SIDE_CAP), 0, BAND)
    start = (GRID_DEV - BAND) * jnp.arange(2, dtype=jnp.int32)[None, :, None]
    return (offsets + start).reshape(N_NODE * 2 * SIDE_CAP).astype(jnp.int32)


def draw_side_count(key, part):
    key = jax.random.fold_in(key, 5)
    fill_key, hot_key = jax.random.split(key, 2)
    counts = jax.random.randint(fill_key, (N_NODE, 2), SIDE_CAP // 4, SIDE_CAP + 1)
    hot_device = jax.random.randint(hot_key, (), 1, N_NODE - 1)
    sender = jnp.arange(N_NODE, dtype=jnp.int32)[:, None]
    toward = sender - 1 + 2 * jnp.arange(2, dtype=jnp.int32)[None, :]
    counts = jnp.where((toward == hot_device) | (sender == hot_device), SIDE_CAP, counts)
    counts = jnp.where((toward < 0) | (toward >= N_NODE), 0, counts)
    return counts.reshape(N_NODE * 2).astype(jnp.int32)


def draw_far_count(key, part):
    key = jax.random.fold_in(key, 9)
    level_key, hot_key = jax.random.split(key, 2)
    level = jax.random.randint(level_key, (N_NODE, N_NODE), 0, 8)
    counts = jnp.where(level < 4, 1, jnp.where(level < 6, 2, jnp.where(level < 7, 3, 4)))
    counts = jnp.minimum(counts, FAR_CAP)
    hot_device = jax.random.randint(hot_key, (), 0, N_NODE)
    sender = jnp.arange(N_NODE, dtype=jnp.int32)[:, None]
    receiver = jnp.arange(N_NODE, dtype=jnp.int32)[None, :]
    counts = jnp.where(receiver == hot_device, FAR_CAP, counts)
    counts = jnp.where(jnp.abs(sender - receiver) <= 1, 0, counts)
    return counts.reshape(N_NODE * N_NODE).astype(jnp.int32)


def draw_window(key, part):
    key = jax.random.fold_in(key, 7)
    reach = jax.random.randint(key, (2, MESH), 1, WINDOW + 1)
    marker = jnp.arange(MESH)[None, :] % 61
    reach = jnp.where(marker == 3, WINDOW, reach)
    reach = jnp.where(marker == 7, 1, reach)
    return reach.astype(jnp.int32)


def draw_w_qkv(key, part):
    key = jax.random.fold_in(key, 11)
    matrix = jax.random.truncated_normal(key, -5.0, 5.0, (CHANNELS, 3 * CHANNELS), jnp.float32) * CHANNELS ** (-0.5)
    matrix = jnp.clip(matrix, -4.0, 4.0)
    return matrix.astype(jnp.bfloat16)


def set_ends(values, rng, smallest, high):
    place = [jax.random.randint(jax.random.fold_in(rng, axis), (), 0, length) for axis, length in enumerate(values.shape)]
    longest = values.shape.index(max(values.shape))
    next_to = place[:longest] + [(place[longest] + 1) % values.shape[longest]] + place[longest + 1:]
    return values.at[tuple(place)].set(smallest).at[tuple(next_to)].set(high)


def block_levels(stream_key, dims, shards, smallest, top_value):
    gain = 1.0
    for dim, blocks in shards:
        heights = jax.random.uniform(jax.random.fold_in(jax.random.fold_in(stream_key, 6), dim), (blocks,), jnp.float32, smallest / len(shards), top_value / len(shards))
        gain = gain * jnp.repeat(jnp.exp(heights), dims[dim] // blocks).reshape((-1,) + (1,) * (len(dims) - 1 - dim))
    return gain


def noise(stream_key, extent, width, most, pieces=(), kind=jnp.bfloat16):
    drawn = width * jax.random.normal(stream_key, extent, jnp.float32)
    if pieces:
        drawn = drawn * block_levels(stream_key, extent, pieces, -0.22, 0.18)
    return jnp.clip(drawn, -most, most).astype(kind)


def setup_inputs(seed: int = 0, part: int = 0) -> dict:
    arg_keys = jax.random.split(jax.random.key(seed), 16)
    own_keys = jax.random.split(jax.random.fold_in(arg_keys[15], part), 16)
    grid_in = noise(own_keys[0], (GRID, CHANNELS), 1.0, 6.0, ((0, 16),))
    mesh_in = noise(own_keys[1], (MESH, CHANNELS), 1.0, 6.0, ((0, 16),))
    own_src = draw_own_src(jax.random.fold_in(jax.random.fold_in(arg_keys[15], part), 71), part)
    own_dst = set_ends(jax.random.randint(own_keys[3], (N_NODE * OWN_CAP,), 0, MESH_DEV), jax.random.fold_in(own_keys[3], 1), 0, MESH_DEV - 1).astype(jnp.int32)
    side_src = draw_side_src(jax.random.fold_in(jax.random.fold_in(arg_keys[15], part), 71), part)
    side_dst = set_ends(jax.random.randint(own_keys[5], (N_NODE * 2 * SIDE_CAP,), 0, MESH_DEV), jax.random.fold_in(own_keys[5], 1), 0, MESH_DEV - 1).astype(jnp.int32)
    side_count = draw_side_count(jax.random.fold_in(jax.random.fold_in(arg_keys[15], part), 71), part)
    far_src = set_ends(jax.random.randint(own_keys[7], (N_NODE * N_NODE * FAR_CAP,), 0, GRID_DEV), jax.random.fold_in(own_keys[7], 1), 0, GRID_DEV - 1).astype(jnp.int32)
    far_dst = set_ends(jax.random.randint(own_keys[8], (N_NODE * N_NODE * FAR_CAP,), 0, MESH_DEV), jax.random.fold_in(own_keys[8], 1), 0, MESH_DEV - 1).astype(jnp.int32)
    far_count = draw_far_count(jax.random.fold_in(jax.random.fold_in(arg_keys[15], part), 71), part)
    window = draw_window(jax.random.fold_in(jax.random.fold_in(arg_keys[15], part), 71), part)
    cotangent = noise(own_keys[11], (MESH, CHANNELS), 1.0, 6.0, ((0, 16),))
    w_edge = noise(arg_keys[12], (CHANNELS, CHANNELS), (4 * CHANNELS) ** -0.5, 0.09375)
    w_qkv = draw_w_qkv(jax.random.fold_in(arg_keys[15], 71), part)
    w_out = noise(arg_keys[14], (CHANNELS, CHANNELS), CHANNELS ** -0.5, 0.1875)
    return dict(grid_in=grid_in, mesh_in=mesh_in, own_src=own_src, own_dst=own_dst, side_src=side_src, side_dst=side_dst, side_count=side_count, far_src=far_src, far_dst=far_dst, far_count=far_count, window=window, cotangent=cotangent, w_edge=w_edge, w_qkv=w_qkv, w_out=w_out)


def layer_stats(latent):
    values = latent.astype(jnp.float32)
    row_mean = lax.optimization_barrier(jnp.mean(values, -1, keepdims=True))
    centred = values - row_mean
    variance = lax.optimization_barrier(jnp.mean(centred * centred, -1, keepdims=True))
    inv_std = lax.rsqrt(variance + 1e-05)
    return (centred * inv_std, inv_std)

def window_mask(query_pos, key_pos, reach_back, reach_ahead, node_total):
    key_at = key_pos[None, :]
    query_at = query_pos[:, None]
    inside = (key_at >= 0) & (key_at < node_total)
    return inside & (key_at >= query_at - reach_back[:, None]) & (key_at <= query_at + reach_ahead[:, None])

def attend_forward(query_rows, key_rows, value_rows, keep_mask, score_scale):
    scores = jnp.einsum('qhe,khe->hqk', query_rows.astype(jnp.float32), key_rows.astype(jnp.float32)) * score_scale
    scores = jnp.where(keep_mask[None], scores, -jnp.inf)
    row_max = lax.optimization_barrier(jnp.max(scores, -1, keepdims=True))
    shifted = jnp.exp(scores - row_max)
    row_probs = shifted / lax.optimization_barrier(jnp.sum(shifted, -1, keepdims=True))
    weights = row_probs.astype(jnp.bfloat16)
    output = jnp.einsum('hqk,khe->qhe', weights.astype(jnp.float32), value_rows.astype(jnp.float32)).astype(jnp.bfloat16)
    return (output, row_probs, weights)

def attend_backward(query_rows, key_rows, value_rows, row_probs, weights, grad_out, score_scale):
    grad_prob = jnp.einsum('qhe,khe->hqk', grad_out.astype(jnp.float32), value_rows.astype(jnp.float32))
    grad_score = (row_probs * (grad_prob - lax.optimization_barrier(jnp.sum(row_probs * grad_prob, -1, keepdims=True)))).astype(jnp.bfloat16)
    grad_query = jnp.einsum('hqk,khe->qhe', grad_score.astype(jnp.float32), key_rows.astype(jnp.float32)) * score_scale
    grad_key = jnp.einsum('hqk,qhe->khe', grad_score.astype(jnp.float32), query_rows.astype(jnp.float32)) * score_scale
    grad_value = jnp.einsum('hqk,qhe->khe', weights.astype(jnp.float32), grad_out.astype(jnp.float32))
    return (grad_query, grad_key, grad_value)

def reference(grid_in, mesh_in, own_src, own_dst, side_src, side_dst, side_count, far_src, far_dst, far_count, window, cotangent, w_edge, w_qkv, w_out):
    projected = jnp.dot(grid_in, w_edge, preferred_element_type=jnp.float32).astype(jnp.bfloat16)
    active = jax.nn.gelu(projected.astype(jnp.float32), approximate=True).astype(jnp.bfloat16)
    side_index = jnp.arange(2 * SIDE_CAP, dtype=jnp.int32)
    side_toward = side_index // SIDE_CAP
    side_rank = side_index % SIDE_CAP
    far_index = jnp.arange(N_NODE * FAR_CAP, dtype=jnp.int32)
    far_toward = far_index // FAR_CAP
    far_rank = far_index % FAR_CAP
    senders = (active.reshape(N_NODE, GRID_DEV, CHANNELS), own_src.reshape(N_NODE, OWN_CAP), own_dst.reshape(N_NODE, OWN_CAP), side_src.reshape(N_NODE, 2 * SIDE_CAP), side_dst.reshape(N_NODE, 2 * SIDE_CAP), side_count.reshape(N_NODE, 2), far_src.reshape(N_NODE, N_NODE * FAR_CAP), far_dst.reshape(N_NODE, N_NODE * FAR_CAP), far_count.reshape(N_NODE, N_NODE), jnp.arange(N_NODE, dtype=jnp.int32))

    def add_sender(aggregate, sender):
        rows, home_src, home_dst, edge_src, edge_dst, edge_count, remote_src, remote_dst, remote_count, sender_at = sender
        aggregate = aggregate.at[sender_at * MESH_DEV + home_dst].add(rows[home_src].astype(jnp.float32))
        side_live = side_rank < edge_count[side_toward]
        side_rows = jnp.clip((sender_at - 1 + 2 * side_toward) * MESH_DEV + edge_dst, 0, MESH - 1)
        aggregate = aggregate.at[side_rows].add(jnp.where(side_live[:, None], rows[edge_src].astype(jnp.float32), 0.0))
        far_live = far_rank < remote_count[far_toward]
        far_rows = far_toward * MESH_DEV + remote_dst
        aggregate = aggregate.at[far_rows].add(jnp.where(far_live[:, None], rows[remote_src].astype(jnp.float32), 0.0))
        return (aggregate, None)
    aggregate, _ = lax.scan(add_sender, jnp.zeros((MESH, CHANNELS), jnp.float32), senders)
    latent = (mesh_in.astype(jnp.float32) + aggregate).astype(jnp.bfloat16)
    normal, inv_std = layer_stats(latent)
    normed = normal.astype(jnp.bfloat16)
    qkv_rows = jnp.dot(normed, w_qkv, preferred_element_type=jnp.float32).astype(jnp.bfloat16)
    qkv_rows = qkv_rows.reshape(MESH, 3, HEADS, HEAD_DIM)
    query_all = qkv_rows[:, 0]
    margin = ((WINDOW, WINDOW), (0, 0), (0, 0))
    key_all = jnp.pad(qkv_rows[:, 1], margin)
    value_all = jnp.pad(qkv_rows[:, 2], margin)
    score_scale = HEAD_DIM ** (-0.5)
    query_block = math.gcd(512, MESH)
    key_span = query_block + 2 * WINDOW
    block_list = jnp.arange(MESH // query_block, dtype=jnp.int32)
    grad_att = jnp.dot(cotangent, w_out.T, preferred_element_type=jnp.float32).astype(jnp.bfloat16)
    grad_att = grad_att.reshape(MESH, HEADS, HEAD_DIM)

    def block_parts(block_at):
        row_start = block_at * query_block
        query_rows = lax.dynamic_slice_in_dim(query_all, row_start, query_block, 0)
        key_rows = lax.dynamic_slice_in_dim(key_all, row_start, key_span, 0)
        value_rows = lax.dynamic_slice_in_dim(value_all, row_start, key_span, 0)
        query_pos = row_start + jnp.arange(query_block, dtype=jnp.int32)
        key_pos = row_start - WINDOW + jnp.arange(key_span, dtype=jnp.int32)
        reach_back = lax.dynamic_slice_in_dim(window[0], row_start, query_block, 0)
        reach_ahead = lax.dynamic_slice_in_dim(window[1], row_start, query_block, 0)
        keep_mask = window_mask(query_pos, key_pos, reach_back, reach_ahead, MESH)
        return (query_rows, key_rows, value_rows, keep_mask)

    def forward_block(block_at):
        query_rows, key_rows, value_rows, keep_mask = block_parts(block_at)
        return attend_forward(query_rows, key_rows, value_rows, keep_mask, score_scale)[0]
    attention = lax.map(forward_block, block_list).reshape(MESH, CHANNELS)
    mesh_out = (latent.astype(jnp.float32) + jnp.dot(attention, w_out, preferred_element_type=jnp.float32)).astype(jnp.bfloat16)

    def backward_block(carried, block_at):
        grad_keys, grad_values = carried
        query_rows, key_rows, value_rows, keep_mask = block_parts(block_at)
        row_start = block_at * query_block
        output, row_probs, weights = attend_forward(query_rows, key_rows, value_rows, keep_mask, score_scale)
        grad_out = lax.dynamic_slice_in_dim(grad_att, row_start, query_block, 0)
        grad_query, grad_key, grad_value = attend_backward(query_rows, key_rows, value_rows, row_probs, weights, grad_out, score_scale)
        grad_keys = lax.dynamic_update_slice_in_dim(grad_keys, lax.dynamic_slice_in_dim(grad_keys, row_start, key_span, 0) + grad_key, row_start, 0)
        grad_values = lax.dynamic_update_slice_in_dim(grad_values, lax.dynamic_slice_in_dim(grad_values, row_start, key_span, 0) + grad_value, row_start, 0)
        return ((grad_keys, grad_values), grad_query)
    zero_grads = jnp.zeros((MESH + 2 * WINDOW, HEADS, HEAD_DIM), jnp.float32)
    (grad_keys, grad_values), grad_queries = lax.scan(backward_block, (zero_grads, zero_grads), block_list)
    grad_qkv = jnp.concatenate([grad_queries.reshape(MESH, CHANNELS), grad_keys[WINDOW:WINDOW + MESH].reshape(MESH, CHANNELS), grad_values[WINDOW:WINDOW + MESH].reshape(MESH, CHANNELS)], 1).astype(jnp.bfloat16)
    grad_normed = jnp.dot(grad_qkv, w_qkv.T, preferred_element_type=jnp.float32)
    centred_grad = grad_normed - lax.optimization_barrier(jnp.mean(grad_normed, -1, keepdims=True)) - normal * lax.optimization_barrier(jnp.mean(grad_normed * normal, -1, keepdims=True))
    mesh_grad = (cotangent.astype(jnp.float32) + inv_std * centred_grad).astype(jnp.bfloat16)
    return (mesh_out, mesh_grad)
```

```python
import jax
import jax.numpy as jnp
from jax import lax
from jax.sharding import PartitionSpec as P

HEADS = 16
BAND = 128
F32 = jnp.float32
BF16 = jnp.bfloat16


def exchange(toward_low, toward_high, axis):
    ends = lax.axis_size(axis) - 1
    from_high = lax.ppermute(toward_low, axis, [(i + 1, i) for i in range(ends)])
    from_low = lax.ppermute(toward_high, axis, [(i, i + 1) for i in range(ends)])
    return from_low, from_high


def onehot_cols(indices, rows):
    return (jnp.arange(rows, dtype=jnp.int32)[:, None] == indices[None, :].astype(jnp.int32)).astype(
        BF16
    )


def edge_counts(dst, src, dst_rows, src_rows):
    return lax.dot_general(
        onehot_cols(dst, dst_rows),
        onehot_cols(src, src_rows),
        (((1,), (1,)), ((), ())),
        preferred_element_type=F32,
    )


def exact_halves(counts):
    upper = counts.astype(BF16)
    lower = (counts - upper.astype(F32)).astype(BF16)
    return upper, lower


def activate(rows, w_edge):
    projected = jnp.dot(rows, w_edge, preferred_element_type=F32).astype(BF16)
    return jax.nn.gelu(projected.astype(F32), approximate=True).astype(BF16)


def layer_stats(latent):
    values = latent.astype(F32)
    row_mean = jnp.mean(values, -1, keepdims=True)
    centred = values - row_mean
    variance = jnp.mean(centred * centred, -1, keepdims=True)
    inv_std = lax.rsqrt(variance + 1e-05)
    return (centred * inv_std, inv_std)


def body(
    grid_in,
    mesh_in,
    own_src,
    own_dst,
    side_src,
    side_dst,
    side_count,
    far_src,
    far_dst,
    far_count,
    window,
    cotangent,
    w_edge,
    w_qkv,
    w_out,
):
    devices = lax.axis_size("node")
    own_index = lax.axis_index("node")
    grid_rows, channels = grid_in.shape
    mesh_rows = mesh_in.shape[0]
    heads = HEADS
    head_dim = channels // heads
    side_slots = side_src.shape[0] // 2
    far_slots = far_src.shape[0]
    far_depth = far_slots // devices
    scale = head_dim ** (-0.5)

    far_live = jnp.arange(far_slots, dtype=jnp.int32) % far_depth < jnp.repeat(far_count, far_depth)
    far_target = jnp.where(far_live, far_dst, mesh_rows).astype(BF16)
    far_rows = lax.dot_general(
        onehot_cols(far_src, grid_rows),
        grid_in,
        (((0,), (0,)), ((), ())),
        preferred_element_type=F32,
    ).astype(BF16)
    far_message = jnp.concatenate(
        [far_rows, jnp.broadcast_to(far_target[:, None], (far_slots, 128))], 1
    )

    def side_message(k, rows, src):
        live = jnp.arange(side_slots, dtype=jnp.int32) < side_count[k]
        dst = jnp.where(live, side_dst[k * side_slots : (k + 1) * side_slots], mesh_rows)
        meta = jnp.concatenate([src, dst, window.reshape(-1)]).astype(BF16)
        meta_rows = -(-meta.shape[0] // (16 * channels)) * 16
        meta = jnp.pad(meta, (0, meta_rows * channels - meta.shape[0])).reshape(meta_rows, channels)
        return jnp.concatenate([rows, cotangent, meta], 0)

    toward_low = side_message(0, grid_in[:BAND], side_src[:side_slots])
    toward_high = side_message(
        1, grid_in[grid_rows - BAND :], side_src[side_slots:] - (grid_rows - BAND)
    )
    from_low, from_high = exchange(toward_low, toward_high, "node")
    got_far = lax.all_to_all(
        far_message.reshape(devices, far_depth, channels + 128),
        "node",
        split_axis=0,
        concat_axis=0,
        tiled=True,
    ).reshape(far_slots, channels + 128)

    own_active = activate(grid_in, w_edge)
    own_counts = edge_counts(own_dst, own_src, mesh_rows, grid_rows).astype(BF16)
    aggregate = jnp.dot(own_counts, own_active, preferred_element_type=F32)

    def unpack(message):
        meta = message[BAND + mesh_rows :].reshape(-1)
        src = meta[:side_slots]
        dst = meta[side_slots : 2 * side_slots]
        reach = meta[2 * side_slots : 2 * side_slots + 2 * mesh_rows].astype(jnp.int32)
        return message[BAND : BAND + mesh_rows], src, dst, reach.reshape(2, mesh_rows)

    low_cot, low_src, low_dst, low_window = unpack(from_low)
    high_cot, high_src, high_dst, high_window = unpack(from_high)
    band_active = activate(jnp.concatenate([from_low[:BAND], from_high[:BAND]], 0), w_edge)
    low_upper, low_lower = exact_halves(edge_counts(low_dst, low_src, mesh_rows, BAND))
    high_upper, high_lower = exact_halves(edge_counts(high_dst, high_src, mesh_rows, BAND))
    side_counts = jnp.concatenate([low_upper, high_upper, low_lower, high_lower], 1)
    aggregate = aggregate + jnp.dot(
        side_counts, jnp.concatenate([band_active, band_active], 0), preferred_element_type=F32
    )

    far_active = activate(got_far[:, :channels], w_edge)
    far_landing = onehot_cols(got_far[:, channels], mesh_rows)
    aggregate = aggregate + jnp.dot(far_landing, far_active, preferred_element_type=F32)

    latent = (mesh_in.astype(F32) + aggregate).astype(BF16)
    normal, inv_std = layer_stats(latent)
    normed = normal.astype(BF16)
    low_normed, high_normed = exchange(normed, normed, "node")

    all_cot = jnp.concatenate([low_cot, cotangent, high_cot], 0)
    grad_att = lax.dot_general(
        all_cot, w_out, (((1,), (1,)), ((), ())), preferred_element_type=F32
    ).astype(BF16)
    grad_heads = grad_att.reshape(3 * mesh_rows, heads, head_dim)

    all_normed = jnp.concatenate([low_normed, normed, high_normed], 0)
    qkv_rows = jnp.dot(all_normed, w_qkv, preferred_element_type=F32).astype(BF16)
    qkv_heads = qkv_rows.reshape(3 * mesh_rows, 3, heads, head_dim)
    query_all, key_all, value_all = qkv_heads[:, 0], qkv_heads[:, 1], qkv_heads[:, 2]
    own = slice(mesh_rows, 2 * mesh_rows)

    place = jnp.arange(3 * mesh_rows, dtype=jnp.int32)
    first = (own_index - 1) * mesh_rows
    inside = (place + first >= 0) & (place + first < devices * mesh_rows)
    all_window = jnp.concatenate([low_window, window, high_window], 1)
    reach_from = place - all_window[0]
    reach_to = place + all_window[1]

    def keep(keys, queries):
        return (
            (place[keys][None, :] >= reach_from[queries][:, None])
            & (place[keys][None, :] <= reach_to[queries][:, None])
            & inside[keys][None, :]
        )

    every = slice(0, 3 * mesh_rows)
    own_query, own_grad = query_all[own], grad_heads[own]
    scores = jnp.einsum("qhe,khe->hqk", own_query, key_all, preferred_element_type=F32) * scale
    scores = jnp.where(keep(every, own)[None], scores, -jnp.inf)
    row_max = jnp.max(scores, -1, keepdims=True)
    shifted = jnp.exp(scores - row_max)
    inv_sum = 1.0 / jnp.sum(shifted, -1, keepdims=True)
    row_probs = shifted * inv_sum
    grad_prob = jnp.einsum("qhe,khe->hqk", own_grad, value_all, preferred_element_type=F32)
    delta = jnp.sum(row_probs * grad_prob, -1, keepdims=True)
    stats = jnp.concatenate([row_max, inv_sum, delta], -1)
    low_stats, high_stats = exchange(stats, stats, "node")

    weights = row_probs.astype(BF16)
    attention = jnp.einsum("hqk,khe->qhe", weights, value_all, preferred_element_type=F32).astype(
        BF16
    )
    mesh_out = (
        latent.astype(F32)
        + jnp.dot(attention.reshape(mesh_rows, channels), w_out, preferred_element_type=F32)
    ).astype(BF16)
    grad_score = (row_probs * (grad_prob - delta)).astype(BF16)
    grad_query = (
        jnp.einsum("hqk,khe->qhe", grad_score, key_all, preferred_element_type=F32) * scale
    )
    grad_key = jnp.einsum(
        "hqk,qhe->khe", grad_score[:, :, own], own_query, preferred_element_type=F32
    )
    grad_value = jnp.einsum(
        "hqk,qhe->khe", weights[:, :, own], own_grad, preferred_element_type=F32
    )

    def near(whole):
        return jnp.concatenate([whole[:mesh_rows], whole[2 * mesh_rows :]], 0)

    near_query, near_grad = near(query_all), near(grad_heads)
    near_stats = jnp.concatenate([low_stats, high_stats], 1)
    near_keep = near(keep(own, every))
    near_scores = (
        jnp.einsum("qhe,khe->hqk", near_query, key_all[own], preferred_element_type=F32) * scale
    )
    near_scores = jnp.where(near_keep[None], near_scores, -jnp.inf)
    near_probs = jnp.exp(near_scores - near_stats[..., :1]) * near_stats[..., 1:2]
    near_grad_prob = jnp.einsum(
        "qhe,khe->hqk", near_grad, value_all[own], preferred_element_type=F32
    )
    near_grad_score = (near_probs * (near_grad_prob - near_stats[..., 2:])).astype(BF16)
    grad_key = grad_key + jnp.einsum(
        "hqk,qhe->khe", near_grad_score, near_query, preferred_element_type=F32
    )
    grad_value = grad_value + jnp.einsum(
        "hqk,qhe->khe", near_probs.astype(BF16), near_grad, preferred_element_type=F32
    )
    grad_qkv = jnp.concatenate(
        [
            grad_query.reshape(mesh_rows, channels),
            (grad_key * scale).reshape(mesh_rows, channels),
            grad_value.reshape(mesh_rows, channels),
        ],
        1,
    ).astype(BF16)
    grad_normed = lax.dot_general(
        grad_qkv, w_qkv, (((1,), (1,)), ((), ())), preferred_element_type=F32
    )
    centred_grad = (
        grad_normed
        - jnp.mean(grad_normed, -1, keepdims=True)
        - normal * jnp.mean(grad_normed * normal, -1, keepdims=True)
    )
    mesh_grad = (cotangent.astype(F32) + inv_std * centred_grad).astype(BF16)
    return (mesh_out, mesh_grad)


def solution(mesh):
    rows = P(("groups", "node"), None)
    flat = P(("groups", "node"))
    placed = (rows, rows) + (flat,) * 8 + (P(None, ("groups", "node")), rows, P(), P(), P())
    return jax.shard_map(
        body, mesh=mesh, in_specs=placed, out_specs=(rows, rows), check_vma=False
    )
```

```python
import functools

import jax
import jax.numpy as jnp
from jax import lax
from jax.experimental import pallas as pl
from jax.experimental.pallas import tpu as pltpu
from jax.sharding import PartitionSpec as P

HEADS = 16
BAND = 128
LANES = 128
F32 = jnp.float32
BF16 = jnp.bfloat16
I32 = jnp.int32
VMEM_LIMIT = 44 * 2**20


def mm(a, b):
    return lax.dot_general(a, b, (((1,), (0,)), ((), ())), preferred_element_type=F32)


def mm_nt(a, b):
    return lax.dot_general(a, b, (((1,), (1,)), ((), ())), preferred_element_type=F32)


def mm_tn(a, b):
    return lax.dot_general(a, b, (((0,), (0,)), ((), ())), preferred_element_type=F32)


def iota(shape, dim):
    return lax.broadcasted_iota(I32, shape, dim)


def call(kernel, outs, args, smem=(), name=None):
    specs = [
        pl.BlockSpec(memory_space=pltpu.SMEM if i in smem else pltpu.VMEM)
        for i in range(len(args))
    ]
    return pl.pallas_call(
        kernel,
        out_shape=[jax.ShapeDtypeStruct(shape, dtype) for shape, dtype in outs],
        in_specs=specs,
        out_specs=[pl.BlockSpec(memory_space=pltpu.VMEM) for _ in outs],
        compiler_params=pltpu.CompilerParams(vmem_limit_bytes=VMEM_LIMIT),
        name=name,
    )(*args)


def exchange(toward_low, toward_high, axis):
    ends = lax.axis_size(axis) - 1
    from_high = lax.ppermute(toward_low, axis, [(i + 1, i) for i in range(ends)])
    from_low = lax.ppermute(toward_high, axis, [(i, i + 1) for i in range(ends)])
    return from_low, from_high


def gelu(projected):
    x = projected.astype(BF16).astype(F32)
    inner = (2.0 / jnp.pi) ** 0.5 * (x + 0.044715 * (x * x * x))
    return (0.5 * x * (1.0 + jnp.tanh(inner))).astype(BF16)


def onehot_rows(index_rows, count):
    parts = [
        jnp.where(iota((count, row.shape[1]), 0) == row, 1.0, 0.0).astype(BF16)
        for row in index_rows
    ]
    return parts[0] if len(parts) == 1 else jnp.concatenate(parts, 1)


def norm_stats(latent):
    values = latent.astype(F32)
    row_mean = jnp.mean(values, -1, keepdims=True)
    centred = values - row_mean
    variance = jnp.mean(centred * centred, -1, keepdims=True)
    inv_std = lax.rsqrt(variance + 1e-05)
    return centred * inv_std, inv_std


def pack_kernel(
    far_count, side_count, grid, cot, window, side_src, side_dst, far_src, far_dst, far_out, low_out, high_out
):
    grid_rows, channels = grid.shape
    mesh_rows = cot.shape[0]
    slots = far_src.shape[1]
    devices = far_count.shape[0]
    depth = slots // devices
    slot = iota((1, slots), 1)
    live = jnp.zeros((1, slots), I32)
    for r in range(devices):
        live = jnp.where(slot // depth == r, far_count[r], live)
    target = jnp.where(slot % depth < live, far_dst[...], mesh_rows).astype(F32)
    place = slot // depth * (2 * depth) + slot % depth
    select = onehot_rows([far_src[...]], grid_rows)
    spread = mm_nt(select, onehot_rows([place], 2 * slots)).astype(BF16)
    rows = mm_tn(spread, grid[...])
    column = jnp.sum(
        jnp.where(iota((2 * slots, slots), 0) == place + depth, target, 0.0), 1, keepdims=True
    )
    far_out[...] = (rows + column).astype(BF16)
    count = side_src.shape[0] // 2
    for k, out in ((0, low_out), (1, high_out)):
        start = 0 if k == 0 else grid_rows - BAND
        out[:BAND] = grid[start : start + BAND]
        out[BAND : BAND + mesh_rows] = cot[...]
        rank = iota((count, LANES), 0) * LANES + iota((count, LANES), 1)
        src = side_src[k * count : (k + 1) * count] - start
        dst = jnp.where(rank < side_count[k], side_dst[k * count : (k + 1) * count], mesh_rows)
        reach = jnp.concatenate([window[...], jnp.zeros((count - 2, mesh_rows), I32)], 0)
        blank = jnp.zeros((count, channels - 2 * LANES - mesh_rows), I32)
        meta = jnp.concatenate([src, dst, reach, blank], 1)
        out[BAND + mesh_rows :] = meta.astype(F32).astype(BF16)


def own_kernel(grid, w_edge, mesh_in, own_src, own_dst, cot, w_out, partial_out, grad_out):
    grid_rows = grid.shape[0]
    mesh_rows = mesh_in.shape[0]
    active = gelu(mm(grid[...], w_edge[...]))
    rows = own_src.shape[0]
    src = onehot_rows([own_src[r : r + 1] for r in range(rows)], grid_rows)
    dst = onehot_rows([own_dst[r : r + 1] for r in range(rows)], mesh_rows)
    counts = mm_nt(dst, src).astype(BF16)
    partial_out[...] = mesh_in[...].astype(F32) + mm(counts, active)
    grad_out[...] = mm_nt(cot[...], w_out[...]).astype(BF16)


def side_kernel(low, high, w_edge, w_out, partial, partial_out, grad_out, window_out):
    mesh_rows = partial.shape[0]
    active = gelu(mm(jnp.concatenate([low[:BAND], high[:BAND]], 0), w_edge[...]))
    uppers, lowers = [], []
    for side in (low, high):
        meta = side[BAND + mesh_rows :].astype(F32).astype(I32)
        count = meta.shape[0]
        src = onehot_rows([meta[r : r + 1, :LANES] for r in range(count)], BAND)
        dst = onehot_rows([meta[r : r + 1, LANES : 2 * LANES] for r in range(count)], mesh_rows)
        counts = mm_nt(dst, src)
        upper = counts.astype(BF16)
        uppers.append(upper)
        lowers.append((counts - upper.astype(F32)).astype(BF16))
        reach = meta[:8, 2 * LANES : 2 * LANES + mesh_rows]
        at = 0 if side is low else mesh_rows
        window_out[:, at : at + mesh_rows] = reach
    counts = jnp.concatenate(uppers + lowers, 1)
    partial_out[...] = partial[...] + mm(counts, jnp.concatenate([active, active], 0))
    both = jnp.concatenate([low[BAND : BAND + mesh_rows], high[BAND : BAND + mesh_rows]], 0)
    grad_out[...] = mm_nt(both, w_out[...]).astype(BF16)


def latent_kernel(depth, far, w_edge, partial, latent_out, normed_out):
    mesh_rows = partial.shape[0]
    slots = far.shape[0]
    rows = far[...]
    active = gelu(mm(rows, w_edge[...]))
    target = pltpu.roll(rows[:, :LANES].astype(F32), slots - depth, 0)
    target = target if mesh_rows == LANES else jnp.broadcast_to(target[:, :1], (slots, mesh_rows))
    is_row = iota((slots, mesh_rows), 0) % (2 * depth) < depth
    hit = (target == iota((slots, mesh_rows), 1).astype(F32)) & is_row
    landing = jnp.where(hit, 1.0, 0.0).astype(BF16)
    latent = (partial[...] + mm_tn(landing, active)).astype(BF16)
    latent_out[...] = latent
    normal, _ = norm_stats(latent)
    normed_out[...] = normal.astype(BF16)


def project_kernel(normed, w_qkv, qkv_out):
    qkv_out[...] = mm(normed[...], w_qkv[...]).astype(BF16)


def halves(rows, scale=None):
    first = iota(rows.shape, 1) < rows.shape[1] // 2
    if scale is not None:
        rows = rows * jnp.asarray(scale, rows.dtype)
    zero = jnp.zeros_like(rows)
    return jnp.concatenate([jnp.where(first, rows, zero), jnp.where(first, zero, rows)], 0)


def merge(stacked):
    m = stacked.shape[0] // 2
    first = iota((m, stacked.shape[1]), 1) < stacked.shape[1] // 2
    return jnp.where(first, stacked[:m], stacked[m:])


def attend_kernel(
    scale,
    pair,
    low_normed,
    high_normed,
    w_qkv,
    own_qkv,
    own_grad,
    window,
    stats_out,
    att_out,
    gq_out,
    gk_out,
    gv_out,
    near_q_out,
    kv,
):
    m, channels = low_normed.shape
    devices = lax.axis_size("node")
    me = lax.axis_index("node")
    near = mm(jnp.concatenate([low_normed[...], high_normed[...]], 0), w_qkv[...]).astype(BF16)
    near_q_out[...] = near[:, :channels] * jnp.asarray(scale, BF16)
    kv[:m] = near[:m, channels:]
    kv[m : 2 * m] = own_qkv[:, channels:]
    kv[2 * m :] = near[m:, channels:]
    key_at = iota((3 * m, m), 0)
    query_at = iota((3 * m, m), 1) + m
    inside = (key_at >= jnp.where(me == 0, m, 0)) & (
        key_at < jnp.where(me == devices - 1, 2 * m, 3 * m)
    )
    keep = (
        inside & (key_at >= query_at - window[0:1, :]) & (key_at <= query_at + window[1:2, :])
    )
    bias = jnp.where(keep, 0.0, -jnp.inf).astype(F32)
    bias = jnp.concatenate([bias, bias], 1)
    pairs = channels // pair
    for p in range(pairs):
        cols = slice(p * pair, (p + 1) * pair)
        key = kv[:, cols]
        value = kv[:, channels + p * pair : channels + (p + 1) * pair]
        q2 = halves(own_qkv[:, cols], scale)
        g2 = halves(own_grad[:, cols])
        scores = mm_nt(key, q2) + bias
        top = jnp.max(scores, 0, keepdims=True)
        shifted = jnp.exp(scores - top)
        inv_sum = 1.0 / jnp.sum(shifted, 0, keepdims=True)
        probs = shifted * inv_sum
        weights = probs.astype(BF16)
        grad_prob = mm_nt(value, g2)
        delta = jnp.sum(probs * grad_prob, 0, keepdims=True)
        grad_score = (probs * (grad_prob - delta)).astype(BF16)
        stats_out[p : p + 1] = top
        stats_out[pairs + p : pairs + p + 1] = inv_sum
        stats_out[2 * pairs + p : 2 * pairs + p + 1] = delta
        att_out[:, cols] = merge(mm_tn(weights, value)).astype(BF16)
        gq_out[:, cols] = (merge(mm_tn(grad_score, key)) * scale).astype(BF16)
        gk_out[:, cols] = mm(grad_score[m : 2 * m], q2)
        gv_out[:, cols] = mm(weights[m : 2 * m], g2)


def output_kernel(latent, attention, w_out, grad_query, w_qkv, mesh_out, grad_normed):
    channels = latent.shape[1]
    mesh_out[...] = (latent[...].astype(F32) + mm(attention[...], w_out[...])).astype(BF16)
    grad_normed[...] = mm_nt(grad_query[...], w_qkv[:, :channels])


def finish_kernel(
    pair,
    low_stats,
    high_stats,
    near_window,
    near_q,
    near_grad,
    own_qkv,
    grad_key,
    grad_value,
    grad_normed,
    w_qkv,
    latent,
    cot,
    grad_out,
    grad_kv,
):
    m, channels = latent.shape
    key_at = iota((m, 2 * m), 0) + m
    lane = iota((m, 2 * m), 1)
    query_at = jnp.where(lane < m, lane, lane + m)
    keep = (key_at >= query_at - near_window[0:1, :]) & (key_at <= query_at + near_window[1:2, :])
    bias = jnp.where(keep, 0.0, -jnp.inf).astype(F32)
    pairs = channels // pair

    def stat(row, second):
        lanes = slice(m, 2 * m) if second else slice(0, m)
        return jnp.concatenate([low_stats[row : row + 1, lanes], high_stats[row : row + 1, lanes]], 1)

    for p in range(pairs):
        cols = slice(p * pair, (p + 1) * pair)
        key2 = halves(own_qkv[:, channels + p * pair : channels + (p + 1) * pair])
        value2 = halves(own_qkv[:, 2 * channels + p * pair : 2 * channels + (p + 1) * pair])
        query = near_q[:, cols]
        grad = near_grad[:, cols]
        scores = mm_nt(key2, query)
        grad_prob = mm_nt(value2, grad)
        weights, grad_scores = [], []
        for h in range(2):
            half = slice(h * m, (h + 1) * m)
            probs = jnp.exp(scores[half] + bias - stat(p, h)) * stat(pairs + p, h)
            weights.append(probs.astype(BF16))
            grad_scores.append((probs * (grad_prob[half] - stat(2 * pairs + p, h))).astype(BF16))
        gk = grad_key[:, cols] + merge(mm(jnp.concatenate(grad_scores, 0), query))
        gv = grad_value[:, cols] + merge(mm(jnp.concatenate(weights, 0), grad))
        grad_kv[:, cols] = gk.astype(BF16)
        grad_kv[:, channels + p * pair : channels + (p + 1) * pair] = gv.astype(BF16)
    total = grad_normed[...] + mm_nt(grad_kv[...], w_qkv[:, channels:])
    normal, inv_std = norm_stats(latent[...])
    centred = (
        total
        - jnp.mean(total, -1, keepdims=True)
        - normal * jnp.mean(total * normal, -1, keepdims=True)
    )
    grad_out[...] = (cot[...].astype(F32) + inv_std * centred).astype(BF16)


def body(
    grid_in,
    mesh_in,
    own_src,
    own_dst,
    side_src,
    side_dst,
    side_count,
    far_src,
    far_dst,
    far_count,
    window,
    cotangent,
    w_edge,
    w_qkv,
    w_out,
):
    devices = lax.axis_size("node")
    grid_rows, channels = grid_in.shape
    m = mesh_in.shape[0]
    far_slots = far_src.shape[0]
    far_depth = far_slots // devices
    head_dim = channels // HEADS
    pair = 2 * head_dim
    pairs = channels // pair
    scale = head_dim ** (-0.5)
    meta_rows = side_src.shape[0] // (2 * LANES)

    far_message, toward_low, toward_high = call(
        pack_kernel,
        [
            ((2 * far_slots, channels), BF16),
            ((BAND + m + meta_rows, channels), BF16),
            ((BAND + m + meta_rows, channels), BF16),
        ],
        [
            far_count,
            side_count,
            grid_in,
            cotangent,
            window,
            side_src.reshape(-1, LANES),
            side_dst.reshape(-1, LANES),
            far_src.reshape(1, far_slots),
            far_dst.reshape(1, far_slots),
        ],
        smem=(0, 1),
        name="pack",
    )
    got_far = lax.all_to_all(
        far_message.reshape(devices, 2 * far_depth, channels),
        "node",
        split_axis=0,
        concat_axis=0,
        tiled=True,
    ).reshape(2 * far_slots, channels)
    from_low, from_high = exchange(toward_low, toward_high, "node")

    partial, own_grad = call(
        own_kernel,
        [((m, channels), F32), ((m, channels), BF16)],
        [
            grid_in,
            w_edge,
            mesh_in,
            own_src.reshape(-1, LANES),
            own_dst.reshape(-1, LANES),
            cotangent,
            w_out,
        ],
        name="own",
    )
    partial, near_grad, near_window = call(
        side_kernel,
        [((m, channels), F32), ((2 * m, channels), BF16), ((8, 2 * m), I32)],
        [from_low, from_high, w_edge, w_out, partial],
        name="side",
    )
    latent, normed = call(
        functools.partial(latent_kernel, far_depth),
        [((m, channels), BF16), ((m, channels), BF16)],
        [got_far, w_edge, partial],
        name="latent",
    )
    low_normed, high_normed = exchange(normed, normed, "node")
    (own_qkv,) = call(project_kernel, [((m, 3 * channels), BF16)], [normed, w_qkv], name="project")

    stats, attention, grad_query, grad_key, grad_value, near_q = pl.pallas_call(
        functools.partial(attend_kernel, scale, pair),
        out_shape=[
            jax.ShapeDtypeStruct((3 * pairs, 2 * m), F32),
            jax.ShapeDtypeStruct((m, channels), BF16),
            jax.ShapeDtypeStruct((m, channels), BF16),
            jax.ShapeDtypeStruct((m, channels), F32),
            jax.ShapeDtypeStruct((m, channels), F32),
            jax.ShapeDtypeStruct((2 * m, channels), BF16),
        ],
        in_specs=[pl.BlockSpec(memory_space=pltpu.VMEM)] * 6,
        out_specs=[pl.BlockSpec(memory_space=pltpu.VMEM)] * 6,
        scratch_shapes=[pltpu.VMEM((3 * m, 2 * channels), BF16)],
        compiler_params=pltpu.CompilerParams(vmem_limit_bytes=VMEM_LIMIT),
        name="attend",
    )(low_normed, high_normed, w_qkv, own_qkv, own_grad, window)
    low_stats, high_stats = exchange(stats, stats, "node")

    mesh_out, grad_normed = call(
        output_kernel,
        [((m, channels), BF16), ((m, channels), F32)],
        [latent, attention, w_out, grad_query, w_qkv],
        name="output",
    )
    mesh_grad = pl.pallas_call(
        functools.partial(finish_kernel, pair),
        out_shape=jax.ShapeDtypeStruct((m, channels), BF16),
        in_specs=[pl.BlockSpec(memory_space=pltpu.VMEM)] * 12,
        out_specs=pl.BlockSpec(memory_space=pltpu.VMEM),
        scratch_shapes=[pltpu.VMEM((m, 2 * channels), BF16)],
        compiler_params=pltpu.CompilerParams(vmem_limit_bytes=VMEM_LIMIT),
        name="finish",
    )(
        low_stats,
        high_stats,
        near_window,
        near_q,
        near_grad,
        own_qkv,
        grad_key,
        grad_value,
        grad_normed,
        w_qkv,
        latent,
        cotangent,
    )
    return (mesh_out, mesh_grad)


def solution(mesh):
    rows = P(("groups", "node"), None)
    flat = P(("groups", "node"))
    placed = (rows, rows) + (flat,) * 8 + (P(None, ("groups", "node")), rows, P(), P(), P())
    return jax.shard_map(
        body, mesh=mesh, in_specs=placed, out_specs=(rows, rows), check_vma=False
    )
```

```python
import functools

import jax
import jax.numpy as jnp
from jax import lax
from jax.experimental import pallas as pl
from jax.experimental.pallas import tpu as pltpu
from jax.sharding import PartitionSpec as P

HEADS = 16
BAND = 128
LANES = 128
F32 = jnp.float32
BF16 = jnp.bfloat16
I32 = jnp.int32
VMEM_LIMIT = 28 * 2**20


def mm(a, b):
    return lax.dot_general(a, b, (((1,), (0,)), ((), ())), preferred_element_type=F32)


def mm_nt(a, b):
    return lax.dot_general(a, b, (((1,), (1,)), ((), ())), preferred_element_type=F32)


def mm_tn(a, b):
    return lax.dot_general(a, b, (((0,), (0,)), ((), ())), preferred_element_type=F32)


def iota(shape, dim):
    return lax.broadcasted_iota(I32, shape, dim)


def call(kernel, outs, args, hbm=(), scratch=(), name=None):
    args = [pltpu.with_memory_space_constraint(a, pltpu.HBM) if i in hbm else a for i, a in enumerate(args)]
    specs = [
        pl.BlockSpec(memory_space=pltpu.HBM if i in hbm else pltpu.VMEM) for i in range(len(args))
    ]
    return pl.pallas_call(
        kernel,
        out_shape=[jax.ShapeDtypeStruct(shape, dtype) for shape, dtype in outs],
        in_specs=specs,
        out_specs=[pl.BlockSpec(memory_space=pltpu.VMEM) for _ in outs],
        scratch_shapes=list(scratch),
        compiler_params=pltpu.CompilerParams(vmem_limit_bytes=VMEM_LIMIT),
        name=name,
    )(*args)


def start_all(pairs, sems):
    copies = [pltpu.make_async_copy(src, dst, sems.at[i]) for i, (src, dst) in enumerate(pairs)]
    for copy in copies:
        copy.start()
    return copies


def like(*arrays):
    return [pltpu.VMEM(a.shape, a.dtype) for a in arrays]


def exchange(toward_low, toward_high, axis):
    ends = lax.axis_size(axis) - 1
    from_high = lax.ppermute(toward_low, axis, [(i + 1, i) for i in range(ends)])
    from_low = lax.ppermute(toward_high, axis, [(i, i + 1) for i in range(ends)])
    return from_low, from_high


def gelu(projected):
    x = projected.astype(BF16).astype(F32)
    inner = (2.0 / jnp.pi) ** 0.5 * (x + 0.044715 * (x * x * x))
    return (0.5 * x * (1.0 + jnp.tanh(inner))).astype(BF16)


def onehot_rows(index_rows, count):
    parts = [
        jnp.where(iota((count, row.shape[1]), 0) == row, 1.0, 0.0).astype(BF16)
        for row in index_rows
    ]
    return parts[0] if len(parts) == 1 else jnp.concatenate(parts, 1)


def norm_stats(latent):
    values = latent.astype(F32)
    row_mean = jnp.mean(values, -1, keepdims=True)
    centred = values - row_mean
    variance = jnp.mean(centred * centred, -1, keepdims=True)
    inv_std = lax.rsqrt(variance + 1e-05)
    return centred * inv_std, inv_std


def pack_kernel(
    grid_hbm,
    cot_hbm,
    window_hbm,
    side_src_hbm,
    side_dst_hbm,
    side_count_hbm,
    far_src_hbm,
    far_dst_hbm,
    far_count_hbm,
    far_out,
    low_out,
    high_out,
    grid,
    window,
    side_src,
    side_dst,
    side_count,
    far_src,
    far_dst,
    far_count,
    sems,
):
    grid_rows, channels = grid.shape
    mesh_rows = cot_hbm.shape[0]
    slots = far_src.shape[1]
    devices = far_count.shape[1]
    depth = slots // devices
    first = grid_rows - BAND
    copies = start_all(
        [
            (far_src_hbm, far_src),
            (far_dst_hbm, far_dst),
            (far_count_hbm, far_count),
            (grid_hbm, grid),
            (side_src_hbm, side_src),
            (side_dst_hbm, side_dst),
            (side_count_hbm, side_count),
            (window_hbm, window),
            (grid_hbm.at[pl.ds(0, BAND)], low_out.at[pl.ds(0, BAND)]),
            (grid_hbm.at[pl.ds(first, BAND)], high_out.at[pl.ds(0, BAND)]),
            (cot_hbm, low_out.at[pl.ds(BAND, mesh_rows)]),
            (cot_hbm, high_out.at[pl.ds(BAND, mesh_rows)]),
        ],
        sems,
    )
    for copy in copies[:4]:
        copy.wait()
    slot = iota((1, slots), 1)
    receiver = jnp.where(iota((devices, slots), 0) == iota((devices, slots), 1) // depth, 1.0, 0.0)
    live = mm(far_count[...].astype(F32).astype(BF16), receiver.astype(BF16))
    target = jnp.where((slot % depth).astype(F32) < live, far_dst[...].astype(F32), 1.0 * mesh_rows)
    place = slot // depth * (2 * depth) + slot % depth
    select = onehot_rows([far_src[...]], grid_rows)
    spread = mm_nt(select, onehot_rows([place], 2 * slots)).astype(BF16)
    rows = mm_tn(spread, grid[...])
    column = jnp.sum(
        jnp.where(iota((2 * slots, slots), 0) == place + depth, target, 0.0), 1, keepdims=True
    )
    far_out[...] = (rows + column).astype(BF16)
    for copy in copies[4:]:
        copy.wait()
    count = side_src.shape[0] // 2
    for k, out in ((0, low_out), (1, high_out)):
        rank = iota((count, LANES), 0) * LANES + iota((count, LANES), 1)
        src = side_src[k * count : (k + 1) * count] - k * first
        live = rank < side_count[:, k : k + 1]
        dst = jnp.where(live, side_dst[k * count : (k + 1) * count], mesh_rows)
        reach = jnp.concatenate([window[...], jnp.zeros((count - 2, mesh_rows), I32)], 0)
        blank = jnp.zeros((count, channels - 2 * LANES - mesh_rows), I32)
        meta = jnp.concatenate([src, dst, reach, blank], 1)
        out[BAND + mesh_rows :] = meta.astype(F32).astype(BF16)


def own_kernel(
    grid_hbm,
    mesh_in_hbm,
    own_src_hbm,
    own_dst_hbm,
    cot_hbm,
    w_edge_hbm,
    w_out_hbm,
    w_qkv_hbm,
    partial_out,
    grad_out,
    w_edge,
    w_out,
    w_qkv,
    grid,
    mesh_in,
    own_src,
    own_dst,
    cot,
    sems,
):
    grid_rows = grid.shape[0]
    mesh_rows = mesh_in.shape[0]
    copies = start_all(
        [
            (own_src_hbm, own_src),
            (own_dst_hbm, own_dst),
            (w_edge_hbm, w_edge),
            (grid_hbm, grid),
            (mesh_in_hbm, mesh_in),
            (cot_hbm, cot),
            (w_out_hbm, w_out),
            (w_qkv_hbm, w_qkv),
        ],
        sems,
    )
    for copy in copies[:2]:
        copy.wait()
    rows = own_src.shape[0]
    src = onehot_rows([own_src[r : r + 1] for r in range(rows)], grid_rows)
    dst = onehot_rows([own_dst[r : r + 1] for r in range(rows)], mesh_rows)
    counts = mm_nt(dst, src).astype(BF16)
    for copy in copies[2:5]:
        copy.wait()
    active = gelu(mm(grid[...], w_edge[...]))
    partial_out[...] = mesh_in[...].astype(F32) + mm(counts, active)
    for copy in copies[5:7]:
        copy.wait()
    grad_out[...] = mm_nt(cot[...], w_out[...]).astype(BF16)
    copies[7].wait()


def side_kernel(low, high, w_edge, w_out, partial, partial_out, grad_out, window_out):
    mesh_rows = partial.shape[0]
    active = gelu(mm(jnp.concatenate([low[:BAND], high[:BAND]], 0), w_edge[...]))
    uppers, lowers = [], []
    for side in (low, high):
        meta = side[BAND + mesh_rows :].astype(F32).astype(I32)
        count = meta.shape[0]
        src = onehot_rows([meta[r : r + 1, :LANES] for r in range(count)], BAND)
        dst = onehot_rows([meta[r : r + 1, LANES : 2 * LANES] for r in range(count)], mesh_rows)
        counts = mm_nt(dst, src)
        upper = counts.astype(BF16)
        uppers.append(upper)
        lowers.append((counts - upper.astype(F32)).astype(BF16))
        reach = meta[:8, 2 * LANES : 2 * LANES + mesh_rows]
        at = 0 if side is low else mesh_rows
        window_out[:, at : at + mesh_rows] = reach
    counts = jnp.concatenate(uppers + lowers, 1)
    partial_out[...] = partial[...] + mm(counts, jnp.concatenate([active, active], 0))
    both = jnp.concatenate([low[BAND : BAND + mesh_rows], high[BAND : BAND + mesh_rows]], 0)
    grad_out[...] = mm_nt(both, w_out[...]).astype(BF16)


def latent_kernel(depth, far, w_edge, partial, latent_out, normed_out):
    mesh_rows = partial.shape[0]
    slots = far.shape[0]
    rows = far[...]
    active = gelu(mm(rows, w_edge[...]))
    target = pltpu.roll(rows[:, :LANES].astype(F32), slots - depth, 0)
    target = target if mesh_rows == LANES else jnp.broadcast_to(target[:, :1], (slots, mesh_rows))
    is_row = iota((slots, mesh_rows), 0) % (2 * depth) < depth
    hit = (target == iota((slots, mesh_rows), 1).astype(F32)) & is_row
    landing = jnp.where(hit, 1.0, 0.0).astype(BF16)
    latent = (partial[...] + mm_tn(landing, active)).astype(BF16)
    latent_out[...] = latent
    normal, _ = norm_stats(latent)
    normed_out[...] = normal.astype(BF16)


def project_kernel(normed, w_qkv, qkv_out):
    qkv_out[...] = mm(normed[...], w_qkv[...]).astype(BF16)


def halves(rows, scale=None):
    first = iota(rows.shape, 1) < rows.shape[1] // 2
    if scale is not None:
        rows = rows * jnp.asarray(scale, rows.dtype)
    zero = jnp.zeros_like(rows)
    return jnp.concatenate([jnp.where(first, rows, zero), jnp.where(first, zero, rows)], 0)


def merge(stacked):
    m = stacked.shape[0] // 2
    first = iota((m, stacked.shape[1]), 1) < stacked.shape[1] // 2
    return jnp.where(first, stacked[:m], stacked[m:])


def attend_kernel(
    scale,
    pair,
    low_normed,
    high_normed,
    w_qkv,
    own_qkv,
    own_grad,
    window_hbm,
    stats_out,
    att_out,
    gq_out,
    gk_out,
    gv_out,
    near_q_out,
    kv,
    window,
    sems,
):
    fetch = start_all([(window_hbm, window)], sems)
    m, channels = low_normed.shape
    devices = lax.axis_size("node")
    me = lax.axis_index("node")
    near = mm(jnp.concatenate([low_normed[...], high_normed[...]], 0), w_qkv[...]).astype(BF16)
    near_q_out[...] = near[:, :channels] * jnp.asarray(scale, BF16)
    kv[:m] = near[:m, channels:]
    kv[m : 2 * m] = own_qkv[:, channels:]
    kv[2 * m :] = near[m:, channels:]
    fetch[0].wait()
    key_at = iota((3 * m, m), 0)
    query_at = iota((3 * m, m), 1) + m
    inside = (key_at >= jnp.where(me == 0, m, 0)) & (
        key_at < jnp.where(me == devices - 1, 2 * m, 3 * m)
    )
    keep = (
        inside & (key_at >= query_at - window[0:1, :]) & (key_at <= query_at + window[1:2, :])
    )
    bias = jnp.where(keep, 0.0, -jnp.inf).astype(F32)
    bias = jnp.concatenate([bias, bias], 1)
    pairs = channels // pair
    for p in range(pairs):
        cols = slice(p * pair, (p + 1) * pair)
        key = kv[:, cols]
        value = kv[:, channels + p * pair : channels + (p + 1) * pair]
        q2 = halves(own_qkv[:, cols], scale)
        g2 = halves(own_grad[:, cols])
        scores = mm_nt(key, q2) + bias
        top = jnp.max(scores, 0, keepdims=True)
        shifted = jnp.exp(scores - top)
        inv_sum = 1.0 / jnp.sum(shifted, 0, keepdims=True)
        probs = shifted * inv_sum
        weights = probs.astype(BF16)
        grad_prob = mm_nt(value, g2)
        delta = jnp.sum(probs * grad_prob, 0, keepdims=True)
        grad_score = (probs * (grad_prob - delta)).astype(BF16)
        stats_out[p : p + 1] = top
        stats_out[pairs + p : pairs + p + 1] = inv_sum
        stats_out[2 * pairs + p : 2 * pairs + p + 1] = delta
        att_out[:, cols] = merge(mm_tn(weights, value)).astype(BF16)
        gq_out[:, cols] = (merge(mm_tn(grad_score, key)) * scale).astype(BF16)
        gk_out[:, cols] = mm(grad_score[m : 2 * m], q2)
        gv_out[:, cols] = mm(weights[m : 2 * m], g2)


def output_kernel(latent, attention, w_out, grad_query, w_qkv, mesh_out, grad_normed):
    channels = latent.shape[1]
    mesh_out[...] = (latent[...].astype(F32) + mm(attention[...], w_out[...])).astype(BF16)
    grad_normed[...] = mm_nt(grad_query[...], w_qkv[:, :channels])


def finish_kernel(
    pair,
    low_stats,
    high_stats,
    near_window,
    near_q,
    near_grad,
    own_qkv,
    grad_key,
    grad_value,
    grad_normed,
    w_qkv,
    latent,
    cot_hbm,
    grad_out,
    grad_kv,
    cot,
    sems,
):
    fetch = start_all([(cot_hbm, cot)], sems)
    m, channels = latent.shape
    key_at = iota((m, 2 * m), 0) + m
    lane = iota((m, 2 * m), 1)
    query_at = jnp.where(lane < m, lane, lane + m)
    keep = (key_at >= query_at - near_window[0:1, :]) & (key_at <= query_at + near_window[1:2, :])
    bias = jnp.where(keep, 0.0, -jnp.inf).astype(F32)
    pairs = channels // pair

    def stat(row, second):
        lanes = slice(m, 2 * m) if second else slice(0, m)
        return jnp.concatenate([low_stats[row : row + 1, lanes], high_stats[row : row + 1, lanes]], 1)

    for p in range(pairs):
        cols = slice(p * pair, (p + 1) * pair)
        key2 = halves(own_qkv[:, channels + p * pair : channels + (p + 1) * pair])
        value2 = halves(own_qkv[:, 2 * channels + p * pair : 2 * channels + (p + 1) * pair])
        query = near_q[:, cols]
        grad = near_grad[:, cols]
        scores = mm_nt(key2, query)
        grad_prob = mm_nt(value2, grad)
        weights, grad_scores = [], []
        for h in range(2):
            half = slice(h * m, (h + 1) * m)
            probs = jnp.exp(scores[half] + bias - stat(p, h)) * stat(pairs + p, h)
            weights.append(probs.astype(BF16))
            grad_scores.append((probs * (grad_prob[half] - stat(2 * pairs + p, h))).astype(BF16))
        gk = grad_key[:, cols] + merge(mm(jnp.concatenate(grad_scores, 0), query))
        gv = grad_value[:, cols] + merge(mm(jnp.concatenate(weights, 0), grad))
        grad_kv[:, cols] = gk.astype(BF16)
        grad_kv[:, channels + p * pair : channels + (p + 1) * pair] = gv.astype(BF16)
    total = grad_normed[...] + mm_nt(grad_kv[...], w_qkv[:, channels:])
    normal, inv_std = norm_stats(latent[...])
    centred = (
        total
        - jnp.mean(total, -1, keepdims=True)
        - normal * jnp.mean(total * normal, -1, keepdims=True)
    )
    fetch[0].wait()
    grad_out[...] = (cot[...].astype(F32) + inv_std * centred).astype(BF16)


def body(
    grid_in,
    mesh_in,
    own_src,
    own_dst,
    side_src,
    side_dst,
    side_count,
    far_src,
    far_dst,
    far_count,
    window,
    cotangent,
    w_edge,
    w_qkv,
    w_out,
):
    devices = lax.axis_size("node")
    grid_rows, channels = grid_in.shape
    m = mesh_in.shape[0]
    far_slots = far_src.shape[0]
    far_depth = far_slots // devices
    head_dim = channels // HEADS
    pair = 2 * head_dim
    pairs = channels // pair
    scale = head_dim ** (-0.5)
    meta_rows = side_src.shape[0] // (2 * LANES)

    side_src, side_dst = side_src.reshape(-1, LANES), side_dst.reshape(-1, LANES)
    own_src, own_dst = own_src.reshape(-1, LANES), own_dst.reshape(-1, LANES)
    far_src, far_dst = far_src.reshape(1, -1), far_dst.reshape(1, -1)
    side_count, far_count = side_count.reshape(1, -1), far_count.reshape(1, -1)
    far_message, toward_low, toward_high = call(
        pack_kernel,
        [
            ((2 * far_slots, channels), BF16),
            ((BAND + m + meta_rows, channels), BF16),
            ((BAND + m + meta_rows, channels), BF16),
        ],
        [
            grid_in,
            cotangent,
            window,
            side_src,
            side_dst,
            side_count,
            far_src,
            far_dst,
            far_count,
        ],
        hbm=range(9),
        scratch=like(
            grid_in, window, side_src, side_dst, side_count, far_src, far_dst, far_count
        )
        + [pltpu.SemaphoreType.DMA((12,))],
        name="pack",
    )
    got_far = lax.all_to_all(
        far_message.reshape(devices, 2 * far_depth, channels),
        "node",
        split_axis=0,
        concat_axis=0,
        tiled=True,
    ).reshape(2 * far_slots, channels)
    from_low, from_high = exchange(toward_low, toward_high, "node")

    partial, own_grad, w_edge, w_out, w_qkv = call(
        own_kernel,
        [
            ((m, channels), F32),
            ((m, channels), BF16),
            (w_edge.shape, BF16),
            (w_out.shape, BF16),
            (w_qkv.shape, BF16),
        ],
        [grid_in, mesh_in, own_src, own_dst, cotangent, w_edge, w_out, w_qkv],
        hbm=range(8),
        scratch=like(grid_in, mesh_in, own_src, own_dst, cotangent)
        + [pltpu.SemaphoreType.DMA((8,))],
        name="own",
    )
    partial, near_grad, near_window = call(
        side_kernel,
        [((m, channels), F32), ((2 * m, channels), BF16), ((8, 2 * m), I32)],
        [from_low, from_high, w_edge, w_out, partial],
        name="side",
    )
    latent, normed = call(
        functools.partial(latent_kernel, far_depth),
        [((m, channels), BF16), ((m, channels), BF16)],
        [got_far, w_edge, partial],
        name="latent",
    )
    low_normed, high_normed = exchange(normed, normed, "node")
    (own_qkv,) = call(project_kernel, [((m, 3 * channels), BF16)], [normed, w_qkv], name="project")

    stats, attention, grad_query, grad_key, grad_value, near_q = call(
        functools.partial(attend_kernel, scale, pair),
        [
            ((3 * pairs, 2 * m), F32),
            ((m, channels), BF16),
            ((m, channels), BF16),
            ((m, channels), F32),
            ((m, channels), F32),
            ((2 * m, channels), BF16),
        ],
        [low_normed, high_normed, w_qkv, own_qkv, own_grad, window],
        hbm=(5,),
        scratch=[pltpu.VMEM((3 * m, 2 * channels), BF16)]
        + like(window)
        + [pltpu.SemaphoreType.DMA((1,))],
        name="attend",
    )
    low_stats, high_stats = exchange(stats, stats, "node")

    mesh_out, grad_normed = call(
        output_kernel,
        [((m, channels), BF16), ((m, channels), F32)],
        [latent, attention, w_out, grad_query, w_qkv],
        name="output",
    )
    (mesh_grad,) = call(
        functools.partial(finish_kernel, pair),
        [((m, channels), BF16)],
        [
            low_stats,
            high_stats,
            near_window,
            near_q,
            near_grad,
            own_qkv,
            grad_key,
            grad_value,
            grad_normed,
            w_qkv,
            latent,
            cotangent,
        ],
        hbm=(11,),
        scratch=[pltpu.VMEM((m, 2 * channels), BF16)]
        + like(cotangent)
        + [pltpu.SemaphoreType.DMA((1,))],
        name="finish",
    )
    return (mesh_out, mesh_grad)


def solution(mesh):
    rows = P(("groups", "node"), None)
    flat = P(("groups", "node"))
    placed = (rows, rows) + (flat,) * 8 + (P(None, ("groups", "node")), rows, P(), P(), P())
    return jax.shard_map(
        body, mesh=mesh, in_specs=placed, out_specs=(rows, rows), check_vma=False
    )
```

```python
import functools

import jax
import jax.numpy as jnp
from jax import lax
from jax.experimental import pallas as pl
from jax.experimental.pallas import tpu as pltpu
from jax.sharding import PartitionSpec as P

HEADS = 16
BAND = 128
LANES = 128
F32 = jnp.float32
BF16 = jnp.bfloat16
I32 = jnp.int32
VMEM_LIMIT = 28 * 2**20
PARTS = 4


def mm(a, b):
    return lax.dot_general(a, b, (((1,), (0,)), ((), ())), preferred_element_type=F32)


def mm_nt(a, b):
    return lax.dot_general(a, b, (((1,), (1,)), ((), ())), preferred_element_type=F32)


def mm_tn(a, b):
    return lax.dot_general(a, b, (((0,), (0,)), ((), ())), preferred_element_type=F32)


def iota(shape, dim):
    return lax.broadcasted_iota(I32, shape, dim)


def call(kernel, outs, args, hbm=(), hbm_outs=(), scratch=(), name=None):
    args = [
        pltpu.with_memory_space_constraint(a, pltpu.HBM) if i in hbm else a
        for i, a in enumerate(args)
    ]

    def specs(count, far):
        return [
            pl.BlockSpec(memory_space=pltpu.HBM if i in far else pltpu.VMEM) for i in range(count)
        ]

    return pl.pallas_call(
        kernel,
        out_shape=[
            (pltpu.HBM if i in hbm_outs else jax.ShapeDtypeStruct)(shape, dtype)
            for i, (shape, dtype) in enumerate(outs)
        ],
        in_specs=specs(len(args), hbm),
        out_specs=specs(len(outs), hbm_outs),
        scratch_shapes=list(scratch),
        compiler_params=pltpu.CompilerParams(vmem_limit_bytes=VMEM_LIMIT),
        name=name,
    )(*args)


def dma(count):
    return pltpu.SemaphoreType.DMA((count,))


def start_all(pairs, sems):
    copies = [pltpu.make_async_copy(src, dst, sems.at[i]) for i, (src, dst) in enumerate(pairs)]
    for copy in copies:
        copy.start()
    return copies


def like(*arrays):
    return [pltpu.VMEM(a.shape, a.dtype) for a in arrays]


def exchange(toward_low, toward_high, axis):
    ends = lax.axis_size(axis) - 1
    from_high = lax.ppermute(toward_low, axis, [(i + 1, i) for i in range(ends)])
    from_low = lax.ppermute(toward_high, axis, [(i, i + 1) for i in range(ends)])
    return from_low, from_high


def pair_gather(rows, axis):
    n = lax.axis_size(axis)
    gathered = [
        lax.all_gather(
            rows,
            axis,
            axis_index_groups=[[(i + k) % n, (i + k + 1) % n] for i in range(0, n, 2)],
            tiled=True,
        )
        for k in range(2)
    ]
    return gathered


def gelu(projected):
    x = projected.astype(BF16).astype(F32)
    inner = (2.0 / jnp.pi) ** 0.5 * (x + 0.044715 * (x * x * x))
    return (0.5 * x * (1.0 + jnp.tanh(inner))).astype(BF16)


def onehot_rows(index_rows, count):
    parts = [
        jnp.where(iota((count, row.shape[1]), 0) == row, 1.0, 0.0).astype(BF16)
        for row in index_rows
    ]
    return parts[0] if len(parts) == 1 else jnp.concatenate(parts, 1)


def norm_stats(latent):
    values = latent.astype(F32)
    row_mean = jnp.mean(values, -1, keepdims=True)
    centred = values - row_mean
    variance = jnp.mean(centred * centred, -1, keepdims=True)
    inv_std = lax.rsqrt(variance + 1e-05)
    return centred * inv_std, inv_std


def pack_kernel(
    grid_hbm,
    window_hbm,
    side_src_hbm,
    side_dst_hbm,
    side_count_hbm,
    far_src_hbm,
    far_dst_hbm,
    far_count_hbm,
    far_out,
    low_out,
    high_out,
    grid,
    window,
    side_src,
    side_dst,
    side_count,
    far_src,
    far_dst,
    far_count,
    far,
    meta,
    sems,
    out_sems,
):
    grid_rows, channels = grid.shape
    mesh_rows = window.shape[1]
    slots = far_src.shape[1]
    devices = far_count.shape[1]
    depth = slots // devices
    first = grid_rows - BAND
    count = side_src.shape[0] // 2
    copies = start_all(
        [
            (far_src_hbm, far_src),
            (far_dst_hbm, far_dst),
            (far_count_hbm, far_count),
            (side_src_hbm, side_src),
            (side_dst_hbm, side_dst),
            (side_count_hbm, side_count),
            (window_hbm, window),
            (grid_hbm, grid),
            (grid_hbm.at[pl.ds(0, BAND)], low_out.at[pl.ds(0, BAND)]),
            (grid_hbm.at[pl.ds(first, BAND)], high_out.at[pl.ds(0, BAND)]),
        ],
        sems,
    )
    for copy in copies[:7]:
        copy.wait()
    for k in range(2):
        rank = iota((count, LANES), 0) * LANES + iota((count, LANES), 1)
        src = side_src[k * count : (k + 1) * count] - k * first
        live = rank < side_count[:, k : k + 1]
        dst = jnp.where(live, side_dst[k * count : (k + 1) * count], mesh_rows)
        reach = jnp.concatenate([window[...], jnp.zeros((count - 2, mesh_rows), I32)], 0)
        blank = jnp.zeros((count, channels - 2 * LANES - mesh_rows), I32)
        meta[k] = jnp.concatenate([src, dst, reach, blank], 1).astype(F32).astype(BF16)
    outs = start_all(
        [
            (meta.at[0], low_out.at[pl.ds(BAND, count)]),
            (meta.at[1], high_out.at[pl.ds(BAND, count)]),
        ],
        out_sems,
    )
    slot = iota((1, slots), 1)
    receiver = jnp.where(iota((devices, slots), 0) == iota((devices, slots), 1) // depth, 1.0, 0.0)
    live = mm(far_count[...].astype(F32).astype(BF16), receiver.astype(BF16))
    target = jnp.where((slot % depth).astype(F32) < live, far_dst[...].astype(F32), 1.0 * mesh_rows)
    place = slot // depth * (2 * depth) + slot % depth
    row = iota((2 * slots, slots), 0)
    source = far_src[...].astype(F32) + 1.0
    source = jnp.sum(jnp.where(row == place, source, 0.0), 1, keepdims=True) - 1.0
    column = jnp.sum(jnp.where(row == place + depth, target, 0.0), 1, keepdims=True)
    pick = jnp.where(iota((2 * slots, grid_rows), 1).astype(F32) == source, 1.0, 0.0).astype(BF16)
    copies[7].wait()
    far[...] = (mm(pick, grid[...]) + column).astype(BF16)
    last = pltpu.make_async_copy(far, far_out, out_sems.at[2])
    last.start()
    for copy in copies[8:] + outs + [last]:
        copy.wait()


def own_kernel(
    grid_hbm,
    mesh_in_hbm,
    own_src_hbm,
    own_dst_hbm,
    w_edge_hbm,
    partial_hbm,
    w_edge,
    grid,
    mesh_in,
    own_src,
    own_dst,
    partial,
    sems,
    out_sems,
):
    grid_rows, channels = grid.shape
    mesh_rows = mesh_in.shape[0]
    copies = start_all(
        [
            (own_src_hbm, own_src),
            (own_dst_hbm, own_dst),
            (grid_hbm, grid),
            (w_edge_hbm, w_edge),
            (mesh_in_hbm, mesh_in),
        ],
        sems,
    )
    for copy in copies[:2]:
        copy.wait()
    rows = own_src.shape[0]
    src = onehot_rows([own_src[r : r + 1] for r in range(rows)], grid_rows)
    dst = onehot_rows([own_dst[r : r + 1] for r in range(rows)], mesh_rows)
    counts = mm_nt(dst, src).astype(BF16)
    for copy in copies[2:]:
        copy.wait()
    step = channels // PARTS
    outs = []
    for c in range(PARTS):
        cols = slice(c * step, (c + 1) * step)
        active = gelu(mm(grid[...], w_edge[:, cols]))
        partial[c] = mesh_in[:, cols].astype(F32) + mm(counts, active)
        outs.append(pltpu.make_async_copy(partial.at[c], partial_hbm.at[c], out_sems.at[c]))
        outs[-1].start()
    for copy in outs:
        copy.wait()


def side_kernel(low_hbm, high_hbm, w_edge, partial_hbm, low, high, partial, sems, out_sems):
    mesh_rows, step = partial.shape[1:]
    copies = start_all(
        [
            (low_hbm.at[pl.ds(BAND, low.shape[0] - BAND)], low.at[pl.ds(BAND, low.shape[0] - BAND)]),
            (high_hbm.at[pl.ds(BAND, low.shape[0] - BAND)], high.at[pl.ds(BAND, low.shape[0] - BAND)]),
            (low_hbm.at[pl.ds(0, BAND)], low.at[pl.ds(0, BAND)]),
            (high_hbm.at[pl.ds(0, BAND)], high.at[pl.ds(0, BAND)]),
        ],
        sems,
    )
    for copy in copies[:2]:
        copy.wait()
    uppers, lowers = [], []
    for side in (low, high):
        meta = side[BAND:].astype(F32).astype(I32)
        count = meta.shape[0]
        src = onehot_rows([meta[r : r + 1, :LANES] for r in range(count)], BAND)
        dst = onehot_rows([meta[r : r + 1, LANES : 2 * LANES] for r in range(count)], mesh_rows)
        counts = mm_nt(dst, src)
        upper = counts.astype(BF16)
        uppers.append(upper)
        lowers.append((counts - upper.astype(F32)).astype(BF16))
    counts = jnp.concatenate(uppers + lowers, 1)
    for copy in copies[2:]:
        copy.wait()
    bands = jnp.concatenate([low[:BAND], high[:BAND]], 0)
    outs = []
    for c in range(PARTS):
        active = gelu(mm(bands, w_edge[:, c * step : (c + 1) * step]))
        partial[c] = mm(counts, jnp.concatenate([active, active], 0))
        outs.append(pltpu.make_async_copy(partial.at[c], partial_hbm.at[c], out_sems.at[c]))
        outs[-1].start()
    for copy in outs:
        copy.wait()


def latent_kernel(
    depth, far, w_edge, own_hbm, side_hbm, latent_out, normed_out, own_part, side_part, sems
):
    copies = start_all([(own_hbm, own_part), (side_hbm, side_part)], sems)
    mesh_rows = latent_out.shape[0]
    slots = far.shape[0]
    rows = far[...]
    active = gelu(mm(rows, w_edge[...]))
    target = pltpu.roll(rows[:, :LANES].astype(F32), slots - depth, 0)
    target = target if mesh_rows == LANES else jnp.broadcast_to(target[:, :1], (slots, mesh_rows))
    is_row = iota((slots, mesh_rows), 0) % (2 * depth) < depth
    hit = (target == iota((slots, mesh_rows), 1).astype(F32)) & is_row
    landing = jnp.where(hit, 1.0, 0.0).astype(BF16)
    landed = mm_tn(landing, active)
    for copy in copies:
        copy.wait()
    total = jnp.concatenate([own_part[c] + side_part[c] for c in range(PARTS)], 1)
    latent = (total + landed).astype(BF16)
    latent_out[...] = latent
    normal, _ = norm_stats(latent)
    normed_out[...] = normal.astype(BF16)


def project_kernel(
    normed, w_qkv_hbm, w_out_hbm, cot_hbm, qkv_out, w_qkv, w_out, cot_out, grad_out, sems
):
    step = normed.shape[1]
    copies = start_all(
        [
            (w_qkv_hbm.at[:, pl.ds(c * step, step)], w_qkv.at[:, pl.ds(c * step, step)])
            for c in range(3)
        ]
        + [(cot_hbm, cot_out), (w_out_hbm, w_out)],
        sems,
    )
    for c in range(3):
        copies[c].wait()
        cols = slice(c * step, (c + 1) * step)
        qkv_out[:, cols] = mm(normed[...], w_qkv[:, cols]).astype(BF16)
    for copy in copies[3:]:
        copy.wait()
    grad_out[...] = mm_nt(cot_out[...], w_out[...]).astype(BF16)


def halves(rows, scale=None):
    first = iota(rows.shape, 1) < rows.shape[1] // 2
    if scale is not None:
        rows = rows * jnp.asarray(scale, rows.dtype)
    zero = jnp.zeros_like(rows)
    return jnp.concatenate([jnp.where(first, rows, zero), jnp.where(first, zero, rows)], 0)


def merge(stacked):
    m = stacked.shape[0] // 2
    first = iota((m, stacked.shape[1]), 1) < stacked.shape[1] // 2
    return jnp.where(first, stacked[:m], stacked[m:])


def attend_kernel(
    scale,
    pair,
    low_normed,
    high_normed,
    w_qkv,
    own_qkv,
    own_grad,
    window_hbm,
    stats_out,
    att_out,
    gq_out,
    gk_out,
    gv_out,
    kv,
    window,
    sems,
):
    fetch = start_all([(window_hbm, window)], sems)
    m, channels = low_normed.shape
    devices = lax.axis_size("node")
    me = lax.axis_index("node")
    near = mm(jnp.concatenate([low_normed[...], high_normed[...]], 0), w_qkv[:, channels:])
    near = near.astype(BF16)
    kv[:m] = near[:m]
    kv[m : 2 * m] = own_qkv[:, channels:]
    kv[2 * m :] = near[m:]
    fetch[0].wait()
    key_at = iota((3 * m, m), 0)
    query_at = iota((3 * m, m), 1) + m
    inside = (key_at >= jnp.where(me == 0, m, 0)) & (
        key_at < jnp.where(me == devices - 1, 2 * m, 3 * m)
    )
    keep = (
        inside & (key_at >= query_at - window[0:1, :]) & (key_at <= query_at + window[1:2, :])
    )
    bias = jnp.where(keep, 0.0, -jnp.inf).astype(F32)
    bias = jnp.concatenate([bias, bias], 1)
    pairs = channels // pair
    for p in range(pairs):
        cols = slice(p * pair, (p + 1) * pair)
        key = kv[:, cols]
        value = kv[:, channels + p * pair : channels + (p + 1) * pair]
        q2 = halves(own_qkv[:, cols], scale)
        g2 = halves(own_grad[:, cols])
        scores = mm_nt(key, q2) + bias
        top = jnp.max(scores, 0, keepdims=True)
        shifted = jnp.exp(scores - top)
        inv_sum = 1.0 / jnp.sum(shifted, 0, keepdims=True)
        probs = shifted * inv_sum
        weights = probs.astype(BF16)
        grad_prob = mm_nt(value, g2)
        delta = jnp.sum(probs * grad_prob, 0, keepdims=True)
        grad_score = (probs * (grad_prob - delta)).astype(BF16)
        stats_out[p : p + 1] = top
        stats_out[pairs + p : pairs + p + 1] = inv_sum
        stats_out[2 * pairs + p : 2 * pairs + p + 1] = delta
        att_out[:, cols] = merge(mm_tn(weights, value)).astype(BF16)
        gq_out[:, cols] = (merge(mm_tn(grad_score, key)) * scale).astype(BF16)
        gk_out[:, cols] = mm(grad_score[m : 2 * m], q2)
        gv_out[:, cols] = mm(weights[m : 2 * m], g2)


def output_kernel(
    scale,
    latent,
    attention,
    w_out,
    grad_query,
    w_qkv,
    low_normed,
    high_normed,
    first_cot_hbm,
    second_cot_hbm,
    mesh_out,
    grad_normed,
    near_q_out,
    near_grad,
    near_cot,
    sems,
):
    m, channels = latent.shape
    low, high = near_cot.at[pl.ds(0, m)], near_cot.at[pl.ds(m, m)]
    odd = lax.axis_index("node") % 2 == 1

    def fetch(before, after):
        return start_all([(before.at[pl.ds(0, m)], low), (after.at[pl.ds(m, m)], high)], sems)

    @pl.when(odd)
    def _():
        fetch(first_cot_hbm, second_cot_hbm)

    @pl.when(jnp.logical_not(odd))
    def _():
        fetch(second_cot_hbm, first_cot_hbm)

    near = mm(jnp.concatenate([low_normed[...], high_normed[...]], 0), w_qkv[:, :channels])
    near_q_out[...] = near.astype(BF16) * jnp.asarray(scale, BF16)
    grad_normed[...] = mm_nt(grad_query[...], w_qkv[:, :channels])
    mesh_out[...] = (latent[...].astype(F32) + mm(attention[...], w_out[...])).astype(BF16)
    pltpu.make_async_copy(first_cot_hbm.at[pl.ds(0, m)], low, sems.at[0]).wait()
    pltpu.make_async_copy(first_cot_hbm.at[pl.ds(m, m)], high, sems.at[1]).wait()
    near_grad[...] = mm_nt(near_cot[...], w_out[...]).astype(BF16)


def finish_kernel(
    pair,
    low_stats,
    high_stats,
    low_hbm,
    high_hbm,
    near_q,
    near_grad,
    own_qkv,
    grad_key,
    grad_value,
    grad_normed,
    w_qkv,
    latent,
    cot,
    grad_out,
    grad_kv,
    metas,
    sems,
):
    m, channels = latent.shape
    count = metas.shape[1]
    fetch = start_all(
        [
            (low_hbm.at[pl.ds(BAND, count)], metas.at[0]),
            (high_hbm.at[pl.ds(BAND, count)], metas.at[1]),
        ],
        sems,
    )
    for copy in fetch:
        copy.wait()
    near_window = jnp.concatenate(
        [metas[k][:8, 2 * LANES : 2 * LANES + m].astype(F32).astype(I32) for k in range(2)], 1
    )
    key_at = iota((m, 2 * m), 0) + m
    lane = iota((m, 2 * m), 1)
    query_at = jnp.where(lane < m, lane, lane + m)
    keep = (key_at >= query_at - near_window[0:1, :]) & (key_at <= query_at + near_window[1:2, :])
    bias = jnp.where(keep, 0.0, -jnp.inf).astype(F32)
    pairs = channels // pair

    def stat(row, second):
        lanes = slice(m, 2 * m) if second else slice(0, m)
        return jnp.concatenate([low_stats[row : row + 1, lanes], high_stats[row : row + 1, lanes]], 1)

    for p in range(pairs):
        cols = slice(p * pair, (p + 1) * pair)
        key2 = halves(own_qkv[:, channels + p * pair : channels + (p + 1) * pair])
        value2 = halves(own_qkv[:, 2 * channels + p * pair : 2 * channels + (p + 1) * pair])
        query = near_q[:, cols]
        grad = near_grad[:, cols]
        scores = mm_nt(key2, query)
        grad_prob = mm_nt(value2, grad)
        weights, grad_scores = [], []
        for h in range(2):
            half = slice(h * m, (h + 1) * m)
            probs = jnp.exp(scores[half] + bias - stat(p, h)) * stat(pairs + p, h)
            weights.append(probs.astype(BF16))
            grad_scores.append((probs * (grad_prob[half] - stat(2 * pairs + p, h))).astype(BF16))
        gk = grad_key[:, cols] + merge(mm(jnp.concatenate(grad_scores, 0), query))
        gv = grad_value[:, cols] + merge(mm(jnp.concatenate(weights, 0), grad))
        grad_kv[:, cols] = gk.astype(BF16)
        grad_kv[:, channels + p * pair : channels + (p + 1) * pair] = gv.astype(BF16)
    total = grad_normed[...] + mm_nt(grad_kv[...], w_qkv[:, channels:])
    normal, inv_std = norm_stats(latent[...])
    centred = (
        total
        - jnp.mean(total, -1, keepdims=True)
        - normal * jnp.mean(total * normal, -1, keepdims=True)
    )
    grad_out[...] = (cot[...].astype(F32) + inv_std * centred).astype(BF16)


def body(
    grid_in,
    mesh_in,
    own_src,
    own_dst,
    side_src,
    side_dst,
    side_count,
    far_src,
    far_dst,
    far_count,
    window,
    cotangent,
    w_edge,
    w_qkv,
    w_out,
):
    devices = lax.axis_size("node")
    grid_rows, channels = grid_in.shape
    m = mesh_in.shape[0]
    far_slots = far_src.shape[0]
    far_depth = far_slots // devices
    head_dim = channels // HEADS
    pair = 2 * head_dim
    pairs = channels // pair
    scale = head_dim ** (-0.5)
    meta_rows = side_src.shape[0] // (2 * LANES)

    side_src, side_dst = side_src.reshape(-1, LANES), side_dst.reshape(-1, LANES)
    own_src, own_dst = own_src.reshape(-1, LANES), own_dst.reshape(-1, LANES)
    far_src, far_dst = far_src.reshape(1, -1), far_dst.reshape(1, -1)
    side_count, far_count = side_count.reshape(1, -1), far_count.reshape(1, -1)
    message = ((BAND + meta_rows, channels), BF16)
    far_message, toward_low, toward_high = call(
        pack_kernel,
        [((2 * far_slots, channels), BF16), message, message],
        [grid_in, window, side_src, side_dst, side_count, far_src, far_dst, far_count],
        hbm=range(8),
        hbm_outs=range(3),
        scratch=like(grid_in, window, side_src, side_dst, side_count, far_src, far_dst, far_count)
        + [
            pltpu.VMEM((2 * far_slots, channels), BF16),
            pltpu.VMEM((2, meta_rows, channels), BF16),
            dma(10),
            dma(3),
        ],
        name="pack",
    )
    got_far = lax.all_to_all(
        far_message.reshape(devices, 2 * far_depth, channels),
        "node",
        split_axis=0,
        concat_axis=0,
        tiled=True,
    ).reshape(2 * far_slots, channels)
    from_low, from_high = exchange(toward_low, toward_high, "node")

    part = (PARTS, m, channels // PARTS)
    own_part, w_edge = call(
        own_kernel,
        [(part, F32), (w_edge.shape, BF16)],
        [grid_in, mesh_in, own_src, own_dst, w_edge],
        hbm=range(5),
        hbm_outs=(0,),
        scratch=like(grid_in, mesh_in, own_src, own_dst) + [pltpu.VMEM(part, F32), dma(5), dma(PARTS)],
        name="own",
    )
    (side_part,) = call(
        side_kernel,
        [(part, F32)],
        [from_low, from_high, w_edge],
        hbm=(0, 1),
        hbm_outs=(0,),
        scratch=like(from_low, from_high) + [pltpu.VMEM(part, F32), dma(4), dma(PARTS)],
        name="side",
    )
    latent, normed = call(
        functools.partial(latent_kernel, far_depth),
        [((m, channels), BF16), ((m, channels), BF16)],
        [got_far, w_edge, own_part, side_part],
        hbm=(2, 3),
        scratch=[pltpu.VMEM(part, F32), pltpu.VMEM(part, F32), dma(2)],
        name="latent",
    )
    low_normed, high_normed = exchange(normed, normed, "node")
    own_qkv, w_qkv, w_out, own_cot, own_grad = call(
        project_kernel,
        [
            ((m, 3 * channels), BF16),
            (w_qkv.shape, BF16),
            (w_out.shape, BF16),
            ((m, channels), BF16),
            ((m, channels), BF16),
        ],
        [normed, w_qkv, w_out, cotangent],
        hbm=(1, 2, 3),
        scratch=[dma(5)],
        name="project",
    )
    low_normed, high_normed, late_cot = lax.optimization_barrier(
        (low_normed, high_normed, cotangent)
    )
    first_cot, second_cot = pair_gather(late_cot, "node")

    stats, attention, grad_query, grad_key, grad_value = call(
        functools.partial(attend_kernel, scale, pair),
        [
            ((3 * pairs, 2 * m), F32),
            ((m, channels), BF16),
            ((m, channels), BF16),
            ((m, channels), F32),
            ((m, channels), F32),
        ],
        [low_normed, high_normed, w_qkv, own_qkv, own_grad, window],
        hbm=(5,),
        scratch=[pltpu.VMEM((3 * m, 2 * channels), BF16)] + like(window) + [dma(1)],
        name="attend",
    )
    low_stats, high_stats = exchange(stats, stats, "node")

    mesh_out, grad_normed, near_q, near_grad = call(
        functools.partial(output_kernel, scale),
        [
            ((m, channels), BF16),
            ((m, channels), F32),
            ((2 * m, channels), BF16),
            ((2 * m, channels), BF16),
        ],
        [
            latent,
            attention,
            w_out,
            grad_query,
            w_qkv,
            low_normed,
            high_normed,
            first_cot,
            second_cot,
        ],
        hbm=(7, 8),
        scratch=[pltpu.VMEM((2 * m, channels), BF16), dma(2)],
        name="output",
    )
    (mesh_grad,) = call(
        functools.partial(finish_kernel, pair),
        [((m, channels), BF16)],
        [
            low_stats,
            high_stats,
            from_low,
            from_high,
            near_q,
            near_grad,
            own_qkv,
            grad_key,
            grad_value,
            grad_normed,
            w_qkv,
            latent,
            own_cot,
        ],
        hbm=(2, 3),
        scratch=[
            pltpu.VMEM((m, 2 * channels), BF16),
            pltpu.VMEM((2, meta_rows, channels), BF16),
            dma(2),
        ],
        name="finish",
    )
    return (mesh_out, mesh_grad)


def solution(mesh):
    rows = P(("groups", "node"), None)
    flat = P(("groups", "node"))
    placed = (rows, rows) + (flat,) * 8 + (P(None, ("groups", "node")), rows, P(), P(), P())
    return jax.shard_map(
        body, mesh=mesh, in_specs=placed, out_specs=(rows, rows), check_vma=False
    )
```

```python
import functools

import jax
import jax.numpy as jnp
from jax import lax
from jax.experimental import pallas as pl
from jax.experimental.pallas import tpu as pltpu
from jax.sharding import PartitionSpec as P

HEADS = 16
BAND = 128
LANES = 128
F32 = jnp.float32
BF16 = jnp.bfloat16
I32 = jnp.int32
VMEM_LIMIT = 28 * 2**20
EARLY = 32


def mm(a, b):
    return lax.dot_general(a, b, (((1,), (0,)), ((), ())), preferred_element_type=F32)


def mm_nt(a, b):
    return lax.dot_general(a, b, (((1,), (1,)), ((), ())), preferred_element_type=F32)


def mm_tn(a, b):
    return lax.dot_general(a, b, (((0,), (0,)), ((), ())), preferred_element_type=F32)


def iota(shape, dim):
    return lax.broadcasted_iota(I32, shape, dim)


def call(kernel, outs, args, hbm=(), hbm_outs=(), scratch=(), name=None):
    args = [
        pltpu.with_memory_space_constraint(a, pltpu.HBM) if i in hbm else a
        for i, a in enumerate(args)
    ]

    def specs(count, far):
        return [
            pl.BlockSpec(memory_space=pltpu.HBM if i in far else pltpu.VMEM) for i in range(count)
        ]

    return pl.pallas_call(
        kernel,
        out_shape=[
            (pltpu.HBM if i in hbm_outs else jax.ShapeDtypeStruct)(shape, dtype)
            for i, (shape, dtype) in enumerate(outs)
        ],
        in_specs=specs(len(args), hbm),
        out_specs=specs(len(outs), hbm_outs),
        scratch_shapes=list(scratch),
        compiler_params=pltpu.CompilerParams(vmem_limit_bytes=VMEM_LIMIT),
        name=name,
    )(*args)


def dma(count):
    return pltpu.SemaphoreType.DMA((count,))


def start_all(pairs, sems):
    copies = [pltpu.make_async_copy(src, dst, sems.at[i]) for i, (src, dst) in enumerate(pairs)]
    for copy in copies:
        copy.start()
    return copies


def like(*arrays):
    return [pltpu.VMEM(a.shape, a.dtype) for a in arrays]


def exchange(toward_low, toward_high, axis):
    ends = lax.axis_size(axis) - 1
    from_high = lax.ppermute(toward_low, axis, [(i + 1, i) for i in range(ends)])
    from_low = lax.ppermute(toward_high, axis, [(i, i + 1) for i in range(ends)])
    return from_low, from_high


def gelu(projected):
    x = projected.astype(BF16).astype(F32)
    inner = (2.0 / jnp.pi) ** 0.5 * (x + 0.044715 * (x * x * x))
    return (0.5 * x * (1.0 + jnp.tanh(inner))).astype(BF16)


def onehot_rows(index_rows, count):
    parts = [
        jnp.where(iota((count, row.shape[1]), 0) == row, 1.0, 0.0).astype(BF16)
        for row in index_rows
    ]
    return parts[0] if len(parts) == 1 else jnp.concatenate(parts, 1)


def norm_stats(latent):
    values = latent.astype(F32)
    row_mean = jnp.mean(values, -1, keepdims=True)
    centred = values - row_mean
    variance = jnp.mean(centred * centred, -1, keepdims=True)
    inv_std = lax.rsqrt(variance + 1e-05)
    return centred * inv_std, inv_std


def pack_kernel(
    grid_hbm,
    cot_hbm,
    window_hbm,
    side_src_hbm,
    side_dst_hbm,
    side_count_hbm,
    far_src_hbm,
    far_dst_hbm,
    far_count_hbm,
    far_out,
    low_out,
    high_out,
    grid,
    cot,
    window,
    side_src,
    side_dst,
    side_count,
    far_src,
    far_dst,
    far_count,
    far,
    meta,
    sems,
    out_sems,
):
    grid_rows, channels = grid.shape
    mesh_rows = window.shape[1]
    slots = far_src.shape[1]
    devices = far_count.shape[1]
    depth = slots // devices
    first = grid_rows - BAND
    count = side_src.shape[0] // 2
    copies = start_all(
        [
            (side_src_hbm, side_src),
            (side_dst_hbm, side_dst),
            (side_count_hbm, side_count),
            (window_hbm, window),
            (grid_hbm, grid),
            (cot_hbm.at[pl.ds(0, EARLY)], cot),
            (far_src_hbm, far_src),
            (far_dst_hbm, far_dst),
            (far_count_hbm, far_count),
        ],
        sems,
    )
    for copy in copies[:4]:
        copy.wait()
    for k in range(2):
        rank = iota((count, LANES), 0) * LANES + iota((count, LANES), 1)
        src = side_src[k * count : (k + 1) * count] - k * first
        live = rank < side_count[:, k : k + 1]
        dst = jnp.where(live, side_dst[k * count : (k + 1) * count], mesh_rows)
        reach = jnp.concatenate([window[...], jnp.zeros((count - 2, mesh_rows), I32)], 0)
        blank = jnp.zeros((count, channels - 2 * LANES - mesh_rows), I32)
        meta[k] = jnp.concatenate([src, dst, reach, blank], 1).astype(F32).astype(BF16)
    for copy in copies[4:6]:
        copy.wait()
    outs = start_all(
        [
            pair
            for k, out in ((0, low_out), (1, high_out))
            for pair in (
                (grid.at[pl.ds(k * first, BAND)], out.at[pl.ds(0, BAND)]),
                (meta.at[k], out.at[pl.ds(BAND, count)]),
                (cot, out.at[pl.ds(BAND + count, EARLY)]),
            )
        ],
        out_sems,
    )
    for copy in copies[6:]:
        copy.wait()
    slot = iota((1, slots), 1)
    receiver = jnp.where(iota((devices, slots), 0) == iota((devices, slots), 1) // depth, 1.0, 0.0)
    live = mm(far_count[...].astype(F32).astype(BF16), receiver.astype(BF16))
    target = jnp.where((slot % depth).astype(F32) < live, far_dst[...].astype(F32), 1.0 * mesh_rows)
    row = iota((2 * slots, slots), 0)
    mine = slot == row // (2 * depth) * depth + row % depth
    source = jnp.sum(jnp.where(mine, far_src[...].astype(F32), 0.0), 1, keepdims=True)
    column = jnp.sum(jnp.where(mine, target, 0.0), 1, keepdims=True)
    pick = jnp.where(iota((2 * slots, grid_rows), 1).astype(F32) == source, 1.0, 0.0).astype(BF16)
    rows = mm(pick, grid[...])
    half = channels // 2
    is_first = iota((2 * slots, half), 0) % (2 * depth) < depth
    far[:, :half] = jnp.where(is_first, rows[:, :half], rows[:, half:]).astype(BF16)
    far[:, half:] = jnp.broadcast_to(column, (2 * slots, LANES)).astype(BF16)
    last = pltpu.make_async_copy(far, far_out, out_sems.at[6])
    last.start()
    for copy in outs + [last]:
        copy.wait()


def own_kernel(
    grid_hbm,
    mesh_in_hbm,
    own_src_hbm,
    own_dst_hbm,
    w_edge_hbm,
    partial_out,
    grid,
    mesh_in,
    own_src,
    own_dst,
    w_edge,
    sems,
):
    grid_rows = grid.shape[0]
    mesh_rows = mesh_in.shape[0]
    copies = start_all(
        [
            (own_src_hbm, own_src),
            (own_dst_hbm, own_dst),
            (grid_hbm, grid),
            (w_edge_hbm, w_edge),
            (mesh_in_hbm, mesh_in),
        ],
        sems,
    )
    for copy in copies[:2]:
        copy.wait()
    rows = own_src.shape[0]
    src = onehot_rows([own_src[r : r + 1] for r in range(rows)], grid_rows)
    dst = onehot_rows([own_dst[r : r + 1] for r in range(rows)], mesh_rows)
    counts = mm_nt(dst, src).astype(BF16)
    for copy in copies[2:]:
        copy.wait()
    active = gelu(mm(grid[...], w_edge[...]))
    partial_out[...] = mesh_in[...].astype(F32) + mm(counts, active)


def mesh_kernel(
    depth,
    low_hbm,
    high_hbm,
    far_hbm,
    w_edge_hbm,
    partial,
    latent_out,
    normed_out,
    window_out,
    cot_out,
    metas,
    bands,
    far,
    w_edge,
    sems,
):
    mesh_rows, channels = partial.shape
    count = metas.shape[1]
    ends = (low_hbm, high_hbm)
    copies = start_all(
        [(ends[k].at[pl.ds(BAND, count)], metas.at[k]) for k in range(2)]
        + [(far_hbm, far)]
        + [(ends[k].at[pl.ds(0, BAND)], bands.at[pl.ds(k * BAND, BAND)]) for k in range(2)]
        + [(w_edge_hbm, w_edge)]
        + [
            (ends[k].at[pl.ds(BAND + count, EARLY)], cot_out.at[pl.ds(k * EARLY, EARLY)])
            for k in range(2)
        ],
        sems,
    )
    for copy in copies[:2]:
        copy.wait()
    uppers, lowers = [], []
    for k in range(2):
        meta = metas[k].astype(F32).astype(I32)
        src = onehot_rows([meta[r : r + 1, :LANES] for r in range(count)], BAND)
        dst = onehot_rows([meta[r : r + 1, LANES : 2 * LANES] for r in range(count)], mesh_rows)
        counts = mm_nt(dst, src)
        upper = counts.astype(BF16)
        uppers.append(upper)
        lowers.append((counts - upper.astype(F32)).astype(BF16))
        window_out[:, k * mesh_rows : (k + 1) * mesh_rows] = meta[:8, 2 * LANES : 2 * LANES + mesh_rows]
    copies[2].wait()
    slots = far.shape[0]
    half = channels // 2
    first = far[:, :half]
    second = pltpu.roll(first.astype(F32), slots - depth, 0).astype(BF16)
    far_rows = jnp.concatenate([first, second], 1)
    target = jnp.transpose(far[:, half:].astype(F32))
    if mesh_rows != LANES:
        target = jnp.broadcast_to(target[:1], (mesh_rows, slots))
    is_row = iota((mesh_rows, slots), 1) % (2 * depth) < depth
    hit = (target == iota((mesh_rows, slots), 0).astype(F32)) & is_row
    landing = jnp.concatenate(uppers + [jnp.where(hit, 1.0, 0.0).astype(BF16)] + lowers, 1)
    for copy in copies[3:6]:
        copy.wait()
    active = gelu(mm(jnp.concatenate([bands[...], far_rows], 0), w_edge[...]))
    active = jnp.concatenate([active, active[: 2 * BAND]], 0)
    latent = (partial[...] + mm(landing, active)).astype(BF16)
    latent_out[...] = latent
    normal, _ = norm_stats(latent)
    normed_out[...] = normal.astype(BF16)
    for copy in copies[6:]:
        copy.wait()


def project_kernel(
    normed, near_cot, w_qkv_hbm, w_out_hbm, cot_hbm, qkv_out, w_qkv, w_out, cot_out, grad_out, near_out, sems
):
    m, step = normed.shape
    copies = start_all(
        [
            (w_qkv_hbm.at[:, pl.ds(c * step, step)], w_qkv.at[:, pl.ds(c * step, step)])
            for c in range(3)
        ]
        + [(cot_hbm, cot_out), (w_out_hbm, w_out)],
        sems,
    )
    for c in range(3):
        copies[c].wait()
        cols = slice(c * step, (c + 1) * step)
        qkv_out[:, cols] = mm(normed[...], w_qkv[:, cols]).astype(BF16)
    for copy in copies[3:]:
        copy.wait()
    grads = mm_nt(jnp.concatenate([cot_out[...], near_cot[...]], 0), w_out[...]).astype(BF16)
    grad_out[...] = grads[:m]
    near_out[...] = grads[m:]


def halves(rows, scale=None):
    first = iota(rows.shape, 1) < rows.shape[1] // 2
    if scale is not None:
        rows = rows * jnp.asarray(scale, rows.dtype)
    zero = jnp.zeros_like(rows)
    return jnp.concatenate([jnp.where(first, rows, zero), jnp.where(first, zero, rows)], 0)


def merge(stacked):
    m = stacked.shape[0] // 2
    first = iota((m, stacked.shape[1]), 1) < stacked.shape[1] // 2
    return jnp.where(first, stacked[:m], stacked[m:])


def attend_kernel(
    scale,
    pair,
    low_normed,
    high_normed,
    w_qkv,
    own_qkv,
    own_grad,
    window_hbm,
    message_out,
    kv,
    weights_out,
    scores_out,
    window,
    sems,
):
    fetch = start_all([(window_hbm, window)], sems)
    m, channels = low_normed.shape
    pairs = channels // pair
    rows = message_out.shape[0] - (m - EARLY)
    message_out[rows:] = own_grad[EARLY:]
    devices = lax.axis_size("node")
    me = lax.axis_index("node")
    near = mm(jnp.concatenate([low_normed[...], high_normed[...]], 0), w_qkv[:, channels:])
    near = near.astype(BF16)
    kv[:m] = near[:m]
    kv[m : 2 * m] = own_qkv[:, channels:]
    kv[2 * m :] = near[m:]
    fetch[0].wait()
    key_at = iota((3 * m, m), 0)
    query_at = iota((3 * m, m), 1) + m
    inside = (key_at >= jnp.where(me == 0, m, 0)) & (
        key_at < jnp.where(me == devices - 1, 2 * m, 3 * m)
    )
    keep = (
        inside & (key_at >= query_at - window[0:1, :]) & (key_at <= query_at + window[1:2, :])
    )
    bias = jnp.transpose(jnp.where(keep, 0.0, -jnp.inf).astype(F32))
    bias = jnp.concatenate([bias, bias], 0)
    lane = iota((2 * m, LANES), 1)
    stats = jnp.zeros((2 * m, LANES), F32)
    for p in range(pairs):
        cols = slice(p * pair, (p + 1) * pair)
        q2 = halves(own_qkv[:, cols], scale)
        g2 = halves(own_grad[:, cols])
        scores = mm_nt(q2, kv[:, cols]) + bias
        top = jnp.max(scores, 1, keepdims=True)
        shifted = jnp.exp(scores - top)
        inv_sum = 1.0 / jnp.sum(shifted, 1, keepdims=True)
        probs = shifted * inv_sum
        weights_out[p] = probs.astype(BF16)
        grad_prob = mm_nt(g2, kv[:, channels + p * pair : channels + (p + 1) * pair])
        delta = jnp.sum(probs * grad_prob, 1, keepdims=True)
        scores_out[p] = (probs * (grad_prob - delta)).astype(BF16)
        stats = jnp.where(lane == p, top, stats)
        stats = jnp.where(lane == pairs + p, inv_sum, stats)
        stats = jnp.where(lane == 2 * pairs + p, delta, stats)
    rest = jnp.transpose(stats)[:rows]
    for part in range(3):
        piece = rest.astype(BF16)
        message_out[:rows, part * 2 * m : (part + 1) * 2 * m] = piece
        rest = rest - piece.astype(F32)
    message_out[:rows, 6 * m :] = jnp.zeros((rows, channels - 6 * m), BF16)


def product_kernel(
    scale,
    pair,
    weights,
    grad_scores,
    kv,
    own_qkv,
    own_grad,
    latent,
    w_out,
    w_qkv,
    low_normed,
    high_normed,
    mesh_out,
    grad_normed,
    grad_key,
    grad_value,
    near_q_out,
    attention,
    grad_query,
):
    m, channels = latent.shape
    for p in range(channels // pair):
        cols = slice(p * pair, (p + 1) * pair)
        key = kv[:, cols]
        value = kv[:, channels + p * pair : channels + (p + 1) * pair]
        attention[:, cols] = merge(mm(weights[p], value)).astype(BF16)
        grad_query[:, cols] = (merge(mm(grad_scores[p], key)) * scale).astype(BF16)
        grad_key[:, cols] = mm_tn(grad_scores[p, :, m : 2 * m], halves(own_qkv[:, cols], scale))
        grad_value[:, cols] = mm_tn(weights[p, :, m : 2 * m], halves(own_grad[:, cols]))
    mesh_out[...] = (latent[...].astype(F32) + mm(attention[...], w_out[...])).astype(BF16)
    grad_normed[...] = mm_nt(grad_query[...], w_qkv[:, :channels])
    near = mm(jnp.concatenate([low_normed[...], high_normed[...]], 0), w_qkv[:, :channels])
    near_q_out[...] = near.astype(BF16) * jnp.asarray(scale, BF16)


def finish_kernel(
    pair,
    low,
    high,
    near_window,
    near_q,
    early_grad,
    own_qkv,
    grad_key,
    grad_value,
    grad_normed,
    w_qkv,
    latent,
    cot,
    grad_out,
    grad_kv,
):
    m, channels = latent.shape
    rows = low.shape[0] - (m - EARLY)
    key_at = iota((m, 2 * m), 0) + m
    lane = iota((m, 2 * m), 1)
    query_at = jnp.where(lane < m, lane, lane + m)
    keep = (key_at >= query_at - near_window[0:1, :]) & (key_at <= query_at + near_window[1:2, :])
    bias = jnp.where(keep, 0.0, -jnp.inf).astype(F32)
    pairs = channels // pair

    def whole(side):
        return sum(side[:rows, k * 2 * m : (k + 1) * 2 * m].astype(F32) for k in (2, 1, 0))

    low_stats, high_stats = whole(low), whole(high)
    stats = [jnp.concatenate([low_stats[:, h * m : (h + 1) * m], high_stats[:, h * m : (h + 1) * m]], 1) for h in range(2)]
    for p in range(pairs):
        cols = slice(p * pair, (p + 1) * pair)
        key2 = halves(own_qkv[:, channels + p * pair : channels + (p + 1) * pair])
        value2 = halves(own_qkv[:, 2 * channels + p * pair : 2 * channels + (p + 1) * pair])
        query = near_q[:, cols]
        grad = jnp.concatenate(
            [early_grad[:EARLY, cols], low[rows:, cols], early_grad[EARLY:, cols], high[rows:, cols]], 0
        )
        scores = mm_nt(key2, query)
        grad_prob = mm_nt(value2, grad)
        weights, grad_scores = [], []
        for h in range(2):
            half = slice(h * m, (h + 1) * m)
            top, inv_sum, delta = (stats[h][k * pairs + p : k * pairs + p + 1] for k in range(3))
            probs = jnp.exp(scores[half] + bias - top) * inv_sum
            weights.append(probs.astype(BF16))
            grad_scores.append((probs * (grad_prob[half] - delta)).astype(BF16))
        gk = grad_key[:, cols] + merge(mm(jnp.concatenate(grad_scores, 0), query))
        gv = grad_value[:, cols] + merge(mm(jnp.concatenate(weights, 0), grad))
        grad_kv[:, cols] = gk.astype(BF16)
        grad_kv[:, channels + p * pair : channels + (p + 1) * pair] = gv.astype(BF16)
    total = grad_normed[...] + mm_nt(grad_kv[...], w_qkv[:, channels:])
    normal, inv_std = norm_stats(latent[...])
    centred = (
        total
        - jnp.mean(total, -1, keepdims=True)
        - normal * jnp.mean(total * normal, -1, keepdims=True)
    )
    grad_out[...] = (cot[...].astype(F32) + inv_std * centred).astype(BF16)


def body(
    grid_in,
    mesh_in,
    own_src,
    own_dst,
    side_src,
    side_dst,
    side_count,
    far_src,
    far_dst,
    far_count,
    window,
    cotangent,
    w_edge,
    w_qkv,
    w_out,
):
    devices = lax.axis_size("node")
    grid_rows, channels = grid_in.shape
    m = mesh_in.shape[0]
    far_slots = far_src.shape[0]
    far_depth = far_slots // devices
    head_dim = channels // HEADS
    pair = 2 * head_dim
    pairs = channels // pair
    scale = head_dim ** (-0.5)
    meta_rows = side_src.shape[0] // (2 * LANES)

    side_src, side_dst = side_src.reshape(-1, LANES), side_dst.reshape(-1, LANES)
    own_src, own_dst = own_src.reshape(-1, LANES), own_dst.reshape(-1, LANES)
    far_src, far_dst = far_src.reshape(1, -1), far_dst.reshape(1, -1)
    side_count, far_count = side_count.reshape(1, -1), far_count.reshape(1, -1)
    message = ((BAND + meta_rows + EARLY, channels), BF16)
    far_block = (2 * far_slots, channels // 2 + LANES)
    far_message, toward_low, toward_high = call(
        pack_kernel,
        [(far_block, BF16), message, message],
        [grid_in, cotangent, window, side_src, side_dst, side_count, far_src, far_dst, far_count],
        hbm=range(9),
        hbm_outs=range(3),
        scratch=like(grid_in, cotangent[:EARLY])
        + like(window, side_src, side_dst, side_count, far_src, far_dst, far_count)
        + [
            pltpu.VMEM(far_block, BF16),
            pltpu.VMEM((2, meta_rows, channels), BF16),
            dma(9),
            dma(7),
        ],
        name="pack",
    )
    from_low, from_high = exchange(toward_low, toward_high, "node")
    got_far = lax.all_to_all(
        far_message.reshape(devices, 2 * far_depth, far_block[1]),
        "node",
        split_axis=0,
        concat_axis=0,
        tiled=True,
    ).reshape(far_block)

    rows = ((m, channels), BF16)
    (own_part,) = call(
        own_kernel,
        [((m, channels), F32)],
        [grid_in, mesh_in, own_src, own_dst, w_edge],
        hbm=range(5),
        scratch=like(grid_in, mesh_in, own_src, own_dst, w_edge) + [dma(5)],
        name="own",
    )
    latent, normed, near_window, near_cot = call(
        functools.partial(mesh_kernel, far_depth),
        [rows, rows, ((8, 2 * m), I32), ((2 * EARLY, channels), BF16)],
        [from_low, from_high, got_far, w_edge, own_part],
        hbm=(0, 1, 2, 3),
        scratch=[
            pltpu.VMEM((2, meta_rows, channels), BF16),
            pltpu.VMEM((2 * BAND, channels), BF16),
            pltpu.VMEM(far_block, BF16),
            pltpu.VMEM(w_edge.shape, BF16),
            dma(8),
        ],
        name="mesh",
    )
    low_normed, high_normed = exchange(normed, normed, "node")
    own_qkv, w_qkv, w_out, own_cot, own_grad, early_grad = call(
        project_kernel,
        [
            ((m, 3 * channels), BF16),
            (w_qkv.shape, BF16),
            (w_out.shape, BF16),
            rows,
            rows,
            ((2 * EARLY, channels), BF16),
        ],
        [normed, near_cot, w_qkv, w_out, cotangent],
        hbm=(2, 3, 4),
        scratch=[dma(5)],
        name="project",
    )
    stat_rows = -(-3 * pairs // 16) * 16
    probs = ((pairs, 2 * m, 3 * m), BF16)
    message, kv, weights, grad_scores = call(
        functools.partial(attend_kernel, scale, pair),
        [((stat_rows + m - EARLY, channels), BF16), ((3 * m, 2 * channels), BF16), probs, probs],
        [low_normed, high_normed, w_qkv, own_qkv, own_grad, window],
        hbm=(5,),
        scratch=like(window) + [dma(1)],
        name="attend",
    )
    low_late, high_late = exchange(message, message, "node")
    mesh_out, grad_normed, grad_key, grad_value, near_q = call(
        functools.partial(product_kernel, scale, pair),
        [
            rows,
            ((m, channels), F32),
            ((m, channels), F32),
            ((m, channels), F32),
            ((2 * m, channels), BF16),
        ],
        [
            weights,
            grad_scores,
            kv,
            own_qkv,
            own_grad,
            latent,
            w_out,
            w_qkv,
            low_normed,
            high_normed,
        ],
        scratch=[pltpu.VMEM((m, channels), BF16)] * 2,
        name="product",
    )
    (mesh_grad,) = call(
        functools.partial(finish_kernel, pair),
        [rows],
        [
            low_late,
            high_late,
            near_window,
            near_q,
            early_grad,
            own_qkv,
            grad_key,
            grad_value,
            grad_normed,
            w_qkv,
            latent,
            own_cot,
        ],
        scratch=[pltpu.VMEM((m, 2 * channels), BF16)],
        name="finish",
    )
    return (mesh_out, mesh_grad)


def solution(mesh):
    rows = P(("groups", "node"), None)
    flat = P(("groups", "node"))
    placed = (rows, rows) + (flat,) * 8 + (P(None, ("groups", "node")), rows, P(), P(), P())
    return jax.shard_map(
        body, mesh=mesh, in_specs=placed, out_specs=(rows, rows), check_vma=False
    )
```

```python
import functools

import jax
import jax.numpy as jnp
from jax import lax
from jax.experimental import pallas as pl
from jax.experimental.pallas import tpu as pltpu
from jax.sharding import PartitionSpec as P

HEADS = 16
BAND = 128
LANES = 128
F32 = jnp.float32
BF16 = jnp.bfloat16
I32 = jnp.int32
VMEM_LIMIT = 28 * 2**20
EARLY = 64


def mm(a, b):
    return lax.dot_general(a, b, (((1,), (0,)), ((), ())), preferred_element_type=F32)


def mm_nt(a, b):
    return lax.dot_general(a, b, (((1,), (1,)), ((), ())), preferred_element_type=F32)


def mm_tn(a, b):
    return lax.dot_general(a, b, (((0,), (0,)), ((), ())), preferred_element_type=F32)


def iota(shape, dim):
    return lax.broadcasted_iota(I32, shape, dim)


def call(kernel, outs, args, hbm=(), hbm_outs=(), scratch=(), name=None):
    args = [
        pltpu.with_memory_space_constraint(a, pltpu.HBM) if i in hbm else a
        for i, a in enumerate(args)
    ]

    def specs(count, far):
        return [
            pl.BlockSpec(memory_space=pltpu.HBM if i in far else pltpu.VMEM) for i in range(count)
        ]

    return pl.pallas_call(
        kernel,
        out_shape=[
            (pltpu.HBM if i in hbm_outs else jax.ShapeDtypeStruct)(shape, dtype)
            for i, (shape, dtype) in enumerate(outs)
        ],
        in_specs=specs(len(args), hbm),
        out_specs=specs(len(outs), hbm_outs),
        scratch_shapes=list(scratch),
        compiler_params=pltpu.CompilerParams(vmem_limit_bytes=VMEM_LIMIT),
        name=name,
    )(*args)


def dma(count):
    return pltpu.SemaphoreType.DMA((count,))


def start_all(pairs, sems):
    copies = [pltpu.make_async_copy(src, dst, sems.at[i]) for i, (src, dst) in enumerate(pairs)]
    for copy in copies:
        copy.start()
    return copies


def like(*arrays):
    return [pltpu.VMEM(a.shape, a.dtype) for a in arrays]


def exchange(chip_message, off_message, axis):
    n = lax.axis_size(axis)
    from_off = lax.ppermute(
        off_message, axis, [p for i in range(1, n - 1, 2) for p in ((i, i + 1), (i + 1, i))]
    )
    from_chip = lax.ppermute(
        chip_message, axis, [p for i in range(0, n, 2) for p in ((i, i + 1), (i + 1, i))]
    )
    return from_chip, from_off


def is_odd():
    return lax.axis_index("node") % 2


def gelu(projected):
    x = projected.astype(BF16).astype(F32)
    inner = (2.0 / jnp.pi) ** 0.5 * (x + 0.044715 * (x * x * x))
    return (0.5 * x * (1.0 + jnp.tanh(inner))).astype(BF16)


def onehot_rows(index_rows, count):
    parts = [
        jnp.where(iota((count, row.shape[1]), 0) == row, 1.0, 0.0).astype(BF16)
        for row in index_rows
    ]
    return parts[0] if len(parts) == 1 else jnp.concatenate(parts, 1)


def norm_stats(latent):
    values = latent.astype(F32)
    row_mean = jnp.mean(values, -1, keepdims=True)
    centred = values - row_mean
    variance = jnp.mean(centred * centred, -1, keepdims=True)
    inv_std = lax.rsqrt(variance + 1e-05)
    return centred * inv_std, inv_std


def pack_kernel(
    grid_hbm,
    cot_hbm,
    window_hbm,
    side_src_hbm,
    side_dst_hbm,
    side_count_hbm,
    far_src_hbm,
    far_dst_hbm,
    far_count_hbm,
    w_edge_hbm,
    far_out,
    chip_out,
    off_out,
    w_edge,
    grid,
    cot,
    window,
    side_src,
    side_dst,
    side_count,
    far_src,
    far_dst,
    far_count,
    far,
    meta,
    sems,
    out_sems,
):
    grid_rows, channels = grid.shape
    mesh_rows = window.shape[1]
    slots = far_src.shape[1]
    devices = far_count.shape[1]
    depth = slots // devices
    first = grid_rows - BAND
    count = side_src.shape[0] // 2
    copies = start_all(
        [
            (side_src_hbm, side_src),
            (side_dst_hbm, side_dst),
            (side_count_hbm, side_count),
            (window_hbm, window),
            (grid_hbm, grid),
            (cot_hbm.at[pl.ds(0, EARLY)], cot),
            (far_src_hbm, far_src),
            (far_dst_hbm, far_dst),
            (far_count_hbm, far_count),
            (w_edge_hbm, w_edge),
        ],
        sems,
    )
    for copy in copies[:4]:
        copy.wait()
    for k in range(2):
        rank = iota((count, LANES), 0) * LANES + iota((count, LANES), 1)
        src = side_src[k * count : (k + 1) * count] - k * first
        live = rank < side_count[:, k : k + 1]
        dst = jnp.where(live, side_dst[k * count : (k + 1) * count], mesh_rows)
        reach = jnp.concatenate([window[...], jnp.zeros((count - 2, mesh_rows), I32)], 0)
        blank = jnp.zeros((count, channels - 2 * LANES - mesh_rows), I32)
        meta[k] = jnp.concatenate([src, dst, reach, blank], 1).astype(F32).astype(BF16)
    for copy in copies[4:6]:
        copy.wait()
    odd = is_odd()
    outs = start_all(
        [
            pair
            for k, out in ((1 - odd, chip_out), (odd, off_out))
            for pair in (
                (grid.at[pl.ds(pl.multiple_of(k * first, BAND), BAND)], out.at[pl.ds(0, BAND)]),
                (meta.at[k], out.at[pl.ds(BAND, count)]),
                (cot, out.at[pl.ds(BAND + count, EARLY)]),
            )
        ],
        out_sems,
    )
    for copy in copies[6:9]:
        copy.wait()
    slot = iota((1, slots), 1)
    receiver = jnp.where(iota((devices, slots), 0) == iota((devices, slots), 1) // depth, 1.0, 0.0)
    live = mm(far_count[...].astype(F32).astype(BF16), receiver.astype(BF16))
    target = jnp.where((slot % depth).astype(F32) < live, far_dst[...].astype(F32), 1.0 * mesh_rows)
    row = iota((2 * slots, slots), 0)
    mine = slot == row // (2 * depth) * depth + row % depth
    source = jnp.sum(jnp.where(mine, far_src[...].astype(F32), 0.0), 1, keepdims=True)
    column = jnp.sum(jnp.where(mine, target, 0.0), 1, keepdims=True)
    pick = jnp.where(iota((2 * slots, grid_rows), 1).astype(F32) == source, 1.0, 0.0).astype(BF16)
    rows = mm(pick, grid[...]).astype(BF16)
    copies[9].wait()
    rows = gelu(mm(rows, w_edge[...]))
    half = channels // 2
    is_first = iota((2 * slots, half), 0) % (2 * depth) < depth
    far[:, :half] = jnp.where(is_first, rows[:, :half], rows[:, half:])
    far[:, half:] = jnp.broadcast_to(column, (2 * slots, LANES)).astype(BF16)
    last = pltpu.make_async_copy(far, far_out, out_sems.at[6])
    last.start()
    for copy in outs + [last]:
        copy.wait()


def own_kernel(
    grid_hbm,
    mesh_in_hbm,
    own_src_hbm,
    own_dst_hbm,
    w_edge,
    partial_out,
    grid,
    mesh_in,
    own_src,
    own_dst,
    sems,
):
    grid_rows = grid.shape[0]
    mesh_rows = mesh_in.shape[0]
    copies = start_all(
        [
            (own_src_hbm, own_src),
            (own_dst_hbm, own_dst),
            (grid_hbm, grid),
            (mesh_in_hbm, mesh_in),
        ],
        sems,
    )
    for copy in copies[:2]:
        copy.wait()
    rows = own_src.shape[0]
    src = onehot_rows([own_src[r : r + 1] for r in range(rows)], grid_rows)
    dst = onehot_rows([own_dst[r : r + 1] for r in range(rows)], mesh_rows)
    counts = mm_nt(dst, src).astype(BF16)
    for copy in copies[2:]:
        copy.wait()
    active = gelu(mm(grid[...], w_edge[...]))
    partial_out[...] = mesh_in[...].astype(F32) + mm(counts, active)


def meta_of(message, count):
    return message[BAND : BAND + count].astype(F32).astype(I32)


def side_kernel(count, chip, off, w_edge, partial, partial_out):
    mesh_rows = partial.shape[0]
    uppers, lowers = [], []
    for side in (chip, off):
        meta = meta_of(side, count)
        src = onehot_rows([meta[r : r + 1, :LANES] for r in range(count)], BAND)
        dst = onehot_rows([meta[r : r + 1, LANES : 2 * LANES] for r in range(count)], mesh_rows)
        counts = mm_nt(dst, src)
        upper = counts.astype(BF16)
        uppers.append(upper)
        lowers.append((counts - upper.astype(F32)).astype(BF16))
    active = gelu(mm(jnp.concatenate([chip[:BAND], off[:BAND]], 0), w_edge[...]))
    landing = jnp.concatenate(uppers + lowers, 1)
    partial_out[...] = partial[...] + mm(landing, jnp.concatenate([active, active], 0))


def latent_kernel(depth, far, partial, latent_out, normed_out):
    mesh_rows, channels = partial.shape
    slots = far.shape[0]
    half = channels // 2
    first = far[:, :half]
    second = pltpu.roll(first.astype(F32), slots - depth, 0).astype(BF16)
    target = jnp.transpose(far[:, half:].astype(F32))
    if mesh_rows != LANES:
        target = jnp.broadcast_to(target[:1], (mesh_rows, slots))
    is_row = iota((mesh_rows, slots), 1) % (2 * depth) < depth
    hit = (target == iota((mesh_rows, slots), 0).astype(F32)) & is_row
    landing = jnp.where(hit, 1.0, 0.0).astype(BF16)
    total = partial[...] + mm(landing, jnp.concatenate([first, second], 1))
    latent = total.astype(BF16)
    latent_out[...] = latent
    normal, _ = norm_stats(latent)
    normed_out[...] = normal.astype(BF16)


def project_kernel(
    normed, chip, off, w_qkv_hbm, w_out_hbm, cot_hbm, qkv_out, w_qkv, w_out, cot_out, grad_out, near_out, sems
):
    m, step = normed.shape
    copies = start_all(
        [
            (w_qkv_hbm.at[:, pl.ds(c * step, step)], w_qkv.at[:, pl.ds(c * step, step)])
            for c in range(3)
        ]
        + [(cot_hbm, cot_out), (w_out_hbm, w_out)],
        sems,
    )
    for c in range(3):
        copies[c].wait()
        cols = slice(c * step, (c + 1) * step)
        qkv_out[:, cols] = mm(normed[...], w_qkv[:, cols]).astype(BF16)
    for copy in copies[3:]:
        copy.wait()
    cots = jnp.concatenate([cot_out[...], chip[-EARLY:], off[-EARLY:]], 0)
    grads = mm_nt(cots, w_out[...]).astype(BF16)
    grad_out[...] = grads[:m]
    near_out[...] = grads[m:]


def halves(rows, scale=None):
    first = iota(rows.shape, 1) < rows.shape[1] // 2
    if scale is not None:
        rows = rows * jnp.asarray(scale, rows.dtype)
    zero = jnp.zeros_like(rows)
    return jnp.concatenate([jnp.where(first, rows, zero), jnp.where(first, zero, rows)], 0)


def merge(stacked):
    m = stacked.shape[0] // 2
    first = iota((m, stacked.shape[1]), 1) < stacked.shape[1] // 2
    return jnp.where(first, stacked[:m], stacked[m:])


def near_places(m):
    odd = is_odd()
    return (1 - odd) * 2 * m, odd * 2 * m


def attend_kernel(
    scale,
    pair,
    chip_normed,
    off_normed,
    w_qkv,
    own_qkv,
    own_grad,
    window_hbm,
    message_out,
    kv,
    weights_out,
    scores_out,
    window,
    sems,
):
    fetch = start_all([(window_hbm, window)], sems)
    m, channels = chip_normed.shape
    pairs = channels // pair
    rows = message_out.shape[0] - (m - EARLY)
    message_out[rows:] = own_grad[EARLY:]
    devices = lax.axis_size("node")
    me = lax.axis_index("node")
    near = mm(jnp.concatenate([chip_normed[...], off_normed[...]], 0), w_qkv[:, channels:])
    near = near.astype(BF16)
    kv[:m] = near[:m]
    kv[m : 2 * m] = own_qkv[:, channels:]
    kv[2 * m :] = near[m:]
    fetch[0].wait()
    row = iota((3 * m, m), 0)
    chip_at, off_at = near_places(m)
    key_at = jnp.where(row < m, row + chip_at, jnp.where(row < 2 * m, row, row - 2 * m + off_at))
    query_at = iota((3 * m, m), 1) + m
    inside = row < jnp.where((me == 0) | (me == devices - 1), 2 * m, 3 * m)
    keep = (
        inside & (key_at >= query_at - window[0:1, :]) & (key_at <= query_at + window[1:2, :])
    )
    bias = jnp.transpose(jnp.where(keep, 0.0, -jnp.inf).astype(F32))
    bias = jnp.concatenate([bias, bias], 0)
    lane = iota((2 * m, LANES), 1)
    stats = jnp.zeros((2 * m, LANES), F32)
    for p in range(pairs):
        cols = slice(p * pair, (p + 1) * pair)
        q2 = halves(own_qkv[:, cols], scale)
        g2 = halves(own_grad[:, cols])
        scores = mm_nt(q2, kv[:, cols]) + bias
        top = jnp.max(scores, 1, keepdims=True)
        shifted = jnp.exp(scores - top)
        inv_sum = 1.0 / jnp.sum(shifted, 1, keepdims=True)
        probs = shifted * inv_sum
        weights_out[p] = probs.astype(BF16)
        grad_prob = mm_nt(g2, kv[:, channels + p * pair : channels + (p + 1) * pair])
        delta = jnp.sum(probs * grad_prob, 1, keepdims=True)
        scores_out[p] = (probs * (grad_prob - delta)).astype(BF16)
        stats = jnp.where(lane == p, top, stats)
        stats = jnp.where(lane == pairs + p, inv_sum, stats)
        stats = jnp.where(lane == 2 * pairs + p, delta, stats)
    rest = jnp.transpose(stats)[:rows]
    for part in range(3):
        piece = rest.astype(BF16)
        message_out[:rows, part * 2 * m : (part + 1) * 2 * m] = piece
        rest = rest - piece.astype(F32)
    message_out[:rows, 6 * m :] = jnp.zeros((rows, channels - 6 * m), BF16)


def product_kernel(
    scale,
    pair,
    weights,
    grad_scores,
    kv,
    own_qkv,
    own_grad,
    latent,
    w_out,
    w_qkv,
    chip_normed,
    off_normed,
    mesh_out,
    grad_normed,
    grad_key,
    grad_value,
    near_q_out,
    attention,
    grad_query,
):
    m, channels = latent.shape
    for p in range(channels // pair):
        cols = slice(p * pair, (p + 1) * pair)
        key = kv[:, cols]
        value = kv[:, channels + p * pair : channels + (p + 1) * pair]
        attention[:, cols] = merge(mm(weights[p], value)).astype(BF16)
        grad_query[:, cols] = (merge(mm(grad_scores[p], key)) * scale).astype(BF16)
        grad_key[:, cols] = mm_tn(grad_scores[p, :, m : 2 * m], halves(own_qkv[:, cols], scale))
        grad_value[:, cols] = mm_tn(weights[p, :, m : 2 * m], halves(own_grad[:, cols]))
    mesh_out[...] = (latent[...].astype(F32) + mm(attention[...], w_out[...])).astype(BF16)
    grad_normed[...] = mm_nt(grad_query[...], w_qkv[:, :channels])
    near = mm(jnp.concatenate([chip_normed[...], off_normed[...]], 0), w_qkv[:, :channels])
    near_q_out[...] = near.astype(BF16) * jnp.asarray(scale, BF16)


def finish_kernel(
    pair,
    count,
    chip,
    off,
    chip_first,
    off_first,
    near_q,
    early_grad,
    own_qkv,
    grad_key,
    grad_value,
    grad_normed,
    w_qkv,
    latent,
    cot,
    grad_out,
    grad_kv,
):
    m, channels = latent.shape
    rows = chip.shape[0] - (m - EARLY)
    reach = [meta_of(side, count)[:8, 2 * LANES : 2 * LANES + m] for side in (chip_first, off_first)]
    reach = jnp.concatenate(reach, 1)
    key_at = iota((m, 2 * m), 0) + m
    lane = iota((m, 2 * m), 1)
    chip_at, off_at = near_places(m)
    query_at = jnp.where(lane < m, lane + chip_at, lane - m + off_at)
    keep = (key_at >= query_at - reach[0:1, :]) & (key_at <= query_at + reach[1:2, :])
    bias = jnp.where(keep, 0.0, -jnp.inf).astype(F32)
    pairs = channels // pair

    def whole(side):
        return sum(side[:rows, k * 2 * m : (k + 1) * 2 * m].astype(F32) for k in (2, 1, 0))

    chip_stats, off_stats = whole(chip), whole(off)
    stats = []
    for h in range(2):
        lanes = slice(h * m, (h + 1) * m)
        stats.append(jnp.concatenate([chip_stats[:, lanes], off_stats[:, lanes]], 1))
    for p in range(pairs):
        cols = slice(p * pair, (p + 1) * pair)
        key2 = halves(own_qkv[:, channels + p * pair : channels + (p + 1) * pair])
        value2 = halves(own_qkv[:, 2 * channels + p * pair : 2 * channels + (p + 1) * pair])
        query = near_q[:, cols]
        grad = jnp.concatenate(
            [early_grad[:EARLY, cols], chip[rows:, cols], early_grad[EARLY:, cols], off[rows:, cols]], 0
        )
        scores = mm_nt(key2, query)
        grad_prob = mm_nt(value2, grad)
        weights, grad_scores = [], []
        for h in range(2):
            half = slice(h * m, (h + 1) * m)
            top, inv_sum, delta = (stats[h][k * pairs + p : k * pairs + p + 1] for k in range(3))
            probs = jnp.exp(scores[half] + bias - top) * inv_sum
            weights.append(probs.astype(BF16))
            grad_scores.append((probs * (grad_prob[half] - delta)).astype(BF16))
        gk = grad_key[:, cols] + merge(mm(jnp.concatenate(grad_scores, 0), query))
        gv = grad_value[:, cols] + merge(mm(jnp.concatenate(weights, 0), grad))
        grad_kv[:, cols] = gk.astype(BF16)
        grad_kv[:, channels + p * pair : channels + (p + 1) * pair] = gv.astype(BF16)
    total = grad_normed[...] + mm_nt(grad_kv[...], w_qkv[:, channels:])
    normal, inv_std = norm_stats(latent[...])
    centred = (
        total
        - jnp.mean(total, -1, keepdims=True)
        - normal * jnp.mean(total * normal, -1, keepdims=True)
    )
    grad_out[...] = (cot[...].astype(F32) + inv_std * centred).astype(BF16)


def body(
    grid_in,
    mesh_in,
    own_src,
    own_dst,
    side_src,
    side_dst,
    side_count,
    far_src,
    far_dst,
    far_count,
    window,
    cotangent,
    w_edge,
    w_qkv,
    w_out,
):
    devices = lax.axis_size("node")
    grid_rows, channels = grid_in.shape
    m = mesh_in.shape[0]
    far_slots = far_src.shape[0]
    far_depth = far_slots // devices
    head_dim = channels // HEADS
    pair = 2 * head_dim
    pairs = channels // pair
    scale = head_dim ** (-0.5)
    meta_rows = side_src.shape[0] // (2 * LANES)

    side_src, side_dst = side_src.reshape(-1, LANES), side_dst.reshape(-1, LANES)
    own_src, own_dst = own_src.reshape(-1, LANES), own_dst.reshape(-1, LANES)
    far_src, far_dst = far_src.reshape(1, -1), far_dst.reshape(1, -1)
    side_count, far_count = side_count.reshape(1, -1), far_count.reshape(1, -1)
    message = ((BAND + meta_rows + EARLY, channels), BF16)
    far_block = (2 * far_slots, channels // 2 + LANES)
    far_message, chip_message, off_message, w_edge = call(
        pack_kernel,
        [(far_block, BF16), message, message, (w_edge.shape, BF16)],
        [grid_in, cotangent, window, side_src, side_dst, side_count, far_src, far_dst, far_count]
        + [w_edge],
        hbm=range(10),
        hbm_outs=range(3),
        scratch=like(grid_in, cotangent[:EARLY])
        + like(window, side_src, side_dst, side_count, far_src, far_dst, far_count)
        + [
            pltpu.VMEM(far_block, BF16),
            pltpu.VMEM((2, meta_rows, channels), BF16),
            dma(10),
            dma(7),
        ],
        name="pack",
    )
    from_chip, from_off = exchange(chip_message, off_message, "node")
    got_far = lax.all_to_all(
        far_message.reshape(devices, 2 * far_depth, far_block[1]),
        "node",
        split_axis=0,
        concat_axis=0,
        tiled=True,
    ).reshape(far_block)

    rows = ((m, channels), BF16)
    (partial,) = call(
        own_kernel,
        [((m, channels), F32)],
        [grid_in, mesh_in, own_src, own_dst, w_edge],
        hbm=range(4),
        scratch=like(grid_in, mesh_in, own_src, own_dst) + [dma(4)],
        name="own",
    )
    (partial,) = call(
        functools.partial(side_kernel, meta_rows),
        [((m, channels), F32)],
        [from_chip, from_off, w_edge, partial],
        name="side",
    )
    latent, normed = call(
        functools.partial(latent_kernel, far_depth), [rows, rows], [got_far, partial], name="latent"
    )
    chip_normed, off_normed = exchange(normed, normed, "node")
    own_qkv, w_qkv, w_out, own_cot, own_grad, early_grad = call(
        project_kernel,
        [
            ((m, 3 * channels), BF16),
            (w_qkv.shape, BF16),
            (w_out.shape, BF16),
            rows,
            rows,
            ((2 * EARLY, channels), BF16),
        ],
        [normed, from_chip, from_off, w_qkv, w_out, cotangent],
        hbm=(3, 4, 5),
        scratch=[dma(5)],
        name="project",
    )
    stat_rows = -(-3 * pairs // 16) * 16
    probs = ((pairs, 2 * m, 3 * m), BF16)
    message, kv, weights, grad_scores = call(
        functools.partial(attend_kernel, scale, pair),
        [((stat_rows + m - EARLY, channels), BF16), ((3 * m, 2 * channels), BF16), probs, probs],
        [chip_normed, off_normed, w_qkv, own_qkv, own_grad, window],
        hbm=(5,),
        scratch=like(window) + [dma(1)],
        name="attend",
    )
    chip_late, off_late = exchange(message, message, "node")
    mesh_out, grad_normed, grad_key, grad_value, near_q = call(
        functools.partial(product_kernel, scale, pair),
        [
            rows,
            ((m, channels), F32),
            ((m, channels), F32),
            ((m, channels), F32),
            ((2 * m, channels), BF16),
        ],
        [
            weights,
            grad_scores,
            kv,
            own_qkv,
            own_grad,
            latent,
            w_out,
            w_qkv,
            chip_normed,
            off_normed,
        ],
        scratch=[pltpu.VMEM((m, channels), BF16)] * 2,
        name="product",
    )
    (mesh_grad,) = call(
        functools.partial(finish_kernel, pair, meta_rows),
        [rows],
        [
            chip_late,
            off_late,
            from_chip,
            from_off,
            near_q,
            early_grad,
            own_qkv,
            grad_key,
            grad_value,
            grad_normed,
            w_qkv,
            latent,
            own_cot,
        ],
        scratch=[pltpu.VMEM((m, 2 * channels), BF16)],
        name="finish",
    )
    return (mesh_out, mesh_grad)


def solution(mesh):
    rows = P(("groups", "node"), None)
    flat = P(("groups", "node"))
    placed = (rows, rows) + (flat,) * 8 + (P(None, ("groups", "node")), rows, P(), P(), P())
    return jax.shard_map(
        body, mesh=mesh, in_specs=placed, out_specs=(rows, rows), check_vma=False
    )
```

```python
import functools

import jax
import jax.numpy as jnp
from jax import lax
from jax.experimental import pallas as pl
from jax.experimental.pallas import tpu as pltpu
from jax.sharding import PartitionSpec as P

HEADS = 16
BAND = 128
LANES = 128
F32 = jnp.float32
BF16 = jnp.bfloat16
I32 = jnp.int32
VMEM_LIMIT = 28 * 2**20
PIECES = 6


def mm(a, b):
    return lax.dot_general(a, b, (((1,), (0,)), ((), ())), preferred_element_type=F32)


def mm_nt(a, b):
    return lax.dot_general(a, b, (((1,), (1,)), ((), ())), preferred_element_type=F32)


def mm_tn(a, b):
    return lax.dot_general(a, b, (((0,), (0,)), ((), ())), preferred_element_type=F32)


def iota(shape, dim):
    return lax.broadcasted_iota(I32, shape, dim)


def call(kernel, outs, args, hbm=(), hbm_outs=(), scratch=(), name=None):
    args = [
        pltpu.with_memory_space_constraint(a, pltpu.HBM) if i in hbm else a
        for i, a in enumerate(args)
    ]

    def specs(count, far):
        return [
            pl.BlockSpec(memory_space=pltpu.HBM if i in far else pltpu.VMEM) for i in range(count)
        ]

    return pl.pallas_call(
        kernel,
        out_shape=[
            (pltpu.HBM if i in hbm_outs else jax.ShapeDtypeStruct)(shape, dtype)
            for i, (shape, dtype) in enumerate(outs)
        ],
        in_specs=specs(len(args), hbm),
        out_specs=specs(len(outs), hbm_outs),
        scratch_shapes=list(scratch),
        compiler_params=pltpu.CompilerParams(vmem_limit_bytes=VMEM_LIMIT),
        name=name,
    )(*args)


def dma(count):
    return pltpu.SemaphoreType.DMA((count,))


def start_all(pairs, sems):
    copies = [pltpu.make_async_copy(src, dst, sems.at[i]) for i, (src, dst) in enumerate(pairs)]
    for copy in copies:
        copy.start()
    return copies


def like(*arrays):
    return [pltpu.VMEM(a.shape, a.dtype) for a in arrays]


def exchange(chip_message, off_message, axis):
    n = lax.axis_size(axis)
    from_off = lax.ppermute(
        off_message, axis, [p for i in range(1, n - 1, 2) for p in ((i, i + 1), (i + 1, i))]
    )
    from_chip = lax.ppermute(
        chip_message, axis, [p for i in range(0, n, 2) for p in ((i, i + 1), (i + 1, i))]
    )
    return from_chip, from_off


def is_odd():
    return lax.axis_index("node") % 2


def gelu(projected):
    x = projected.astype(BF16).astype(F32)
    inner = (2.0 / jnp.pi) ** 0.5 * (x + 0.044715 * (x * x * x))
    return (0.5 * x * (1.0 + jnp.tanh(inner))).astype(BF16)


def onehot_rows(index_rows, count):
    parts = [
        jnp.where(iota((count, row.shape[1]), 0) == row, 1.0, 0.0).astype(BF16)
        for row in index_rows
    ]
    return parts[0] if len(parts) == 1 else jnp.concatenate(parts, 1)


def norm_stats(latent):
    values = latent.astype(F32)
    row_mean = jnp.mean(values, -1, keepdims=True)
    centred = values - row_mean
    variance = jnp.mean(centred * centred, -1, keepdims=True)
    inv_std = lax.rsqrt(variance + 1e-05)
    return centred * inv_std, inv_std


def pack_kernel(
    grid_hbm,
    window_hbm,
    side_src_hbm,
    side_dst_hbm,
    side_count_hbm,
    far_src_hbm,
    far_dst_hbm,
    far_count_hbm,
    w_edge_hbm,
    far_out,
    chip_out,
    off_out,
    w_edge,
    grid,
    window,
    side_src,
    side_dst,
    side_count,
    far_src,
    far_dst,
    far_count,
    far,
    meta,
    sems,
    out_sems,
):
    grid_rows, channels = grid.shape
    mesh_rows = window.shape[1]
    slots = far_src.shape[1]
    devices = far_count.shape[1]
    depth = slots // devices
    first = grid_rows - BAND
    count = side_src.shape[0] // 2
    copies = start_all(
        [
            (side_src_hbm, side_src),
            (side_dst_hbm, side_dst),
            (side_count_hbm, side_count),
            (window_hbm, window),
            (grid_hbm, grid),
            (far_src_hbm, far_src),
            (far_dst_hbm, far_dst),
            (far_count_hbm, far_count),
            (w_edge_hbm, w_edge),
        ],
        sems,
    )
    for copy in copies[:4]:
        copy.wait()
    for k in range(2):
        rank = iota((count, LANES), 0) * LANES + iota((count, LANES), 1)
        src = side_src[k * count : (k + 1) * count] - k * first
        live = rank < side_count[:, k : k + 1]
        dst = jnp.where(live, side_dst[k * count : (k + 1) * count], mesh_rows)
        reach = jnp.concatenate([window[...], jnp.zeros((count - 2, mesh_rows), I32)], 0)
        blank = jnp.zeros((count, channels - 2 * LANES - mesh_rows), I32)
        meta[k] = jnp.concatenate([src, dst, reach, blank], 1).astype(F32).astype(BF16)
    copies[4].wait()
    odd = is_odd()
    outs = start_all(
        [
            pair
            for k, out in ((1 - odd, chip_out), (odd, off_out))
            for pair in (
                (grid.at[pl.ds(pl.multiple_of(k * first, BAND), BAND)], out.at[pl.ds(0, BAND)]),
                (meta.at[k], out.at[pl.ds(BAND, count)]),
            )
        ],
        out_sems,
    )
    for copy in copies[5:8]:
        copy.wait()
    slot = iota((1, slots), 1)
    receiver = jnp.where(iota((devices, slots), 0) == iota((devices, slots), 1) // depth, 1.0, 0.0)
    live = mm(far_count[...].astype(F32).astype(BF16), receiver.astype(BF16))
    target = jnp.where((slot % depth).astype(F32) < live, far_dst[...].astype(F32), 1.0 * mesh_rows)
    row = iota((2 * slots, slots), 0)
    mine = slot == row // (2 * depth) * depth + row % depth
    source = jnp.sum(jnp.where(mine, far_src[...].astype(F32), 0.0), 1, keepdims=True)
    column = jnp.sum(jnp.where(mine, target, 0.0), 1, keepdims=True)
    pick = jnp.where(iota((2 * slots, grid_rows), 1).astype(F32) == source, 1.0, 0.0).astype(BF16)
    rows = mm(pick, grid[...]).astype(BF16)
    copies[8].wait()
    rows = gelu(mm(rows, w_edge[...]))
    half = channels // 2
    is_first = iota((2 * slots, half), 0) % (2 * depth) < depth
    far[:, :half] = jnp.where(is_first, rows[:, :half], rows[:, half:])
    far[:, half:] = jnp.broadcast_to(column, (2 * slots, LANES)).astype(BF16)
    last = pltpu.make_async_copy(far, far_out, out_sems.at[4])
    last.start()
    for copy in outs + [last]:
        copy.wait()


def own_kernel(
    grid_hbm,
    mesh_in_hbm,
    own_src_hbm,
    own_dst_hbm,
    w_edge,
    partial_out,
    grid,
    mesh_in,
    own_src,
    own_dst,
    sems,
):
    grid_rows = grid.shape[0]
    mesh_rows = mesh_in.shape[0]
    copies = start_all(
        [
            (own_src_hbm, own_src),
            (own_dst_hbm, own_dst),
            (grid_hbm, grid),
            (mesh_in_hbm, mesh_in),
        ],
        sems,
    )
    for copy in copies[:2]:
        copy.wait()
    rows = own_src.shape[0]
    src = onehot_rows([own_src[r : r + 1] for r in range(rows)], grid_rows)
    dst = onehot_rows([own_dst[r : r + 1] for r in range(rows)], mesh_rows)
    counts = mm_nt(dst, src).astype(BF16)
    for copy in copies[2:]:
        copy.wait()
    active = gelu(mm(grid[...], w_edge[...]))
    partial_out[...] = mesh_in[...].astype(F32) + mm(counts, active)


def meta_of(message, count):
    return message[BAND : BAND + count].astype(F32).astype(I32)


def side_kernel(count, chip, off, w_edge, partial, partial_out):
    mesh_rows = partial.shape[0]
    uppers, lowers = [], []
    for side in (chip, off):
        meta = meta_of(side, count)
        src = onehot_rows([meta[r : r + 1, :LANES] for r in range(count)], BAND)
        dst = onehot_rows([meta[r : r + 1, LANES : 2 * LANES] for r in range(count)], mesh_rows)
        counts = mm_nt(dst, src)
        upper = counts.astype(BF16)
        uppers.append(upper)
        lowers.append((counts - upper.astype(F32)).astype(BF16))
    active = gelu(mm(jnp.concatenate([chip[:BAND], off[:BAND]], 0), w_edge[...]))
    landing = jnp.concatenate(uppers + lowers, 1)
    partial_out[...] = partial[...] + mm(landing, jnp.concatenate([active, active], 0))


def latent_kernel(depth, far, partial, latent_out, normed_out):
    mesh_rows, channels = partial.shape
    slots = far.shape[0]
    half = channels // 2
    first = far[:, :half]
    second = pltpu.roll(first.astype(F32), slots - depth, 0).astype(BF16)
    target = jnp.transpose(far[:, half:].astype(F32))
    if mesh_rows != LANES:
        target = jnp.broadcast_to(target[:1], (mesh_rows, slots))
    is_row = iota((mesh_rows, slots), 1) % (2 * depth) < depth
    hit = (target == iota((mesh_rows, slots), 0).astype(F32)) & is_row
    landing = jnp.where(hit, 1.0, 0.0).astype(BF16)
    total = partial[...] + mm(landing, jnp.concatenate([first, second], 1))
    latent = total.astype(BF16)
    latent_out[...] = latent
    normal, _ = norm_stats(latent)
    normed_out[...] = normal.astype(BF16)


def project_kernel(
    normed, w_qkv_hbm, w_out_hbm, cot_hbm, qkv_out, w_qkv, w_out, cot_out, grad_out, sems
):
    width = w_qkv.shape[1] // PIECES
    pieces = [pl.ds(c * width, width) for c in range(PIECES)]
    copies = [
        pltpu.make_async_copy(src, dst, sems.at[i])
        for i, (src, dst) in enumerate(
            [(cot_hbm, cot_out), (w_out_hbm, w_out)]
            + [(w_qkv_hbm.at[:, piece], w_qkv.at[:, piece]) for piece in pieces]
        )
    ]
    for copy in copies[:4]:
        copy.start()
    copies[0].wait()
    copies[1].wait()
    copies[4].start()
    copies[5].start()
    grad_out[...] = mm_nt(cot_out[...], w_out[...]).astype(BF16)
    for c in range(PIECES):
        copies[2 + c].wait()
        if c + 6 < len(copies):
            copies[c + 6].start()
        cols = slice(c * width, (c + 1) * width)
        qkv_out[:, cols] = mm(normed[...], w_qkv[:, cols]).astype(BF16)


def halves(rows, scale=None):
    first = iota(rows.shape, 1) < rows.shape[1] // 2
    if scale is not None:
        rows = rows * jnp.asarray(scale, rows.dtype)
    zero = jnp.zeros_like(rows)
    return jnp.concatenate([jnp.where(first, rows, zero), jnp.where(first, zero, rows)], 0)


def merge(stacked):
    m = stacked.shape[0] // 2
    first = iota((m, stacked.shape[1]), 1) < stacked.shape[1] // 2
    return jnp.where(first, stacked[:m], stacked[m:])


def near_places(m):
    odd = is_odd()
    return (1 - odd) * 2 * m, odd * 2 * m


def attend_kernel(
    scale,
    pair,
    chip_normed,
    off_normed,
    w_qkv,
    own_qkv,
    own_grad,
    window_hbm,
    stats_out,
    kv,
    weights_out,
    scores_out,
    window,
    sems,
):
    fetch = start_all([(window_hbm, window)], sems)
    m, channels = chip_normed.shape
    pairs = channels // pair
    devices = lax.axis_size("node")
    me = lax.axis_index("node")
    near = mm(jnp.concatenate([chip_normed[...], off_normed[...]], 0), w_qkv[:, channels:])
    near = near.astype(BF16)
    kv[:m] = near[:m]
    kv[m : 2 * m] = own_qkv[:, channels:]
    kv[2 * m :] = near[m:]
    fetch[0].wait()
    row = iota((3 * m, m), 0)
    chip_at, off_at = near_places(m)
    key_at = jnp.where(row < m, row + chip_at, jnp.where(row < 2 * m, row, row - 2 * m + off_at))
    query_at = iota((3 * m, m), 1) + m
    inside = row < jnp.where((me == 0) | (me == devices - 1), 2 * m, 3 * m)
    keep = (
        inside & (key_at >= query_at - window[0:1, :]) & (key_at <= query_at + window[1:2, :])
    )
    bias = jnp.transpose(jnp.where(keep, 0.0, -jnp.inf).astype(F32))
    bias = jnp.concatenate([bias, bias], 0)
    lane = iota((2 * m, LANES), 1)
    stats = jnp.zeros((2 * m, LANES), F32)
    for p in range(pairs):
        cols = slice(p * pair, (p + 1) * pair)
        q2 = halves(own_qkv[:, cols], scale)
        g2 = halves(own_grad[:, cols])
        scores = mm_nt(q2, kv[:, cols]) + bias
        top = jnp.max(scores, 1, keepdims=True)
        shifted = jnp.exp(scores - top)
        inv_sum = 1.0 / jnp.sum(shifted, 1, keepdims=True)
        probs = shifted * inv_sum
        weights_out[p] = probs.astype(BF16)
        grad_prob = mm_nt(g2, kv[:, channels + p * pair : channels + (p + 1) * pair])
        delta = jnp.sum(probs * grad_prob, 1, keepdims=True)
        scores_out[p] = (probs * (grad_prob - delta)).astype(BF16)
        stats = jnp.where(lane == p, top, stats)
        stats = jnp.where(lane == pairs + p, inv_sum, stats)
        stats = jnp.where(lane == 2 * pairs + p, delta, stats)
    stats_out[...] = jnp.transpose(stats)[: 3 * pairs]


def product_kernel(
    scale,
    pair,
    weights,
    grad_scores,
    kv,
    own_qkv,
    own_grad,
    latent,
    w_out,
    w_qkv,
    chip_normed,
    off_normed,
    mesh_out,
    grad_normed,
    grad_key,
    grad_value,
    near_q_out,
    attention,
    grad_query,
):
    m, channels = latent.shape
    for p in range(channels // pair):
        cols = slice(p * pair, (p + 1) * pair)
        key = kv[:, cols]
        value = kv[:, channels + p * pair : channels + (p + 1) * pair]
        attention[:, cols] = merge(mm(weights[p], value)).astype(BF16)
        grad_query[:, cols] = (merge(mm(grad_scores[p], key)) * scale).astype(BF16)
        grad_key[:, cols] = mm_tn(grad_scores[p, :, m : 2 * m], halves(own_qkv[:, cols], scale))
        grad_value[:, cols] = mm_tn(weights[p, :, m : 2 * m], halves(own_grad[:, cols]))
    mesh_out[...] = (latent[...].astype(F32) + mm(attention[...], w_out[...])).astype(BF16)
    grad_normed[...] = mm_nt(grad_query[...], w_qkv[:, :channels])
    near = mm(jnp.concatenate([chip_normed[...], off_normed[...]], 0), w_qkv[:, :channels])
    near_q_out[...] = near.astype(BF16) * jnp.asarray(scale, BF16)


def finish_kernel(
    pair,
    count,
    chip_stats,
    off_stats,
    chip_first,
    off_first,
    near_q,
    chip_grad,
    off_grad,
    own_qkv,
    grad_key,
    grad_value,
    grad_normed,
    w_qkv,
    latent,
    cot,
    grad_out,
    grad_kv,
):
    m, channels = latent.shape
    reach = [meta_of(side, count)[:8, 2 * LANES : 2 * LANES + m] for side in (chip_first, off_first)]
    reach = jnp.concatenate(reach, 1)
    key_at = iota((m, 2 * m), 0) + m
    lane = iota((m, 2 * m), 1)
    chip_at, off_at = near_places(m)
    query_at = jnp.where(lane < m, lane + chip_at, lane - m + off_at)
    keep = (key_at >= query_at - reach[0:1, :]) & (key_at <= query_at + reach[1:2, :])
    bias = jnp.where(keep, 0.0, -jnp.inf).astype(F32)
    pairs = channels // pair

    stats = []
    for h in range(2):
        lanes = slice(h * m, (h + 1) * m)
        stats.append(jnp.concatenate([chip_stats[:, lanes], off_stats[:, lanes]], 1))
    for p in range(pairs):
        cols = slice(p * pair, (p + 1) * pair)
        key2 = halves(own_qkv[:, channels + p * pair : channels + (p + 1) * pair])
        value2 = halves(own_qkv[:, 2 * channels + p * pair : 2 * channels + (p + 1) * pair])
        query = near_q[:, cols]
        grad = jnp.concatenate([chip_grad[:, cols], off_grad[:, cols]], 0)
        scores = mm_nt(key2, query)
        grad_prob = mm_nt(value2, grad)
        weights, grad_scores = [], []
        for h in range(2):
            half = slice(h * m, (h + 1) * m)
            top, inv_sum, delta = (stats[h][k * pairs + p : k * pairs + p + 1] for k in range(3))
            probs = jnp.exp(scores[half] + bias - top) * inv_sum
            weights.append(probs.astype(BF16))
            grad_scores.append((probs * (grad_prob[half] - delta)).astype(BF16))
        gk = grad_key[:, cols] + merge(mm(jnp.concatenate(grad_scores, 0), query))
        gv = grad_value[:, cols] + merge(mm(jnp.concatenate(weights, 0), grad))
        grad_kv[:, cols] = gk.astype(BF16)
        grad_kv[:, channels + p * pair : channels + (p + 1) * pair] = gv.astype(BF16)
    total = grad_normed[...] + mm_nt(grad_kv[...], w_qkv[:, channels:])
    normal, inv_std = norm_stats(latent[...])
    centred = (
        total
        - jnp.mean(total, -1, keepdims=True)
        - normal * jnp.mean(total * normal, -1, keepdims=True)
    )
    grad_out[...] = (cot[...].astype(F32) + inv_std * centred).astype(BF16)


def body(
    grid_in,
    mesh_in,
    own_src,
    own_dst,
    side_src,
    side_dst,
    side_count,
    far_src,
    far_dst,
    far_count,
    window,
    cotangent,
    w_edge,
    w_qkv,
    w_out,
):
    devices = lax.axis_size("node")
    grid_rows, channels = grid_in.shape
    m = mesh_in.shape[0]
    far_slots = far_src.shape[0]
    far_depth = far_slots // devices
    head_dim = channels // HEADS
    pair = 2 * head_dim
    pairs = channels // pair
    scale = head_dim ** (-0.5)
    meta_rows = side_src.shape[0] // (2 * LANES)

    side_src, side_dst = side_src.reshape(-1, LANES), side_dst.reshape(-1, LANES)
    own_src, own_dst = own_src.reshape(-1, LANES), own_dst.reshape(-1, LANES)
    far_src, far_dst = far_src.reshape(1, -1), far_dst.reshape(1, -1)
    side_count, far_count = side_count.reshape(1, -1), far_count.reshape(1, -1)
    message = ((BAND + meta_rows, channels), BF16)
    far_block = (2 * far_slots, channels // 2 + LANES)
    far_message, chip_message, off_message, w_edge = call(
        pack_kernel,
        [(far_block, BF16), message, message, (w_edge.shape, BF16)],
        [grid_in, window, side_src, side_dst, side_count, far_src, far_dst, far_count, w_edge],
        hbm=range(9),
        hbm_outs=range(3),
        scratch=like(grid_in, window, side_src, side_dst, side_count, far_src, far_dst, far_count)
        + [
            pltpu.VMEM(far_block, BF16),
            pltpu.VMEM((2, meta_rows, channels), BF16),
            dma(9),
            dma(5),
        ],
        name="pack",
    )
    from_chip, from_off = exchange(chip_message, off_message, "node")
    got_far = lax.all_to_all(
        far_message.reshape(devices, 2 * far_depth, far_block[1]),
        "node",
        split_axis=0,
        concat_axis=0,
        tiled=True,
    ).reshape(far_block)

    rows = ((m, channels), BF16)
    (partial,) = call(
        own_kernel,
        [((m, channels), F32)],
        [grid_in, mesh_in, own_src, own_dst, w_edge],
        hbm=range(4),
        scratch=like(grid_in, mesh_in, own_src, own_dst) + [dma(4)],
        name="own",
    )
    (partial,) = call(
        functools.partial(side_kernel, meta_rows),
        [((m, channels), F32)],
        [from_chip, from_off, w_edge, partial],
        name="side",
    )
    latent, normed = call(
        functools.partial(latent_kernel, far_depth), [rows, rows], [got_far, partial], name="latent"
    )
    chip_normed, off_normed = exchange(normed, normed, "node")
    own_qkv, w_qkv, w_out, own_cot, own_grad = call(
        project_kernel,
        [((m, 3 * channels), BF16), (w_qkv.shape, BF16), (w_out.shape, BF16), rows, rows],
        [normed, w_qkv, w_out, cotangent],
        hbm=(1, 2, 3),
        scratch=[dma(PIECES + 2)],
        name="project",
    )
    chip_grad, off_grad = exchange(own_grad, own_grad, "node")
    probs = ((pairs, 2 * m, 3 * m), BF16)
    stats, kv, weights, grad_scores = call(
        functools.partial(attend_kernel, scale, pair),
        [((3 * pairs, 2 * m), F32), ((3 * m, 2 * channels), BF16), probs, probs],
        [chip_normed, off_normed, w_qkv, own_qkv, own_grad, window],
        hbm=(5,),
        scratch=like(window) + [dma(1)],
        name="attend",
    )
    chip_stats, off_stats = exchange(stats, stats, "node")
    mesh_out, grad_normed, grad_key, grad_value, near_q = call(
        functools.partial(product_kernel, scale, pair),
        [
            rows,
            ((m, channels), F32),
            ((m, channels), F32),
            ((m, channels), F32),
            ((2 * m, channels), BF16),
        ],
        [
            weights,
            grad_scores,
            kv,
            own_qkv,
            own_grad,
            latent,
            w_out,
            w_qkv,
            chip_normed,
            off_normed,
        ],
        scratch=[pltpu.VMEM((m, channels), BF16)] * 2,
        name="product",
    )
    (mesh_grad,) = call(
        functools.partial(finish_kernel, pair, meta_rows),
        [rows],
        [
            chip_stats,
            off_stats,
            from_chip,
            from_off,
            near_q,
            chip_grad,
            off_grad,
            own_qkv,
            grad_key,
            grad_value,
            grad_normed,
            w_qkv,
            latent,
            own_cot,
        ],
        scratch=[pltpu.VMEM((m, 2 * channels), BF16)],
        name="finish",
    )
    return (mesh_out, mesh_grad)


def solution(mesh):
    rows = P(("groups", "node"), None)
    flat = P(("groups", "node"))
    placed = (rows, rows) + (flat,) * 8 + (P(None, ("groups", "node")), rows, P(), P(), P())
    return jax.shard_map(
        body, mesh=mesh, in_specs=placed, out_specs=(rows, rows), check_vma=False
    )
```

```python
import functools

import jax
import jax.numpy as jnp
from jax import lax
from jax.experimental import pallas as pl
from jax.experimental.pallas import tpu as pltpu
from jax.sharding import PartitionSpec as P

HEADS = 16
BAND = 128
LANES = 128
F32 = jnp.float32
BF16 = jnp.bfloat16
I32 = jnp.int32
VMEM_LIMIT = 28 * 2**20
PIECES = 6


def mm(a, b):
    return lax.dot_general(a, b, (((1,), (0,)), ((), ())), preferred_element_type=F32)


def mm_nt(a, b):
    return lax.dot_general(a, b, (((1,), (1,)), ((), ())), preferred_element_type=F32)


def mm_tn(a, b):
    return lax.dot_general(a, b, (((0,), (0,)), ((), ())), preferred_element_type=F32)


def iota(shape, dim):
    return lax.broadcasted_iota(I32, shape, dim)


def call(kernel, outs, args, hbm=(), hbm_outs=(), anywhere=(), scratch=(), name=None):
    args = [
        pltpu.with_memory_space_constraint(a, pltpu.HBM) if i in hbm else a
        for i, a in enumerate(args)
    ]

    def specs(count, far, free=()):
        return [
            pl.BlockSpec(
                memory_space=pltpu.HBM if i in far else pl.ANY if i in free else pltpu.VMEM
            )
            for i in range(count)
        ]

    return pl.pallas_call(
        kernel,
        out_shape=[
            (pltpu.HBM if i in hbm_outs else jax.ShapeDtypeStruct)(shape, dtype)
            for i, (shape, dtype) in enumerate(outs)
        ],
        in_specs=specs(len(args), hbm, anywhere),
        out_specs=specs(len(outs), hbm_outs),
        scratch_shapes=list(scratch),
        compiler_params=pltpu.CompilerParams(vmem_limit_bytes=VMEM_LIMIT),
        name=name,
    )(*args)


def dma(count):
    return pltpu.SemaphoreType.DMA((count,))


def start_all(pairs, sems):
    copies = [pltpu.make_async_copy(src, dst, sems.at[i]) for i, (src, dst) in enumerate(pairs)]
    for copy in copies:
        copy.start()
    return copies


def like(*arrays):
    return [pltpu.VMEM(a.shape, a.dtype) for a in arrays]


def exchange(chip_message, off_message, axis):
    n = lax.axis_size(axis)
    from_off = lax.ppermute(
        off_message, axis, [p for i in range(1, n - 1, 2) for p in ((i, i + 1), (i + 1, i))]
    )
    from_chip = lax.ppermute(
        chip_message, axis, [p for i in range(0, n, 2) for p in ((i, i + 1), (i + 1, i))]
    )
    return from_chip, from_off


def is_odd():
    return lax.axis_index("node") % 2


def gelu(projected):
    x = projected.astype(BF16).astype(F32)
    inner = (2.0 / jnp.pi) ** 0.5 * (x + 0.044715 * (x * x * x))
    return (0.5 * x * (1.0 + jnp.tanh(inner))).astype(BF16)


def onehot_rows(index_rows, count):
    parts = [
        jnp.where(iota((count, row.shape[1]), 0) == row, 1.0, 0.0).astype(BF16)
        for row in index_rows
    ]
    return parts[0] if len(parts) == 1 else jnp.concatenate(parts, 1)


def norm_stats(latent):
    values = latent.astype(F32)
    row_mean = jnp.mean(values, -1, keepdims=True)
    centred = values - row_mean
    variance = jnp.mean(centred * centred, -1, keepdims=True)
    inv_std = lax.rsqrt(variance + 1e-05)
    return centred * inv_std, inv_std


def band_kernel(
    grid_hbm,
    window_hbm,
    side_src_hbm,
    side_dst_hbm,
    side_count_hbm,
    chip_out,
    off_out,
    bands,
    window,
    side_src,
    side_dst,
    side_count,
    meta,
    sems,
    out_sems,
):
    grid_rows, channels = grid_hbm.shape
    mesh_rows = window.shape[1]
    first = grid_rows - BAND
    count = side_src.shape[0] // 2
    copies = start_all(
        [
            (side_src_hbm, side_src),
            (side_dst_hbm, side_dst),
            (side_count_hbm, side_count),
            (window_hbm, window),
            (grid_hbm.at[pl.ds(0, BAND)], bands.at[0]),
            (grid_hbm.at[pl.ds(first, BAND)], bands.at[1]),
        ],
        sems,
    )
    for copy in copies[:4]:
        copy.wait()
    for k in range(2):
        rank = iota((count, LANES), 0) * LANES + iota((count, LANES), 1)
        src = side_src[k * count : (k + 1) * count] - k * first
        live = rank < side_count[:, k : k + 1]
        dst = jnp.where(live, side_dst[k * count : (k + 1) * count], mesh_rows)
        reach = jnp.concatenate([window[...], jnp.zeros((count - 2, mesh_rows), I32)], 0)
        blank = jnp.zeros((count, channels - 2 * LANES - mesh_rows), I32)
        meta[k] = jnp.concatenate([src, dst, reach, blank], 1).astype(F32).astype(BF16)
    for copy in copies[4:]:
        copy.wait()
    odd = is_odd()
    outs = start_all(
        [
            pair
            for k, out in ((1 - odd, chip_out), (odd, off_out))
            for pair in (
                (bands.at[k], out.at[pl.ds(0, BAND)]),
                (meta.at[k], out.at[pl.ds(BAND, count)]),
            )
        ],
        out_sems,
    )
    for copy in outs:
        copy.wait()


def far_kernel(
    mesh_rows,
    grid_hbm,
    far_src_hbm,
    far_dst_hbm,
    far_count_hbm,
    w_edge_hbm,
    chip_message,
    far_out,
    w_edge,
    grid,
    far_src,
    far_dst,
    far_count,
    far,
    sems,
    out_sems,
):
    grid_rows, channels = grid.shape
    slots = far_src.shape[1]
    devices = far_count.shape[1]
    depth = slots // devices
    copies = start_all(
        [
            (far_src_hbm, far_src),
            (far_dst_hbm, far_dst),
            (far_count_hbm, far_count),
            (grid_hbm, grid),
            (w_edge_hbm, w_edge),
        ],
        sems,
    )
    for copy in copies[:3]:
        copy.wait()
    slot = iota((1, slots), 1)
    receiver = jnp.where(iota((devices, slots), 0) == iota((devices, slots), 1) // depth, 1.0, 0.0)
    live = mm(far_count[...].astype(F32).astype(BF16), receiver.astype(BF16))
    target = jnp.where((slot % depth).astype(F32) < live, far_dst[...].astype(F32), 1.0 * mesh_rows)
    row = iota((2 * slots, slots), 0)
    mine = slot == row // (2 * depth) * depth + row % depth
    source = jnp.sum(jnp.where(mine, far_src[...].astype(F32), 0.0), 1, keepdims=True)
    column = jnp.sum(jnp.where(mine, target, 0.0), 1, keepdims=True)
    pick = jnp.where(iota((2 * slots, grid_rows), 1).astype(F32) == source, 1.0, 0.0).astype(BF16)
    half = channels // 2
    far[:, half:] = jnp.broadcast_to(column, (2 * slots, LANES)).astype(BF16)
    copies[3].wait()
    rows = mm(pick, grid[...]).astype(BF16)
    copies[4].wait()
    rows = gelu(mm(rows, w_edge[...]))
    is_first = iota((2 * slots, half), 0) % (2 * depth) < depth
    far[:, :half] = jnp.where(is_first, rows[:, :half], rows[:, half:])
    last = pltpu.make_async_copy(far, far_out, out_sems.at[0])
    last.start()
    last.wait()


def own_kernel(
    grid_hbm,
    mesh_in_hbm,
    own_src_hbm,
    own_dst_hbm,
    cot_hbm,
    w_out_hbm,
    w_edge,
    partial_out,
    grad_out,
    grid,
    mesh_in,
    own_src,
    own_dst,
    cot,
    w_out,
    sems,
):
    grid_rows = grid.shape[0]
    mesh_rows = mesh_in.shape[0]
    copies = start_all(
        [
            (own_src_hbm, own_src),
            (own_dst_hbm, own_dst),
            (grid_hbm, grid),
            (mesh_in_hbm, mesh_in),
            (cot_hbm, cot),
            (w_out_hbm, w_out),
        ],
        sems,
    )
    for copy in copies[:2]:
        copy.wait()
    rows = own_src.shape[0]
    src = onehot_rows([own_src[r : r + 1] for r in range(rows)], grid_rows)
    dst = onehot_rows([own_dst[r : r + 1] for r in range(rows)], mesh_rows)
    counts = mm_nt(dst, src).astype(BF16)
    for copy in copies[2:4]:
        copy.wait()
    active = gelu(mm(grid[...], w_edge[...]))
    partial_out[...] = mesh_in[...].astype(F32) + mm(counts, active)
    for copy in copies[4:]:
        copy.wait()
    grad_out[...] = mm_nt(cot[...], w_out[...]).astype(BF16)


def meta_of(message, count):
    return message[BAND : BAND + count].astype(F32).astype(I32)


def side_kernel(count, chip, off, w_edge, partial, partial_out):
    mesh_rows = partial.shape[0]
    uppers, lowers = [], []
    for side in (chip, off):
        meta = meta_of(side, count)
        src = onehot_rows([meta[r : r + 1, :LANES] for r in range(count)], BAND)
        dst = onehot_rows([meta[r : r + 1, LANES : 2 * LANES] for r in range(count)], mesh_rows)
        counts = mm_nt(dst, src)
        upper = counts.astype(BF16)
        uppers.append(upper)
        lowers.append((counts - upper.astype(F32)).astype(BF16))
    active = gelu(mm(jnp.concatenate([chip[:BAND], off[:BAND]], 0), w_edge[...]))
    landing = jnp.concatenate(uppers + lowers, 1)
    partial_out[...] = partial[...] + mm(landing, jnp.concatenate([active, active], 0))


def latent_kernel(depth, far, partial, latent_out, normed_out):
    mesh_rows, channels = partial.shape
    slots = far.shape[0]
    half = channels // 2
    first = far[:, :half]
    second = pltpu.roll(first.astype(F32), slots - depth, 0).astype(BF16)
    target = jnp.transpose(far[:, half:].astype(F32))
    if mesh_rows != LANES:
        target = jnp.broadcast_to(target[:1], (mesh_rows, slots))
    is_row = iota((mesh_rows, slots), 1) % (2 * depth) < depth
    hit = (target == iota((mesh_rows, slots), 0).astype(F32)) & is_row
    landing = jnp.where(hit, 1.0, 0.0).astype(BF16)
    total = partial[...] + mm(landing, jnp.concatenate([first, second], 1))
    latent = total.astype(BF16)
    latent_out[...] = latent
    normal, _ = norm_stats(latent)
    normed_out[...] = normal.astype(BF16)


def project_kernel(normed, own_grad, w_qkv_hbm, qkv_out, w_qkv, grad_out, sems):
    grad_out[...] = own_grad[...]
    width = w_qkv.shape[1] // PIECES
    pieces = [pl.ds(c * width, width) for c in range(PIECES)]
    copies = start_all([(w_qkv_hbm.at[:, piece], w_qkv.at[:, piece]) for piece in pieces], sems)
    for c in range(PIECES):
        copies[c].wait()
        cols = slice(c * width, (c + 1) * width)
        qkv_out[:, cols] = mm(normed[...], w_qkv[:, cols]).astype(BF16)


def halves(rows, scale=None):
    first = iota(rows.shape, 1) < rows.shape[1] // 2
    if scale is not None:
        rows = rows * jnp.asarray(scale, rows.dtype)
    zero = jnp.zeros_like(rows)
    return jnp.concatenate([jnp.where(first, rows, zero), jnp.where(first, zero, rows)], 0)


def merge(stacked):
    m = stacked.shape[0] // 2
    first = iota((m, stacked.shape[1]), 1) < stacked.shape[1] // 2
    return jnp.where(first, stacked[:m], stacked[m:])


def near_places(m):
    odd = is_odd()
    return (1 - odd) * 2 * m, odd * 2 * m


def attend_kernel(
    scale,
    pair,
    chip_normed,
    off_normed,
    w_qkv,
    own_qkv,
    own_grad,
    window_hbm,
    stats_out,
    kv,
    weights_out,
    scores_out,
    window,
    sems,
):
    fetch = start_all([(window_hbm, window)], sems)
    m, channels = chip_normed.shape
    pairs = channels // pair
    devices = lax.axis_size("node")
    me = lax.axis_index("node")
    near = mm(jnp.concatenate([chip_normed[...], off_normed[...]], 0), w_qkv[:, channels:])
    near = near.astype(BF16)
    kv[:m] = near[:m]
    kv[m : 2 * m] = own_qkv[:, channels:]
    kv[2 * m :] = near[m:]
    fetch[0].wait()
    row = iota((3 * m, m), 0)
    chip_at, off_at = near_places(m)
    key_at = jnp.where(row < m, row + chip_at, jnp.where(row < 2 * m, row, row - 2 * m + off_at))
    query_at = iota((3 * m, m), 1) + m
    inside = row < jnp.where((me == 0) | (me == devices - 1), 2 * m, 3 * m)
    keep = (
        inside & (key_at >= query_at - window[0:1, :]) & (key_at <= query_at + window[1:2, :])
    )
    bias = jnp.transpose(jnp.where(keep, 0.0, -jnp.inf).astype(F32))
    bias = jnp.concatenate([bias, bias], 0)
    lane = iota((2 * m, LANES), 1)
    stats = jnp.zeros((2 * m, LANES), F32)
    for p in range(pairs):
        cols = slice(p * pair, (p + 1) * pair)
        q2 = halves(own_qkv[:, cols], scale)
        g2 = halves(own_grad[:, cols])
        scores = mm_nt(q2, kv[:, cols]) + bias
        top = jnp.max(scores, 1, keepdims=True)
        shifted = jnp.exp(scores - top)
        inv_sum = 1.0 / jnp.sum(shifted, 1, keepdims=True)
        probs = shifted * inv_sum
        weights_out[p] = probs.astype(BF16)
        grad_prob = mm_nt(g2, kv[:, channels + p * pair : channels + (p + 1) * pair])
        delta = jnp.sum(probs * grad_prob, 1, keepdims=True)
        scores_out[p] = (probs * (grad_prob - delta)).astype(BF16)
        stats = jnp.where(lane == p, top, stats)
        stats = jnp.where(lane == pairs + p, inv_sum, stats)
        stats = jnp.where(lane == 2 * pairs + p, delta, stats)
    stats_out[...] = jnp.transpose(stats)[: 3 * pairs]


def product_kernel(
    scale,
    pair,
    weights,
    grad_scores,
    kv,
    own_qkv,
    own_grad,
    latent,
    w_out_hbm,
    w_qkv,
    chip_normed,
    off_normed,
    mesh_out,
    grad_normed,
    grad_key,
    grad_value,
    near_q_out,
    attention,
    grad_query,
    w_out,
    sems,
):
    fetch = start_all([(w_out_hbm, w_out)], sems)
    m, channels = latent.shape
    for p in range(channels // pair):
        cols = slice(p * pair, (p + 1) * pair)
        key = kv[:, cols]
        value = kv[:, channels + p * pair : channels + (p + 1) * pair]
        attention[:, cols] = merge(mm(weights[p], value)).astype(BF16)
        grad_query[:, cols] = (merge(mm(grad_scores[p], key)) * scale).astype(BF16)
        grad_key[:, cols] = mm_tn(grad_scores[p, :, m : 2 * m], halves(own_qkv[:, cols], scale))
        grad_value[:, cols] = mm_tn(weights[p, :, m : 2 * m], halves(own_grad[:, cols]))
    near = mm(jnp.concatenate([chip_normed[...], off_normed[...]], 0), w_qkv[:, :channels])
    near_q_out[...] = near.astype(BF16) * jnp.asarray(scale, BF16)
    grad_normed[...] = mm_nt(grad_query[...], w_qkv[:, :channels])
    fetch[0].wait()
    mesh_out[...] = (latent[...].astype(F32) + mm(attention[...], w_out[...])).astype(BF16)


def finish_kernel(
    pair,
    count,
    chip_stats,
    off_stats,
    chip_first,
    off_first,
    near_q,
    chip_grad,
    off_grad,
    own_qkv,
    grad_key,
    grad_value,
    grad_normed,
    w_qkv,
    latent,
    cot_hbm,
    grad_out,
    grad_kv,
    cot,
    sems,
):
    fetch = start_all([(cot_hbm, cot)], sems)
    m, channels = latent.shape
    reach = [meta_of(side, count)[:8, 2 * LANES : 2 * LANES + m] for side in (chip_first, off_first)]
    reach = jnp.concatenate(reach, 1)
    key_at = iota((m, 2 * m), 0) + m
    lane = iota((m, 2 * m), 1)
    chip_at, off_at = near_places(m)
    query_at = jnp.where(lane < m, lane + chip_at, lane - m + off_at)
    keep = (key_at >= query_at - reach[0:1, :]) & (key_at <= query_at + reach[1:2, :])
    bias = jnp.where(keep, 0.0, -jnp.inf).astype(F32)
    pairs = channels // pair

    stats = []
    for h in range(2):
        lanes = slice(h * m, (h + 1) * m)
        stats.append(jnp.concatenate([chip_stats[:, lanes], off_stats[:, lanes]], 1))
    for p in range(pairs):
        cols = slice(p * pair, (p + 1) * pair)
        key2 = halves(own_qkv[:, channels + p * pair : channels + (p + 1) * pair])
        value2 = halves(own_qkv[:, 2 * channels + p * pair : 2 * channels + (p + 1) * pair])
        query = near_q[:, cols]
        grad = jnp.concatenate([chip_grad[:, cols], off_grad[:, cols]], 0)
        scores = mm_nt(key2, query)
        grad_prob = mm_nt(value2, grad)
        weights, grad_scores = [], []
        for h in range(2):
            half = slice(h * m, (h + 1) * m)
            top, inv_sum, delta = (stats[h][k * pairs + p : k * pairs + p + 1] for k in range(3))
            probs = jnp.exp(scores[half] + bias - top) * inv_sum
            weights.append(probs.astype(BF16))
            grad_scores.append((probs * (grad_prob[half] - delta)).astype(BF16))
        gk = grad_key[:, cols] + merge(mm(jnp.concatenate(grad_scores, 0), query))
        gv = grad_value[:, cols] + merge(mm(jnp.concatenate(weights, 0), grad))
        grad_kv[:, cols] = gk.astype(BF16)
        grad_kv[:, channels + p * pair : channels + (p + 1) * pair] = gv.astype(BF16)
    total = grad_normed[...] + mm_nt(grad_kv[...], w_qkv[:, channels:])
    normal, inv_std = norm_stats(latent[...])
    centred = (
        total
        - jnp.mean(total, -1, keepdims=True)
        - normal * jnp.mean(total * normal, -1, keepdims=True)
    )
    fetch[0].wait()
    grad_out[...] = (cot[...].astype(F32) + inv_std * centred).astype(BF16)


def body(
    grid_in,
    mesh_in,
    own_src,
    own_dst,
    side_src,
    side_dst,
    side_count,
    far_src,
    far_dst,
    far_count,
    window,
    cotangent,
    w_edge,
    w_qkv,
    w_out,
):
    devices = lax.axis_size("node")
    grid_rows, channels = grid_in.shape
    m = mesh_in.shape[0]
    far_slots = far_src.shape[0]
    far_depth = far_slots // devices
    head_dim = channels // HEADS
    pair = 2 * head_dim
    pairs = channels // pair
    scale = head_dim ** (-0.5)
    meta_rows = side_src.shape[0] // (2 * LANES)

    side_src, side_dst = side_src.reshape(-1, LANES), side_dst.reshape(-1, LANES)
    own_src, own_dst = own_src.reshape(-1, LANES), own_dst.reshape(-1, LANES)
    far_src, far_dst = far_src.reshape(1, -1), far_dst.reshape(1, -1)
    side_count, far_count = side_count.reshape(1, -1), far_count.reshape(1, -1)
    message = ((BAND + meta_rows, channels), BF16)
    far_block = (2 * far_slots, channels // 2 + LANES)
    chip_message, off_message = call(
        band_kernel,
        [message, message],
        [grid_in, window, side_src, side_dst, side_count],
        hbm=range(5),
        hbm_outs=range(2),
        scratch=[pltpu.VMEM((2, BAND, channels), BF16)]
        + like(window, side_src, side_dst, side_count)
        + [pltpu.VMEM((2, meta_rows, channels), BF16), dma(6), dma(4)],
        name="bands",
    )
    from_chip, from_off = exchange(chip_message, off_message, "node")
    far_message, w_edge = call(
        functools.partial(far_kernel, m),
        [(far_block, BF16), (w_edge.shape, BF16)],
        [grid_in, far_src, far_dst, far_count, w_edge, from_chip],
        hbm=range(5),
        anywhere=(5,),
        hbm_outs=(0,),
        scratch=like(grid_in, far_src, far_dst, far_count)
        + [pltpu.VMEM(far_block, BF16), dma(5), dma(1)],
        name="far",
    )
    got_far = lax.all_to_all(
        far_message.reshape(devices, 2 * far_depth, far_block[1]),
        "node",
        split_axis=0,
        concat_axis=0,
        tiled=True,
    ).reshape(far_block)

    rows = ((m, channels), BF16)
    partial, own_grad = call(
        own_kernel,
        [((m, channels), F32), rows],
        [grid_in, mesh_in, own_src, own_dst, cotangent, w_out, w_edge],
        hbm=range(6),
        scratch=like(grid_in, mesh_in, own_src, own_dst, cotangent, w_out) + [dma(6)],
        name="own",
    )
    (partial,) = call(
        functools.partial(side_kernel, meta_rows),
        [((m, channels), F32)],
        [from_chip, from_off, w_edge, partial],
        name="side",
    )
    latent, normed = call(
        functools.partial(latent_kernel, far_depth), [rows, rows], [got_far, partial], name="latent"
    )
    chip_normed, off_normed = exchange(normed, normed, "node")
    own_qkv, w_qkv, own_grad = call(
        project_kernel,
        [((m, 3 * channels), BF16), (w_qkv.shape, BF16), rows],
        [normed, own_grad, w_qkv],
        hbm=(2,),
        scratch=[dma(PIECES)],
        name="project",
    )
    chip_grad, off_grad = exchange(own_grad, own_grad, "node")
    probs = ((pairs, 2 * m, 3 * m), BF16)
    stats, kv, weights, grad_scores = call(
        functools.partial(attend_kernel, scale, pair),
        [((3 * pairs, 2 * m), F32), ((3 * m, 2 * channels), BF16), probs, probs],
        [chip_normed, off_normed, w_qkv, own_qkv, own_grad, window],
        hbm=(5,),
        scratch=like(window) + [dma(1)],
        name="attend",
    )
    chip_stats, off_stats = exchange(stats, stats, "node")
    mesh_out, grad_normed, grad_key, grad_value, near_q = call(
        functools.partial(product_kernel, scale, pair),
        [
            rows,
            ((m, channels), F32),
            ((m, channels), F32),
            ((m, channels), F32),
            ((2 * m, channels), BF16),
        ],
        [
            weights,
            grad_scores,
            kv,
            own_qkv,
            own_grad,
            latent,
            w_out,
            w_qkv,
            chip_normed,
            off_normed,
        ],
        hbm=(6,),
        scratch=[pltpu.VMEM((m, channels), BF16)] * 2 + like(w_out) + [dma(1)],
        name="product",
    )
    (mesh_grad,) = call(
        functools.partial(finish_kernel, pair, meta_rows),
        [rows],
        [
            chip_stats,
            off_stats,
            from_chip,
            from_off,
            near_q,
            chip_grad,
            off_grad,
            own_qkv,
            grad_key,
            grad_value,
            grad_normed,
            w_qkv,
            latent,
            cotangent,
        ],
        hbm=(13,),
        scratch=[pltpu.VMEM((m, 2 * channels), BF16)] + like(cotangent) + [dma(1)],
        name="finish",
    )
    return (mesh_out, mesh_grad)


def solution(mesh):
    rows = P(("groups", "node"), None)
    flat = P(("groups", "node"))
    placed = (rows, rows) + (flat,) * 8 + (P(None, ("groups", "node")), rows, P(), P(), P())
    return jax.shard_map(
        body, mesh=mesh, in_specs=placed, out_specs=(rows, rows), check_vma=False
    )
```

```python
import functools

import jax
import jax.numpy as jnp
from jax import lax
from jax.experimental import pallas as pl
from jax.experimental.pallas import tpu as pltpu
from jax.sharding import PartitionSpec as P

HEADS = 16
BAND = 128
LANES = 128
F32 = jnp.float32
BF16 = jnp.bfloat16
I32 = jnp.int32
VMEM_LIMIT = 28 * 2**20
PIECES = 6


def mm(a, b):
    return lax.dot_general(a, b, (((1,), (0,)), ((), ())), preferred_element_type=F32)


def mm_nt(a, b):
    return lax.dot_general(a, b, (((1,), (1,)), ((), ())), preferred_element_type=F32)


def mm_tn(a, b):
    return lax.dot_general(a, b, (((0,), (0,)), ((), ())), preferred_element_type=F32)


def iota(shape, dim):
    return lax.broadcasted_iota(I32, shape, dim)


def call(kernel, outs, args, hbm=(), hbm_outs=(), scratch=(), name=None, flops=None):
    args = [
        pltpu.with_memory_space_constraint(a, pltpu.HBM) if i in hbm else a
        for i, a in enumerate(args)
    ]

    def specs(count, far):
        return [
            pl.BlockSpec(memory_space=pltpu.HBM if i in far else pltpu.VMEM) for i in range(count)
        ]

    return pl.pallas_call(
        kernel,
        out_shape=[
            (pltpu.HBM if i in hbm_outs else jax.ShapeDtypeStruct)(shape, dtype)
            for i, (shape, dtype) in enumerate(outs)
        ],
        in_specs=specs(len(args), hbm),
        out_specs=specs(len(outs), hbm_outs),
        scratch_shapes=list(scratch),
        compiler_params=pltpu.CompilerParams(vmem_limit_bytes=VMEM_LIMIT),
        cost_estimate=flops and pl.CostEstimate(flops=flops, transcendentals=0, bytes_accessed=0),
        name=name,
    )(*args)


def dma(count):
    return pltpu.SemaphoreType.DMA((count,))


def start_all(pairs, sems):
    copies = [pltpu.make_async_copy(src, dst, sems.at[i]) for i, (src, dst) in enumerate(pairs)]
    for copy in copies:
        copy.start()
    return copies


def like(*arrays):
    return [pltpu.VMEM(a.shape, a.dtype) for a in arrays]


def exchange(chip_message, off_message, axis):
    n = lax.axis_size(axis)
    from_off = lax.ppermute(
        off_message, axis, [p for i in range(1, n - 1, 2) for p in ((i, i + 1), (i + 1, i))]
    )
    from_chip = lax.ppermute(
        chip_message, axis, [p for i in range(0, n, 2) for p in ((i, i + 1), (i + 1, i))]
    )
    return from_chip, from_off


def is_odd():
    return lax.axis_index("node") % 2


def gelu(projected):
    x = projected.astype(BF16).astype(F32)
    inner = (2.0 / jnp.pi) ** 0.5 * (x + 0.044715 * (x * x * x))
    return (0.5 * x * (1.0 + jnp.tanh(inner))).astype(BF16)


def onehot_rows(index_rows, count):
    parts = [
        jnp.where(iota((count, row.shape[1]), 0) == row, 1.0, 0.0).astype(BF16)
        for row in index_rows
    ]
    return parts[0] if len(parts) == 1 else jnp.concatenate(parts, 1)


def norm_stats(latent):
    values = latent.astype(F32)
    row_mean = jnp.mean(values, -1, keepdims=True)
    centred = values - row_mean
    variance = jnp.mean(centred * centred, -1, keepdims=True)
    inv_std = lax.rsqrt(variance + 1e-05)
    return centred * inv_std, inv_std


def pack_kernel(
    grid_hbm,
    window_hbm,
    side_src_hbm,
    side_dst_hbm,
    side_count_hbm,
    far_src_hbm,
    far_dst_hbm,
    far_count_hbm,
    w_edge_hbm,
    far_out,
    chip_out,
    off_out,
    w_edge,
    grid,
    window,
    side_src,
    side_dst,
    side_count,
    far_src,
    far_dst,
    far_count,
    far,
    meta,
    sems,
    out_sems,
):
    grid_rows, channels = grid.shape
    mesh_rows = window.shape[1]
    slots = far_src.shape[1]
    devices = far_count.shape[1]
    depth = slots // devices
    first = grid_rows - BAND
    count = side_src.shape[0] // 2
    copies = start_all(
        [
            (side_src_hbm, side_src),
            (side_dst_hbm, side_dst),
            (side_count_hbm, side_count),
            (window_hbm, window),
            (grid_hbm, grid),
            (far_src_hbm, far_src),
            (far_dst_hbm, far_dst),
            (far_count_hbm, far_count),
            (w_edge_hbm, w_edge),
        ],
        sems,
    )
    for copy in copies[:4]:
        copy.wait()
    for k in range(2):
        rank = iota((count, LANES), 0) * LANES + iota((count, LANES), 1)
        src = side_src[k * count : (k + 1) * count] - k * first
        live = rank < side_count[:, k : k + 1]
        dst = jnp.where(live, side_dst[k * count : (k + 1) * count], mesh_rows)
        reach = jnp.concatenate([window[...], jnp.zeros((count - 2, mesh_rows), I32)], 0)
        blank = jnp.zeros((count, channels - 2 * LANES - mesh_rows), I32)
        meta[k] = jnp.concatenate([src, dst, reach, blank], 1).astype(F32).astype(BF16)
    copies[4].wait()
    odd = is_odd()
    outs = start_all(
        [
            pair
            for k, out in ((1 - odd, chip_out), (odd, off_out))
            for pair in (
                (grid.at[pl.ds(pl.multiple_of(k * first, BAND), BAND)], out.at[pl.ds(0, BAND)]),
                (meta.at[k], out.at[pl.ds(BAND, count)]),
            )
        ],
        out_sems,
    )
    for copy in copies[5:8]:
        copy.wait()
    slot = iota((1, slots), 1)
    receiver = jnp.where(iota((devices, slots), 0) == iota((devices, slots), 1) // depth, 1.0, 0.0)
    live = mm(far_count[...].astype(F32).astype(BF16), receiver.astype(BF16))
    target = jnp.where((slot % depth).astype(F32) < live, far_dst[...].astype(F32), 1.0 * mesh_rows)
    row = iota((2 * slots, slots), 0)
    mine = slot == row // (2 * depth) * depth + row % depth
    source = jnp.sum(jnp.where(mine, far_src[...].astype(F32), 0.0), 1, keepdims=True)
    column = jnp.sum(jnp.where(mine, target, 0.0), 1, keepdims=True)
    pick = jnp.where(iota((2 * slots, grid_rows), 1).astype(F32) == source, 1.0, 0.0).astype(BF16)
    rows = mm(pick, grid[...]).astype(BF16)
    copies[8].wait()
    rows = gelu(mm(rows, w_edge[...]))
    half = channels // 2
    is_first = iota((2 * slots, half), 0) % (2 * depth) < depth
    far[:, :half] = jnp.where(is_first, rows[:, :half], rows[:, half:])
    far[:, half:] = jnp.broadcast_to(column, (2 * slots, LANES)).astype(BF16)
    last = pltpu.make_async_copy(far, far_out, out_sems.at[4])
    last.start()
    for copy in outs + [last]:
        copy.wait()


def own_kernel(
    grid_hbm,
    mesh_in_hbm,
    own_src_hbm,
    own_dst_hbm,
    cot_hbm,
    w_out_hbm,
    w_edge,
    partial_out,
    grad_hbm,
    grid,
    mesh_in,
    own_src,
    own_dst,
    cot,
    w_out,
    grad,
    sems,
):
    grid_rows = grid.shape[0]
    mesh_rows = mesh_in.shape[0]
    copies = start_all(
        [
            (own_src_hbm, own_src),
            (own_dst_hbm, own_dst),
            (cot_hbm, cot),
            (w_out_hbm, w_out),
            (grid_hbm, grid),
            (mesh_in_hbm, mesh_in),
        ],
        sems,
    )
    for copy in copies[:2]:
        copy.wait()
    rows = own_src.shape[0]
    src = onehot_rows([own_src[r : r + 1] for r in range(rows)], grid_rows)
    dst = onehot_rows([own_dst[r : r + 1] for r in range(rows)], mesh_rows)
    counts = mm_nt(dst, src).astype(BF16)
    for copy in copies[2:4]:
        copy.wait()
    grad[...] = mm_nt(cot[...], w_out[...]).astype(BF16)
    out = pltpu.make_async_copy(grad, grad_hbm, sems.at[6])
    out.start()
    for copy in copies[4:]:
        copy.wait()
    active = gelu(mm(grid[...], w_edge[...]))
    partial_out[...] = mesh_in[...].astype(F32) + mm(counts, active)
    out.wait()


def meta_of(message, count):
    return message[BAND : BAND + count].astype(F32).astype(I32)


def side_kernel(count, chip, off, w_edge, partial, partial_out):
    mesh_rows = partial.shape[0]
    uppers, lowers = [], []
    for side in (chip, off):
        meta = meta_of(side, count)
        src = onehot_rows([meta[r : r + 1, :LANES] for r in range(count)], BAND)
        dst = onehot_rows([meta[r : r + 1, LANES : 2 * LANES] for r in range(count)], mesh_rows)
        counts = mm_nt(dst, src)
        upper = counts.astype(BF16)
        uppers.append(upper)
        lowers.append((counts - upper.astype(F32)).astype(BF16))
    active = gelu(mm(jnp.concatenate([chip[:BAND], off[:BAND]], 0), w_edge[...]))
    landing = jnp.concatenate(uppers + lowers, 1)
    partial_out[...] = partial[...] + mm(landing, jnp.concatenate([active, active], 0))


def latent_kernel(depth, far, partial, latent_out, normed_out):
    mesh_rows, channels = partial.shape
    slots = far.shape[0]
    half = channels // 2
    first = far[:, :half]
    second = pltpu.roll(first.astype(F32), slots - depth, 0).astype(BF16)
    target = jnp.transpose(far[:, half:].astype(F32))
    if mesh_rows != LANES:
        target = jnp.broadcast_to(target[:1], (mesh_rows, slots))
    is_row = iota((mesh_rows, slots), 1) % (2 * depth) < depth
    hit = (target == iota((mesh_rows, slots), 0).astype(F32)) & is_row
    landing = jnp.where(hit, 1.0, 0.0).astype(BF16)
    total = partial[...] + mm(landing, jnp.concatenate([first, second], 1))
    latent = total.astype(BF16)
    latent_out[...] = latent
    normal, _ = norm_stats(latent)
    normed_out[...] = normal.astype(BF16)


def project_kernel(normed, grad_hbm, w_qkv_hbm, qkv_out, w_qkv, grad_out, sems):
    width = w_qkv.shape[1] // PIECES
    pieces = [pl.ds(c * width, width) for c in range(PIECES)]
    copies = start_all(
        [(w_qkv_hbm.at[:, piece], w_qkv.at[:, piece]) for piece in pieces] + [(grad_hbm, grad_out)],
        sems,
    )
    for c in range(PIECES):
        copies[c].wait()
        cols = slice(c * width, (c + 1) * width)
        qkv_out[:, cols] = mm(normed[...], w_qkv[:, cols]).astype(BF16)
    copies[PIECES].wait()


def halves(rows, scale=None):
    first = iota(rows.shape, 1) < rows.shape[1] // 2
    if scale is not None:
        rows = rows * jnp.asarray(scale, rows.dtype)
    zero = jnp.zeros_like(rows)
    return jnp.concatenate([jnp.where(first, rows, zero), jnp.where(first, zero, rows)], 0)


def merge(stacked):
    m = stacked.shape[0] // 2
    first = iota((m, stacked.shape[1]), 1) < stacked.shape[1] // 2
    return jnp.where(first, stacked[:m], stacked[m:])


def near_places(m):
    odd = is_odd()
    return (1 - odd) * 2 * m, odd * 2 * m


def attend_kernel(
    scale,
    pair,
    chip_normed,
    off_normed,
    w_qkv,
    own_qkv,
    own_grad,
    window_hbm,
    w_out_hbm,
    cot_hbm,
    stats_out,
    kv,
    weights_out,
    scores_out,
    w_out,
    cot,
    window,
    sems,
):
    fetch = start_all([(window_hbm, window), (w_out_hbm, w_out), (cot_hbm, cot)], sems)
    m, channels = chip_normed.shape
    pairs = channels // pair
    devices = lax.axis_size("node")
    me = lax.axis_index("node")
    near = mm(jnp.concatenate([chip_normed[...], off_normed[...]], 0), w_qkv[:, channels:])
    near = near.astype(BF16)
    kv[:m] = near[:m]
    kv[m : 2 * m] = own_qkv[:, channels:]
    kv[2 * m :] = near[m:]
    fetch[0].wait()
    row = iota((3 * m, m), 0)
    chip_at, off_at = near_places(m)
    key_at = jnp.where(row < m, row + chip_at, jnp.where(row < 2 * m, row, row - 2 * m + off_at))
    query_at = iota((3 * m, m), 1) + m
    inside = row < jnp.where((me == 0) | (me == devices - 1), 2 * m, 3 * m)
    keep = (
        inside & (key_at >= query_at - window[0:1, :]) & (key_at <= query_at + window[1:2, :])
    )
    bias = jnp.transpose(jnp.where(keep, 0.0, -jnp.inf).astype(F32))
    bias = jnp.concatenate([bias, bias], 0)
    lane = iota((2 * m, LANES), 1)
    stats = jnp.zeros((2 * m, LANES), F32)
    for p in range(pairs):
        cols = slice(p * pair, (p + 1) * pair)
        q2 = halves(own_qkv[:, cols], scale)
        g2 = halves(own_grad[:, cols])
        scores = mm_nt(q2, kv[:, cols]) + bias
        top = jnp.max(scores, 1, keepdims=True)
        shifted = jnp.exp(scores - top)
        inv_sum = 1.0 / jnp.sum(shifted, 1, keepdims=True)
        probs = shifted * inv_sum
        weights_out[p] = probs.astype(BF16)
        grad_prob = mm_nt(g2, kv[:, channels + p * pair : channels + (p + 1) * pair])
        delta = jnp.sum(probs * grad_prob, 1, keepdims=True)
        scores_out[p] = (probs * (grad_prob - delta)).astype(BF16)
        stats = jnp.where(lane == p, top, stats)
        stats = jnp.where(lane == pairs + p, inv_sum, stats)
        stats = jnp.where(lane == 2 * pairs + p, delta, stats)
    stats_out[...] = jnp.transpose(stats)[: 3 * pairs]
    for copy in fetch[1:]:
        copy.wait()


def product_kernel(
    scale,
    pair,
    weights,
    grad_scores,
    kv,
    own_qkv,
    own_grad,
    latent,
    w_out,
    w_qkv,
    chip_normed,
    off_normed,
    mesh_out,
    grad_normed,
    grad_key,
    grad_value,
    near_q_out,
    attention,
    grad_query,
):
    m, channels = latent.shape
    for p in range(channels // pair):
        cols = slice(p * pair, (p + 1) * pair)
        key = kv[:, cols]
        value = kv[:, channels + p * pair : channels + (p + 1) * pair]
        attention[:, cols] = merge(mm(weights[p], value)).astype(BF16)
        grad_query[:, cols] = (merge(mm(grad_scores[p], key)) * scale).astype(BF16)
        grad_key[:, cols] = mm_tn(grad_scores[p, :, m : 2 * m], halves(own_qkv[:, cols], scale))
        grad_value[:, cols] = mm_tn(weights[p, :, m : 2 * m], halves(own_grad[:, cols]))
    mesh_out[...] = (latent[...].astype(F32) + mm(attention[...], w_out[...])).astype(BF16)
    grad_normed[...] = mm_nt(grad_query[...], w_qkv[:, :channels])
    near = mm(jnp.concatenate([chip_normed[...], off_normed[...]], 0), w_qkv[:, :channels])
    near_q_out[...] = near.astype(BF16) * jnp.asarray(scale, BF16)


def finish_kernel(
    pair,
    count,
    chip_stats,
    off_stats,
    chip_first,
    off_first,
    near_q,
    chip_grad,
    off_grad,
    own_qkv,
    grad_key,
    grad_value,
    grad_normed,
    w_qkv,
    latent,
    cot,
    grad_out,
    grad_kv,
):
    m, channels = latent.shape
    reach = [meta_of(side, count)[:8, 2 * LANES : 2 * LANES + m] for side in (chip_first, off_first)]
    reach = jnp.concatenate(reach, 1)
    key_at = iota((m, 2 * m), 0) + m
    lane = iota((m, 2 * m), 1)
    chip_at, off_at = near_places(m)
    query_at = jnp.where(lane < m, lane + chip_at, lane - m + off_at)
    keep = (key_at >= query_at - reach[0:1, :]) & (key_at <= query_at + reach[1:2, :])
    bias = jnp.where(keep, 0.0, -jnp.inf).astype(F32)
    pairs = channels // pair

    stats = []
    for h in range(2):
        lanes = slice(h * m, (h + 1) * m)
        stats.append(jnp.concatenate([chip_stats[:, lanes], off_stats[:, lanes]], 1))
    for p in range(pairs):
        cols = slice(p * pair, (p + 1) * pair)
        key2 = halves(own_qkv[:, channels + p * pair : channels + (p + 1) * pair])
        value2 = halves(own_qkv[:, 2 * channels + p * pair : 2 * channels + (p + 1) * pair])
        query = near_q[:, cols]
        grad = jnp.concatenate([chip_grad[:, cols], off_grad[:, cols]], 0)
        scores = mm_nt(key2, query)
        grad_prob = mm_nt(value2, grad)
        weights, grad_scores = [], []
        for h in range(2):
            half = slice(h * m, (h + 1) * m)
            top, inv_sum, delta = (stats[h][k * pairs + p : k * pairs + p + 1] for k in range(3))
            probs = jnp.exp(scores[half] + bias - top) * inv_sum
            weights.append(probs.astype(BF16))
            grad_scores.append((probs * (grad_prob[half] - delta)).astype(BF16))
        gk = grad_key[:, cols] + merge(mm(jnp.concatenate(grad_scores, 0), query))
        gv = grad_value[:, cols] + merge(mm(jnp.concatenate(weights, 0), grad))
        grad_kv[:, cols] = gk.astype(BF16)
        grad_kv[:, channels + p * pair : channels + (p + 1) * pair] = gv.astype(BF16)
    total = grad_normed[...] + mm_nt(grad_kv[...], w_qkv[:, channels:])
    normal, inv_std = norm_stats(latent[...])
    centred = (
        total
        - jnp.mean(total, -1, keepdims=True)
        - normal * jnp.mean(total * normal, -1, keepdims=True)
    )
    grad_out[...] = (cot[...].astype(F32) + inv_std * centred).astype(BF16)


def body(
    grid_in,
    mesh_in,
    own_src,
    own_dst,
    side_src,
    side_dst,
    side_count,
    far_src,
    far_dst,
    far_count,
    window,
    cotangent,
    w_edge,
    w_qkv,
    w_out,
):
    devices = lax.axis_size("node")
    grid_rows, channels = grid_in.shape
    m = mesh_in.shape[0]
    far_slots = far_src.shape[0]
    far_depth = far_slots // devices
    head_dim = channels // HEADS
    pair = 2 * head_dim
    pairs = channels // pair
    scale = head_dim ** (-0.5)
    meta_rows = side_src.shape[0] // (2 * LANES)

    side_src, side_dst = side_src.reshape(-1, LANES), side_dst.reshape(-1, LANES)
    own_src, own_dst = own_src.reshape(-1, LANES), own_dst.reshape(-1, LANES)
    far_src, far_dst = far_src.reshape(1, -1), far_dst.reshape(1, -1)
    side_count, far_count = side_count.reshape(1, -1), far_count.reshape(1, -1)
    message = ((BAND + meta_rows, channels), BF16)
    far_block = (2 * far_slots, channels // 2 + LANES)
    far_message, chip_message, off_message, w_edge = call(
        pack_kernel,
        [(far_block, BF16), message, message, (w_edge.shape, BF16)],
        [grid_in, window, side_src, side_dst, side_count, far_src, far_dst, far_count, w_edge],
        hbm=range(9),
        hbm_outs=range(3),
        scratch=like(grid_in, window, side_src, side_dst, side_count, far_src, far_dst, far_count)
        + [
            pltpu.VMEM(far_block, BF16),
            pltpu.VMEM((2, meta_rows, channels), BF16),
            dma(9),
            dma(5),
        ],
        name="pack",
    )
    from_chip, from_off = exchange(chip_message, off_message, "node")
    got_far = lax.all_to_all(
        far_message.reshape(devices, 2 * far_depth, far_block[1]),
        "node",
        split_axis=0,
        concat_axis=0,
        tiled=True,
    ).reshape(far_block)

    rows = ((m, channels), BF16)
    partial, own_grad = call(
        own_kernel,
        [((m, channels), F32), rows],
        [grid_in, mesh_in, own_src, own_dst, cotangent, w_out, w_edge],
        hbm=range(6),
        hbm_outs=(1,),
        scratch=like(grid_in, mesh_in, own_src, own_dst, cotangent, w_out, cotangent) + [dma(7)],
        name="own",
    )
    (partial,) = call(
        functools.partial(side_kernel, meta_rows),
        [((m, channels), F32)],
        [from_chip, from_off, w_edge, partial],
        name="side",
        flops=8 * 10**9,
    )
    latent, normed = call(
        functools.partial(latent_kernel, far_depth), [rows, rows], [got_far, partial], name="latent"
    )
    chip_normed, off_normed = exchange(normed, normed, "node")
    own_qkv, w_qkv, own_grad = call(
        project_kernel,
        [((m, 3 * channels), BF16), (w_qkv.shape, BF16), rows],
        [normed, own_grad, w_qkv],
        hbm=(1, 2),
        scratch=[dma(PIECES + 1)],
        name="project",
    )
    chip_grad, off_grad = exchange(own_grad, own_grad, "node")
    probs = ((pairs, 2 * m, 3 * m), BF16)
    stats, kv, weights, grad_scores, w_out, cotangent = call(
        functools.partial(attend_kernel, scale, pair),
        [
            ((3 * pairs, 2 * m), F32),
            ((3 * m, 2 * channels), BF16),
            probs,
            probs,
            (w_out.shape, BF16),
            rows,
        ],
        [chip_normed, off_normed, w_qkv, own_qkv, own_grad, window, w_out, cotangent],
        hbm=(5, 6, 7),
        scratch=like(window) + [dma(3)],
        name="attend",
    )
    chip_stats, off_stats = exchange(stats, stats, "node")
    mesh_out, grad_normed, grad_key, grad_value, near_q = call(
        functools.partial(product_kernel, scale, pair),
        [
            rows,
            ((m, channels), F32),
            ((m, channels), F32),
            ((m, channels), F32),
            ((2 * m, channels), BF16),
        ],
        [
            weights,
            grad_scores,
            kv,
            own_qkv,
            own_grad,
            latent,
            w_out,
            w_qkv,
            chip_normed,
            off_normed,
        ],
        scratch=[pltpu.VMEM((m, channels), BF16)] * 2,
        name="product",
    )
    (mesh_grad,) = call(
        functools.partial(finish_kernel, pair, meta_rows),
        [rows],
        [
            chip_stats,
            off_stats,
            from_chip,
            from_off,
            near_q,
            chip_grad,
            off_grad,
            own_qkv,
            grad_key,
            grad_value,
            grad_normed,
            w_qkv,
            latent,
            cotangent,
        ],
        scratch=[pltpu.VMEM((m, 2 * channels), BF16)],
        name="finish",
    )
    return (mesh_out, mesh_grad)


def solution(mesh):
    rows = P(("groups", "node"), None)
    flat = P(("groups", "node"))
    placed = (rows, rows) + (flat,) * 8 + (P(None, ("groups", "node")), rows, P(), P(), P())
    return jax.shard_map(
        body, mesh=mesh, in_specs=placed, out_specs=(rows, rows), check_vma=False
    )
```

```python
import functools

import jax
import jax.numpy as jnp
from jax import lax
from jax.experimental import pallas as pl
from jax.experimental.pallas import tpu as pltpu
from jax.sharding import PartitionSpec as P

HEADS = 16
BAND = 128
LANES = 128
F32 = jnp.float32
BF16 = jnp.bfloat16
I32 = jnp.int32
VMEM_LIMIT = 28 * 2**20
PIECES = 2


def mm(a, b):
    return lax.dot_general(a, b, (((1,), (0,)), ((), ())), preferred_element_type=F32)


def mm_nt(a, b):
    return lax.dot_general(a, b, (((1,), (1,)), ((), ())), preferred_element_type=F32)


def mm_tn(a, b):
    return lax.dot_general(a, b, (((0,), (0,)), ((), ())), preferred_element_type=F32)


def iota(shape, dim):
    return lax.broadcasted_iota(I32, shape, dim)


def call(kernel, outs, args, hbm=(), hbm_outs=(), scratch=(), name=None, flops=None):
    args = [
        pltpu.with_memory_space_constraint(a, pltpu.HBM) if i in hbm else a
        for i, a in enumerate(args)
    ]

    def specs(count, far):
        return [
            pl.BlockSpec(memory_space=pltpu.HBM if i in far else pltpu.VMEM) for i in range(count)
        ]

    return pl.pallas_call(
        kernel,
        out_shape=[
            (pltpu.HBM if i in hbm_outs else jax.ShapeDtypeStruct)(shape, dtype)
            for i, (shape, dtype) in enumerate(outs)
        ],
        in_specs=specs(len(args), hbm),
        out_specs=specs(len(outs), hbm_outs),
        scratch_shapes=list(scratch),
        compiler_params=pltpu.CompilerParams(vmem_limit_bytes=VMEM_LIMIT),
        cost_estimate=flops and pl.CostEstimate(flops=flops, transcendentals=0, bytes_accessed=0),
        name=name,
    )(*args)


def dma(count):
    return pltpu.SemaphoreType.DMA((count,))


def start_all(pairs, sems):
    copies = [pltpu.make_async_copy(src, dst, sems.at[i]) for i, (src, dst) in enumerate(pairs)]
    for copy in copies:
        copy.start()
    return copies


def like(*arrays):
    return [pltpu.VMEM(a.shape, a.dtype) for a in arrays]


def exchange(chip_message, off_message, axis):
    n = lax.axis_size(axis)
    from_off = lax.ppermute(
        off_message, axis, [p for i in range(1, n - 1, 2) for p in ((i, i + 1), (i + 1, i))]
    )
    from_chip = lax.ppermute(
        chip_message, axis, [p for i in range(0, n, 2) for p in ((i, i + 1), (i + 1, i))]
    )
    return from_chip, from_off


def is_odd():
    return lax.axis_index("node") % 2


def gelu(projected):
    x = projected.astype(BF16).astype(F32)
    inner = (2.0 / jnp.pi) ** 0.5 * (x + 0.044715 * (x * x * x))
    return (0.5 * x * (1.0 + jnp.tanh(inner))).astype(BF16)


def onehot_rows(index_rows, count):
    parts = [
        jnp.where(iota((count, row.shape[1]), 0) == row, 1.0, 0.0).astype(BF16)
        for row in index_rows
    ]
    return parts[0] if len(parts) == 1 else jnp.concatenate(parts, 1)


def norm_stats(latent):
    values = latent.astype(F32)
    row_mean = jnp.mean(values, -1, keepdims=True)
    centred = values - row_mean
    variance = jnp.mean(centred * centred, -1, keepdims=True)
    inv_std = lax.rsqrt(variance + 1e-05)
    return centred * inv_std, inv_std


def pack_kernel(
    grid_hbm,
    window_hbm,
    side_src_hbm,
    side_dst_hbm,
    side_count_hbm,
    far_src_hbm,
    far_dst_hbm,
    far_count_hbm,
    w_edge_hbm,
    far_out,
    chip_out,
    off_out,
    w_edge,
    grid,
    window,
    side_src,
    side_dst,
    side_count,
    far_src,
    far_dst,
    far_count,
    far,
    meta,
    sems,
    out_sems,
):
    grid_rows, channels = grid.shape
    mesh_rows = window.shape[1]
    slots = far_src.shape[1]
    devices = far_count.shape[1]
    depth = slots // devices
    first = grid_rows - BAND
    count = side_src.shape[0] // 2
    copies = start_all(
        [
            (side_src_hbm, side_src),
            (side_dst_hbm, side_dst),
            (side_count_hbm, side_count),
            (window_hbm, window),
            (grid_hbm, grid),
            (far_src_hbm, far_src),
            (far_dst_hbm, far_dst),
            (far_count_hbm, far_count),
            (w_edge_hbm, w_edge),
        ],
        sems,
    )
    for copy in copies[:4]:
        copy.wait()
    for k in range(2):
        rank = iota((count, LANES), 0) * LANES + iota((count, LANES), 1)
        src = side_src[k * count : (k + 1) * count] - k * first
        live = rank < side_count[:, k : k + 1]
        dst = jnp.where(live, side_dst[k * count : (k + 1) * count], mesh_rows)
        reach = jnp.concatenate([window[...], jnp.zeros((count - 2, mesh_rows), I32)], 0)
        blank = jnp.zeros((count, channels - 2 * LANES - mesh_rows), I32)
        meta[k] = jnp.concatenate([src, dst, reach, blank], 1).astype(F32).astype(BF16)
    copies[4].wait()
    odd = is_odd()
    outs = start_all(
        [
            pair
            for k, out in ((1 - odd, chip_out), (odd, off_out))
            for pair in (
                (grid.at[pl.ds(pl.multiple_of(k * first, BAND), BAND)], out.at[pl.ds(0, BAND)]),
                (meta.at[k], out.at[pl.ds(BAND, count)]),
            )
        ],
        out_sems,
    )
    for copy in copies[5:8]:
        copy.wait()
    slot = iota((1, slots), 1)
    receiver = jnp.where(iota((devices, slots), 0) == iota((devices, slots), 1) // depth, 1.0, 0.0)
    live = mm(far_count[...].astype(F32).astype(BF16), receiver.astype(BF16))
    target = jnp.where((slot % depth).astype(F32) < live, far_dst[...].astype(F32), 1.0 * mesh_rows)
    row = iota((2 * slots, slots), 0)
    mine = slot == row // (2 * depth) * depth + row % depth
    source = jnp.sum(jnp.where(mine, far_src[...].astype(F32), 0.0), 1, keepdims=True)
    column = jnp.sum(jnp.where(mine, target, 0.0), 1, keepdims=True)
    pick = jnp.where(iota((2 * slots, grid_rows), 1).astype(F32) == source, 1.0, 0.0).astype(BF16)
    rows = mm(pick, grid[...]).astype(BF16)
    copies[8].wait()
    rows = gelu(mm(rows, w_edge[...]))
    half = channels // 2
    is_first = iota((2 * slots, half), 0) % (2 * depth) < depth
    far[:, :half] = jnp.where(is_first, rows[:, :half], rows[:, half:])
    far[:, half:] = jnp.broadcast_to(column, (2 * slots, LANES)).astype(BF16)
    last = pltpu.make_async_copy(far, far_out, out_sems.at[4])
    last.start()
    for copy in outs + [last]:
        copy.wait()


def own_kernel(
    grid_hbm,
    mesh_in_hbm,
    own_src_hbm,
    own_dst_hbm,
    cot_hbm,
    w_out_hbm,
    w_edge,
    partial_out,
    grad_hbm,
    grid,
    mesh_in,
    own_src,
    own_dst,
    cot,
    w_out,
    grad,
    sems,
):
    grid_rows = grid.shape[0]
    mesh_rows = mesh_in.shape[0]
    copies = start_all(
        [
            (own_src_hbm, own_src),
            (own_dst_hbm, own_dst),
            (cot_hbm, cot),
            (w_out_hbm, w_out),
            (grid_hbm, grid),
            (mesh_in_hbm, mesh_in),
        ],
        sems,
    )
    for copy in copies[:2]:
        copy.wait()
    rows = own_src.shape[0]
    src = onehot_rows([own_src[r : r + 1] for r in range(rows)], grid_rows)
    dst = onehot_rows([own_dst[r : r + 1] for r in range(rows)], mesh_rows)
    counts = mm_nt(dst, src).astype(BF16)
    for copy in copies[2:4]:
        copy.wait()
    grad[...] = mm_nt(cot[...], w_out[...]).astype(BF16)
    out = pltpu.make_async_copy(grad, grad_hbm, sems.at[6])
    out.start()
    for copy in copies[4:]:
        copy.wait()
    active = gelu(mm(grid[...], w_edge[...]))
    partial_out[...] = mesh_in[...].astype(F32) + mm(counts, active)
    out.wait()


def meta_of(message, count):
    return message[BAND : BAND + count].astype(F32).astype(I32)


def side_kernel(count, chip, off, w_edge, partial, partial_out):
    mesh_rows = partial.shape[0]
    uppers, lowers = [], []
    for side in (chip, off):
        meta = meta_of(side, count)
        src = onehot_rows([meta[r : r + 1, :LANES] for r in range(count)], BAND)
        dst = onehot_rows([meta[r : r + 1, LANES : 2 * LANES] for r in range(count)], mesh_rows)
        counts = mm_nt(dst, src)
        upper = counts.astype(BF16)
        uppers.append(upper)
        lowers.append((counts - upper.astype(F32)).astype(BF16))
    active = gelu(mm(jnp.concatenate([chip[:BAND], off[:BAND]], 0), w_edge[...]))
    landing = jnp.concatenate(uppers + lowers, 1)
    partial_out[...] = partial[...] + mm(landing, jnp.concatenate([active, active], 0))


def latent_kernel(depth, far, partial, latent_out, normed_out, normal_out, inv_std_out):
    mesh_rows, channels = partial.shape
    slots = far.shape[0]
    half = channels // 2
    first = far[:, :half]
    second = pltpu.roll(first.astype(F32), slots - depth, 0).astype(BF16)
    target = jnp.transpose(far[:, half:].astype(F32))
    if mesh_rows != LANES:
        target = jnp.broadcast_to(target[:1], (mesh_rows, slots))
    is_row = iota((mesh_rows, slots), 1) % (2 * depth) < depth
    hit = (target == iota((mesh_rows, slots), 0).astype(F32)) & is_row
    landing = jnp.where(hit, 1.0, 0.0).astype(BF16)
    total = partial[...] + mm(landing, jnp.concatenate([first, second], 1))
    latent = total.astype(BF16)
    latent_out[...] = latent
    normal, inv_std = norm_stats(latent)
    normed_out[...] = normal.astype(BF16)
    normal_out[...] = normal
    inv_std_out[...] = jnp.broadcast_to(inv_std, inv_std_out.shape)


def halves(rows, scale=None):
    first = iota(rows.shape, 1) < rows.shape[1] // 2
    if scale is not None:
        rows = rows * jnp.asarray(scale, rows.dtype)
    zero = jnp.zeros_like(rows)
    return jnp.concatenate([jnp.where(first, rows, zero), jnp.where(first, zero, rows)], 0)


def merge(stacked):
    m = stacked.shape[0] // 2
    first = iota((m, stacked.shape[1]), 1) < stacked.shape[1] // 2
    return jnp.where(first, stacked[:m], stacked[m:])


def project_kernel(
    scale, pair, normed, grad_hbm, w_qkv_hbm, qkv_out, w_qkv, grad_out, scores_out, products_out, sems
):
    m, channels = normed.shape
    width = channels // PIECES
    starts = [part * channels + c * width for c in range(PIECES) for part in range(3)]
    copies = start_all(
        [(grad_hbm, grad_out)]
        + [(w_qkv_hbm.at[:, pl.ds(at, width)], w_qkv.at[:, pl.ds(at, width)]) for at in starts],
        sems,
    )
    for i, at in enumerate(starts):
        copies[1 + i].wait()
        cols = slice(at, at + width)
        qkv_out[:, cols] = mm(normed[...], w_qkv[:, cols]).astype(BF16)
        if i % 3 < 2:
            continue
        if i == 2:
            copies[0].wait()
        for p in range(i // 3 * width // pair, (i // 3 + 1) * width // pair):
            q, k, v = (
                slice(part * channels + p * pair, part * channels + (p + 1) * pair)
                for part in range(3)
            )
            scores_out[p] = mm_nt(halves(qkv_out[:, q], scale), qkv_out[:, k])
            products_out[p] = mm_nt(halves(grad_out[:, q]), qkv_out[:, v])


def near_places(m):
    odd = is_odd()
    return (1 - odd) * 2 * m, odd * 2 * m


def attend_kernel(
    scale,
    pair,
    chip_normed,
    off_normed,
    w_qkv,
    own_qkv,
    own_grad,
    own_scores,
    own_products,
    window_hbm,
    w_out_hbm,
    cot_hbm,
    stats_out,
    kv,
    weights_out,
    scores_out,
    w_out,
    cot,
    window,
    sems,
):
    fetch = start_all([(window_hbm, window), (w_out_hbm, w_out), (cot_hbm, cot)], sems)
    m, channels = chip_normed.shape
    pairs = channels // pair
    devices = lax.axis_size("node")
    me = lax.axis_index("node")
    near = mm(jnp.concatenate([chip_normed[...], off_normed[...]], 0), w_qkv[:, channels:])
    kv[: 2 * m] = near.astype(BF16)
    kv[2 * m :] = own_qkv[:, channels:]
    fetch[0].wait()
    row = iota((3 * m, m), 0)
    chip_at, off_at = near_places(m)
    key_at = jnp.where(row < m, row + chip_at, jnp.where(row < 2 * m, row - m + off_at, row - m))
    query_at = iota((3 * m, m), 1) + m
    missing = (row >= m) & (row < 2 * m) & ((me == 0) | (me == devices - 1))
    keep = (key_at >= query_at - window[0:1, :]) & (key_at <= query_at + window[1:2, :])
    bias = jnp.transpose(jnp.where(keep & jnp.logical_not(missing), 0.0, -jnp.inf).astype(F32))
    bias = jnp.concatenate([bias, bias], 0)
    lane = iota((2 * m, LANES), 1)
    stats = jnp.zeros((2 * m, LANES), F32)

    def multiply(p):
        cols = slice(p * pair, (p + 1) * pair)
        value_cols = slice(channels + p * pair, channels + (p + 1) * pair)
        return (
            mm_nt(halves(own_qkv[:, cols], scale), kv[: 2 * m, cols]),
            mm_nt(halves(own_grad[:, cols]), kv[: 2 * m, value_cols]),
        )

    ahead = multiply(0)
    for p in range(pairs):
        scores, grad_prob = ahead
        if p + 1 < pairs:
            ahead = multiply(p + 1)
        scores = jnp.concatenate([scores, own_scores[p]], 1) + bias
        grad_prob = jnp.concatenate([grad_prob, own_products[p]], 1)
        top = jnp.max(scores, 1, keepdims=True)
        shifted = jnp.exp(scores - top)
        inv_sum = 1.0 / jnp.sum(shifted, 1, keepdims=True)
        probs = shifted * inv_sum
        weights_out[p] = probs.astype(BF16)
        delta = jnp.sum(probs * grad_prob, 1, keepdims=True)
        scores_out[p] = (probs * (grad_prob - delta)).astype(BF16)
        stats = jnp.where(lane == p, top, stats)
        stats = jnp.where(lane == pairs + p, inv_sum, stats)
        stats = jnp.where(lane == 2 * pairs + p, delta, stats)
    stats_out[...] = jnp.transpose(stats)[: 3 * pairs]
    for copy in fetch[1:]:
        copy.wait()


def product_kernel(
    scale,
    pair,
    weights,
    grad_scores,
    kv,
    own_qkv,
    own_grad,
    latent,
    w_out,
    w_qkv,
    chip_normed,
    off_normed,
    mesh_out,
    grad_normed,
    grad_key,
    grad_value,
    near_q_out,
    attention,
    grad_query,
):
    m, channels = latent.shape
    for p in range(channels // pair):
        cols = slice(p * pair, (p + 1) * pair)
        key = kv[:, cols]
        value = kv[:, channels + p * pair : channels + (p + 1) * pair]
        attention[:, cols] = merge(mm(weights[p], value)).astype(BF16)
        grad_query[:, cols] = (merge(mm(grad_scores[p], key)) * scale).astype(BF16)
        grad_key[:, cols] = mm_tn(grad_scores[p, :, 2 * m :], halves(own_qkv[:, cols], scale))
        grad_value[:, cols] = mm_tn(weights[p, :, 2 * m :], halves(own_grad[:, cols]))
    mesh_out[...] = (latent[...].astype(F32) + mm(attention[...], w_out[...])).astype(BF16)
    grad_normed[...] = mm_nt(grad_query[...], w_qkv[:, :channels])
    near = mm(jnp.concatenate([chip_normed[...], off_normed[...]], 0), w_qkv[:, :channels])
    near_q_out[...] = near.astype(BF16) * jnp.asarray(scale, BF16)


def finish_kernel(
    pair,
    count,
    chip_stats,
    off_stats,
    chip_first,
    off_first,
    near_q,
    chip_grad,
    off_grad,
    own_qkv,
    grad_key,
    grad_value,
    grad_normed,
    w_qkv,
    normal,
    inv_std,
    cot,
    grad_out,
):
    m, channels = normal.shape
    reach = [meta_of(side, count)[:8, 2 * LANES : 2 * LANES + m] for side in (chip_first, off_first)]
    reach = jnp.concatenate(reach, 1)
    key_at = iota((m, 2 * m), 0) + m
    lane = iota((m, 2 * m), 1)
    chip_at, off_at = near_places(m)
    query_at = jnp.where(lane < m, lane + chip_at, lane - m + off_at)
    keep = (key_at >= query_at - reach[0:1, :]) & (key_at <= query_at + reach[1:2, :])
    bias = jnp.where(keep, 0.0, -jnp.inf).astype(F32)
    pairs = channels // pair

    stats = []
    for h in range(2):
        lanes = slice(h * m, (h + 1) * m)
        stats.append(jnp.concatenate([chip_stats[:, lanes], off_stats[:, lanes]], 1))

    def multiply(p):
        cols = slice(p * pair, (p + 1) * pair)
        key2 = halves(own_qkv[:, channels + p * pair : channels + (p + 1) * pair])
        value2 = halves(own_qkv[:, 2 * channels + p * pair : 2 * channels + (p + 1) * pair])
        query = near_q[:, cols]
        grad = jnp.concatenate([chip_grad[:, cols], off_grad[:, cols]], 0)
        return query, grad, mm_nt(key2, query), mm_nt(value2, grad)

    total = grad_normed[...]
    group = pairs // 2
    gks, gvs = [], []
    ahead = multiply(0)
    for p in range(pairs):
        cols = slice(p * pair, (p + 1) * pair)
        query, grad, scores, grad_prob = ahead
        if p + 1 < pairs:
            ahead = multiply(p + 1)
        weights, grad_scores = [], []
        for h in range(2):
            half = slice(h * m, (h + 1) * m)
            top, inv_sum, delta = (stats[h][k * pairs + p : k * pairs + p + 1] for k in range(3))
            probs = jnp.exp(scores[half] + bias - top) * inv_sum
            weights.append(probs.astype(BF16))
            grad_scores.append((probs * (grad_prob[half] - delta)).astype(BF16))
        gk = grad_key[:, cols] + merge(mm(jnp.concatenate(grad_scores, 0), query))
        gv = grad_value[:, cols] + merge(mm(jnp.concatenate(weights, 0), grad))
        gks.append(gk.astype(BF16))
        gvs.append(gv.astype(BF16))
        if len(gks) == group:
            at = channels + (p + 1 - group) * pair
            width = group * pair
            total = total + mm_nt(jnp.concatenate(gks, 1), w_qkv[:, at : at + width])
            at = at + channels
            total = total + mm_nt(jnp.concatenate(gvs, 1), w_qkv[:, at : at + width])
            gks, gvs = [], []
    centred = (
        total
        - jnp.mean(total, -1, keepdims=True)
        - normal[...] * jnp.mean(total * normal[...], -1, keepdims=True)
    )
    grad_out[...] = (cot[...].astype(F32) + inv_std[:, :1] * centred).astype(BF16)


def body(
    grid_in,
    mesh_in,
    own_src,
    own_dst,
    side_src,
    side_dst,
    side_count,
    far_src,
    far_dst,
    far_count,
    window,
    cotangent,
    w_edge,
    w_qkv,
    w_out,
):
    devices = lax.axis_size("node")
    grid_rows, channels = grid_in.shape
    m = mesh_in.shape[0]
    far_slots = far_src.shape[0]
    far_depth = far_slots // devices
    head_dim = channels // HEADS
    pair = 2 * head_dim
    pairs = channels // pair
    scale = head_dim ** (-0.5)
    meta_rows = side_src.shape[0] // (2 * LANES)

    side_src, side_dst = side_src.reshape(-1, LANES), side_dst.reshape(-1, LANES)
    own_src, own_dst = own_src.reshape(-1, LANES), own_dst.reshape(-1, LANES)
    far_src, far_dst = far_src.reshape(1, -1), far_dst.reshape(1, -1)
    side_count, far_count = side_count.reshape(1, -1), far_count.reshape(1, -1)
    message = ((BAND + meta_rows, channels), BF16)
    far_block = (2 * far_slots, channels // 2 + LANES)
    far_message, chip_message, off_message, w_edge = call(
        pack_kernel,
        [(far_block, BF16), message, message, (w_edge.shape, BF16)],
        [grid_in, window, side_src, side_dst, side_count, far_src, far_dst, far_count, w_edge],
        hbm=range(9),
        hbm_outs=range(3),
        scratch=like(grid_in, window, side_src, side_dst, side_count, far_src, far_dst, far_count)
        + [
            pltpu.VMEM(far_block, BF16),
            pltpu.VMEM((2, meta_rows, channels), BF16),
            dma(9),
            dma(5),
        ],
        name="pack",
    )
    from_chip, from_off = exchange(chip_message, off_message, "node")
    got_far = lax.all_to_all(
        far_message.reshape(devices, 2 * far_depth, far_block[1]),
        "node",
        split_axis=0,
        concat_axis=0,
        tiled=True,
    ).reshape(far_block)

    rows = ((m, channels), BF16)
    partial, own_grad = call(
        own_kernel,
        [((m, channels), F32), rows],
        [grid_in, mesh_in, own_src, own_dst, cotangent, w_out, w_edge],
        hbm=range(6),
        hbm_outs=(1,),
        scratch=like(grid_in, mesh_in, own_src, own_dst, cotangent, w_out, cotangent) + [dma(7)],
        name="own",
    )
    (partial,) = call(
        functools.partial(side_kernel, meta_rows),
        [((m, channels), F32)],
        [from_chip, from_off, w_edge, partial],
        name="side",
        flops=8 * 10**9,
    )
    latent, normed, normal, inv_std = call(
        functools.partial(latent_kernel, far_depth),
        [rows, rows, ((m, channels), F32), ((m, LANES), F32)],
        [got_far, partial],
        name="latent",
    )
    chip_normed, off_normed = exchange(normed, normed, "node")
    own_block = ((pairs, 2 * m, m), F32)
    own_qkv, w_qkv, own_grad, own_scores, own_products = call(
        functools.partial(project_kernel, scale, pair),
        [((m, 3 * channels), BF16), (w_qkv.shape, BF16), rows, own_block, own_block],
        [normed, own_grad, w_qkv],
        hbm=(1, 2),
        scratch=[dma(3 * PIECES + 1)],
        name="project",
    )
    chip_grad, off_grad = exchange(own_grad, own_grad, "node")
    probs = ((pairs, 2 * m, 3 * m), BF16)
    stats, kv, weights, grad_scores, w_out, cotangent = call(
        functools.partial(attend_kernel, scale, pair),
        [
            ((3 * pairs, 2 * m), F32),
            ((3 * m, 2 * channels), BF16),
            probs,
            probs,
            (w_out.shape, BF16),
            rows,
        ],
        [chip_normed, off_normed, w_qkv, own_qkv, own_grad, own_scores, own_products]
        + [window, w_out, cotangent],
        hbm=(7, 8, 9),
        scratch=like(window) + [dma(3)],
        name="attend",
    )
    chip_stats, off_stats = exchange(stats, stats, "node")
    mesh_out, grad_normed, grad_key, grad_value, near_q = call(
        functools.partial(product_kernel, scale, pair),
        [
            rows,
            ((m, channels), F32),
            ((m, channels), F32),
            ((m, channels), F32),
            ((2 * m, channels), BF16),
        ],
        [
            weights,
            grad_scores,
            kv,
            own_qkv,
            own_grad,
            latent,
            w_out,
            w_qkv,
            chip_normed,
            off_normed,
        ],
        scratch=[pltpu.VMEM((m, channels), BF16)] * 2,
        name="product",
    )
    (mesh_grad,) = call(
        functools.partial(finish_kernel, pair, meta_rows),
        [rows],
        [
            chip_stats,
            off_stats,
            from_chip,
            from_off,
            near_q,
            chip_grad,
            off_grad,
            own_qkv,
            grad_key,
            grad_value,
            grad_normed,
            w_qkv,
            normal,
            inv_std,
            cotangent,
        ],
        name="finish",
    )
    return (mesh_out, mesh_grad)


def solution(mesh):
    rows = P(("groups", "node"), None)
    flat = P(("groups", "node"))
    placed = (rows, rows) + (flat,) * 8 + (P(None, ("groups", "node")), rows, P(), P(), P())
    return jax.shard_map(
        body, mesh=mesh, in_specs=placed, out_specs=(rows, rows), check_vma=False
    )
```

```python
import functools

import jax
import jax.numpy as jnp
from jax import lax
from jax.experimental import pallas as pl
from jax.experimental.pallas import tpu as pltpu
from jax.sharding import PartitionSpec as P

HEADS = 16
BAND = 128
LANES = 128
F32 = jnp.float32
BF16 = jnp.bfloat16
I32 = jnp.int32
VMEM_LIMIT = 28 * 2**20
PIECES = 2


def mm(a, b):
    return lax.dot_general(a, b, (((1,), (0,)), ((), ())), preferred_element_type=F32)


def mm_nt(a, b):
    return lax.dot_general(a, b, (((1,), (1,)), ((), ())), preferred_element_type=F32)


def mm_tn(a, b):
    return lax.dot_general(a, b, (((0,), (0,)), ((), ())), preferred_element_type=F32)


def iota(shape, dim):
    return lax.broadcasted_iota(I32, shape, dim)


def call(kernel, outs, args, hbm=(), hbm_outs=(), scratch=(), name=None, flops=None):
    args = [
        pltpu.with_memory_space_constraint(a, pltpu.HBM) if i in hbm else a
        for i, a in enumerate(args)
    ]

    def specs(count, far):
        return [
            pl.BlockSpec(memory_space=pltpu.HBM if i in far else pltpu.VMEM) for i in range(count)
        ]

    return pl.pallas_call(
        kernel,
        out_shape=[
            (pltpu.HBM if i in hbm_outs else jax.ShapeDtypeStruct)(shape, dtype)
            for i, (shape, dtype) in enumerate(outs)
        ],
        in_specs=specs(len(args), hbm),
        out_specs=specs(len(outs), hbm_outs),
        scratch_shapes=list(scratch),
        compiler_params=pltpu.CompilerParams(vmem_limit_bytes=VMEM_LIMIT),
        cost_estimate=flops and pl.CostEstimate(flops=flops, transcendentals=0, bytes_accessed=0),
        name=name,
    )(*args)


def dma(count):
    return pltpu.SemaphoreType.DMA((count,))


def start_all(pairs, sems):
    copies = [pltpu.make_async_copy(src, dst, sems.at[i]) for i, (src, dst) in enumerate(pairs)]
    for copy in copies:
        copy.start()
    return copies


def like(*arrays):
    return [pltpu.VMEM(a.shape, a.dtype) for a in arrays]


def exchange(chip_message, off_message, axis):
    n = lax.axis_size(axis)
    from_off = lax.ppermute(
        off_message, axis, [p for i in range(1, n - 1, 2) for p in ((i, i + 1), (i + 1, i))]
    )
    from_chip = lax.ppermute(
        chip_message, axis, [p for i in range(0, n, 2) for p in ((i, i + 1), (i + 1, i))]
    )
    return from_chip, from_off


def is_odd():
    return lax.axis_index("node") % 2


def gelu(projected):
    x = projected.astype(BF16).astype(F32)
    inner = (2.0 / jnp.pi) ** 0.5 * (x + 0.044715 * (x * x * x))
    return (0.5 * x * (1.0 + jnp.tanh(inner))).astype(BF16)


def onehot_rows(index_rows, count):
    parts = [
        jnp.where(iota((count, row.shape[1]), 0) == row, 1.0, 0.0).astype(BF16)
        for row in index_rows
    ]
    return parts[0] if len(parts) == 1 else jnp.concatenate(parts, 1)


def norm_stats(latent):
    values = latent.astype(F32)
    row_mean = jnp.mean(values, -1, keepdims=True)
    centred = values - row_mean
    variance = jnp.mean(centred * centred, -1, keepdims=True)
    inv_std = lax.rsqrt(variance + 1e-05)
    return centred * inv_std, inv_std


def pack_kernel(
    grid_hbm,
    window_hbm,
    side_src_hbm,
    side_dst_hbm,
    side_count_hbm,
    far_src_hbm,
    far_dst_hbm,
    far_count_hbm,
    w_edge_hbm,
    far_out,
    chip_out,
    off_out,
    w_edge,
    grid,
    window,
    side_src,
    side_dst,
    side_count,
    far_src,
    far_dst,
    far_count,
    far,
    meta,
    sems,
    out_sems,
):
    grid_rows, channels = grid.shape
    mesh_rows = window.shape[1]
    slots = far_src.shape[1]
    devices = far_count.shape[1]
    depth = slots // devices
    first = grid_rows - BAND
    count = side_src.shape[0] // 2
    copies = start_all(
        [
            (side_src_hbm, side_src),
            (side_dst_hbm, side_dst),
            (side_count_hbm, side_count),
            (window_hbm, window),
            (grid_hbm, grid),
            (far_src_hbm, far_src),
            (far_dst_hbm, far_dst),
            (far_count_hbm, far_count),
            (w_edge_hbm, w_edge),
        ],
        sems,
    )
    for copy in copies[:4]:
        copy.wait()
    for k in range(2):
        rank = iota((count, LANES), 0) * LANES + iota((count, LANES), 1)
        src = side_src[k * count : (k + 1) * count] - k * first
        live = rank < side_count[:, k : k + 1]
        dst = jnp.where(live, side_dst[k * count : (k + 1) * count], mesh_rows)
        reach = jnp.concatenate([window[...], jnp.zeros((count - 2, mesh_rows), I32)], 0)
        blank = jnp.zeros((count, channels - 2 * LANES - mesh_rows), I32)
        meta[k] = jnp.concatenate([src, dst, reach, blank], 1).astype(F32).astype(BF16)
    copies[4].wait()
    odd = is_odd()
    outs = start_all(
        [
            pair
            for k, out in ((1 - odd, chip_out), (odd, off_out))
            for pair in (
                (grid.at[pl.ds(pl.multiple_of(k * first, BAND), BAND)], out.at[pl.ds(0, BAND)]),
                (meta.at[k], out.at[pl.ds(BAND, count)]),
            )
        ],
        out_sems,
    )
    for copy in copies[5:8]:
        copy.wait()
    slot = iota((1, slots), 1)
    receiver = jnp.where(iota((devices, slots), 0) == iota((devices, slots), 1) // depth, 1.0, 0.0)
    live = mm(far_count[...].astype(F32).astype(BF16), receiver.astype(BF16))
    target = jnp.where((slot % depth).astype(F32) < live, far_dst[...].astype(F32), 1.0 * mesh_rows)
    row = iota((2 * slots, slots), 0)
    mine = slot == row // (2 * depth) * depth + row % depth
    source = jnp.sum(jnp.where(mine, far_src[...].astype(F32), 0.0), 1, keepdims=True)
    column = jnp.sum(jnp.where(mine, target, 0.0), 1, keepdims=True)
    pick = jnp.where(iota((2 * slots, grid_rows), 1).astype(F32) == source, 1.0, 0.0).astype(BF16)
    rows = mm(pick, grid[...]).astype(BF16)
    copies[8].wait()
    rows = gelu(mm(rows, w_edge[...]))
    half = channels // 2
    is_first = iota((2 * slots, half), 0) % (2 * depth) < depth
    far[:, :half] = jnp.where(is_first, rows[:, :half], rows[:, half:])
    far[:, half:] = jnp.broadcast_to(column, (2 * slots, LANES)).astype(BF16)
    last = pltpu.make_async_copy(far, far_out, out_sems.at[4])
    last.start()
    for copy in outs + [last]:
        copy.wait()


def own_kernel(
    grid_hbm,
    mesh_in_hbm,
    own_src_hbm,
    own_dst_hbm,
    cot_hbm,
    w_out_hbm,
    w_edge,
    partial_out,
    grad_hbm,
    grid,
    mesh_in,
    own_src,
    own_dst,
    cot,
    w_out,
    grad,
    sems,
):
    grid_rows = grid.shape[0]
    mesh_rows = mesh_in.shape[0]
    copies = start_all(
        [
            (own_src_hbm, own_src),
            (own_dst_hbm, own_dst),
            (cot_hbm, cot),
            (w_out_hbm, w_out),
            (grid_hbm, grid),
            (mesh_in_hbm, mesh_in),
        ],
        sems,
    )
    for copy in copies[:2]:
        copy.wait()
    rows = own_src.shape[0]
    src = onehot_rows([own_src[r : r + 1] for r in range(rows)], grid_rows)
    dst = onehot_rows([own_dst[r : r + 1] for r in range(rows)], mesh_rows)
    counts = mm_nt(dst, src).astype(BF16)
    for copy in copies[2:4]:
        copy.wait()
    grad[...] = mm_nt(cot[...], w_out[...]).astype(BF16)
    out = pltpu.make_async_copy(grad, grad_hbm, sems.at[6])
    out.start()
    for copy in copies[4:]:
        copy.wait()
    active = gelu(mm(grid[...], w_edge[...]))
    partial_out[...] = mesh_in[...].astype(F32) + mm(counts, active)
    out.wait()


def meta_of(message, count):
    return message[BAND : BAND + count].astype(F32).astype(I32)


def side_kernel(count, chip, off, w_edge, partial, partial_out):
    mesh_rows = partial.shape[0]
    uppers, lowers = [], []
    for side in (chip, off):
        meta = meta_of(side, count)
        src = onehot_rows([meta[r : r + 1, :LANES] for r in range(count)], BAND)
        dst = onehot_rows([meta[r : r + 1, LANES : 2 * LANES] for r in range(count)], mesh_rows)
        counts = mm_nt(dst, src)
        upper = counts.astype(BF16)
        uppers.append(upper)
        lowers.append((counts - upper.astype(F32)).astype(BF16))
    active = gelu(mm(jnp.concatenate([chip[:BAND], off[:BAND]], 0), w_edge[...]))
    landing = jnp.concatenate(uppers + lowers, 1)
    partial_out[...] = partial[...] + mm(landing, jnp.concatenate([active, active], 0))


def latent_kernel(depth, far, partial, latent_out, normed_out, normal_out, inv_std_out):
    mesh_rows, channels = partial.shape
    slots = far.shape[0]
    half = channels // 2
    first = far[:, :half]
    second = pltpu.roll(first.astype(F32), slots - depth, 0).astype(BF16)
    target = jnp.transpose(far[:, half:].astype(F32))
    if mesh_rows != LANES:
        target = jnp.broadcast_to(target[:1], (mesh_rows, slots))
    is_row = iota((mesh_rows, slots), 1) % (2 * depth) < depth
    hit = (target == iota((mesh_rows, slots), 0).astype(F32)) & is_row
    landing = jnp.where(hit, 1.0, 0.0).astype(BF16)
    total = partial[...] + mm(landing, jnp.concatenate([first, second], 1))
    latent = total.astype(BF16)
    latent_out[...] = latent
    normal, inv_std = norm_stats(latent)
    normed_out[...] = normal.astype(BF16)
    normal_out[...] = normal
    inv_std_out[...] = jnp.broadcast_to(inv_std, inv_std_out.shape)


def halves(rows, scale=None):
    first = iota(rows.shape, 1) < rows.shape[1] // 2
    if scale is not None:
        rows = rows * jnp.asarray(scale, rows.dtype)
    zero = jnp.zeros_like(rows)
    return jnp.concatenate([jnp.where(first, rows, zero), jnp.where(first, zero, rows)], 0)


def merge(stacked):
    m = stacked.shape[0] // 2
    first = iota((m, stacked.shape[1]), 1) < stacked.shape[1] // 2
    return jnp.where(first, stacked[:m], stacked[m:])


def project_kernel(
    scale, pair, normed, grad_hbm, w_qkv_hbm, qkv_out, w_qkv, grad_out, scores_out, products_out, sems
):
    m, channels = normed.shape
    width = channels // PIECES
    starts = [part * channels + c * width for c in range(PIECES) for part in range(3)]
    copies = start_all(
        [(grad_hbm, grad_out)]
        + [(w_qkv_hbm.at[:, pl.ds(at, width)], w_qkv.at[:, pl.ds(at, width)]) for at in starts],
        sems,
    )
    for i, at in enumerate(starts):
        copies[1 + i].wait()
        cols = slice(at, at + width)
        qkv_out[:, cols] = mm(normed[...], w_qkv[:, cols]).astype(BF16)
        if i % 3 < 2:
            continue
        if i == 2:
            copies[0].wait()
        for p in range(i // 3 * width // pair, (i // 3 + 1) * width // pair):
            q, k, v = (
                slice(part * channels + p * pair, part * channels + (p + 1) * pair)
                for part in range(3)
            )
            scores_out[p] = mm_nt(halves(qkv_out[:, q], scale), qkv_out[:, k])
            products_out[p] = mm_nt(halves(grad_out[:, q]), qkv_out[:, v])


def near_places(m):
    odd = is_odd()
    return (1 - odd) * 2 * m, odd * 2 * m


def attend_kernel(
    scale,
    pair,
    chip_normed,
    off_normed,
    w_qkv,
    own_qkv,
    own_grad,
    own_scores,
    own_products,
    window_hbm,
    w_out_hbm,
    cot_hbm,
    stats_out,
    kv,
    weights_out,
    scores_out,
    w_out,
    cot,
    window,
    sems,
):
    fetch = start_all([(window_hbm, window), (w_out_hbm, w_out), (cot_hbm, cot)], sems)
    m, channels = chip_normed.shape
    pairs = channels // pair
    devices = lax.axis_size("node")
    me = lax.axis_index("node")
    near = jnp.concatenate([chip_normed[...], off_normed[...]], 0)

    def bring(group):
        blocks = []
        for part in range(2):
            at = part * channels + group * 2 * pair
            block = mm(near, w_qkv[:, channels + at : channels + at + 2 * pair]).astype(BF16)
            kv[: 2 * m, at : at + 2 * pair] = block
            blocks.append(block)
        return blocks

    brought = {0: bring(0)}
    kv[2 * m :] = own_qkv[:, channels:]
    fetch[0].wait()
    row = iota((3 * m, m), 0)
    chip_at, off_at = near_places(m)
    key_at = jnp.where(row < m, row + chip_at, jnp.where(row < 2 * m, row - m + off_at, row - m))
    query_at = iota((3 * m, m), 1) + m
    missing = (row >= m) & (row < 2 * m) & ((me == 0) | (me == devices - 1))
    keep = (key_at >= query_at - window[0:1, :]) & (key_at <= query_at + window[1:2, :])
    bias = jnp.transpose(jnp.where(keep & jnp.logical_not(missing), 0.0, -jnp.inf).astype(F32))
    bias = jnp.concatenate([bias, bias], 0)
    lane = iota((2 * m, LANES), 1)
    stats = jnp.zeros((2 * m, LANES), F32)

    def multiply(p):
        cols = slice(p * pair, (p + 1) * pair)
        keys, values = (b[:, p % 2 * pair : (p % 2 + 1) * pair] for b in brought[p // 2])
        return (
            mm_nt(halves(own_qkv[:, cols], scale), keys),
            mm_nt(halves(own_grad[:, cols]), values),
        )

    ahead = multiply(0)
    for p in range(pairs):
        scores, grad_prob = ahead
        if p + 1 < pairs:
            if p % 2 == 0 and p + 2 < pairs:
                brought[p // 2 + 1] = bring(p // 2 + 1)
            ahead = multiply(p + 1)
        scores = jnp.concatenate([scores, own_scores[p]], 1) + bias
        grad_prob = jnp.concatenate([grad_prob, own_products[p]], 1)
        top = jnp.max(scores, 1, keepdims=True)
        shifted = jnp.exp(scores - top)
        inv_sum = 1.0 / jnp.sum(shifted, 1, keepdims=True)
        probs = shifted * inv_sum
        weights_out[p] = probs.astype(BF16)
        delta = jnp.sum(probs * grad_prob, 1, keepdims=True)
        scores_out[p] = (probs * (grad_prob - delta)).astype(BF16)
        stats = jnp.where(lane == p, top, stats)
        stats = jnp.where(lane == pairs + p, inv_sum, stats)
        stats = jnp.where(lane == 2 * pairs + p, delta, stats)
    stats_out[...] = jnp.transpose(stats)[: 3 * pairs]
    for copy in fetch[1:]:
        copy.wait()


def product_kernel(
    scale,
    pair,
    weights,
    grad_scores,
    kv,
    own_qkv,
    own_grad,
    latent,
    w_out,
    w_qkv,
    chip_normed,
    off_normed,
    mesh_out_hbm,
    grad_normed,
    grad_key,
    grad_value,
    near_q_out,
    attention,
    grad_query,
    mesh_out,
    sems,
):
    m, channels = latent.shape
    pairs = channels // pair
    for p in range(pairs):
        cols = slice(p * pair, (p + 1) * pair)
        value = kv[:, channels + p * pair : channels + (p + 1) * pair]
        attention[:, cols] = merge(mm(weights[p], value)).astype(BF16)
    mesh_out[...] = (latent[...].astype(F32) + mm(attention[...], w_out[...])).astype(BF16)
    out = pltpu.make_async_copy(mesh_out, mesh_out_hbm, sems.at[0])
    out.start()
    for p in range(pairs):
        cols = slice(p * pair, (p + 1) * pair)
        grad_query[:, cols] = (merge(mm(grad_scores[p], kv[:, cols])) * scale).astype(BF16)
    for p in range(pairs):
        cols = slice(p * pair, (p + 1) * pair)
        grad_key[:, cols] = mm_tn(grad_scores[p, :, 2 * m :], halves(own_qkv[:, cols], scale))
        grad_value[:, cols] = mm_tn(weights[p, :, 2 * m :], halves(own_grad[:, cols]))
    grad_normed[...] = mm_nt(grad_query[...], w_qkv[:, :channels])
    near = mm(jnp.concatenate([chip_normed[...], off_normed[...]], 0), w_qkv[:, :channels])
    near_q_out[...] = near.astype(BF16) * jnp.asarray(scale, BF16)
    out.wait()


def finish_kernel(
    pair,
    count,
    chip_stats,
    off_stats,
    chip_first,
    off_first,
    near_q,
    chip_grad,
    off_grad,
    own_qkv,
    grad_key,
    grad_value,
    grad_normed,
    w_qkv,
    normal,
    inv_std,
    cot,
    grad_out,
):
    m, channels = normal.shape
    reach = [meta_of(side, count)[:8, 2 * LANES : 2 * LANES + m] for side in (chip_first, off_first)]
    reach = jnp.concatenate(reach, 1)
    key_at = iota((m, 2 * m), 0) + m
    lane = iota((m, 2 * m), 1)
    chip_at, off_at = near_places(m)
    query_at = jnp.where(lane < m, lane + chip_at, lane - m + off_at)
    keep = (key_at >= query_at - reach[0:1, :]) & (key_at <= query_at + reach[1:2, :])
    bias = jnp.where(keep, 0.0, -jnp.inf).astype(F32)
    pairs = channels // pair

    stats = []
    for h in range(2):
        lanes = slice(h * m, (h + 1) * m)
        stats.append(jnp.concatenate([chip_stats[:, lanes], off_stats[:, lanes]], 1))

    def multiply(p):
        cols = slice(p * pair, (p + 1) * pair)
        key2 = halves(own_qkv[:, channels + p * pair : channels + (p + 1) * pair])
        value2 = halves(own_qkv[:, 2 * channels + p * pair : 2 * channels + (p + 1) * pair])
        query = near_q[:, cols]
        grad = jnp.concatenate([chip_grad[:, cols], off_grad[:, cols]], 0)
        return query, grad, mm_nt(key2, query), mm_nt(value2, grad)

    total = grad_normed[...]
    group = pairs // 2
    gks, gvs = [], []
    ahead = multiply(0)
    for p in range(pairs):
        cols = slice(p * pair, (p + 1) * pair)
        query, grad, scores, grad_prob = ahead
        if p + 1 < pairs:
            ahead = multiply(p + 1)
        weights, grad_scores = [], []
        for h in range(2):
            half = slice(h * m, (h + 1) * m)
            top, inv_sum, delta = (stats[h][k * pairs + p : k * pairs + p + 1] for k in range(3))
            probs = jnp.exp(scores[half] + bias - top) * inv_sum
            weights.append(probs.astype(BF16))
            grad_scores.append((probs * (grad_prob[half] - delta)).astype(BF16))
        gk = grad_key[:, cols] + merge(mm(jnp.concatenate(grad_scores, 0), query))
        gv = grad_value[:, cols] + merge(mm(jnp.concatenate(weights, 0), grad))
        gks.append(gk.astype(BF16))
        gvs.append(gv.astype(BF16))
        if len(gks) == group:
            at = channels + (p + 1 - group) * pair
            width = group * pair
            total = total + mm_nt(jnp.concatenate(gks, 1), w_qkv[:, at : at + width])
            at = at + channels
            total = total + mm_nt(jnp.concatenate(gvs, 1), w_qkv[:, at : at + width])
            gks, gvs = [], []
    centred = (
        total
        - jnp.mean(total, -1, keepdims=True)
        - normal[...] * jnp.mean(total * normal[...], -1, keepdims=True)
    )
    grad_out[...] = (cot[...].astype(F32) + inv_std[:, :1] * centred).astype(BF16)


def body(
    grid_in,
    mesh_in,
    own_src,
    own_dst,
    side_src,
    side_dst,
    side_count,
    far_src,
    far_dst,
    far_count,
    window,
    cotangent,
    w_edge,
    w_qkv,
    w_out,
):
    devices = lax.axis_size("node")
    grid_rows, channels = grid_in.shape
    m = mesh_in.shape[0]
    far_slots = far_src.shape[0]
    far_depth = far_slots // devices
    head_dim = channels // HEADS
    pair = 2 * head_dim
    pairs = channels // pair
    scale = head_dim ** (-0.5)
    meta_rows = side_src.shape[0] // (2 * LANES)

    side_src, side_dst = side_src.reshape(-1, LANES), side_dst.reshape(-1, LANES)
    own_src, own_dst = own_src.reshape(-1, LANES), own_dst.reshape(-1, LANES)
    far_src, far_dst = far_src.reshape(1, -1), far_dst.reshape(1, -1)
    side_count, far_count = side_count.reshape(1, -1), far_count.reshape(1, -1)
    message = ((BAND + meta_rows, channels), BF16)
    far_block = (2 * far_slots, channels // 2 + LANES)
    far_message, chip_message, off_message, w_edge = call(
        pack_kernel,
        [(far_block, BF16), message, message, (w_edge.shape, BF16)],
        [grid_in, window, side_src, side_dst, side_count, far_src, far_dst, far_count, w_edge],
        hbm=range(9),
        hbm_outs=range(3),
        scratch=like(grid_in, window, side_src, side_dst, side_count, far_src, far_dst, far_count)
        + [
            pltpu.VMEM(far_block, BF16),
            pltpu.VMEM((2, meta_rows, channels), BF16),
            dma(9),
            dma(5),
        ],
        name="pack",
    )
    from_chip, from_off = exchange(chip_message, off_message, "node")
    got_far = lax.all_to_all(
        far_message.reshape(devices, 2 * far_depth, far_block[1]),
        "node",
        split_axis=0,
        concat_axis=0,
        tiled=True,
    ).reshape(far_block)

    rows = ((m, channels), BF16)
    partial, own_grad = call(
        own_kernel,
        [((m, channels), F32), rows],
        [grid_in, mesh_in, own_src, own_dst, cotangent, w_out, w_edge],
        hbm=range(6),
        hbm_outs=(1,),
        scratch=like(grid_in, mesh_in, own_src, own_dst, cotangent, w_out, cotangent) + [dma(7)],
        name="own",
    )
    (partial,) = call(
        functools.partial(side_kernel, meta_rows),
        [((m, channels), F32)],
        [from_chip, from_off, w_edge, partial],
        name="side",
        flops=8 * 10**9,
    )
    latent, normed, normal, inv_std = call(
        functools.partial(latent_kernel, far_depth),
        [rows, rows, ((m, channels), F32), ((m, LANES), F32)],
        [got_far, partial],
        name="latent",
    )
    chip_normed, off_normed = exchange(normed, normed, "node")
    own_block = ((pairs, 2 * m, m), F32)
    own_qkv, w_qkv, own_grad, own_scores, own_products = call(
        functools.partial(project_kernel, scale, pair),
        [((m, 3 * channels), BF16), (w_qkv.shape, BF16), rows, own_block, own_block],
        [normed, own_grad, w_qkv],
        hbm=(1, 2),
        scratch=[dma(3 * PIECES + 1)],
        name="project",
    )
    chip_grad, off_grad = exchange(own_grad, own_grad, "node")
    probs = ((pairs, 2 * m, 3 * m), BF16)
    stats, kv, weights, grad_scores, w_out, cotangent = call(
        functools.partial(attend_kernel, scale, pair),
        [
            ((3 * pairs, 2 * m), F32),
            ((3 * m, 2 * channels), BF16),
            probs,
            probs,
            (w_out.shape, BF16),
            rows,
        ],
        [chip_normed, off_normed, w_qkv, own_qkv, own_grad, own_scores, own_products]
        + [window, w_out, cotangent],
        hbm=(7, 8, 9),
        scratch=like(window) + [dma(3)],
        name="attend",
    )
    chip_stats, off_stats = exchange(stats, stats, "node")
    mesh_out, grad_normed, grad_key, grad_value, near_q = call(
        functools.partial(product_kernel, scale, pair),
        [
            rows,
            ((m, channels), F32),
            ((m, channels), F32),
            ((m, channels), F32),
            ((2 * m, channels), BF16),
        ],
        [
            weights,
            grad_scores,
            kv,
            own_qkv,
            own_grad,
            latent,
            w_out,
            w_qkv,
            chip_normed,
            off_normed,
        ],
        hbm_outs=(0,),
        scratch=[pltpu.VMEM((m, channels), BF16)] * 3 + [dma(1)],
        name="product",
    )
    (mesh_grad,) = call(
        functools.partial(finish_kernel, pair, meta_rows),
        [rows],
        [
            chip_stats,
            off_stats,
            from_chip,
            from_off,
            near_q,
            chip_grad,
            off_grad,
            own_qkv,
            grad_key,
            grad_value,
            grad_normed,
            w_qkv,
            normal,
            inv_std,
            cotangent,
        ],
        name="finish",
    )
    return (mesh_out, mesh_grad)


def solution(mesh):
    rows = P(("groups", "node"), None)
    flat = P(("groups", "node"))
    placed = (rows, rows) + (flat,) * 8 + (P(None, ("groups", "node")), rows, P(), P(), P())
    return jax.shard_map(
        body, mesh=mesh, in_specs=placed, out_specs=(rows, rows), check_vma=False
    )
```

```python
import functools

import jax
import jax.numpy as jnp
from jax import lax
from jax.experimental import pallas as pl
from jax.experimental.pallas import tpu as pltpu
from jax.sharding import PartitionSpec as P

HEADS = 16
BAND = 128
LANES = 128
F32 = jnp.float32
BF16 = jnp.bfloat16
I32 = jnp.int32
VMEM_LIMIT = 28 * 2**20
PIECES = 2


def mm(a, b):
    return lax.dot_general(a, b, (((1,), (0,)), ((), ())), preferred_element_type=F32)


def mm_nt(a, b):
    return lax.dot_general(a, b, (((1,), (1,)), ((), ())), preferred_element_type=F32)


def mm_tn(a, b):
    return lax.dot_general(a, b, (((0,), (0,)), ((), ())), preferred_element_type=F32)


def iota(shape, dim):
    return lax.broadcasted_iota(I32, shape, dim)


def call(kernel, outs, args, hbm=(), hbm_outs=(), scratch=(), name=None, flops=None):
    args = [
        pltpu.with_memory_space_constraint(a, pltpu.HBM) if i in hbm else a
        for i, a in enumerate(args)
    ]

    def specs(count, far):
        return [
            pl.BlockSpec(memory_space=pltpu.HBM if i in far else pltpu.VMEM) for i in range(count)
        ]

    return pl.pallas_call(
        kernel,
        out_shape=[
            (pltpu.HBM if i in hbm_outs else jax.ShapeDtypeStruct)(shape, dtype)
            for i, (shape, dtype) in enumerate(outs)
        ],
        in_specs=specs(len(args), hbm),
        out_specs=specs(len(outs), hbm_outs),
        scratch_shapes=list(scratch),
        compiler_params=pltpu.CompilerParams(vmem_limit_bytes=VMEM_LIMIT),
        cost_estimate=flops and pl.CostEstimate(flops=flops, transcendentals=0, bytes_accessed=0),
        name=name,
    )(*args)


def dma(count):
    return pltpu.SemaphoreType.DMA((count,))


def start_all(pairs, sems):
    copies = [pltpu.make_async_copy(src, dst, sems.at[i]) for i, (src, dst) in enumerate(pairs)]
    for copy in copies:
        copy.start()
    return copies


def like(*arrays):
    return [pltpu.VMEM(a.shape, a.dtype) for a in arrays]


def exchange(chip_message, off_message, axis):
    n = lax.axis_size(axis)
    from_off = lax.ppermute(
        off_message, axis, [p for i in range(1, n - 1, 2) for p in ((i, i + 1), (i + 1, i))]
    )
    from_chip = lax.ppermute(
        chip_message, axis, [p for i in range(0, n, 2) for p in ((i, i + 1), (i + 1, i))]
    )
    return from_chip, from_off


def is_odd():
    return lax.axis_index("node") % 2


def gelu(projected):
    x = projected.astype(BF16).astype(F32)
    inner = (2.0 / jnp.pi) ** 0.5 * (x + 0.044715 * (x * x * x))
    return (0.5 * x * (1.0 + jnp.tanh(inner))).astype(BF16)


def onehot_rows(index_rows, count):
    parts = [
        jnp.where(iota((count, row.shape[1]), 0) == row, 1.0, 0.0).astype(BF16)
        for row in index_rows
    ]
    return parts[0] if len(parts) == 1 else jnp.concatenate(parts, 1)


def norm_stats(latent):
    values = latent.astype(F32)
    row_mean = jnp.mean(values, -1, keepdims=True)
    centred = values - row_mean
    variance = jnp.mean(centred * centred, -1, keepdims=True)
    inv_std = lax.rsqrt(variance + 1e-05)
    return centred * inv_std, inv_std


def pack_kernel(
    grid_hbm,
    window_hbm,
    side_src_hbm,
    side_dst_hbm,
    side_count_hbm,
    far_src_hbm,
    far_dst_hbm,
    far_count_hbm,
    w_edge_hbm,
    far_out,
    chip_out,
    off_out,
    w_edge,
    grid,
    window,
    side_src,
    side_dst,
    side_count,
    far_src,
    far_dst,
    far_count,
    far,
    meta,
    sems,
    out_sems,
):
    grid_rows, channels = grid.shape
    mesh_rows = window.shape[1]
    slots = far_src.shape[1]
    devices = far_count.shape[1]
    depth = slots // devices
    first = grid_rows - BAND
    count = side_src.shape[0] // 2
    copies = start_all(
        [
            (side_src_hbm, side_src),
            (side_dst_hbm, side_dst),
            (side_count_hbm, side_count),
            (window_hbm, window),
            (grid_hbm, grid),
            (far_src_hbm, far_src),
            (far_dst_hbm, far_dst),
            (far_count_hbm, far_count),
            (w_edge_hbm, w_edge),
        ],
        sems,
    )
    for copy in copies[:4]:
        copy.wait()
    for k in range(2):
        rank = iota((count, LANES), 0) * LANES + iota((count, LANES), 1)
        src = side_src[k * count : (k + 1) * count] - k * first
        live = rank < side_count[:, k : k + 1]
        dst = jnp.where(live, side_dst[k * count : (k + 1) * count], mesh_rows)
        reach = jnp.concatenate([window[...], jnp.zeros((count - 2, mesh_rows), I32)], 0)
        blank = jnp.zeros((count, channels - 2 * LANES - mesh_rows), I32)
        meta[k] = jnp.concatenate([src, dst, reach, blank], 1).astype(F32).astype(BF16)
    copies[4].wait()
    odd = is_odd()
    outs = start_all(
        [
            pair
            for k, out in ((1 - odd, chip_out), (odd, off_out))
            for pair in (
                (grid.at[pl.ds(pl.multiple_of(k * first, BAND), BAND)], out.at[pl.ds(0, BAND)]),
                (meta.at[k], out.at[pl.ds(BAND, count)]),
            )
        ],
        out_sems,
    )
    for copy in copies[5:8]:
        copy.wait()
    slot = iota((1, slots), 1)
    receiver = jnp.where(iota((devices, slots), 0) == iota((devices, slots), 1) // depth, 1.0, 0.0)
    live = mm(far_count[...].astype(F32).astype(BF16), receiver.astype(BF16))
    target = jnp.where((slot % depth).astype(F32) < live, far_dst[...].astype(F32), 1.0 * mesh_rows)
    row = iota((2 * slots, slots), 0)
    mine = slot == row // (2 * depth) * depth + row % depth
    source = jnp.sum(jnp.where(mine, far_src[...].astype(F32), 0.0), 1, keepdims=True)
    column = jnp.sum(jnp.where(mine, target, 0.0), 1, keepdims=True)
    pick = jnp.where(iota((2 * slots, grid_rows), 1).astype(F32) == source, 1.0, 0.0).astype(BF16)
    rows = mm(pick, grid[...]).astype(BF16)
    copies[8].wait()
    rows = gelu(mm(rows, w_edge[...]))
    half = channels // 2
    is_first = iota((2 * slots, half), 0) % (2 * depth) < depth
    far[:, :half] = jnp.where(is_first, rows[:, :half], rows[:, half:])
    far[:, half:] = jnp.broadcast_to(column, (2 * slots, LANES)).astype(BF16)
    last = pltpu.make_async_copy(far, far_out, out_sems.at[4])
    last.start()
    for copy in outs + [last]:
        copy.wait()


def own_kernel(
    grid_hbm,
    mesh_in_hbm,
    own_src_hbm,
    own_dst_hbm,
    cot_hbm,
    w_out_hbm,
    w_edge,
    partial_out,
    grad_hbm,
    grid,
    mesh_in,
    own_src,
    own_dst,
    cot,
    w_out,
    grad,
    sems,
):
    grid_rows = grid.shape[0]
    mesh_rows = mesh_in.shape[0]
    copies = start_all(
        [
            (own_src_hbm, own_src),
            (own_dst_hbm, own_dst),
            (cot_hbm, cot),
            (w_out_hbm, w_out),
            (grid_hbm, grid),
            (mesh_in_hbm, mesh_in),
        ],
        sems,
    )
    for copy in copies[:2]:
        copy.wait()
    rows = own_src.shape[0]
    src = onehot_rows([own_src[r : r + 1] for r in range(rows)], grid_rows)
    dst = onehot_rows([own_dst[r : r + 1] for r in range(rows)], mesh_rows)
    counts = mm_nt(dst, src).astype(BF16)
    for copy in copies[2:4]:
        copy.wait()
    grad[...] = mm_nt(cot[...], w_out[...]).astype(BF16)
    out = pltpu.make_async_copy(grad, grad_hbm, sems.at[6])
    out.start()
    for copy in copies[4:]:
        copy.wait()
    active = gelu(mm(grid[...], w_edge[...]))
    partial_out[...] = mesh_in[...].astype(F32) + mm(counts, active)
    out.wait()


def meta_of(message, count):
    return message[BAND : BAND + count].astype(F32).astype(I32)


def side_kernel(count, chip, off, w_edge, partial, partial_out):
    mesh_rows = partial.shape[0]
    uppers, lowers = [], []
    for side in (chip, off):
        meta = meta_of(side, count)
        src = onehot_rows([meta[r : r + 1, :LANES] for r in range(count)], BAND)
        dst = onehot_rows([meta[r : r + 1, LANES : 2 * LANES] for r in range(count)], mesh_rows)
        counts = mm_nt(dst, src)
        upper = counts.astype(BF16)
        uppers.append(upper)
        lowers.append((counts - upper.astype(F32)).astype(BF16))
    active = gelu(mm(jnp.concatenate([chip[:BAND], off[:BAND]], 0), w_edge[...]))
    landing = jnp.concatenate(uppers + lowers, 1)
    partial_out[...] = partial[...] + mm(landing, jnp.concatenate([active, active], 0))


def latent_kernel(depth, far, partial, latent_out, normed_out, normal_out, inv_std_out):
    mesh_rows, channels = partial.shape
    slots = far.shape[0]
    half = channels // 2
    first = far[:, :half]
    second = pltpu.roll(first.astype(F32), slots - depth, 0).astype(BF16)
    target = jnp.transpose(far[:, half:].astype(F32))
    if mesh_rows != LANES:
        target = jnp.broadcast_to(target[:1], (mesh_rows, slots))
    is_row = iota((mesh_rows, slots), 1) % (2 * depth) < depth
    hit = (target == iota((mesh_rows, slots), 0).astype(F32)) & is_row
    landing = jnp.where(hit, 1.0, 0.0).astype(BF16)
    total = partial[...] + mm(landing, jnp.concatenate([first, second], 1))
    latent = total.astype(BF16)
    latent_out[...] = latent
    normal, inv_std = norm_stats(latent)
    normed_out[...] = normal.astype(BF16)
    normal_out[...] = normal
    inv_std_out[...] = jnp.broadcast_to(inv_std, inv_std_out.shape)


def halves(rows, scale=None):
    first = iota(rows.shape, 1) < rows.shape[1] // 2
    if scale is not None:
        rows = rows * jnp.asarray(scale, rows.dtype)
    zero = jnp.zeros_like(rows)
    return jnp.concatenate([jnp.where(first, rows, zero), jnp.where(first, zero, rows)], 0)


def merge(stacked):
    m = stacked.shape[0] // 2
    first = iota((m, stacked.shape[1]), 1) < stacked.shape[1] // 2
    return jnp.where(first, stacked[:m], stacked[m:])


def project_kernel(
    scale, pair, normed, grad_hbm, w_qkv_hbm, qkv_out, w_qkv, grad_out, scores_out, products_out, sems
):
    m, channels = normed.shape
    width = channels // PIECES
    starts = [part * channels + c * width for c in range(PIECES) for part in range(3)]
    copies = start_all(
        [(grad_hbm, grad_out)]
        + [(w_qkv_hbm.at[:, pl.ds(at, width)], w_qkv.at[:, pl.ds(at, width)]) for at in starts],
        sems,
    )
    for i, at in enumerate(starts):
        copies[1 + i].wait()
        cols = slice(at, at + width)
        qkv_out[:, cols] = mm(normed[...], w_qkv[:, cols]).astype(BF16)
        if i % 3 < 2:
            continue
        if i == 2:
            copies[0].wait()
        for p in range(i // 3 * width // pair, (i // 3 + 1) * width // pair):
            q, k, v = (
                slice(part * channels + p * pair, part * channels + (p + 1) * pair)
                for part in range(3)
            )
            scores_out[p] = mm_nt(halves(qkv_out[:, q], scale), qkv_out[:, k])
            products_out[p] = mm_nt(halves(grad_out[:, q]), qkv_out[:, v])


def near_places(m):
    odd = is_odd()
    return (1 - odd) * 2 * m, odd * 2 * m


def attend_kernel(
    scale,
    pair,
    chip_normed,
    off_normed,
    w_qkv,
    own_qkv,
    own_grad,
    own_scores,
    own_products,
    window_hbm,
    w_out_hbm,
    cot_hbm,
    stats_out,
    kv,
    weights_out,
    scores_out,
    near_q,
    w_out,
    cot,
    window,
    sems,
):
    fetch = start_all([(window_hbm, window), (w_out_hbm, w_out), (cot_hbm, cot)], sems)
    m, channels = chip_normed.shape
    pairs = channels // pair
    devices = lax.axis_size("node")
    me = lax.axis_index("node")
    near = jnp.concatenate([chip_normed[...], off_normed[...]], 0)

    def bring(group):
        cols = slice(group * 2 * pair, (group + 1) * 2 * pair)
        near_q[:, cols] = mm(near, w_qkv[:, cols]).astype(BF16) * jnp.asarray(scale, BF16)
        blocks = []
        for part in range(2):
            at = part * channels + group * 2 * pair
            block = mm(near, w_qkv[:, channels + at : channels + at + 2 * pair]).astype(BF16)
            kv[: 2 * m, at : at + 2 * pair] = block
            blocks.append(block)
        return blocks

    brought = {0: bring(0)}
    kv[2 * m :] = own_qkv[:, channels:]
    fetch[0].wait()
    row = iota((3 * m, m), 0)
    chip_at, off_at = near_places(m)
    key_at = jnp.where(row < m, row + chip_at, jnp.where(row < 2 * m, row - m + off_at, row - m))
    query_at = iota((3 * m, m), 1) + m
    missing = (row >= m) & (row < 2 * m) & ((me == 0) | (me == devices - 1))
    keep = (key_at >= query_at - window[0:1, :]) & (key_at <= query_at + window[1:2, :])
    bias = jnp.transpose(jnp.where(keep & jnp.logical_not(missing), 0.0, -jnp.inf).astype(F32))
    bias = jnp.concatenate([bias, bias], 0)
    lane = iota((2 * m, LANES), 1)
    stats = jnp.zeros((2 * m, LANES), F32)

    def multiply(p):
        cols = slice(p * pair, (p + 1) * pair)
        keys, values = (b[:, p % 2 * pair : (p % 2 + 1) * pair] for b in brought[p // 2])
        return (
            mm_nt(halves(own_qkv[:, cols], scale), keys),
            mm_nt(halves(own_grad[:, cols]), values),
        )

    ahead = multiply(0)
    for p in range(pairs):
        scores, grad_prob = ahead
        if p + 1 < pairs:
            if p % 2 == 0 and p + 2 < pairs:
                brought[p // 2 + 1] = bring(p // 2 + 1)
            ahead = multiply(p + 1)
        scores = jnp.concatenate([scores, own_scores[p]], 1) + bias
        grad_prob = jnp.concatenate([grad_prob, own_products[p]], 1)
        top = jnp.max(scores, 1, keepdims=True)
        shifted = jnp.exp(scores - top)
        inv_sum = 1.0 / jnp.sum(shifted, 1, keepdims=True)
        probs = shifted * inv_sum
        weights_out[p] = probs.astype(BF16)
        delta = jnp.sum(probs * grad_prob, 1, keepdims=True)
        scores_out[p] = (probs * (grad_prob - delta)).astype(BF16)
        stats = jnp.where(lane == p, top, stats)
        stats = jnp.where(lane == pairs + p, inv_sum, stats)
        stats = jnp.where(lane == 2 * pairs + p, delta, stats)
    stats_out[...] = jnp.transpose(stats)[: 3 * pairs]
    for copy in fetch[1:]:
        copy.wait()


def product_kernel(
    scale,
    pair,
    weights,
    grad_scores,
    kv,
    own_qkv,
    own_grad,
    latent,
    w_out,
    w_qkv,
    mesh_out_hbm,
    grad_normed,
    grad_key,
    grad_value,
    attention,
    grad_query,
    mesh_out,
    sems,
):
    m, channels = latent.shape
    pairs = channels // pair
    for p in range(pairs):
        cols = slice(p * pair, (p + 1) * pair)
        value = kv[:, channels + p * pair : channels + (p + 1) * pair]
        attention[:, cols] = merge(mm(weights[p], value)).astype(BF16)
    mesh_out[...] = (latent[...].astype(F32) + mm(attention[...], w_out[...])).astype(BF16)
    out = pltpu.make_async_copy(mesh_out, mesh_out_hbm, sems.at[0])
    out.start()
    for p in range(pairs):
        cols = slice(p * pair, (p + 1) * pair)
        grad_query[:, cols] = (merge(mm(grad_scores[p], kv[:, cols])) * scale).astype(BF16)
    for p in range(pairs):
        cols = slice(p * pair, (p + 1) * pair)
        grad_key[:, cols] = mm_tn(grad_scores[p, :, 2 * m :], halves(own_qkv[:, cols], scale))
        grad_value[:, cols] = mm_tn(weights[p, :, 2 * m :], halves(own_grad[:, cols]))
    grad_normed[...] = mm_nt(grad_query[...], w_qkv[:, :channels])
    out.wait()


def finish_kernel(
    pair,
    count,
    chip_stats,
    off_stats,
    chip_first,
    off_first,
    near_q,
    chip_grad,
    off_grad,
    own_qkv,
    grad_key,
    grad_value,
    grad_normed,
    w_qkv,
    normal,
    inv_std,
    cot,
    grad_out,
):
    m, channels = normal.shape
    reach = [meta_of(side, count)[:8, 2 * LANES : 2 * LANES + m] for side in (chip_first, off_first)]
    reach = jnp.concatenate(reach, 1)
    key_at = iota((m, 2 * m), 0) + m
    lane = iota((m, 2 * m), 1)
    chip_at, off_at = near_places(m)
    query_at = jnp.where(lane < m, lane + chip_at, lane - m + off_at)
    keep = (key_at >= query_at - reach[0:1, :]) & (key_at <= query_at + reach[1:2, :])
    bias = jnp.where(keep, 0.0, -jnp.inf).astype(F32)
    pairs = channels // pair

    stats = []
    for h in range(2):
        lanes = slice(h * m, (h + 1) * m)
        stats.append(jnp.concatenate([chip_stats[:, lanes], off_stats[:, lanes]], 1))

    def multiply(p):
        cols = slice(p * pair, (p + 1) * pair)
        key2 = halves(own_qkv[:, channels + p * pair : channels + (p + 1) * pair])
        value2 = halves(own_qkv[:, 2 * channels + p * pair : 2 * channels + (p + 1) * pair])
        query = near_q[:, cols]
        grad = jnp.concatenate([chip_grad[:, cols], off_grad[:, cols]], 0)
        return query, grad, mm_nt(key2, query), mm_nt(value2, grad)

    total = grad_normed[...]
    group = 2
    gks, gvs = [], []
    ahead = multiply(0)
    for p in range(pairs):
        cols = slice(p * pair, (p + 1) * pair)
        query, grad, scores, grad_prob = ahead
        if p + 1 < pairs:
            ahead = multiply(p + 1)
        weights, grad_scores = [], []
        for h in range(2):
            half = slice(h * m, (h + 1) * m)
            top, inv_sum, delta = (stats[h][k * pairs + p : k * pairs + p + 1] for k in range(3))
            probs = jnp.exp(scores[half] + bias - top) * inv_sum
            weights.append(probs.astype(BF16))
            grad_scores.append((probs * (grad_prob[half] - delta)).astype(BF16))
        gk = grad_key[:, cols] + merge(mm(jnp.concatenate(grad_scores, 0), query))
        gv = grad_value[:, cols] + merge(mm(jnp.concatenate(weights, 0), grad))
        gks.append(gk.astype(BF16))
        gvs.append(gv.astype(BF16))
        if len(gks) == group:
            at = channels + (p + 1 - group) * pair
            width = group * pair
            total = total + mm_nt(jnp.concatenate(gks, 1), w_qkv[:, at : at + width])
            at = at + channels
            total = total + mm_nt(jnp.concatenate(gvs, 1), w_qkv[:, at : at + width])
            gks, gvs = [], []
    centred = (
        total
        - jnp.mean(total, -1, keepdims=True)
        - normal[...] * jnp.mean(total * normal[...], -1, keepdims=True)
    )
    grad_out[...] = (cot[...].astype(F32) + inv_std[:, :1] * centred).astype(BF16)


def body(
    grid_in,
    mesh_in,
    own_src,
    own_dst,
    side_src,
    side_dst,
    side_count,
    far_src,
    far_dst,
    far_count,
    window,
    cotangent,
    w_edge,
    w_qkv,
    w_out,
):
    devices = lax.axis_size("node")
    grid_rows, channels = grid_in.shape
    m = mesh_in.shape[0]
    far_slots = far_src.shape[0]
    far_depth = far_slots // devices
    head_dim = channels // HEADS
    pair = 2 * head_dim
    pairs = channels // pair
    scale = head_dim ** (-0.5)
    meta_rows = side_src.shape[0] // (2 * LANES)

    side_src, side_dst = side_src.reshape(-1, LANES), side_dst.reshape(-1, LANES)
    own_src, own_dst = own_src.reshape(-1, LANES), own_dst.reshape(-1, LANES)
    far_src, far_dst = far_src.reshape(1, -1), far_dst.reshape(1, -1)
    side_count, far_count = side_count.reshape(1, -1), far_count.reshape(1, -1)
    message = ((BAND + meta_rows, channels), BF16)
    far_block = (2 * far_slots, channels // 2 + LANES)
    far_message, chip_message, off_message, w_edge = call(
        pack_kernel,
        [(far_block, BF16), message, message, (w_edge.shape, BF16)],
        [grid_in, window, side_src, side_dst, side_count, far_src, far_dst, far_count, w_edge],
        hbm=range(9),
        hbm_outs=range(3),
        scratch=like(grid_in, window, side_src, side_dst, side_count, far_src, far_dst, far_count)
        + [
            pltpu.VMEM(far_block, BF16),
            pltpu.VMEM((2, meta_rows, channels), BF16),
            dma(9),
            dma(5),
        ],
        name="pack",
    )
    from_chip, from_off = exchange(chip_message, off_message, "node")
    got_far = lax.all_to_all(
        far_message.reshape(devices, 2 * far_depth, far_block[1]),
        "node",
        split_axis=0,
        concat_axis=0,
        tiled=True,
    ).reshape(far_block)

    rows = ((m, channels), BF16)
    partial, own_grad = call(
        own_kernel,
        [((m, channels), F32), rows],
        [grid_in, mesh_in, own_src, own_dst, cotangent, w_out, w_edge],
        hbm=range(6),
        hbm_outs=(1,),
        scratch=like(grid_in, mesh_in, own_src, own_dst, cotangent, w_out, cotangent) + [dma(7)],
        name="own",
    )
    (partial,) = call(
        functools.partial(side_kernel, meta_rows),
        [((m, channels), F32)],
        [from_chip, from_off, w_edge, partial],
        name="side",
        flops=8 * 10**9,
    )
    latent, normed, normal, inv_std = call(
        functools.partial(latent_kernel, far_depth),
        [rows, rows, ((m, channels), F32), ((m, LANES), F32)],
        [got_far, partial],
        name="latent",
    )
    chip_normed, off_normed = exchange(normed, normed, "node")
    own_block = ((pairs, 2 * m, m), F32)
    own_qkv, w_qkv, own_grad, own_scores, own_products = call(
        functools.partial(project_kernel, scale, pair),
        [((m, 3 * channels), BF16), (w_qkv.shape, BF16), rows, own_block, own_block],
        [normed, own_grad, w_qkv],
        hbm=(1, 2),
        scratch=[dma(3 * PIECES + 1)],
        name="project",
    )
    chip_grad, off_grad = exchange(own_grad, own_grad, "node")
    probs = ((pairs, 2 * m, 3 * m), BF16)
    stats, kv, weights, grad_scores, near_q, w_out, cotangent = call(
        functools.partial(attend_kernel, scale, pair),
        [
            ((3 * pairs, 2 * m), F32),
            ((3 * m, 2 * channels), BF16),
            probs,
            probs,
            ((2 * m, channels), BF16),
            (w_out.shape, BF16),
            rows,
        ],
        [chip_normed, off_normed, w_qkv, own_qkv, own_grad, own_scores, own_products]
        + [window, w_out, cotangent],
        hbm=(7, 8, 9),
        scratch=like(window) + [dma(3)],
        name="attend",
    )
    chip_stats, off_stats = exchange(stats, stats, "node")
    mesh_out, grad_normed, grad_key, grad_value = call(
        functools.partial(product_kernel, scale, pair),
        [
            rows,
            ((m, channels), F32),
            ((m, channels), F32),
            ((m, channels), F32),
        ],
        [
            weights,
            grad_scores,
            kv,
            own_qkv,
            own_grad,
            latent,
            w_out,
            w_qkv,
        ],
        hbm_outs=(0,),
        scratch=[pltpu.VMEM((m, channels), BF16)] * 3 + [dma(1)],
        name="product",
    )
    (mesh_grad,) = call(
        functools.partial(finish_kernel, pair, meta_rows),
        [rows],
        [
            chip_stats,
            off_stats,
            from_chip,
            from_off,
            near_q,
            chip_grad,
            off_grad,
            own_qkv,
            grad_key,
            grad_value,
            grad_normed,
            w_qkv,
            normal,
            inv_std,
            cotangent,
        ],
        name="finish",
    )
    return (mesh_out, mesh_grad)


def solution(mesh):
    rows = P(("groups", "node"), None)
    flat = P(("groups", "node"))
    placed = (rows, rows) + (flat,) * 8 + (P(None, ("groups", "node")), rows, P(), P(), P())
    return jax.shard_map(
        body, mesh=mesh, in_specs=placed, out_specs=(rows, rows), check_vma=False
    )
```

```python
import functools

import jax
import jax.numpy as jnp
from jax import lax
from jax.experimental import pallas as pl
from jax.experimental.pallas import tpu as pltpu
from jax.sharding import PartitionSpec as P

HEADS = 16
BAND = 128
LANES = 128
F32 = jnp.float32
BF16 = jnp.bfloat16
I32 = jnp.int32
VMEM_LIMIT = 28 * 2**20
PIECES = 2


def mm(a, b):
    return lax.dot_general(a, b, (((1,), (0,)), ((), ())), preferred_element_type=F32)


def mm_nt(a, b):
    return lax.dot_general(a, b, (((1,), (1,)), ((), ())), preferred_element_type=F32)


def mm_tn(a, b):
    return lax.dot_general(a, b, (((0,), (0,)), ((), ())), preferred_element_type=F32)


def iota(shape, dim):
    return lax.broadcasted_iota(I32, shape, dim)


def call(kernel, outs, args, hbm=(), hbm_outs=(), scratch=(), name=None, flops=None):
    args = [
        pltpu.with_memory_space_constraint(a, pltpu.HBM) if i in hbm else a
        for i, a in enumerate(args)
    ]

    def specs(count, far):
        return [
            pl.BlockSpec(memory_space=pltpu.HBM if i in far else pltpu.VMEM) for i in range(count)
        ]

    return pl.pallas_call(
        kernel,
        out_shape=[
            (pltpu.HBM if i in hbm_outs else jax.ShapeDtypeStruct)(shape, dtype)
            for i, (shape, dtype) in enumerate(outs)
        ],
        in_specs=specs(len(args), hbm),
        out_specs=specs(len(outs), hbm_outs),
        scratch_shapes=list(scratch),
        compiler_params=pltpu.CompilerParams(vmem_limit_bytes=VMEM_LIMIT),
        cost_estimate=flops and pl.CostEstimate(flops=flops, transcendentals=0, bytes_accessed=0),
        name=name,
    )(*args)


def dma(count):
    return pltpu.SemaphoreType.DMA((count,))


def start_all(pairs, sems):
    copies = [pltpu.make_async_copy(src, dst, sems.at[i]) for i, (src, dst) in enumerate(pairs)]
    for copy in copies:
        copy.start()
    return copies


def like(*arrays):
    return [pltpu.VMEM(a.shape, a.dtype) for a in arrays]


def exchange(chip_message, off_message, axis):
    n = lax.axis_size(axis)
    from_off = lax.ppermute(
        off_message, axis, [p for i in range(1, n - 1, 2) for p in ((i, i + 1), (i + 1, i))]
    )
    from_chip = lax.ppermute(
        chip_message, axis, [p for i in range(0, n, 2) for p in ((i, i + 1), (i + 1, i))]
    )
    return from_chip, from_off


def is_odd():
    return lax.axis_index("node") % 2


def gelu(projected):
    x = projected.astype(BF16).astype(F32)
    inner = (2.0 / jnp.pi) ** 0.5 * (x + 0.044715 * (x * x * x))
    return (0.5 * x * (1.0 + jnp.tanh(inner))).astype(BF16)


def onehot_rows(index_rows, count):
    parts = [
        jnp.where(iota((count, row.shape[1]), 0) == row, 1.0, 0.0).astype(BF16)
        for row in index_rows
    ]
    return parts[0] if len(parts) == 1 else jnp.concatenate(parts, 1)


def norm_stats(latent):
    values = latent.astype(F32)
    row_mean = jnp.mean(values, -1, keepdims=True)
    centred = values - row_mean
    variance = jnp.mean(centred * centred, -1, keepdims=True)
    inv_std = lax.rsqrt(variance + 1e-05)
    return centred * inv_std, inv_std


def pack_kernel(
    grid_hbm,
    window_hbm,
    side_src_hbm,
    side_dst_hbm,
    side_count_hbm,
    far_src_hbm,
    far_dst_hbm,
    far_count_hbm,
    w_edge_hbm,
    far_out,
    chip_out,
    off_out,
    w_edge,
    grid,
    window,
    side_src,
    side_dst,
    side_count,
    far_src,
    far_dst,
    far_count,
    far,
    meta,
    sems,
    out_sems,
):
    grid_rows, channels = grid.shape
    mesh_rows = window.shape[1]
    slots = far_src.shape[1]
    devices = far_count.shape[1]
    depth = slots // devices
    first = grid_rows - BAND
    count = side_src.shape[0] // 2
    copies = start_all(
        [
            (side_src_hbm, side_src),
            (side_dst_hbm, side_dst),
            (side_count_hbm, side_count),
            (window_hbm, window),
            (grid_hbm, grid),
            (far_src_hbm, far_src),
            (far_dst_hbm, far_dst),
            (far_count_hbm, far_count),
            (w_edge_hbm, w_edge),
        ],
        sems,
    )
    for copy in copies[:4]:
        copy.wait()
    for k in range(2):
        rank = iota((count, LANES), 0) * LANES + iota((count, LANES), 1)
        src = side_src[k * count : (k + 1) * count] - k * first
        live = rank < side_count[:, k : k + 1]
        dst = jnp.where(live, side_dst[k * count : (k + 1) * count], mesh_rows)
        reach = jnp.concatenate([window[...], jnp.zeros((count - 2, mesh_rows), I32)], 0)
        blank = jnp.zeros((count, channels - 2 * LANES - mesh_rows), I32)
        meta[k] = jnp.concatenate([src, dst, reach, blank], 1).astype(F32).astype(BF16)
    copies[4].wait()
    odd = is_odd()
    outs = start_all(
        [
            pair
            for k, out in ((1 - odd, chip_out), (odd, off_out))
            for pair in (
                (grid.at[pl.ds(pl.multiple_of(k * first, BAND), BAND)], out.at[pl.ds(0, BAND)]),
                (meta.at[k], out.at[pl.ds(BAND, count)]),
            )
        ],
        out_sems,
    )
    for copy in copies[5:8]:
        copy.wait()
    slot = iota((1, slots), 1)
    receiver = jnp.where(iota((devices, slots), 0) == iota((devices, slots), 1) // depth, 1.0, 0.0)
    live = mm(far_count[...].astype(F32).astype(BF16), receiver.astype(BF16))
    target = jnp.where((slot % depth).astype(F32) < live, far_dst[...].astype(F32), 1.0 * mesh_rows)
    row = iota((2 * slots, slots), 0)
    mine = slot == row // (2 * depth) * depth + row % depth
    source = jnp.sum(jnp.where(mine, far_src[...].astype(F32), 0.0), 1, keepdims=True)
    column = jnp.sum(jnp.where(mine, target, 0.0), 1, keepdims=True)
    pick = jnp.where(iota((2 * slots, grid_rows), 1).astype(F32) == source, 1.0, 0.0).astype(BF16)
    rows = mm(pick, grid[...]).astype(BF16)
    copies[8].wait()
    rows = gelu(mm(rows, w_edge[...]))
    half = channels // 2
    is_first = iota((2 * slots, half), 0) % (2 * depth) < depth
    far[:, :half] = jnp.where(is_first, rows[:, :half], rows[:, half:])
    far[:, half:] = jnp.broadcast_to(column, (2 * slots, LANES)).astype(BF16)
    last = pltpu.make_async_copy(far, far_out, out_sems.at[4])
    last.start()
    for copy in outs + [last]:
        copy.wait()


def own_kernel(
    grid_hbm,
    mesh_in_hbm,
    own_src_hbm,
    own_dst_hbm,
    cot_hbm,
    w_out_hbm,
    w_edge,
    partial_out,
    grad_hbm,
    grid,
    mesh_in,
    own_src,
    own_dst,
    cot,
    w_out,
    grad,
    sems,
):
    grid_rows = grid.shape[0]
    mesh_rows = mesh_in.shape[0]
    copies = start_all(
        [
            (own_src_hbm, own_src),
            (own_dst_hbm, own_dst),
            (cot_hbm, cot),
            (w_out_hbm, w_out),
            (grid_hbm, grid),
            (mesh_in_hbm, mesh_in),
        ],
        sems,
    )
    for copy in copies[:2]:
        copy.wait()
    rows = own_src.shape[0]
    src = onehot_rows([own_src[r : r + 1] for r in range(rows)], grid_rows)
    dst = onehot_rows([own_dst[r : r + 1] for r in range(rows)], mesh_rows)
    counts = mm_nt(dst, src).astype(BF16)
    for copy in copies[2:4]:
        copy.wait()
    grad[...] = mm_nt(cot[...], w_out[...]).astype(BF16)
    out = pltpu.make_async_copy(grad, grad_hbm, sems.at[6])
    out.start()
    for copy in copies[4:]:
        copy.wait()
    active = gelu(mm(grid[...], w_edge[...]))
    partial_out[...] = mesh_in[...].astype(F32) + mm(counts, active)
    out.wait()


def meta_of(message, count):
    return message[BAND : BAND + count].astype(F32).astype(I32)


def side_kernel(count, chip, off, w_edge, partial, partial_out):
    mesh_rows = partial.shape[0]
    uppers, lowers = [], []
    for side in (chip, off):
        meta = meta_of(side, count)
        src = onehot_rows([meta[r : r + 1, :LANES] for r in range(count)], BAND)
        dst = onehot_rows([meta[r : r + 1, LANES : 2 * LANES] for r in range(count)], mesh_rows)
        counts = mm_nt(dst, src)
        upper = counts.astype(BF16)
        uppers.append(upper)
        lowers.append((counts - upper.astype(F32)).astype(BF16))
    active = gelu(mm(jnp.concatenate([chip[:BAND], off[:BAND]], 0), w_edge[...]))
    landing = jnp.concatenate(uppers + lowers, 1)
    partial_out[...] = partial[...] + mm(landing, jnp.concatenate([active, active], 0))


def latent_kernel(depth, far, partial, latent_out, normed_out, normal_out, inv_std_out):
    mesh_rows, channels = partial.shape
    slots = far.shape[0]
    half = channels // 2
    first = far[:, :half]
    second = pltpu.roll(first.astype(F32), slots - depth, 0).astype(BF16)
    target = jnp.transpose(far[:, half:].astype(F32))
    if mesh_rows != LANES:
        target = jnp.broadcast_to(target[:1], (mesh_rows, slots))
    is_row = iota((mesh_rows, slots), 1) % (2 * depth) < depth
    hit = (target == iota((mesh_rows, slots), 0).astype(F32)) & is_row
    landing = jnp.where(hit, 1.0, 0.0).astype(BF16)
    total = partial[...] + mm(landing, jnp.concatenate([first, second], 1))
    latent = total.astype(BF16)
    latent_out[...] = latent
    normal, inv_std = norm_stats(latent)
    normed_out[...] = normal.astype(BF16)
    normal_out[...] = normal
    inv_std_out[...] = jnp.broadcast_to(inv_std, inv_std_out.shape)


def halves(rows, scale=None):
    first = iota(rows.shape, 1) < rows.shape[1] // 2
    if scale is not None:
        rows = rows * jnp.asarray(scale, rows.dtype)
    zero = jnp.zeros_like(rows)
    return jnp.concatenate([jnp.where(first, rows, zero), jnp.where(first, zero, rows)], 0)


def merge(stacked):
    m = stacked.shape[0] // 2
    first = iota((m, stacked.shape[1]), 1) < stacked.shape[1] // 2
    return jnp.where(first, stacked[:m], stacked[m:])


def project_kernel(
    scale, pair, normed, grad_hbm, w_qkv_hbm, qkv_out, w_qkv, grad_out, scores_out, products_out, sems
):
    m, channels = normed.shape
    width = channels // PIECES
    starts = [part * channels + c * width for c in range(PIECES) for part in range(3)]
    copies = start_all(
        [(grad_hbm, grad_out)]
        + [(w_qkv_hbm.at[:, pl.ds(at, width)], w_qkv.at[:, pl.ds(at, width)]) for at in starts],
        sems,
    )
    for i, at in enumerate(starts):
        copies[1 + i].wait()
        cols = slice(at, at + width)
        qkv_out[:, cols] = mm(normed[...], w_qkv[:, cols]).astype(BF16)
        if i % 3 < 2:
            continue
        if i == 2:
            copies[0].wait()
        for p in range(i // 3 * width // pair, (i // 3 + 1) * width // pair):
            q, k, v = (
                slice(part * channels + p * pair, part * channels + (p + 1) * pair)
                for part in range(3)
            )
            scores_out[p] = mm_nt(halves(qkv_out[:, q], scale), qkv_out[:, k])
            products_out[p] = mm_nt(halves(grad_out[:, q]), qkv_out[:, v])


def near_places(m):
    odd = is_odd()
    return (1 - odd) * 2 * m, odd * 2 * m


def attend_kernel(
    scale,
    pair,
    chip_normed,
    off_normed,
    w_qkv,
    own_qkv,
    own_grad,
    own_scores,
    own_products,
    window_hbm,
    w_out_hbm,
    cot_hbm,
    stats_out,
    attention,
    grad_query,
    weights_out,
    scores_out,
    near_q,
    w_out,
    cot,
    window,
    sems,
):
    fetch = start_all([(window_hbm, window), (w_out_hbm, w_out), (cot_hbm, cot)], sems)
    m, channels = chip_normed.shape
    pairs = channels // pair
    devices = lax.axis_size("node")
    me = lax.axis_index("node")
    near = jnp.concatenate([chip_normed[...], off_normed[...]], 0)

    def bring(group):
        cols = slice(group * 2 * pair, (group + 1) * 2 * pair)
        near_q[:, cols] = mm(near, w_qkv[:, cols]).astype(BF16) * jnp.asarray(scale, BF16)
        blocks = []
        for part in range(1, 3):
            at = part * channels + group * 2 * pair
            blocks.append(mm(near, w_qkv[:, at : at + 2 * pair]).astype(BF16))
        return blocks

    brought = {0: bring(0)}
    fetch[0].wait()
    row = iota((3 * m, m), 0)
    chip_at, off_at = near_places(m)
    key_at = jnp.where(row < m, row + chip_at, jnp.where(row < 2 * m, row - m + off_at, row - m))
    query_at = iota((3 * m, m), 1) + m
    missing = (row >= m) & (row < 2 * m) & ((me == 0) | (me == devices - 1))
    keep = (key_at >= query_at - window[0:1, :]) & (key_at <= query_at + window[1:2, :])
    bias = jnp.transpose(jnp.where(keep & jnp.logical_not(missing), 0.0, -jnp.inf).astype(F32))
    bias = jnp.concatenate([bias, bias], 0)
    lane = iota((2 * m, LANES), 1)
    stats = jnp.zeros((2 * m, LANES), F32)

    def near_of(p):
        return [b[:, p % 2 * pair : (p % 2 + 1) * pair] for b in brought[p // 2]]

    def multiply(p):
        cols = slice(p * pair, (p + 1) * pair)
        keys, values = near_of(p)
        return (
            mm_nt(halves(own_qkv[:, cols], scale), keys),
            mm_nt(halves(own_grad[:, cols]), values),
        )

    ahead = multiply(0)
    for p in range(pairs):
        scores, grad_prob = ahead
        if p + 1 < pairs:
            if p % 2 == 0 and p + 2 < pairs:
                brought[p // 2 + 1] = bring(p // 2 + 1)
            ahead = multiply(p + 1)
        scores = jnp.concatenate([scores, own_scores[p]], 1) + bias
        grad_prob = jnp.concatenate([grad_prob, own_products[p]], 1)
        top = jnp.max(scores, 1, keepdims=True)
        shifted = jnp.exp(scores - top)
        inv_sum = 1.0 / jnp.sum(shifted, 1, keepdims=True)
        probs = shifted * inv_sum
        weights = probs.astype(BF16)
        delta = jnp.sum(probs * grad_prob, 1, keepdims=True)
        grad_scores = (probs * (grad_prob - delta)).astype(BF16)
        weights_out[p] = weights[:, 2 * m :]
        scores_out[p] = grad_scores[:, 2 * m :]
        keys, values = (
            jnp.concatenate([block, own_qkv[:, at + p * pair : at + (p + 1) * pair]], 0)
            for block, at in zip(near_of(p), (channels, 2 * channels))
        )
        cols = slice(p * pair, (p + 1) * pair)
        attention[:, cols] = merge(mm(weights, values)).astype(BF16)
        grad_query[:, cols] = (merge(mm(grad_scores, keys)) * scale).astype(BF16)
        stats = jnp.where(lane == p, top, stats)
        stats = jnp.where(lane == pairs + p, inv_sum, stats)
        stats = jnp.where(lane == 2 * pairs + p, delta, stats)
    stats_out[...] = jnp.transpose(stats)[: 3 * pairs]
    for copy in fetch[1:]:
        copy.wait()


def product_kernel(
    scale,
    pair,
    weights,
    grad_scores,
    attention,
    grad_query,
    own_qkv,
    own_grad,
    latent,
    w_out,
    w_qkv,
    mesh_out_hbm,
    grad_normed,
    grad_key,
    grad_value,
    mesh_out,
    sems,
):
    m, channels = latent.shape
    mesh_out[...] = (latent[...].astype(F32) + mm(attention[...], w_out[...])).astype(BF16)
    out = pltpu.make_async_copy(mesh_out, mesh_out_hbm, sems.at[0])
    out.start()
    for p in range(channels // pair):
        cols = slice(p * pair, (p + 1) * pair)
        grad_key[:, cols] = mm_tn(grad_scores[p], halves(own_qkv[:, cols], scale))
        grad_value[:, cols] = mm_tn(weights[p], halves(own_grad[:, cols]))
    grad_normed[...] = mm_nt(grad_query[...], w_qkv[:, :channels])
    out.wait()


def finish_kernel(
    pair,
    count,
    chip_stats,
    off_stats,
    chip_first,
    off_first,
    near_q,
    chip_grad,
    off_grad,
    own_qkv,
    grad_key,
    grad_value,
    grad_normed,
    w_qkv,
    normal,
    inv_std,
    cot,
    grad_out,
):
    m, channels = normal.shape
    reach = [meta_of(side, count)[:8, 2 * LANES : 2 * LANES + m] for side in (chip_first, off_first)]
    reach = jnp.concatenate(reach, 1)
    key_at = iota((m, 2 * m), 0) + m
    lane = iota((m, 2 * m), 1)
    chip_at, off_at = near_places(m)
    query_at = jnp.where(lane < m, lane + chip_at, lane - m + off_at)
    keep = (key_at >= query_at - reach[0:1, :]) & (key_at <= query_at + reach[1:2, :])
    bias = jnp.where(keep, 0.0, -jnp.inf).astype(F32)
    pairs = channels // pair

    stats = []
    for h in range(2):
        lanes = slice(h * m, (h + 1) * m)
        stats.append(jnp.concatenate([chip_stats[:, lanes], off_stats[:, lanes]], 1))

    def multiply(p):
        cols = slice(p * pair, (p + 1) * pair)
        key2 = halves(own_qkv[:, channels + p * pair : channels + (p + 1) * pair])
        value2 = halves(own_qkv[:, 2 * channels + p * pair : 2 * channels + (p + 1) * pair])
        query = near_q[:, cols]
        grad = jnp.concatenate([chip_grad[:, cols], off_grad[:, cols]], 0)
        return query, grad, mm_nt(key2, query), mm_nt(value2, grad)

    total = grad_normed[...]
    group = 2
    gks, gvs = [], []
    ahead = multiply(0)
    for p in range(pairs):
        cols = slice(p * pair, (p + 1) * pair)
        query, grad, scores, grad_prob = ahead
        if p + 1 < pairs:
            ahead = multiply(p + 1)
        weights, grad_scores = [], []
        for h in range(2):
            half = slice(h * m, (h + 1) * m)
            top, inv_sum, delta = (stats[h][k * pairs + p : k * pairs + p + 1] for k in range(3))
            probs = jnp.exp(scores[half] + bias - top) * inv_sum
            weights.append(probs.astype(BF16))
            grad_scores.append((probs * (grad_prob[half] - delta)).astype(BF16))
        gk = grad_key[:, cols] + merge(mm(jnp.concatenate(grad_scores, 0), query))
        gv = grad_value[:, cols] + merge(mm(jnp.concatenate(weights, 0), grad))
        gks.append(gk.astype(BF16))
        gvs.append(gv.astype(BF16))
        if len(gks) == group:
            at = channels + (p + 1 - group) * pair
            width = group * pair
            total = total + mm_nt(jnp.concatenate(gks, 1), w_qkv[:, at : at + width])
            at = at + channels
            total = total + mm_nt(jnp.concatenate(gvs, 1), w_qkv[:, at : at + width])
            gks, gvs = [], []
    centred = (
        total
        - jnp.mean(total, -1, keepdims=True)
        - normal[...] * jnp.mean(total * normal[...], -1, keepdims=True)
    )
    grad_out[...] = (cot[...].astype(F32) + inv_std[:, :1] * centred).astype(BF16)


def body(
    grid_in,
    mesh_in,
    own_src,
    own_dst,
    side_src,
    side_dst,
    side_count,
    far_src,
    far_dst,
    far_count,
    window,
    cotangent,
    w_edge,
    w_qkv,
    w_out,
):
    devices = lax.axis_size("node")
    grid_rows, channels = grid_in.shape
    m = mesh_in.shape[0]
    far_slots = far_src.shape[0]
    far_depth = far_slots // devices
    head_dim = channels // HEADS
    pair = 2 * head_dim
    pairs = channels // pair
    scale = head_dim ** (-0.5)
    meta_rows = side_src.shape[0] // (2 * LANES)

    side_src, side_dst = side_src.reshape(-1, LANES), side_dst.reshape(-1, LANES)
    own_src, own_dst = own_src.reshape(-1, LANES), own_dst.reshape(-1, LANES)
    far_src, far_dst = far_src.reshape(1, -1), far_dst.reshape(1, -1)
    side_count, far_count = side_count.reshape(1, -1), far_count.reshape(1, -1)
    message = ((BAND + meta_rows, channels), BF16)
    far_block = (2 * far_slots, channels // 2 + LANES)
    far_message, chip_message, off_message, w_edge = call(
        pack_kernel,
        [(far_block, BF16), message, message, (w_edge.shape, BF16)],
        [grid_in, window, side_src, side_dst, side_count, far_src, far_dst, far_count, w_edge],
        hbm=range(9),
        hbm_outs=range(3),
        scratch=like(grid_in, window, side_src, side_dst, side_count, far_src, far_dst, far_count)
        + [
            pltpu.VMEM(far_block, BF16),
            pltpu.VMEM((2, meta_rows, channels), BF16),
            dma(9),
            dma(5),
        ],
        name="pack",
    )
    from_chip, from_off = exchange(chip_message, off_message, "node")
    got_far = lax.all_to_all(
        far_message.reshape(devices, 2 * far_depth, far_block[1]),
        "node",
        split_axis=0,
        concat_axis=0,
        tiled=True,
    ).reshape(far_block)

    rows = ((m, channels), BF16)
    partial, own_grad = call(
        own_kernel,
        [((m, channels), F32), rows],
        [grid_in, mesh_in, own_src, own_dst, cotangent, w_out, w_edge],
        hbm=range(6),
        hbm_outs=(1,),
        scratch=like(grid_in, mesh_in, own_src, own_dst, cotangent, w_out, cotangent) + [dma(7)],
        name="own",
    )
    (partial,) = call(
        functools.partial(side_kernel, meta_rows),
        [((m, channels), F32)],
        [from_chip, from_off, w_edge, partial],
        name="side",
        flops=8 * 10**9,
    )
    latent, normed, normal, inv_std = call(
        functools.partial(latent_kernel, far_depth),
        [rows, rows, ((m, channels), F32), ((m, LANES), F32)],
        [got_far, partial],
        name="latent",
    )
    chip_normed, off_normed = exchange(normed, normed, "node")
    own_block = ((pairs, 2 * m, m), F32)
    own_qkv, w_qkv, own_grad, own_scores, own_products = call(
        functools.partial(project_kernel, scale, pair),
        [((m, 3 * channels), BF16), (w_qkv.shape, BF16), rows, own_block, own_block],
        [normed, own_grad, w_qkv],
        hbm=(1, 2),
        scratch=[dma(3 * PIECES + 1)],
        name="project",
    )
    chip_grad, off_grad = exchange(own_grad, own_grad, "node")
    probs = ((pairs, 2 * m, m), BF16)
    stats, attention, grad_query, weights, grad_scores, near_q, w_out, cotangent = call(
        functools.partial(attend_kernel, scale, pair),
        [
            ((3 * pairs, 2 * m), F32),
            rows,
            rows,
            probs,
            probs,
            ((2 * m, channels), BF16),
            (w_out.shape, BF16),
            rows,
        ],
        [chip_normed, off_normed, w_qkv, own_qkv, own_grad, own_scores, own_products]
        + [window, w_out, cotangent],
        hbm=(7, 8, 9),
        scratch=like(window) + [dma(3)],
        name="attend",
    )
    chip_stats, off_stats = exchange(stats, stats, "node")
    mesh_out, grad_normed, grad_key, grad_value = call(
        functools.partial(product_kernel, scale, pair),
        [
            rows,
            ((m, channels), F32),
            ((m, channels), F32),
            ((m, channels), F32),
        ],
        [
            weights,
            grad_scores,
            attention,
            grad_query,
            own_qkv,
            own_grad,
            latent,
            w_out,
            w_qkv,
        ],
        hbm_outs=(0,),
        scratch=[pltpu.VMEM((m, channels), BF16), dma(1)],
        name="product",
    )
    (mesh_grad,) = call(
        functools.partial(finish_kernel, pair, meta_rows),
        [rows],
        [
            chip_stats,
            off_stats,
            from_chip,
            from_off,
            near_q,
            chip_grad,
            off_grad,
            own_qkv,
            grad_key,
            grad_value,
            grad_normed,
            w_qkv,
            normal,
            inv_std,
            cotangent,
        ],
        name="finish",
    )
    return (mesh_out, mesh_grad)


def solution(mesh):
    rows = P(("groups", "node"), None)
    flat = P(("groups", "node"))
    placed = (rows, rows) + (flat,) * 8 + (P(None, ("groups", "node")), rows, P(), P(), P())
    return jax.shard_map(
        body, mesh=mesh, in_specs=placed, out_specs=(rows, rows), check_vma=False
    )
```

```python
import functools

import jax
import jax.numpy as jnp
from jax import lax
from jax.experimental import pallas as pl
from jax.experimental.pallas import tpu as pltpu
from jax.sharding import PartitionSpec as P

HEADS = 16
BAND = 128
LANES = 128
F32 = jnp.float32
BF16 = jnp.bfloat16
I32 = jnp.int32
VMEM_LIMIT = 28 * 2**20
PIECES = 2
CHUNK = 64


def mm(a, b):
    return lax.dot_general(a, b, (((1,), (0,)), ((), ())), preferred_element_type=F32)


def mm_nt(a, b):
    return lax.dot_general(a, b, (((1,), (1,)), ((), ())), preferred_element_type=F32)


def mm_tn(a, b):
    return lax.dot_general(a, b, (((0,), (0,)), ((), ())), preferred_element_type=F32)


def iota(shape, dim):
    return lax.broadcasted_iota(I32, shape, dim)


def call(kernel, outs, args, hbm=(), hbm_outs=(), scratch=(), name=None, flops=None):
    args = [
        pltpu.with_memory_space_constraint(a, pltpu.HBM) if i in hbm else a
        for i, a in enumerate(args)
    ]

    def specs(count, far):
        return [
            pl.BlockSpec(memory_space=pltpu.HBM if i in far else pltpu.VMEM) for i in range(count)
        ]

    return pl.pallas_call(
        kernel,
        out_shape=[
            (pltpu.HBM if i in hbm_outs else jax.ShapeDtypeStruct)(shape, dtype)
            for i, (shape, dtype) in enumerate(outs)
        ],
        in_specs=specs(len(args), hbm),
        out_specs=specs(len(outs), hbm_outs),
        scratch_shapes=list(scratch),
        compiler_params=pltpu.CompilerParams(vmem_limit_bytes=VMEM_LIMIT),
        cost_estimate=flops and pl.CostEstimate(flops=flops, transcendentals=0, bytes_accessed=0),
        name=name,
    )(*args)


def dma(count):
    return pltpu.SemaphoreType.DMA((count,))


def start_all(pairs, sems):
    copies = [pltpu.make_async_copy(src, dst, sems.at[i]) for i, (src, dst) in enumerate(pairs)]
    for copy in copies:
        copy.start()
    return copies


def like(*arrays):
    return [pltpu.VMEM(a.shape, a.dtype) for a in arrays]


def exchange(chip_message, off_message, axis):
    n = lax.axis_size(axis)
    from_off = lax.ppermute(
        off_message, axis, [p for i in range(1, n - 1, 2) for p in ((i, i + 1), (i + 1, i))]
    )
    from_chip = lax.ppermute(
        chip_message, axis, [p for i in range(0, n, 2) for p in ((i, i + 1), (i + 1, i))]
    )
    return from_chip, from_off


def is_odd():
    return lax.axis_index("node") % 2


def gelu(projected):
    x = projected.astype(BF16).astype(F32)
    inner = (2.0 / jnp.pi) ** 0.5 * (x + 0.044715 * (x * x * x))
    return (0.5 * x * (1.0 + jnp.tanh(inner))).astype(BF16)


def onehot_rows(index_rows, count):
    parts = [
        jnp.where(iota((count, row.shape[1]), 0) == row, 1.0, 0.0).astype(BF16)
        for row in index_rows
    ]
    return parts[0] if len(parts) == 1 else jnp.concatenate(parts, 1)


def norm_stats(latent):
    values = latent.astype(F32)
    row_mean = jnp.mean(values, -1, keepdims=True)
    centred = values - row_mean
    variance = jnp.mean(centred * centred, -1, keepdims=True)
    inv_std = lax.rsqrt(variance + 1e-05)
    return centred * inv_std, inv_std


def pack_kernel(
    grid_hbm,
    window_hbm,
    side_src_hbm,
    side_dst_hbm,
    side_count_hbm,
    far_src_hbm,
    far_dst_hbm,
    far_count_hbm,
    w_edge_hbm,
    far_out,
    chip_out,
    off_out,
    w_edge,
    grid,
    window,
    side_src,
    side_dst,
    side_count,
    far_src,
    far_dst,
    far_count,
    far,
    meta,
    sems,
    out_sems,
):
    grid_rows, channels = grid.shape
    mesh_rows = window.shape[1]
    slots = far_src.shape[1]
    devices = far_count.shape[1]
    depth = slots // devices
    first = grid_rows - BAND
    count = side_src.shape[0] // 2
    copies = start_all(
        [
            (side_src_hbm, side_src),
            (side_dst_hbm, side_dst),
            (side_count_hbm, side_count),
            (window_hbm, window),
            (grid_hbm, grid),
            (far_src_hbm, far_src),
            (far_dst_hbm, far_dst),
            (far_count_hbm, far_count),
            (w_edge_hbm, w_edge),
        ],
        sems,
    )
    for copy in copies[:4]:
        copy.wait()
    for k in range(2):
        rank = iota((count, LANES), 0) * LANES + iota((count, LANES), 1)
        src = side_src[k * count : (k + 1) * count] - k * first
        live = rank < side_count[:, k : k + 1]
        dst = jnp.where(live, side_dst[k * count : (k + 1) * count], mesh_rows)
        reach = jnp.concatenate([window[...], jnp.zeros((count - 2, mesh_rows), I32)], 0)
        blank = jnp.zeros((count, channels - 2 * LANES - mesh_rows), I32)
        meta[k] = jnp.concatenate([src, dst, reach, blank], 1).astype(F32).astype(BF16)
    copies[4].wait()
    odd = is_odd()
    outs = start_all(
        [
            pair
            for k, out in ((1 - odd, chip_out), (odd, off_out))
            for pair in (
                (grid.at[pl.ds(pl.multiple_of(k * first, BAND), BAND)], out.at[pl.ds(0, BAND)]),
                (meta.at[k], out.at[pl.ds(BAND, count)]),
            )
        ],
        out_sems,
    )
    for copy in copies[5:8]:
        copy.wait()
    slot = iota((1, slots), 1)
    receiver = jnp.where(iota((devices, slots), 0) == iota((devices, slots), 1) // depth, 1.0, 0.0)
    live = mm(far_count[...].astype(F32).astype(BF16), receiver.astype(BF16))
    target = jnp.where((slot % depth).astype(F32) < live, far_dst[...].astype(F32), 1.0 * mesh_rows)
    row = iota((2 * slots, slots), 0)
    mine = slot == row // (2 * depth) * depth + row % depth
    source = jnp.sum(jnp.where(mine, far_src[...].astype(F32), 0.0), 1, keepdims=True)
    column = jnp.sum(jnp.where(mine, target, 0.0), 1, keepdims=True)
    pick = jnp.where(iota((2 * slots, grid_rows), 1).astype(F32) == source, 1.0, 0.0).astype(BF16)
    rows = mm(pick, grid[...]).astype(BF16)
    copies[8].wait()
    rows = gelu(mm(rows, w_edge[...]))
    half = channels // 2
    is_first = iota((2 * slots, half), 0) % (2 * depth) < depth
    far[:, :half] = jnp.where(is_first, rows[:, :half], rows[:, half:])
    far[:, half:] = jnp.broadcast_to(column, (2 * slots, LANES)).astype(BF16)
    last = pltpu.make_async_copy(far, far_out, out_sems.at[4])
    last.start()
    for copy in outs + [last]:
        copy.wait()


def own_kernel(
    grid_hbm,
    mesh_in_hbm,
    own_src_hbm,
    own_dst_hbm,
    cot_hbm,
    w_out_hbm,
    w_edge,
    partial_out,
    grad_hbm,
    grid,
    mesh_in,
    own_src,
    own_dst,
    cot,
    w_out,
    grad,
    sems,
):
    grid_rows = grid.shape[0]
    mesh_rows = mesh_in.shape[0]
    copies = start_all(
        [
            (own_src_hbm, own_src),
            (own_dst_hbm, own_dst),
            (cot_hbm, cot),
            (w_out_hbm, w_out),
            (grid_hbm, grid),
            (mesh_in_hbm, mesh_in),
        ],
        sems,
    )
    for copy in copies[:2]:
        copy.wait()
    rows = own_src.shape[0]
    src = onehot_rows([own_src[r : r + 1] for r in range(rows)], grid_rows)
    dst = onehot_rows([own_dst[r : r + 1] for r in range(rows)], mesh_rows)
    counts = mm_nt(dst, src).astype(BF16)
    for copy in copies[2:4]:
        copy.wait()
    grad[...] = mm_nt(cot[...], w_out[...]).astype(BF16)
    out = pltpu.make_async_copy(grad, grad_hbm, sems.at[6])
    out.start()
    for copy in copies[4:]:
        copy.wait()
    active = gelu(mm(grid[...], w_edge[...]))
    partial_out[...] = mesh_in[...].astype(F32) + mm(counts, active)
    out.wait()


def meta_of(message, count):
    return message[BAND : BAND + count].astype(F32).astype(I32)


def side_kernel(count, chip, off, w_edge, partial, partial_out):
    mesh_rows = partial.shape[0]
    uppers, lowers = [], []
    for side in (chip, off):
        meta = meta_of(side, count)
        src = onehot_rows([meta[r : r + 1, :LANES] for r in range(count)], BAND)
        dst = onehot_rows([meta[r : r + 1, LANES : 2 * LANES] for r in range(count)], mesh_rows)
        counts = mm_nt(dst, src)
        upper = counts.astype(BF16)
        uppers.append(upper)
        lowers.append((counts - upper.astype(F32)).astype(BF16))
    active = gelu(mm(jnp.concatenate([chip[:BAND], off[:BAND]], 0), w_edge[...]))
    landing = jnp.concatenate(uppers + lowers, 1)
    partial_out[...] = partial[...] + mm(landing, jnp.concatenate([active, active], 0))


def latent_kernel(depth, far, partial, latent_out, normed_out, normal_out, inv_std_out):
    mesh_rows, channels = partial.shape
    slots = far.shape[0]
    half = channels // 2
    first = far[:, :half]
    second = pltpu.roll(first.astype(F32), slots - depth, 0).astype(BF16)
    target = jnp.transpose(far[:, half:].astype(F32))
    if mesh_rows != LANES:
        target = jnp.broadcast_to(target[:1], (mesh_rows, slots))
    is_row = iota((mesh_rows, slots), 1) % (2 * depth) < depth
    hit = (target == iota((mesh_rows, slots), 0).astype(F32)) & is_row
    landing = jnp.where(hit, 1.0, 0.0).astype(BF16)
    total = partial[...] + mm(landing, jnp.concatenate([first, second], 1))
    latent = total.astype(BF16)
    latent_out[...] = latent
    normal, inv_std = norm_stats(latent)
    normed_out[...] = normal.astype(BF16)
    normal_out[...] = normal
    inv_std_out[...] = jnp.broadcast_to(inv_std, inv_std_out.shape)


def halves(rows, scale=None):
    first = iota(rows.shape, 1) < rows.shape[1] // 2
    if scale is not None:
        rows = rows * jnp.asarray(scale, rows.dtype)
    zero = jnp.zeros_like(rows)
    return jnp.concatenate([jnp.where(first, rows, zero), jnp.where(first, zero, rows)], 0)


def merge(stacked):
    m = stacked.shape[0] // 2
    first = iota((m, stacked.shape[1]), 1) < stacked.shape[1] // 2
    return jnp.where(first, stacked[:m], stacked[m:])


def project_kernel(
    scale, pair, normed, grad_hbm, w_qkv_hbm, qkv_out, w_qkv, grad_out, scores_out, products_out, sems
):
    m, channels = normed.shape
    width = channels // PIECES
    starts = [part * channels + c * width for c in range(PIECES) for part in range(3)]
    copies = start_all(
        [(grad_hbm, grad_out)]
        + [(w_qkv_hbm.at[:, pl.ds(at, width)], w_qkv.at[:, pl.ds(at, width)]) for at in starts],
        sems,
    )
    for i, at in enumerate(starts):
        copies[1 + i].wait()
        cols = slice(at, at + width)
        qkv_out[:, cols] = mm(normed[...], w_qkv[:, cols]).astype(BF16)
        if i % 3 < 2:
            continue
        if i == 2:
            copies[0].wait()
        for p in range(i // 3 * width // pair, (i // 3 + 1) * width // pair):
            q, k, v = (
                slice(part * channels + p * pair, part * channels + (p + 1) * pair)
                for part in range(3)
            )
            scores_out[p] = mm_nt(halves(qkv_out[:, q], scale), qkv_out[:, k])
            products_out[p] = mm_nt(halves(grad_out[:, q]), qkv_out[:, v])


def near_places(m):
    odd = is_odd()
    return (1 - odd) * 2 * m, odd * 2 * m


def attend_kernel(
    scale,
    pair,
    chip_normed,
    off_normed,
    w_qkv,
    own_qkv,
    own_grad,
    own_scores,
    own_products,
    window_hbm,
    w_out_hbm,
    cot_hbm,
    stats_out,
    attention,
    grad_query,
    weights_out,
    scores_out,
    near_q,
    w_out,
    cot,
    window,
    sems,
):
    fetch = start_all([(window_hbm, window), (w_out_hbm, w_out), (cot_hbm, cot)], sems)
    m, channels = chip_normed.shape
    pairs = channels // pair
    devices = lax.axis_size("node")
    me = lax.axis_index("node")
    near = jnp.concatenate([chip_normed[...], off_normed[...]], 0)

    def bring(group):
        cols = slice(group * 2 * pair, (group + 1) * 2 * pair)
        near_q[:, cols] = mm(near, w_qkv[:, cols]).astype(BF16) * jnp.asarray(scale, BF16)
        blocks = []
        for part in range(1, 3):
            at = part * channels + group * 2 * pair
            blocks.append(mm(near, w_qkv[:, at : at + 2 * pair]).astype(BF16))
        return blocks

    brought = {0: bring(0)}
    fetch[0].wait()
    row = iota((3 * m, m), 0)
    chip_at, off_at = near_places(m)
    key_at = jnp.where(row < m, row + chip_at, jnp.where(row < 2 * m, row - m + off_at, row - m))
    query_at = iota((3 * m, m), 1) + m
    missing = (row >= m) & (row < 2 * m) & ((me == 0) | (me == devices - 1))
    keep = (key_at >= query_at - window[0:1, :]) & (key_at <= query_at + window[1:2, :])
    bias = jnp.transpose(jnp.where(keep & jnp.logical_not(missing), 0.0, -jnp.inf).astype(F32))
    lane = iota((CHUNK, LANES), 1)
    stats = [jnp.zeros((CHUNK, LANES), F32) for _ in range(2 * m // CHUNK)]

    def near_of(p):
        return [b[:, p % 2 * pair : (p % 2 + 1) * pair] for b in brought[p // 2]]

    def multiply(p):
        cols = slice(p * pair, (p + 1) * pair)
        keys, values = near_of(p)
        return (
            mm_nt(halves(own_qkv[:, cols], scale), keys),
            mm_nt(halves(own_grad[:, cols]), values),
        )

    ahead = multiply(0)
    for p in range(pairs):
        scores, grad_prob = ahead
        if p + 1 < pairs:
            if p % 2 == 0 and p + 2 < pairs:
                brought[p // 2 + 1] = bring(p // 2 + 1)
            ahead = multiply(p + 1)
        weights, grad_scores = [], []
        for at in range(0, 2 * m, CHUNK):
            part = slice(at, at + CHUNK)
            place = slice(at % m, at % m + CHUNK)
            raw = jnp.concatenate([scores[part], own_scores[p, part]], 1) + bias[place]
            top = jnp.max(raw, 1, keepdims=True)
            shifted = jnp.exp(raw - top)
            inv_sum = 1.0 / jnp.sum(shifted, 1, keepdims=True)
            probs = shifted * inv_sum
            product = jnp.concatenate([grad_prob[part], own_products[p, part]], 1)
            delta = jnp.sum(probs * product, 1, keepdims=True)
            weights.append(probs.astype(BF16))
            grad_scores.append((probs * (product - delta)).astype(BF16))
            for k, column in enumerate((top, inv_sum, delta)):
                stats[at // CHUNK] = jnp.where(lane == k * pairs + p, column, stats[at // CHUNK])
        weights = jnp.concatenate(weights, 0)
        grad_scores = jnp.concatenate(grad_scores, 0)
        weights_out[p] = weights[:, 2 * m :]
        scores_out[p] = grad_scores[:, 2 * m :]
        keys, values = (
            jnp.concatenate([block, own_qkv[:, at + p * pair : at + (p + 1) * pair]], 0)
            for block, at in zip(near_of(p), (channels, 2 * channels))
        )
        cols = slice(p * pair, (p + 1) * pair)
        attention[:, cols] = merge(mm(weights, values)).astype(BF16)
        grad_query[:, cols] = (merge(mm(grad_scores, keys)) * scale).astype(BF16)
    stats_out[...] = jnp.transpose(jnp.concatenate(stats, 0))[: 3 * pairs]
    for copy in fetch[1:]:
        copy.wait()


def product_kernel(
    scale,
    pair,
    weights,
    grad_scores,
    attention,
    grad_query,
    own_qkv,
    own_grad,
    latent,
    w_out,
    w_qkv,
    mesh_out_hbm,
    grad_normed,
    grad_key,
    grad_value,
    mesh_out,
    sems,
):
    m, channels = latent.shape
    mesh_out[...] = (latent[...].astype(F32) + mm(attention[...], w_out[...])).astype(BF16)
    out = pltpu.make_async_copy(mesh_out, mesh_out_hbm, sems.at[0])
    out.start()
    for p in range(channels // pair):
        cols = slice(p * pair, (p + 1) * pair)
        grad_key[:, cols] = mm_tn(grad_scores[p], halves(own_qkv[:, cols], scale))
        grad_value[:, cols] = mm_tn(weights[p], halves(own_grad[:, cols]))
    grad_normed[...] = mm_nt(grad_query[...], w_qkv[:, :channels])
    out.wait()


def finish_kernel(
    pair,
    count,
    chip_stats,
    off_stats,
    chip_first,
    off_first,
    near_q,
    chip_grad,
    off_grad,
    own_qkv,
    grad_key,
    grad_value,
    grad_normed,
    w_qkv,
    normal,
    inv_std,
    cot,
    grad_out,
):
    m, channels = normal.shape
    reach = [meta_of(side, count)[:8, 2 * LANES : 2 * LANES + m] for side in (chip_first, off_first)]
    reach = jnp.concatenate(reach, 1)
    key_at = iota((m, 2 * m), 0) + m
    lane = iota((m, 2 * m), 1)
    chip_at, off_at = near_places(m)
    query_at = jnp.where(lane < m, lane + chip_at, lane - m + off_at)
    keep = (key_at >= query_at - reach[0:1, :]) & (key_at <= query_at + reach[1:2, :])
    bias = jnp.where(keep, 0.0, -jnp.inf).astype(F32)
    pairs = channels // pair

    stats = []
    for h in range(2):
        lanes = slice(h * m, (h + 1) * m)
        stats.append(jnp.concatenate([chip_stats[:, lanes], off_stats[:, lanes]], 1))

    def multiply(p):
        cols = slice(p * pair, (p + 1) * pair)
        key2 = halves(own_qkv[:, channels + p * pair : channels + (p + 1) * pair])
        value2 = halves(own_qkv[:, 2 * channels + p * pair : 2 * channels + (p + 1) * pair])
        query = near_q[:, cols]
        grad = jnp.concatenate([chip_grad[:, cols], off_grad[:, cols]], 0)
        return query, grad, mm_nt(key2, query), mm_nt(value2, grad)

    total = grad_normed[...]
    group = 2
    gks, gvs = [], []
    ahead = multiply(0)
    for p in range(pairs):
        cols = slice(p * pair, (p + 1) * pair)
        query, grad, scores, grad_prob = ahead
        if p + 1 < pairs:
            ahead = multiply(p + 1)
        weights, grad_scores = [], []
        for at in range(0, 2 * m, CHUNK):
            part = slice(at, at + CHUNK)
            place = slice(at % m, at % m + CHUNK)
            top, inv_sum, delta = (
                stats[at // m][k * pairs + p : k * pairs + p + 1] for k in range(3)
            )
            probs = jnp.exp(scores[part] + bias[place] - top) * inv_sum
            weights.append(probs.astype(BF16))
            grad_scores.append((probs * (grad_prob[part] - delta)).astype(BF16))
        gk = grad_key[:, cols] + merge(mm(jnp.concatenate(grad_scores, 0), query))
        gv = grad_value[:, cols] + merge(mm(jnp.concatenate(weights, 0), grad))
        gks.append(gk.astype(BF16))
        gvs.append(gv.astype(BF16))
        if len(gks) == group:
            at = channels + (p + 1 - group) * pair
            width = group * pair
            total = total + mm_nt(jnp.concatenate(gks, 1), w_qkv[:, at : at + width])
            at = at + channels
            total = total + mm_nt(jnp.concatenate(gvs, 1), w_qkv[:, at : at + width])
            gks, gvs = [], []
    centred = (
        total
        - jnp.mean(total, -1, keepdims=True)
        - normal[...] * jnp.mean(total * normal[...], -1, keepdims=True)
    )
    grad_out[...] = (cot[...].astype(F32) + inv_std[:, :1] * centred).astype(BF16)


def body(
    grid_in,
    mesh_in,
    own_src,
    own_dst,
    side_src,
    side_dst,
    side_count,
    far_src,
    far_dst,
    far_count,
    window,
    cotangent,
    w_edge,
    w_qkv,
    w_out,
):
    devices = lax.axis_size("node")
    grid_rows, channels = grid_in.shape
    m = mesh_in.shape[0]
    far_slots = far_src.shape[0]
    far_depth = far_slots // devices
    head_dim = channels // HEADS
    pair = 2 * head_dim
    pairs = channels // pair
    scale = head_dim ** (-0.5)
    meta_rows = side_src.shape[0] // (2 * LANES)

    side_src, side_dst = side_src.reshape(-1, LANES), side_dst.reshape(-1, LANES)
    own_src, own_dst = own_src.reshape(-1, LANES), own_dst.reshape(-1, LANES)
    far_src, far_dst = far_src.reshape(1, -1), far_dst.reshape(1, -1)
    side_count, far_count = side_count.reshape(1, -1), far_count.reshape(1, -1)
    message = ((BAND + meta_rows, channels), BF16)
    far_block = (2 * far_slots, channels // 2 + LANES)
    far_message, chip_message, off_message, w_edge = call(
        pack_kernel,
        [(far_block, BF16), message, message, (w_edge.shape, BF16)],
        [grid_in, window, side_src, side_dst, side_count, far_src, far_dst, far_count, w_edge],
        hbm=range(9),
        hbm_outs=range(3),
        scratch=like(grid_in, window, side_src, side_dst, side_count, far_src, far_dst, far_count)
        + [
            pltpu.VMEM(far_block, BF16),
            pltpu.VMEM((2, meta_rows, channels), BF16),
            dma(9),
            dma(5),
        ],
        name="pack",
    )
    from_chip, from_off = exchange(chip_message, off_message, "node")
    got_far = lax.all_to_all(
        far_message.reshape(devices, 2 * far_depth, far_block[1]),
        "node",
        split_axis=0,
        concat_axis=0,
        tiled=True,
    ).reshape(far_block)

    rows = ((m, channels), BF16)
    partial, own_grad = call(
        own_kernel,
        [((m, channels), F32), rows],
        [grid_in, mesh_in, own_src, own_dst, cotangent, w_out, w_edge],
        hbm=range(6),
        hbm_outs=(1,),
        scratch=like(grid_in, mesh_in, own_src, own_dst, cotangent, w_out, cotangent) + [dma(7)],
        name="own",
    )
    (partial,) = call(
        functools.partial(side_kernel, meta_rows),
        [((m, channels), F32)],
        [from_chip, from_off, w_edge, partial],
        name="side",
        flops=8 * 10**9,
    )
    latent, normed, normal, inv_std = call(
        functools.partial(latent_kernel, far_depth),
        [rows, rows, ((m, channels), F32), ((m, LANES), F32)],
        [got_far, partial],
        name="latent",
    )
    chip_normed, off_normed = exchange(normed, normed, "node")
    own_block = ((pairs, 2 * m, m), F32)
    own_qkv, w_qkv, own_grad, own_scores, own_products = call(
        functools.partial(project_kernel, scale, pair),
        [((m, 3 * channels), BF16), (w_qkv.shape, BF16), rows, own_block, own_block],
        [normed, own_grad, w_qkv],
        hbm=(1, 2),
        scratch=[dma(3 * PIECES + 1)],
        name="project",
    )
    chip_grad, off_grad = exchange(own_grad, own_grad, "node")
    probs = ((pairs, 2 * m, m), BF16)
    stats, attention, grad_query, weights, grad_scores, near_q, w_out, cotangent = call(
        functools.partial(attend_kernel, scale, pair),
        [
            ((3 * pairs, 2 * m), F32),
            rows,
            rows,
            probs,
            probs,
            ((2 * m, channels), BF16),
            (w_out.shape, BF16),
            rows,
        ],
        [chip_normed, off_normed, w_qkv, own_qkv, own_grad, own_scores, own_products]
        + [window, w_out, cotangent],
        hbm=(7, 8, 9),
        scratch=like(window) + [dma(3)],
        name="attend",
    )
    chip_stats, off_stats = exchange(stats, stats, "node")
    mesh_out, grad_normed, grad_key, grad_value = call(
        functools.partial(product_kernel, scale, pair),
        [
            rows,
            ((m, channels), F32),
            ((m, channels), F32),
            ((m, channels), F32),
        ],
        [
            weights,
            grad_scores,
            attention,
            grad_query,
            own_qkv,
            own_grad,
            latent,
            w_out,
            w_qkv,
        ],
        hbm_outs=(0,),
        scratch=[pltpu.VMEM((m, channels), BF16), dma(1)],
        name="product",
    )
    (mesh_grad,) = call(
        functools.partial(finish_kernel, pair, meta_rows),
        [rows],
        [
            chip_stats,
            off_stats,
            from_chip,
            from_off,
            near_q,
            chip_grad,
            off_grad,
            own_qkv,
            grad_key,
            grad_value,
            grad_normed,
            w_qkv,
            normal,
            inv_std,
            cotangent,
        ],
        name="finish",
    )
    return (mesh_out, mesh_grad)


def solution(mesh):
    rows = P(("groups", "node"), None)
    flat = P(("groups", "node"))
    placed = (rows, rows) + (flat,) * 8 + (P(None, ("groups", "node")), rows, P(), P(), P())
    return jax.shard_map(
        body, mesh=mesh, in_specs=placed, out_specs=(rows, rows), check_vma=False
    )
```

```python
import functools

import jax
import jax.numpy as jnp
from jax import lax
from jax.experimental import pallas as pl
from jax.experimental.pallas import tpu as pltpu
from jax.sharding import PartitionSpec as P

HEADS = 16
BAND = 128
LANES = 128
F32 = jnp.float32
BF16 = jnp.bfloat16
I32 = jnp.int32
VMEM_LIMIT = 28 * 2**20
PIECES = 2
CHUNK = 64


def mm(a, b):
    return lax.dot_general(a, b, (((1,), (0,)), ((), ())), preferred_element_type=F32)


def mm_nt(a, b):
    return lax.dot_general(a, b, (((1,), (1,)), ((), ())), preferred_element_type=F32)


def mm_tn(a, b):
    return lax.dot_general(a, b, (((0,), (0,)), ((), ())), preferred_element_type=F32)


def iota(shape, dim):
    return lax.broadcasted_iota(I32, shape, dim)


def call(kernel, outs, args, hbm=(), hbm_outs=(), scratch=(), name=None, flops=None):
    args = [
        pltpu.with_memory_space_constraint(a, pltpu.HBM) if i in hbm else a
        for i, a in enumerate(args)
    ]

    def specs(count, far):
        return [
            pl.BlockSpec(memory_space=pltpu.HBM if i in far else pltpu.VMEM) for i in range(count)
        ]

    return pl.pallas_call(
        kernel,
        out_shape=[
            (pltpu.HBM if i in hbm_outs else jax.ShapeDtypeStruct)(shape, dtype)
            for i, (shape, dtype) in enumerate(outs)
        ],
        in_specs=specs(len(args), hbm),
        out_specs=specs(len(outs), hbm_outs),
        scratch_shapes=list(scratch),
        compiler_params=pltpu.CompilerParams(vmem_limit_bytes=VMEM_LIMIT),
        cost_estimate=flops and pl.CostEstimate(flops=flops, transcendentals=0, bytes_accessed=0),
        name=name,
    )(*args)


def dma(count):
    return pltpu.SemaphoreType.DMA((count,))


def start_all(pairs, sems):
    copies = [pltpu.make_async_copy(src, dst, sems.at[i]) for i, (src, dst) in enumerate(pairs)]
    for copy in copies:
        copy.start()
    return copies


def like(*arrays):
    return [pltpu.VMEM(a.shape, a.dtype) for a in arrays]


def exchange(chip_message, off_message, axis):
    n = lax.axis_size(axis)
    from_off = lax.ppermute(
        off_message, axis, [p for i in range(1, n - 1, 2) for p in ((i, i + 1), (i + 1, i))]
    )
    from_chip = lax.ppermute(
        chip_message, axis, [p for i in range(0, n, 2) for p in ((i, i + 1), (i + 1, i))]
    )
    return from_chip, from_off


def is_odd():
    return lax.axis_index("node") % 2


def gelu(projected):
    x = projected.astype(BF16).astype(F32)
    inner = (2.0 / jnp.pi) ** 0.5 * (x + 0.044715 * (x * x * x))
    return (0.5 * x * (1.0 + jnp.tanh(inner))).astype(BF16)


def onehot_rows(index_rows, count):
    parts = [
        jnp.where(iota((count, row.shape[1]), 0) == row, 1.0, 0.0).astype(BF16)
        for row in index_rows
    ]
    return parts[0] if len(parts) == 1 else jnp.concatenate(parts, 1)


def norm_stats(latent):
    values = latent.astype(F32)
    row_mean = jnp.mean(values, -1, keepdims=True)
    centred = values - row_mean
    variance = jnp.mean(centred * centred, -1, keepdims=True)
    inv_std = lax.rsqrt(variance + 1e-05)
    return centred * inv_std, inv_std


def pack_kernel(
    grid_hbm,
    window_hbm,
    side_src_hbm,
    side_dst_hbm,
    side_count_hbm,
    far_src_hbm,
    far_dst_hbm,
    far_count_hbm,
    w_edge_hbm,
    far_out,
    chip_out,
    off_out,
    w_edge,
    grid,
    window,
    side_src,
    side_dst,
    side_count,
    far_src,
    far_dst,
    far_count,
    far,
    meta,
    sems,
    out_sems,
):
    grid_rows, channels = grid.shape
    mesh_rows = window.shape[1]
    slots = far_src.shape[1]
    devices = far_count.shape[1]
    depth = slots // devices
    first = grid_rows - BAND
    count = side_src.shape[0] // 2
    copies = start_all(
        [
            (side_src_hbm, side_src),
            (side_dst_hbm, side_dst),
            (side_count_hbm, side_count),
            (window_hbm, window),
            (grid_hbm, grid),
            (far_src_hbm, far_src),
            (far_dst_hbm, far_dst),
            (far_count_hbm, far_count),
            (w_edge_hbm, w_edge),
        ],
        sems,
    )
    for copy in copies[:4]:
        copy.wait()
    for k in range(2):
        rank = iota((count, LANES), 0) * LANES + iota((count, LANES), 1)
        src = side_src[k * count : (k + 1) * count] - k * first
        live = rank < side_count[:, k : k + 1]
        dst = jnp.where(live, side_dst[k * count : (k + 1) * count], mesh_rows)
        reach = jnp.concatenate([window[...], jnp.zeros((count - 2, mesh_rows), I32)], 0)
        blank = jnp.zeros((count, channels - 2 * LANES - mesh_rows), I32)
        meta[k] = jnp.concatenate([src, dst, reach, blank], 1).astype(F32).astype(BF16)
    copies[4].wait()
    odd = is_odd()
    outs = start_all(
        [
            pair
            for k, out in ((1 - odd, chip_out), (odd, off_out))
            for pair in (
                (grid.at[pl.ds(pl.multiple_of(k * first, BAND), BAND)], out.at[pl.ds(0, BAND)]),
                (meta.at[k], out.at[pl.ds(BAND, count)]),
            )
        ],
        out_sems,
    )
    for copy in copies[5:8]:
        copy.wait()
    slot = iota((1, slots), 1)
    receiver = jnp.where(iota((devices, slots), 0) == iota((devices, slots), 1) // depth, 1.0, 0.0)
    live = mm(far_count[...].astype(F32).astype(BF16), receiver.astype(BF16))
    target = jnp.where((slot % depth).astype(F32) < live, far_dst[...].astype(F32), 1.0 * mesh_rows)
    row = iota((2 * slots, slots), 0)
    mine = slot == row // (2 * depth) * depth + row % depth
    source = jnp.sum(jnp.where(mine, far_src[...].astype(F32), 0.0), 1, keepdims=True)
    column = jnp.sum(jnp.where(mine, target, 0.0), 1, keepdims=True)
    pick = jnp.where(iota((2 * slots, grid_rows), 1).astype(F32) == source, 1.0, 0.0).astype(BF16)
    rows = mm(pick, grid[...]).astype(BF16)
    copies[8].wait()
    rows = gelu(mm(rows, w_edge[...]))
    half = channels // 2
    is_first = iota((2 * slots, half), 0) % (2 * depth) < depth
    far[:, :half] = jnp.where(is_first, rows[:, :half], rows[:, half:])
    far[:, half:] = jnp.broadcast_to(column, (2 * slots, LANES)).astype(BF16)
    last = pltpu.make_async_copy(far, far_out, out_sems.at[4])
    last.start()
    for copy in outs + [last]:
        copy.wait()


def own_kernel(
    grid_hbm,
    mesh_in_hbm,
    own_src_hbm,
    own_dst_hbm,
    cot_hbm,
    w_out_hbm,
    w_edge,
    partial_out,
    grad_hbm,
    grid,
    mesh_in,
    own_src,
    own_dst,
    cot,
    w_out,
    grad,
    sems,
):
    grid_rows = grid.shape[0]
    mesh_rows = mesh_in.shape[0]
    copies = start_all(
        [
            (own_src_hbm, own_src),
            (own_dst_hbm, own_dst),
            (cot_hbm, cot),
            (w_out_hbm, w_out),
            (grid_hbm, grid),
            (mesh_in_hbm, mesh_in),
        ],
        sems,
    )
    for copy in copies[:2]:
        copy.wait()
    rows = own_src.shape[0]
    src = onehot_rows([own_src[r : r + 1] for r in range(rows)], grid_rows)
    dst = onehot_rows([own_dst[r : r + 1] for r in range(rows)], mesh_rows)
    counts = mm_nt(dst, src).astype(BF16)
    for copy in copies[2:4]:
        copy.wait()
    grad[...] = mm_nt(cot[...], w_out[...]).astype(BF16)
    out = pltpu.make_async_copy(grad, grad_hbm, sems.at[6])
    out.start()
    for copy in copies[4:]:
        copy.wait()
    active = gelu(mm(grid[...], w_edge[...]))
    partial_out[...] = mesh_in[...].astype(F32) + mm(counts, active)
    out.wait()


def meta_of(message, count):
    return message[BAND : BAND + count].astype(F32).astype(I32)


def side_kernel(count, chip, off, w_edge, partial, partial_out):
    mesh_rows = partial.shape[0]
    uppers, lowers = [], []
    for side in (chip, off):
        meta = meta_of(side, count)
        src = onehot_rows([meta[r : r + 1, :LANES] for r in range(count)], BAND)
        dst = onehot_rows([meta[r : r + 1, LANES : 2 * LANES] for r in range(count)], mesh_rows)
        counts = mm_nt(dst, src)
        upper = counts.astype(BF16)
        uppers.append(upper)
        lowers.append((counts - upper.astype(F32)).astype(BF16))
    active = gelu(mm(jnp.concatenate([chip[:BAND], off[:BAND]], 0), w_edge[...]))
    landing = jnp.concatenate(uppers + lowers, 1)
    partial_out[...] = partial[...] + mm(landing, jnp.concatenate([active, active], 0))


def latent_kernel(depth, far, partial, latent_out, normed_out, normal_out, inv_std_out):
    mesh_rows, channels = partial.shape
    slots = far.shape[0]
    half = channels // 2
    first = far[:, :half]
    second = pltpu.roll(first.astype(F32), slots - depth, 0).astype(BF16)
    target = jnp.transpose(far[:, half:].astype(F32))
    if mesh_rows != LANES:
        target = jnp.broadcast_to(target[:1], (mesh_rows, slots))
    is_row = iota((mesh_rows, slots), 1) % (2 * depth) < depth
    hit = (target == iota((mesh_rows, slots), 0).astype(F32)) & is_row
    landing = jnp.where(hit, 1.0, 0.0).astype(BF16)
    total = partial[...] + mm(landing, jnp.concatenate([first, second], 1))
    latent = total.astype(BF16)
    latent_out[...] = latent
    normal, inv_std = norm_stats(latent)
    normed_out[...] = normal.astype(BF16)
    normal_out[...] = normal
    inv_std_out[...] = jnp.broadcast_to(inv_std, inv_std_out.shape)


def halves(rows, scale=None):
    first = iota(rows.shape, 1) < rows.shape[1] // 2
    if scale is not None:
        rows = rows * jnp.asarray(scale, rows.dtype)
    zero = jnp.zeros_like(rows)
    return jnp.concatenate([jnp.where(first, rows, zero), jnp.where(first, zero, rows)], 0)


def merge(stacked):
    m = stacked.shape[0] // 2
    first = iota((m, stacked.shape[1]), 1) < stacked.shape[1] // 2
    return jnp.where(first, stacked[:m], stacked[m:])


def near_places(m):
    odd = is_odd()
    return (1 - odd) * 2 * m, odd * 2 * m


def project_kernel(
    scale,
    pair,
    count,
    normed,
    chip_first,
    off_first,
    window_hbm,
    grad_hbm,
    w_qkv_hbm,
    qkv_out,
    w_qkv,
    grad_out,
    scores_out,
    products_out,
    bias_out,
    near_bias_out,
    window,
    sems,
):
    m, channels = normed.shape
    width = channels // PIECES
    starts = [part * channels + c * width for c in range(PIECES) for part in range(3)]
    copies = start_all(
        [(grad_hbm, grad_out)]
        + [(w_qkv_hbm.at[:, pl.ds(at, width)], w_qkv.at[:, pl.ds(at, width)]) for at in starts]
        + [(window_hbm, window)],
        sems,
    )
    chip_at, off_at = near_places(m)
    reach = [meta_of(side, count)[:8, 2 * LANES : 2 * LANES + m] for side in (chip_first, off_first)]
    reach = jnp.concatenate(reach, 1)
    key_at = iota((m, 2 * m), 0) + m
    lane = iota((m, 2 * m), 1)
    query_at = jnp.where(lane < m, lane + chip_at, lane - m + off_at)
    keep = (key_at >= query_at - reach[0:1, :]) & (key_at <= query_at + reach[1:2, :])
    near_bias_out[...] = jnp.where(keep, 0.0, -jnp.inf).astype(F32)
    copies[-1].wait()
    me = lax.axis_index("node")
    row = iota((3 * m, m), 0)
    key_at = jnp.where(row < m, row + chip_at, jnp.where(row < 2 * m, row - m + off_at, row - m))
    query_at = iota((3 * m, m), 1) + m
    at_end = (me == 0) | (me == lax.axis_size("node") - 1)
    missing = (row >= m) & (row < 2 * m) & at_end
    keep = (key_at >= query_at - window[0:1, :]) & (key_at <= query_at + window[1:2, :])
    bias = jnp.where(keep & jnp.logical_not(missing), 0.0, -jnp.inf).astype(F32)
    bias_out[...] = jnp.transpose(bias)
    for i, at in enumerate(starts):
        copies[1 + i].wait()
        cols = slice(at, at + width)
        qkv_out[:, cols] = mm(normed[...], w_qkv[:, cols]).astype(BF16)
        if i % 3 < 2:
            continue
        if i == 2:
            copies[0].wait()
        for p in range(i // 3 * width // pair, (i // 3 + 1) * width // pair):
            q, k, v = (
                slice(part * channels + p * pair, part * channels + (p + 1) * pair)
                for part in range(3)
            )
            scores_out[p] = mm_nt(halves(qkv_out[:, q], scale), qkv_out[:, k])
            products_out[p] = mm_nt(halves(grad_out[:, q]), qkv_out[:, v])


def attend_kernel(
    scale,
    pair,
    chip_normed,
    off_normed,
    w_qkv,
    own_qkv,
    own_grad,
    own_scores,
    own_products,
    bias,
    w_out_hbm,
    cot_hbm,
    stats_out,
    attention,
    grad_query,
    weights_out,
    scores_out,
    near_q,
    w_out,
    cot,
    sems,
):
    fetch = start_all([(w_out_hbm, w_out), (cot_hbm, cot)], sems)
    m, channels = chip_normed.shape
    pairs = channels // pair
    near = jnp.concatenate([chip_normed[...], off_normed[...]], 0)

    def bring(group):
        cols = slice(group * 2 * pair, (group + 1) * 2 * pair)
        near_q[:, cols] = mm(near, w_qkv[:, cols]).astype(BF16) * jnp.asarray(scale, BF16)
        blocks = []
        for part in range(1, 3):
            at = part * channels + group * 2 * pair
            blocks.append(mm(near, w_qkv[:, at : at + 2 * pair]).astype(BF16))
        return blocks

    brought = {0: bring(0)}
    lane = iota((CHUNK, LANES), 1)
    stats = [jnp.zeros((CHUNK, LANES), F32) for _ in range(2 * m // CHUNK)]

    def near_of(p):
        return [b[:, p % 2 * pair : (p % 2 + 1) * pair] for b in brought[p // 2]]

    def multiply(p):
        cols = slice(p * pair, (p + 1) * pair)
        keys, values = near_of(p)
        return (
            mm_nt(halves(own_qkv[:, cols], scale), keys),
            mm_nt(halves(own_grad[:, cols]), values),
        )

    ahead = multiply(0)
    for p in range(pairs):
        scores, grad_prob = ahead
        if p + 1 < pairs:
            if p % 2 == 0 and p + 2 < pairs:
                brought[p // 2 + 1] = bring(p // 2 + 1)
            ahead = multiply(p + 1)
        weights, grad_scores = [], []
        for at in range(0, 2 * m, CHUNK):
            part = slice(at, at + CHUNK)
            place = slice(at % m, at % m + CHUNK)
            raw = jnp.concatenate([scores[part], own_scores[p, part]], 1) + bias[place]
            top = jnp.max(raw, 1, keepdims=True)
            shifted = jnp.exp(raw - top)
            inv_sum = 1.0 / jnp.sum(shifted, 1, keepdims=True)
            probs = shifted * inv_sum
            product = jnp.concatenate([grad_prob[part], own_products[p, part]], 1)
            delta = jnp.sum(probs * product, 1, keepdims=True)
            weights.append(probs.astype(BF16))
            grad_scores.append((probs * (product - delta)).astype(BF16))
            for k, column in enumerate((top, inv_sum, delta)):
                stats[at // CHUNK] = jnp.where(lane == k * pairs + p, column, stats[at // CHUNK])
        weights = jnp.concatenate(weights, 0)
        grad_scores = jnp.concatenate(grad_scores, 0)
        weights_out[p] = weights[:, 2 * m :]
        scores_out[p] = grad_scores[:, 2 * m :]
        keys, values = (
            jnp.concatenate([block, own_qkv[:, at + p * pair : at + (p + 1) * pair]], 0)
            for block, at in zip(near_of(p), (channels, 2 * channels))
        )
        cols = slice(p * pair, (p + 1) * pair)
        attention[:, cols] = merge(mm(weights, values)).astype(BF16)
        grad_query[:, cols] = (merge(mm(grad_scores, keys)) * scale).astype(BF16)
    stats_out[...] = jnp.transpose(jnp.concatenate(stats, 0))[: 3 * pairs]
    for copy in fetch:
        copy.wait()


def product_kernel(
    scale,
    pair,
    weights,
    grad_scores,
    attention,
    grad_query,
    own_qkv,
    own_grad,
    latent,
    w_out,
    w_qkv,
    mesh_out_hbm,
    grad_normed,
    grad_key,
    grad_value,
    mesh_out,
    sems,
):
    m, channels = latent.shape
    mesh_out[...] = (latent[...].astype(F32) + mm(attention[...], w_out[...])).astype(BF16)
    out = pltpu.make_async_copy(mesh_out, mesh_out_hbm, sems.at[0])
    out.start()
    for p in range(channels // pair):
        cols = slice(p * pair, (p + 1) * pair)
        grad_key[:, cols] = mm_tn(grad_scores[p], halves(own_qkv[:, cols], scale))
        grad_value[:, cols] = mm_tn(weights[p], halves(own_grad[:, cols]))
    grad_normed[...] = mm_nt(grad_query[...], w_qkv[:, :channels])
    out.wait()


def finish_kernel(
    pair,
    chip_stats,
    off_stats,
    bias,
    near_q,
    chip_grad,
    off_grad,
    own_qkv,
    grad_key,
    grad_value,
    grad_normed,
    w_qkv,
    normal,
    inv_std,
    cot,
    grad_out,
):
    m, channels = normal.shape
    pairs = channels // pair

    stats = []
    for h in range(2):
        lanes = slice(h * m, (h + 1) * m)
        stats.append(jnp.concatenate([chip_stats[:, lanes], off_stats[:, lanes]], 1))

    def multiply(p):
        cols = slice(p * pair, (p + 1) * pair)
        key2 = halves(own_qkv[:, channels + p * pair : channels + (p + 1) * pair])
        value2 = halves(own_qkv[:, 2 * channels + p * pair : 2 * channels + (p + 1) * pair])
        query = near_q[:, cols]
        grad = jnp.concatenate([chip_grad[:, cols], off_grad[:, cols]], 0)
        return query, grad, mm_nt(key2, query), mm_nt(value2, grad)

    turned = None
    group = 2
    gks, gvs = [], []
    ahead = multiply(0)
    for p in range(pairs):
        cols = slice(p * pair, (p + 1) * pair)
        query, grad, scores, grad_prob = ahead
        if p + 1 < pairs:
            ahead = multiply(p + 1)
        weights, grad_scores = [], []
        for at in range(0, 2 * m, CHUNK):
            part = slice(at, at + CHUNK)
            place = slice(at % m, at % m + CHUNK)
            top, inv_sum, delta = (
                stats[at // m][k * pairs + p : k * pairs + p + 1] for k in range(3)
            )
            probs = jnp.exp(scores[part] + bias[place] - top) * inv_sum
            weights.append(probs.astype(BF16))
            grad_scores.append((probs * (grad_prob[part] - delta)).astype(BF16))
        gk = grad_key[:, cols] + merge(mm(jnp.concatenate(grad_scores, 0), query))
        gv = grad_value[:, cols] + merge(mm(jnp.concatenate(weights, 0), grad))
        gks.append(gk.astype(BF16))
        gvs.append(gv.astype(BF16))
        if len(gks) == group:
            at = channels + (p + 1 - group) * pair
            width = group * pair
            for blocks, start in ((gks, at), (gvs, at + channels)):
                piece = mm_nt(w_qkv[:, start : start + width], jnp.concatenate(blocks, 1))
                turned = piece if turned is None else turned + piece
            gks, gvs = [], []
    total = grad_normed[...] + jnp.transpose(turned)
    centred = (
        total
        - jnp.mean(total, -1, keepdims=True)
        - normal[...] * jnp.mean(total * normal[...], -1, keepdims=True)
    )
    grad_out[...] = (cot[...].astype(F32) + inv_std[:, :1] * centred).astype(BF16)


def body(
    grid_in,
    mesh_in,
    own_src,
    own_dst,
    side_src,
    side_dst,
    side_count,
    far_src,
    far_dst,
    far_count,
    window,
    cotangent,
    w_edge,
    w_qkv,
    w_out,
):
    devices = lax.axis_size("node")
    grid_rows, channels = grid_in.shape
    m = mesh_in.shape[0]
    far_slots = far_src.shape[0]
    far_depth = far_slots // devices
    head_dim = channels // HEADS
    pair = 2 * head_dim
    pairs = channels // pair
    scale = head_dim ** (-0.5)
    meta_rows = side_src.shape[0] // (2 * LANES)

    side_src, side_dst = side_src.reshape(-1, LANES), side_dst.reshape(-1, LANES)
    own_src, own_dst = own_src.reshape(-1, LANES), own_dst.reshape(-1, LANES)
    far_src, far_dst = far_src.reshape(1, -1), far_dst.reshape(1, -1)
    side_count, far_count = side_count.reshape(1, -1), far_count.reshape(1, -1)
    message = ((BAND + meta_rows, channels), BF16)
    far_block = (2 * far_slots, channels // 2 + LANES)
    far_message, chip_message, off_message, w_edge = call(
        pack_kernel,
        [(far_block, BF16), message, message, (w_edge.shape, BF16)],
        [grid_in, window, side_src, side_dst, side_count, far_src, far_dst, far_count, w_edge],
        hbm=range(9),
        hbm_outs=range(3),
        scratch=like(grid_in, window, side_src, side_dst, side_count, far_src, far_dst, far_count)
        + [
            pltpu.VMEM(far_block, BF16),
            pltpu.VMEM((2, meta_rows, channels), BF16),
            dma(9),
            dma(5),
        ],
        name="pack",
    )
    from_chip, from_off = exchange(chip_message, off_message, "node")
    got_far = lax.all_to_all(
        far_message.reshape(devices, 2 * far_depth, far_block[1]),
        "node",
        split_axis=0,
        concat_axis=0,
        tiled=True,
    ).reshape(far_block)

    rows = ((m, channels), BF16)
    partial, own_grad = call(
        own_kernel,
        [((m, channels), F32), rows],
        [grid_in, mesh_in, own_src, own_dst, cotangent, w_out, w_edge],
        hbm=range(6),
        hbm_outs=(1,),
        scratch=like(grid_in, mesh_in, own_src, own_dst, cotangent, w_out, cotangent) + [dma(7)],
        name="own",
    )
    (partial,) = call(
        functools.partial(side_kernel, meta_rows),
        [((m, channels), F32)],
        [from_chip, from_off, w_edge, partial],
        name="side",
        flops=8 * 10**9,
    )
    latent, normed, normal, inv_std = call(
        functools.partial(latent_kernel, far_depth),
        [rows, rows, ((m, channels), F32), ((m, LANES), F32)],
        [got_far, partial],
        name="latent",
    )
    chip_normed, off_normed = exchange(normed, normed, "node")
    own_block = ((pairs, 2 * m, m), F32)
    own_qkv, w_qkv, own_grad, own_scores, own_products, bias, near_bias = call(
        functools.partial(project_kernel, scale, pair, meta_rows),
        [((m, 3 * channels), BF16), (w_qkv.shape, BF16), rows, own_block, own_block]
        + [((m, 3 * m), F32), ((m, 2 * m), F32)],
        [normed, from_chip, from_off, window, own_grad, w_qkv],
        hbm=(3, 4, 5),
        scratch=like(window) + [dma(3 * PIECES + 2)],
        name="project",
    )
    chip_grad, off_grad = exchange(own_grad, own_grad, "node")
    probs = ((pairs, 2 * m, m), BF16)
    stats, attention, grad_query, weights, grad_scores, near_q, w_out, cotangent = call(
        functools.partial(attend_kernel, scale, pair),
        [
            ((3 * pairs, 2 * m), F32),
            rows,
            rows,
            probs,
            probs,
            ((2 * m, channels), BF16),
            (w_out.shape, BF16),
            rows,
        ],
        [chip_normed, off_normed, w_qkv, own_qkv, own_grad, own_scores, own_products]
        + [bias, w_out, cotangent],
        hbm=(8, 9),
        scratch=[dma(2)],
        name="attend",
    )
    chip_stats, off_stats = exchange(stats, stats, "node")
    mesh_out, grad_normed, grad_key, grad_value = call(
        functools.partial(product_kernel, scale, pair),
        [
            rows,
            ((m, channels), F32),
            ((m, channels), F32),
            ((m, channels), F32),
        ],
        [
            weights,
            grad_scores,
            attention,
            grad_query,
            own_qkv,
            own_grad,
            latent,
            w_out,
            w_qkv,
        ],
        hbm_outs=(0,),
        scratch=[pltpu.VMEM((m, channels), BF16), dma(1)],
        name="product",
    )
    (mesh_grad,) = call(
        functools.partial(finish_kernel, pair),
        [rows],
        [
            chip_stats,
            off_stats,
            near_bias,
            near_q,
            chip_grad,
            off_grad,
            own_qkv,
            grad_key,
            grad_value,
            grad_normed,
            w_qkv,
            normal,
            inv_std,
            cotangent,
        ],
        name="finish",
    )
    return (mesh_out, mesh_grad)


def solution(mesh):
    rows = P(("groups", "node"), None)
    flat = P(("groups", "node"))
    placed = (rows, rows) + (flat,) * 8 + (P(None, ("groups", "node")), rows, P(), P(), P())
    return jax.shard_map(
        body, mesh=mesh, in_specs=placed, out_specs=(rows, rows), check_vma=False
    )
```

```python
import functools

import jax
import jax.numpy as jnp
from jax import lax
from jax.experimental import pallas as pl
from jax.experimental.pallas import tpu as pltpu
from jax.sharding import PartitionSpec as P

HEADS = 16
BAND = 128
LANES = 128
F32 = jnp.float32
BF16 = jnp.bfloat16
I32 = jnp.int32
VMEM_LIMIT = 28 * 2**20
PIECES = 2
CHUNK = 64


def mm(a, b):
    return lax.dot_general(a, b, (((1,), (0,)), ((), ())), preferred_element_type=F32)


def mm_nt(a, b):
    return lax.dot_general(a, b, (((1,), (1,)), ((), ())), preferred_element_type=F32)


def mm_tn(a, b):
    return lax.dot_general(a, b, (((0,), (0,)), ((), ())), preferred_element_type=F32)


def iota(shape, dim):
    return lax.broadcasted_iota(I32, shape, dim)


def call(kernel, outs, args, hbm=(), hbm_outs=(), scratch=(), name=None, flops=None):
    args = [
        pltpu.with_memory_space_constraint(a, pltpu.HBM) if i in hbm else a
        for i, a in enumerate(args)
    ]

    def specs(count, far):
        return [
            pl.BlockSpec(memory_space=pltpu.HBM if i in far else pltpu.VMEM) for i in range(count)
        ]

    return pl.pallas_call(
        kernel,
        out_shape=[
            (pltpu.HBM if i in hbm_outs else jax.ShapeDtypeStruct)(shape, dtype)
            for i, (shape, dtype) in enumerate(outs)
        ],
        in_specs=specs(len(args), hbm),
        out_specs=specs(len(outs), hbm_outs),
        scratch_shapes=list(scratch),
        compiler_params=pltpu.CompilerParams(vmem_limit_bytes=VMEM_LIMIT),
        cost_estimate=flops and pl.CostEstimate(flops=flops, transcendentals=0, bytes_accessed=0),
        name=name,
    )(*args)


def dma(count):
    return pltpu.SemaphoreType.DMA((count,))


def start_all(pairs, sems):
    copies = [pltpu.make_async_copy(src, dst, sems.at[i]) for i, (src, dst) in enumerate(pairs)]
    for copy in copies:
        copy.start()
    return copies


def like(*arrays):
    return [pltpu.VMEM(a.shape, a.dtype) for a in arrays]


def exchange(chip_message, off_message, axis):
    n = lax.axis_size(axis)
    from_off = lax.ppermute(
        off_message, axis, [p for i in range(1, n - 1, 2) for p in ((i, i + 1), (i + 1, i))]
    )
    from_chip = lax.ppermute(
        chip_message, axis, [p for i in range(0, n, 2) for p in ((i, i + 1), (i + 1, i))]
    )
    return from_chip, from_off


def is_odd():
    return lax.axis_index("node") % 2


def everywhere():
    return lax.axis_index("node") >= 0


def gelu(projected):
    x = projected.astype(BF16).astype(F32)
    inner = (2.0 / jnp.pi) ** 0.5 * (x + 0.044715 * (x * x * x))
    return (0.5 * x * (1.0 + jnp.tanh(inner))).astype(BF16)


def onehot_rows(index_rows, count):
    parts = [
        jnp.where(iota((count, row.shape[1]), 0) == row, 1.0, 0.0).astype(BF16)
        for row in index_rows
    ]
    return parts[0] if len(parts) == 1 else jnp.concatenate(parts, 1)


def norm_stats(latent):
    values = latent.astype(F32)
    row_mean = jnp.mean(values, -1, keepdims=True)
    centred = values - row_mean
    variance = jnp.mean(centred * centred, -1, keepdims=True)
    inv_std = lax.rsqrt(variance + 1e-05)
    return centred * inv_std, inv_std


def pack_kernel(
    grid_hbm,
    window_hbm,
    side_src_hbm,
    side_dst_hbm,
    side_count_hbm,
    far_src_hbm,
    far_dst_hbm,
    far_count_hbm,
    w_edge_hbm,
    far_out,
    chip_out,
    off_out,
    w_edge,
    grid,
    window,
    side_src,
    side_dst,
    side_count,
    far_src,
    far_dst,
    far_count,
    far,
    meta,
    sems,
    out_sems,
):
    grid_rows, channels = grid.shape
    mesh_rows = window.shape[1]
    slots = far_src.shape[1]
    devices = far_count.shape[1]
    depth = slots // devices
    first = grid_rows - BAND
    count = side_src.shape[0] // 2
    copies = start_all(
        [
            (side_src_hbm, side_src),
            (side_dst_hbm, side_dst),
            (side_count_hbm, side_count),
            (window_hbm, window),
            (grid_hbm, grid),
            (far_src_hbm, far_src),
            (far_dst_hbm, far_dst),
            (far_count_hbm, far_count),
            (w_edge_hbm, w_edge),
        ],
        sems,
    )
    for copy in copies[:4]:
        copy.wait()
    for k in range(2):
        rank = iota((count, LANES), 0) * LANES + iota((count, LANES), 1)
        src = side_src[k * count : (k + 1) * count] - k * first
        live = rank < side_count[:, k : k + 1]
        dst = jnp.where(live, side_dst[k * count : (k + 1) * count], mesh_rows)
        reach = jnp.concatenate([window[...], jnp.zeros((count - 2, mesh_rows), I32)], 0)
        blank = jnp.zeros((count, channels - 2 * LANES - mesh_rows), I32)
        meta[k] = jnp.concatenate([src, dst, reach, blank], 1).astype(F32).astype(BF16)
    copies[4].wait()
    odd = is_odd()
    outs = start_all(
        [
            pair
            for k, out in ((1 - odd, chip_out), (odd, off_out))
            for pair in (
                (grid.at[pl.ds(pl.multiple_of(k * first, BAND), BAND)], out.at[pl.ds(0, BAND)]),
                (meta.at[k], out.at[pl.ds(BAND, count)]),
            )
        ],
        out_sems,
    )
    for copy in copies[5:8]:
        copy.wait()
    slot = iota((1, slots), 1)
    receiver = jnp.where(iota((devices, slots), 0) == iota((devices, slots), 1) // depth, 1.0, 0.0)
    live = mm(far_count[...].astype(F32).astype(BF16), receiver.astype(BF16))
    target = jnp.where((slot % depth).astype(F32) < live, far_dst[...].astype(F32), 1.0 * mesh_rows)
    row = iota((2 * slots, slots), 0)
    mine = slot == row // (2 * depth) * depth + row % depth
    source = jnp.sum(jnp.where(mine, far_src[...].astype(F32), 0.0), 1, keepdims=True)
    column = jnp.sum(jnp.where(mine, target, 0.0), 1, keepdims=True)
    pick = jnp.where(iota((2 * slots, grid_rows), 1).astype(F32) == source, 1.0, 0.0).astype(BF16)
    rows = mm(pick, grid[...]).astype(BF16)
    copies[8].wait()
    rows = gelu(mm(rows, w_edge[...]))
    half = channels // 2
    is_first = iota((2 * slots, half), 0) % (2 * depth) < depth
    far[:, :half] = jnp.where(is_first, rows[:, :half], rows[:, half:])
    far[:, half:] = jnp.broadcast_to(column, (2 * slots, LANES)).astype(BF16)
    last = pltpu.make_async_copy(far, far_out, out_sems.at[4])
    last.start()
    for copy in outs + [last]:
        copy.wait()


def own_kernel(
    grid_hbm,
    mesh_in_hbm,
    own_src_hbm,
    own_dst_hbm,
    cot_hbm,
    w_out_hbm,
    w_edge,
    partial_out,
    grad_hbm,
    grid,
    mesh_in,
    own_src,
    own_dst,
    cot,
    w_out,
    grad,
    sems,
):
    grid_rows = grid.shape[0]
    mesh_rows = mesh_in.shape[0]
    copies = start_all(
        [
            (own_src_hbm, own_src),
            (own_dst_hbm, own_dst),
            (cot_hbm, cot),
            (w_out_hbm, w_out),
            (grid_hbm, grid),
            (mesh_in_hbm, mesh_in),
        ],
        sems,
    )
    for copy in copies[:2]:
        copy.wait()
    rows = own_src.shape[0]
    src = onehot_rows([own_src[r : r + 1] for r in range(rows)], grid_rows)
    dst = onehot_rows([own_dst[r : r + 1] for r in range(rows)], mesh_rows)
    counts = mm_nt(dst, src).astype(BF16)
    for copy in copies[2:4]:
        copy.wait()
    grad[...] = mm_nt(cot[...], w_out[...]).astype(BF16)
    out = pltpu.make_async_copy(grad, grad_hbm, sems.at[6])
    out.start()
    for copy in copies[4:]:
        copy.wait()
    active = gelu(mm(grid[...], w_edge[...]))
    partial_out[...] = mesh_in[...].astype(F32) + mm(counts, active)
    out.wait()


def meta_of(message, count):
    return message[BAND : BAND + count].astype(F32).astype(I32)


def side_kernel(count, chip, off, w_edge, partial, partial_out):
    mesh_rows = partial.shape[0]
    uppers, lowers = [], []
    for side in (chip, off):
        meta = meta_of(side, count)
        src = onehot_rows([meta[r : r + 1, :LANES] for r in range(count)], BAND)
        dst = onehot_rows([meta[r : r + 1, LANES : 2 * LANES] for r in range(count)], mesh_rows)
        counts = mm_nt(dst, src)
        upper = counts.astype(BF16)
        uppers.append(upper)
        lowers.append((counts - upper.astype(F32)).astype(BF16))
    active = gelu(mm(jnp.concatenate([chip[:BAND], off[:BAND]], 0), w_edge[...]))
    landing = jnp.concatenate(uppers + lowers, 1)
    partial_out[...] = partial[...] + mm(landing, jnp.concatenate([active, active], 0))


def latent_kernel(depth, far, partial, latent_out, normed_out, normal_out, inv_std_out):
    mesh_rows, channels = partial.shape
    slots = far.shape[0]
    half = channels // 2
    first = far[:, :half]
    second = pltpu.roll(first.astype(F32), slots - depth, 0).astype(BF16)
    target = jnp.transpose(far[:, half:].astype(F32))
    if mesh_rows != LANES:
        target = jnp.broadcast_to(target[:1], (mesh_rows, slots))
    is_row = iota((mesh_rows, slots), 1) % (2 * depth) < depth
    hit = (target == iota((mesh_rows, slots), 0).astype(F32)) & is_row
    landing = jnp.where(hit, 1.0, 0.0).astype(BF16)
    total = partial[...] + mm(landing, jnp.concatenate([first, second], 1))
    latent = total.astype(BF16)
    latent_out[...] = latent
    normal, inv_std = norm_stats(latent)
    normed_out[...] = normal.astype(BF16)
    normal_out[...] = normal
    inv_std_out[...] = jnp.broadcast_to(inv_std, inv_std_out.shape)


def halves(rows, scale=None):
    first = iota(rows.shape, 1) < rows.shape[1] // 2
    if scale is not None:
        rows = rows * jnp.asarray(scale, rows.dtype)
    zero = jnp.zeros_like(rows)
    return jnp.concatenate([jnp.where(first, rows, zero), jnp.where(first, zero, rows)], 0)


def merge(stacked):
    m = stacked.shape[0] // 2
    first = iota((m, stacked.shape[1]), 1) < stacked.shape[1] // 2
    return jnp.where(first, stacked[:m], stacked[m:])


def near_places(m):
    odd = is_odd()
    return (1 - odd) * 2 * m, odd * 2 * m


def project_kernel(
    scale,
    pair,
    count,
    normed,
    chip_first,
    off_first,
    window_hbm,
    grad_hbm,
    w_qkv_hbm,
    qkv_out,
    w_qkv,
    grad_out,
    scores_out,
    products_out,
    bias_out,
    near_bias_out,
    window,
    sems,
):
    m, channels = normed.shape
    width = channels // PIECES
    starts = [part * channels + c * width for c in range(PIECES) for part in range(3)]
    copies = start_all(
        [(grad_hbm, grad_out)]
        + [(w_qkv_hbm.at[:, pl.ds(at, width)], w_qkv.at[:, pl.ds(at, width)]) for at in starts]
        + [(window_hbm, window)],
        sems,
    )
    def masks():
        chip_at, off_at = near_places(m)
        reach = [meta_of(side, count)[:8, 2 * LANES : 2 * LANES + m] for side in (chip_first, off_first)]
        reach = jnp.concatenate(reach, 1)
        key_at = iota((m, 2 * m), 0) + m
        lane = iota((m, 2 * m), 1)
        query_at = jnp.where(lane < m, lane + chip_at, lane - m + off_at)
        keep = (key_at >= query_at - reach[0:1, :]) & (key_at <= query_at + reach[1:2, :])
        near_bias_out[...] = jnp.where(keep, 0.0, -jnp.inf).astype(F32)
        copies[-1].wait()
        me = lax.axis_index("node")
        row = iota((3 * m, m), 0)
        key_at = jnp.where(row < m, row + chip_at, jnp.where(row < 2 * m, row - m + off_at, row - m))
        query_at = iota((3 * m, m), 1) + m
        at_end = (me == 0) | (me == lax.axis_size("node") - 1)
        missing = (row >= m) & (row < 2 * m) & at_end
        keep = (key_at >= query_at - window[0:1, :]) & (key_at <= query_at + window[1:2, :])
        bias = jnp.where(keep & jnp.logical_not(missing), 0.0, -jnp.inf).astype(F32)
        bias_out[...] = jnp.transpose(bias)

    for i, at in enumerate(starts):
        copies[1 + i].wait()
        cols = slice(at, at + width)
        qkv_out[:, cols] = mm(normed[...], w_qkv[:, cols]).astype(BF16)
        if i == 0:
            masks()
        if i % 3 < 2:
            continue
        if i == 2:
            copies[0].wait()
        for p in range(i // 3 * width // pair, (i // 3 + 1) * width // pair):
            q, k, v = (
                slice(part * channels + p * pair, part * channels + (p + 1) * pair)
                for part in range(3)
            )
            scores_out[p] = mm_nt(halves(qkv_out[:, q], scale), qkv_out[:, k])
            products_out[p] = mm_nt(halves(grad_out[:, q]), qkv_out[:, v])


def attend_kernel(
    scale,
    pair,
    chip_normed,
    off_normed,
    w_qkv,
    own_qkv,
    own_grad,
    own_scores,
    own_products,
    bias,
    w_out_hbm,
    cot_hbm,
    stats_out,
    attention,
    grad_query,
    weights_out,
    scores_out,
    near_q,
    w_out,
    cot,
    sems,
):
    fetch = start_all([(w_out_hbm, w_out), (cot_hbm, cot)], sems)
    m, channels = chip_normed.shape
    pairs = channels // pair

    @pl.when(everywhere())
    def _():
        near = jnp.concatenate([chip_normed[...], off_normed[...]], 0)

        def bring(group):
            cols = slice(group * 2 * pair, (group + 1) * 2 * pair)
            near_q[:, cols] = mm(near, w_qkv[:, cols]).astype(BF16) * jnp.asarray(scale, BF16)
            blocks = []
            for part in range(1, 3):
                at = part * channels + group * 2 * pair
                blocks.append(mm(near, w_qkv[:, at : at + 2 * pair]).astype(BF16))
            return blocks

        brought = {0: bring(0)}
        lane = iota((CHUNK, LANES), 1)
        stats = [jnp.zeros((CHUNK, LANES), F32) for _ in range(2 * m // CHUNK)]

        def near_of(p):
            return [b[:, p % 2 * pair : (p % 2 + 1) * pair] for b in brought[p // 2]]

        def multiply(p):
            cols = slice(p * pair, (p + 1) * pair)
            keys, values = near_of(p)
            return (
                mm_nt(halves(own_qkv[:, cols], scale), keys),
                mm_nt(halves(own_grad[:, cols]), values),
            )

        ahead = multiply(0)
        for p in range(pairs):
            scores, grad_prob = ahead
            if p + 1 < pairs:
                if p % 2 == 0 and p + 2 < pairs:
                    brought[p // 2 + 1] = bring(p // 2 + 1)
                ahead = multiply(p + 1)
            weights, grad_scores = [], []
            for at in range(0, 2 * m, CHUNK):
                part = slice(at, at + CHUNK)
                place = slice(at % m, at % m + CHUNK)
                raw = jnp.concatenate([scores[part], own_scores[p, part]], 1) + bias[place]
                top = jnp.max(raw, 1, keepdims=True)
                shifted = jnp.exp(raw - top)
                inv_sum = 1.0 / jnp.sum(shifted, 1, keepdims=True)
                probs = shifted * inv_sum
                product = jnp.concatenate([grad_prob[part], own_products[p, part]], 1)
                delta = jnp.sum(probs * product, 1, keepdims=True)
                weights.append(probs.astype(BF16))
                grad_scores.append((probs * (product - delta)).astype(BF16))
                for k, column in enumerate((top, inv_sum, delta)):
                    stats[at // CHUNK] = jnp.where(lane == k * pairs + p, column, stats[at // CHUNK])
            weights = jnp.concatenate(weights, 0)
            grad_scores = jnp.concatenate(grad_scores, 0)
            weights_out[p] = weights[:, 2 * m :]
            scores_out[p] = grad_scores[:, 2 * m :]
            keys, values = (
                jnp.concatenate([block, own_qkv[:, at + p * pair : at + (p + 1) * pair]], 0)
                for block, at in zip(near_of(p), (channels, 2 * channels))
            )
            cols = slice(p * pair, (p + 1) * pair)
            attention[:, cols] = merge(mm(weights, values)).astype(BF16)
            grad_query[:, cols] = (merge(mm(grad_scores, keys)) * scale).astype(BF16)
        stats_out[...] = jnp.transpose(jnp.concatenate(stats, 0))[: 3 * pairs]

    for copy in fetch:
        copy.wait()


def product_kernel(
    scale,
    pair,
    weights,
    grad_scores,
    attention,
    grad_query,
    own_qkv,
    own_grad,
    latent,
    w_out,
    w_qkv,
    mesh_out_hbm,
    grad_normed,
    grad_key,
    grad_value,
    mesh_out,
    sems,
):
    m, channels = latent.shape
    mesh_out[...] = (latent[...].astype(F32) + mm(attention[...], w_out[...])).astype(BF16)
    out = pltpu.make_async_copy(mesh_out, mesh_out_hbm, sems.at[0])
    out.start()

    @pl.when(everywhere())
    def _():
        for p in range(channels // pair):
            cols = slice(p * pair, (p + 1) * pair)
            grad_key[:, cols] = mm_tn(grad_scores[p], halves(own_qkv[:, cols], scale))
            grad_value[:, cols] = mm_tn(weights[p], halves(own_grad[:, cols]))
        grad_normed[...] = mm_nt(grad_query[...], w_qkv[:, :channels])

    out.wait()


def finish_kernel(
    pair,
    chip_stats,
    off_stats,
    bias,
    near_q,
    chip_grad,
    off_grad,
    own_qkv,
    grad_key,
    grad_value,
    grad_normed,
    w_qkv,
    normal,
    inv_std,
    cot,
    grad_out,
):
    m, channels = normal.shape
    pairs = channels // pair

    stats = []
    for h in range(2):
        lanes = slice(h * m, (h + 1) * m)
        stats.append(jnp.concatenate([chip_stats[:, lanes], off_stats[:, lanes]], 1))

    def multiply(p):
        cols = slice(p * pair, (p + 1) * pair)
        key2 = halves(own_qkv[:, channels + p * pair : channels + (p + 1) * pair])
        value2 = halves(own_qkv[:, 2 * channels + p * pair : 2 * channels + (p + 1) * pair])
        query = near_q[:, cols]
        grad = jnp.concatenate([chip_grad[:, cols], off_grad[:, cols]], 0)
        return query, grad, mm_nt(key2, query), mm_nt(value2, grad)

    total = grad_normed[...]
    group = 2
    gks, gvs = [], []
    ahead = multiply(0)
    for p in range(pairs):
        cols = slice(p * pair, (p + 1) * pair)
        query, grad, scores, grad_prob = ahead
        if p + 1 < pairs:
            ahead = multiply(p + 1)
        weights, grad_scores = [], []
        for at in range(0, 2 * m, CHUNK):
            part = slice(at, at + CHUNK)
            place = slice(at % m, at % m + CHUNK)
            top, inv_sum, delta = (
                stats[at // m][k * pairs + p : k * pairs + p + 1] for k in range(3)
            )
            probs = jnp.exp(scores[part] + bias[place] - top) * inv_sum
            weights.append(probs.astype(BF16))
            grad_scores.append((probs * (grad_prob[part] - delta)).astype(BF16))
        gk = grad_key[:, cols] + merge(mm(jnp.concatenate(grad_scores, 0), query))
        gv = grad_value[:, cols] + merge(mm(jnp.concatenate(weights, 0), grad))
        gks.append(gk.astype(BF16))
        gvs.append(gv.astype(BF16))
        if len(gks) == group:
            at = channels + (p + 1 - group) * pair
            width = group * pair
            for blocks, start in ((gks, at), (gvs, at + channels)):
                total = total + mm_nt(
                    jnp.concatenate(blocks, 1), w_qkv[:, start : start + width]
                )
            gks, gvs = [], []
    centred = (
        total
        - jnp.mean(total, -1, keepdims=True)
        - normal[...] * jnp.mean(total * normal[...], -1, keepdims=True)
    )
    grad_out[...] = (cot[...].astype(F32) + inv_std[:, :1] * centred).astype(BF16)


def body(
    grid_in,
    mesh_in,
    own_src,
    own_dst,
    side_src,
    side_dst,
    side_count,
    far_src,
    far_dst,
    far_count,
    window,
    cotangent,
    w_edge,
    w_qkv,
    w_out,
):
    devices = lax.axis_size("node")
    grid_rows, channels = grid_in.shape
    m = mesh_in.shape[0]
    far_slots = far_src.shape[0]
    far_depth = far_slots // devices
    head_dim = channels // HEADS
    pair = 2 * head_dim
    pairs = channels // pair
    scale = head_dim ** (-0.5)
    meta_rows = side_src.shape[0] // (2 * LANES)

    side_src, side_dst = side_src.reshape(-1, LANES), side_dst.reshape(-1, LANES)
    own_src, own_dst = own_src.reshape(-1, LANES), own_dst.reshape(-1, LANES)
    far_src, far_dst = far_src.reshape(1, -1), far_dst.reshape(1, -1)
    side_count, far_count = side_count.reshape(1, -1), far_count.reshape(1, -1)
    message = ((BAND + meta_rows, channels), BF16)
    far_block = (2 * far_slots, channels // 2 + LANES)
    far_message, chip_message, off_message, w_edge = call(
        pack_kernel,
        [(far_block, BF16), message, message, (w_edge.shape, BF16)],
        [grid_in, window, side_src, side_dst, side_count, far_src, far_dst, far_count, w_edge],
        hbm=range(9),
        hbm_outs=range(3),
        scratch=like(grid_in, window, side_src, side_dst, side_count, far_src, far_dst, far_count)
        + [
            pltpu.VMEM(far_block, BF16),
            pltpu.VMEM((2, meta_rows, channels), BF16),
            dma(9),
            dma(5),
        ],
        name="pack",
    )
    from_chip, from_off = exchange(chip_message, off_message, "node")
    got_far = lax.all_to_all(
        far_message.reshape(devices, 2 * far_depth, far_block[1]),
        "node",
        split_axis=0,
        concat_axis=0,
        tiled=True,
    ).reshape(far_block)

    rows = ((m, channels), BF16)
    partial, own_grad = call(
        own_kernel,
        [((m, channels), F32), rows],
        [grid_in, mesh_in, own_src, own_dst, cotangent, w_out, w_edge],
        hbm=range(6),
        hbm_outs=(1,),
        scratch=like(grid_in, mesh_in, own_src, own_dst, cotangent, w_out, cotangent) + [dma(7)],
        name="own",
    )
    (partial,) = call(
        functools.partial(side_kernel, meta_rows),
        [((m, channels), F32)],
        [from_chip, from_off, w_edge, partial],
        name="side",
        flops=8 * 10**9,
    )
    latent, normed, normal, inv_std = call(
        functools.partial(latent_kernel, far_depth),
        [rows, rows, ((m, channels), F32), ((m, LANES), F32)],
        [got_far, partial],
        name="latent",
    )
    chip_normed, off_normed = exchange(normed, normed, "node")
    own_block = ((pairs, 2 * m, m), F32)
    own_qkv, w_qkv, own_grad, own_scores, own_products, bias, near_bias = call(
        functools.partial(project_kernel, scale, pair, meta_rows),
        [((m, 3 * channels), BF16), (w_qkv.shape, BF16), rows, own_block, own_block]
        + [((m, 3 * m), F32), ((m, 2 * m), F32)],
        [normed, from_chip, from_off, window, own_grad, w_qkv],
        hbm=(3, 4, 5),
        scratch=like(window) + [dma(3 * PIECES + 2)],
        name="project",
    )
    chip_grad, off_grad = exchange(own_grad, own_grad, "node")
    probs = ((pairs, 2 * m, m), BF16)
    stats, attention, grad_query, weights, grad_scores, near_q, w_out, cotangent = call(
        functools.partial(attend_kernel, scale, pair),
        [
            ((3 * pairs, 2 * m), F32),
            rows,
            rows,
            probs,
            probs,
            ((2 * m, channels), BF16),
            (w_out.shape, BF16),
            rows,
        ],
        [chip_normed, off_normed, w_qkv, own_qkv, own_grad, own_scores, own_products]
        + [bias, w_out, cotangent],
        hbm=(8, 9),
        scratch=[dma(2)],
        name="attend",
    )
    chip_stats, off_stats = exchange(stats, stats, "node")
    mesh_out, grad_normed, grad_key, grad_value = call(
        functools.partial(product_kernel, scale, pair),
        [
            rows,
            ((m, channels), F32),
            ((m, channels), F32),
            ((m, channels), F32),
        ],
        [
            weights,
            grad_scores,
            attention,
            grad_query,
            own_qkv,
            own_grad,
            latent,
            w_out,
            w_qkv,
        ],
        hbm_outs=(0,),
        scratch=[pltpu.VMEM((m, channels), BF16), dma(1)],
        name="product",
    )
    (mesh_grad,) = call(
        functools.partial(finish_kernel, pair),
        [rows],
        [
            chip_stats,
            off_stats,
            near_bias,
            near_q,
            chip_grad,
            off_grad,
            own_qkv,
            grad_key,
            grad_value,
            grad_normed,
            w_qkv,
            normal,
            inv_std,
            cotangent,
        ],
        name="finish",
    )
    return (mesh_out, mesh_grad)


def solution(mesh):
    rows = P(("groups", "node"), None)
    flat = P(("groups", "node"))
    placed = (rows, rows) + (flat,) * 8 + (P(None, ("groups", "node")), rows, P(), P(), P())
    return jax.shard_map(
        body, mesh=mesh, in_specs=placed, out_specs=(rows, rows), check_vma=False
    )
```

```python
import functools

import jax
import jax.numpy as jnp
from jax import lax
from jax.experimental import pallas as pl
from jax.experimental.pallas import tpu as pltpu
from jax.sharding import PartitionSpec as P

HEADS = 16
BAND = 128
LANES = 128
F32 = jnp.float32
BF16 = jnp.bfloat16
I32 = jnp.int32
VMEM_LIMIT = 28 * 2**20
PIECES = 4
CHUNK = 64


def mm(a, b):
    return lax.dot_general(a, b, (((1,), (0,)), ((), ())), preferred_element_type=F32)


def mm_nt(a, b):
    return lax.dot_general(a, b, (((1,), (1,)), ((), ())), preferred_element_type=F32)


def mm_tn(a, b):
    return lax.dot_general(a, b, (((0,), (0,)), ((), ())), preferred_element_type=F32)


def iota(shape, dim):
    return lax.broadcasted_iota(I32, shape, dim)


def call(kernel, outs, args, hbm=(), hbm_outs=(), scratch=(), name=None, flops=None):
    args = [
        pltpu.with_memory_space_constraint(a, pltpu.HBM) if i in hbm else a
        for i, a in enumerate(args)
    ]

    def specs(count, far):
        return [
            pl.BlockSpec(memory_space=pltpu.HBM if i in far else pltpu.VMEM) for i in range(count)
        ]

    return pl.pallas_call(
        kernel,
        out_shape=[
            (pltpu.HBM if i in hbm_outs else jax.ShapeDtypeStruct)(shape, dtype)
            for i, (shape, dtype) in enumerate(outs)
        ],
        in_specs=specs(len(args), hbm),
        out_specs=specs(len(outs), hbm_outs),
        scratch_shapes=list(scratch),
        compiler_params=pltpu.CompilerParams(vmem_limit_bytes=VMEM_LIMIT),
        cost_estimate=flops and pl.CostEstimate(flops=flops, transcendentals=0, bytes_accessed=0),
        name=name,
    )(*args)


def dma(count):
    return pltpu.SemaphoreType.DMA((count,))


def start_all(pairs, sems):
    copies = [pltpu.make_async_copy(src, dst, sems.at[i]) for i, (src, dst) in enumerate(pairs)]
    for copy in copies:
        copy.start()
    return copies


def like(*arrays):
    return [pltpu.VMEM(a.shape, a.dtype) for a in arrays]


def exchange(chip_message, off_message, axis):
    n = lax.axis_size(axis)
    from_off = lax.ppermute(
        off_message, axis, [p for i in range(1, n - 1, 2) for p in ((i, i + 1), (i + 1, i))]
    )
    from_chip = lax.ppermute(
        chip_message, axis, [p for i in range(0, n, 2) for p in ((i, i + 1), (i + 1, i))]
    )
    return from_chip, from_off


def is_odd():
    return lax.axis_index("node") % 2


def everywhere():
    return lax.axis_index("node") >= 0


def gelu(projected):
    x = projected.astype(BF16).astype(F32)
    inner = (2.0 / jnp.pi) ** 0.5 * (x + 0.044715 * (x * x * x))
    return (0.5 * x * (1.0 + jnp.tanh(inner))).astype(BF16)


def onehot_rows(index_rows, count):
    parts = [
        jnp.where(iota((count, row.shape[1]), 0) == row, 1.0, 0.0).astype(BF16)
        for row in index_rows
    ]
    return parts[0] if len(parts) == 1 else jnp.concatenate(parts, 1)


def norm_stats(latent):
    values = latent.astype(F32)
    row_mean = jnp.mean(values, -1, keepdims=True)
    centred = values - row_mean
    variance = jnp.mean(centred * centred, -1, keepdims=True)
    inv_std = lax.rsqrt(variance + 1e-05)
    return centred * inv_std, inv_std


def pack_kernel(
    grid_hbm,
    window_hbm,
    side_src_hbm,
    side_dst_hbm,
    side_count_hbm,
    far_src_hbm,
    far_dst_hbm,
    far_count_hbm,
    w_edge_hbm,
    far_out,
    chip_out,
    off_out,
    w_edge,
    grid,
    window,
    side_src,
    side_dst,
    side_count,
    far_src,
    far_dst,
    far_count,
    far,
    meta,
    sems,
    out_sems,
):
    grid_rows, channels = grid.shape
    mesh_rows = window.shape[1]
    slots = far_src.shape[1]
    devices = far_count.shape[1]
    depth = slots // devices
    first = grid_rows - BAND
    count = side_src.shape[0] // 2
    copies = start_all(
        [
            (side_src_hbm, side_src),
            (side_dst_hbm, side_dst),
            (side_count_hbm, side_count),
            (window_hbm, window),
            (grid_hbm, grid),
            (far_src_hbm, far_src),
            (far_dst_hbm, far_dst),
            (far_count_hbm, far_count),
            (w_edge_hbm, w_edge),
        ],
        sems,
    )
    for copy in copies[:4]:
        copy.wait()
    for k in range(2):
        rank = iota((count, LANES), 0) * LANES + iota((count, LANES), 1)
        src = side_src[k * count : (k + 1) * count] - k * first
        live = rank < side_count[:, k : k + 1]
        dst = jnp.where(live, side_dst[k * count : (k + 1) * count], mesh_rows)
        reach = jnp.concatenate([window[...], jnp.zeros((count - 2, mesh_rows), I32)], 0)
        blank = jnp.zeros((count, channels - 2 * LANES - mesh_rows), I32)
        meta[k] = jnp.concatenate([src, dst, reach, blank], 1).astype(F32).astype(BF16)
    copies[4].wait()
    odd = is_odd()
    outs = start_all(
        [
            pair
            for k, out in ((1 - odd, chip_out), (odd, off_out))
            for pair in (
                (grid.at[pl.ds(pl.multiple_of(k * first, BAND), BAND)], out.at[pl.ds(0, BAND)]),
                (meta.at[k], out.at[pl.ds(BAND, count)]),
            )
        ],
        out_sems,
    )
    for copy in copies[5:8]:
        copy.wait()
    slot = iota((1, slots), 1)
    receiver = jnp.where(iota((devices, slots), 0) == iota((devices, slots), 1) // depth, 1.0, 0.0)
    live = mm(far_count[...].astype(F32).astype(BF16), receiver.astype(BF16))
    target = jnp.where((slot % depth).astype(F32) < live, far_dst[...].astype(F32), 1.0 * mesh_rows)
    row = iota((2 * slots, slots), 0)
    mine = slot == row // (2 * depth) * depth + row % depth
    source = jnp.sum(jnp.where(mine, far_src[...].astype(F32), 0.0), 1, keepdims=True)
    column = jnp.sum(jnp.where(mine, target, 0.0), 1, keepdims=True)
    pick = jnp.where(iota((2 * slots, grid_rows), 1).astype(F32) == source, 1.0, 0.0).astype(BF16)
    rows = mm(pick, grid[...]).astype(BF16)
    copies[8].wait()
    rows = gelu(mm(rows, w_edge[...]))
    half = channels // 2
    is_first = iota((2 * slots, half), 0) % (2 * depth) < depth
    far[:, :half] = jnp.where(is_first, rows[:, :half], rows[:, half:])
    far[:, half:] = jnp.broadcast_to(column, (2 * slots, LANES)).astype(BF16)
    last = pltpu.make_async_copy(far, far_out, out_sems.at[4])
    last.start()
    for copy in outs + [last]:
        copy.wait()


def own_kernel(
    grid_hbm,
    mesh_in_hbm,
    own_src_hbm,
    own_dst_hbm,
    cot_hbm,
    w_out_hbm,
    w_edge,
    partial_out,
    grad_hbm,
    grid,
    mesh_in,
    own_src,
    own_dst,
    cot,
    w_out,
    grad,
    sems,
):
    grid_rows = grid.shape[0]
    mesh_rows = mesh_in.shape[0]
    copies = start_all(
        [
            (own_src_hbm, own_src),
            (own_dst_hbm, own_dst),
            (cot_hbm, cot),
            (w_out_hbm, w_out),
            (grid_hbm, grid),
            (mesh_in_hbm, mesh_in),
        ],
        sems,
    )
    for copy in copies[:2]:
        copy.wait()
    rows = own_src.shape[0]
    src = onehot_rows([own_src[r : r + 1] for r in range(rows)], grid_rows)
    dst = onehot_rows([own_dst[r : r + 1] for r in range(rows)], mesh_rows)
    counts = mm_nt(dst, src).astype(BF16)
    for copy in copies[2:4]:
        copy.wait()
    grad[...] = mm_nt(cot[...], w_out[...]).astype(BF16)
    out = pltpu.make_async_copy(grad, grad_hbm, sems.at[6])
    out.start()
    for copy in copies[4:]:
        copy.wait()
    active = gelu(mm(grid[...], w_edge[...]))
    partial_out[...] = mesh_in[...].astype(F32) + mm(counts, active)
    out.wait()


def meta_of(message, count):
    return message[BAND : BAND + count].astype(F32).astype(I32)


def side_kernel(count, chip, off, w_edge, partial, partial_out):
    mesh_rows = partial.shape[0]
    uppers, lowers = [], []
    for side in (chip, off):
        meta = meta_of(side, count)
        src = onehot_rows([meta[r : r + 1, :LANES] for r in range(count)], BAND)
        dst = onehot_rows([meta[r : r + 1, LANES : 2 * LANES] for r in range(count)], mesh_rows)
        counts = mm_nt(dst, src)
        upper = counts.astype(BF16)
        uppers.append(upper)
        lowers.append((counts - upper.astype(F32)).astype(BF16))
    active = gelu(mm(jnp.concatenate([chip[:BAND], off[:BAND]], 0), w_edge[...]))
    landing = jnp.concatenate(uppers + lowers, 1)
    partial_out[...] = partial[...] + mm(landing, jnp.concatenate([active, active], 0))


def latent_kernel(depth, far, partial, latent_out, normed_out, normal_out, inv_std_out):
    mesh_rows, channels = partial.shape
    slots = far.shape[0]
    half = channels // 2
    first = far[:, :half]
    second = pltpu.roll(first.astype(F32), slots - depth, 0).astype(BF16)
    target = jnp.transpose(far[:, half:].astype(F32))
    if mesh_rows != LANES:
        target = jnp.broadcast_to(target[:1], (mesh_rows, slots))
    is_row = iota((mesh_rows, slots), 1) % (2 * depth) < depth
    hit = (target == iota((mesh_rows, slots), 0).astype(F32)) & is_row
    landing = jnp.where(hit, 1.0, 0.0).astype(BF16)
    total = partial[...] + mm(landing, jnp.concatenate([first, second], 1))
    latent = total.astype(BF16)
    latent_out[...] = latent
    normal, inv_std = norm_stats(latent)
    normed_out[...] = normal.astype(BF16)
    normal_out[...] = normal
    inv_std_out[...] = jnp.broadcast_to(inv_std, inv_std_out.shape)


def halves(rows, scale=None):
    first = iota(rows.shape, 1) < rows.shape[1] // 2
    if scale is not None:
        rows = rows * jnp.asarray(scale, rows.dtype)
    zero = jnp.zeros_like(rows)
    return jnp.concatenate([jnp.where(first, rows, zero), jnp.where(first, zero, rows)], 0)


def merge(stacked):
    m = stacked.shape[0] // 2
    first = iota((m, stacked.shape[1]), 1) < stacked.shape[1] // 2
    return jnp.where(first, stacked[:m], stacked[m:])


def near_places(m):
    odd = is_odd()
    return (1 - odd) * 2 * m, odd * 2 * m


def project_kernel(
    scale,
    pair,
    count,
    normed,
    chip_first,
    off_first,
    window_hbm,
    grad_hbm,
    w_qkv_hbm,
    qkv_out,
    w_qkv,
    grad_out,
    scores_out,
    products_out,
    bias_out,
    near_bias_out,
    window,
    sems,
):
    m, channels = normed.shape
    width = channels // PIECES
    starts = [part * channels + c * width for c in range(PIECES) for part in range(3)]
    copies = start_all(
        [(window_hbm, window), (grad_hbm, grad_out)]
        + [(w_qkv_hbm.at[:, pl.ds(at, width)], w_qkv.at[:, pl.ds(at, width)]) for at in starts],
        sems,
    )
    copies[0].wait()
    def masks():
        chip_at, off_at = near_places(m)
        reach = [meta_of(side, count)[:8, 2 * LANES : 2 * LANES + m] for side in (chip_first, off_first)]
        reach = jnp.concatenate(reach, 1)
        key_at = iota((m, 2 * m), 0) + m
        lane = iota((m, 2 * m), 1)
        query_at = jnp.where(lane < m, lane + chip_at, lane - m + off_at)
        keep = (key_at >= query_at - reach[0:1, :]) & (key_at <= query_at + reach[1:2, :])
        near_bias_out[...] = jnp.where(keep, 0.0, -jnp.inf).astype(F32)
        me = lax.axis_index("node")
        row = iota((3 * m, m), 0)
        key_at = jnp.where(row < m, row + chip_at, jnp.where(row < 2 * m, row - m + off_at, row - m))
        query_at = iota((3 * m, m), 1) + m
        at_end = (me == 0) | (me == lax.axis_size("node") - 1)
        missing = (row >= m) & (row < 2 * m) & at_end
        keep = (key_at >= query_at - window[0:1, :]) & (key_at <= query_at + window[1:2, :])
        bias = jnp.where(keep & jnp.logical_not(missing), 0.0, -jnp.inf).astype(F32)
        bias_out[...] = jnp.transpose(bias)

    masks()
    copies[1].wait()
    for i, at in enumerate(starts):
        copies[2 + i].wait()
        cols = slice(at, at + width)
        qkv_out[:, cols] = mm(normed[...], w_qkv[:, cols]).astype(BF16)
        for p in range(i // 3 * width // pair, (i // 3 + 1) * width // pair):
            q, k, v = (
                slice(part * channels + p * pair, part * channels + (p + 1) * pair)
                for part in range(3)
            )
            if i % 3 == 1:
                scores_out[p] = mm_nt(halves(qkv_out[:, q], scale), qkv_out[:, k])
            if i % 3 == 2:
                products_out[p] = mm_nt(halves(grad_out[:, q]), qkv_out[:, v])


def attend_kernel(
    scale,
    pair,
    chip_normed,
    off_normed,
    w_qkv,
    own_qkv,
    own_grad,
    own_scores,
    own_products,
    bias,
    w_out_hbm,
    cot_hbm,
    stats_out,
    attention,
    grad_query,
    weights_out,
    scores_out,
    near_q,
    w_out,
    cot,
    sems,
):
    fetch = start_all([(w_out_hbm, w_out), (cot_hbm, cot)], sems)
    m, channels = chip_normed.shape
    pairs = channels // pair

    @pl.when(everywhere())
    def _():
        near = jnp.concatenate([chip_normed[...], off_normed[...]], 0)

        def bring(group):
            cols = slice(group * 2 * pair, (group + 1) * 2 * pair)
            near_q[:, cols] = mm(near, w_qkv[:, cols]).astype(BF16) * jnp.asarray(scale, BF16)
            blocks = []
            for part in range(1, 3):
                at = part * channels + group * 2 * pair
                blocks.append(mm(near, w_qkv[:, at : at + 2 * pair]).astype(BF16))
            return blocks

        brought = {0: bring(0)}
        lane = iota((CHUNK, LANES), 1)
        stats = [jnp.zeros((CHUNK, LANES), F32) for _ in range(2 * m // CHUNK)]

        def near_of(p):
            return [b[:, p % 2 * pair : (p % 2 + 1) * pair] for b in brought[p // 2]]

        def multiply(p):
            cols = slice(p * pair, (p + 1) * pair)
            keys, values = near_of(p)
            return (
                mm_nt(halves(own_qkv[:, cols], scale), keys),
                mm_nt(halves(own_grad[:, cols]), values),
            )

        ahead = multiply(0)
        for p in range(pairs):
            scores, grad_prob = ahead
            if p + 1 < pairs:
                if p % 2 == 0 and p + 2 < pairs:
                    brought[p // 2 + 1] = bring(p // 2 + 1)
                ahead = multiply(p + 1)
            weights, grad_scores = [], []
            for at in range(0, 2 * m, CHUNK):
                part = slice(at, at + CHUNK)
                place = slice(at % m, at % m + CHUNK)
                raw = jnp.concatenate([scores[part], own_scores[p, part]], 1) + bias[place]
                top = jnp.max(raw, 1, keepdims=True)
                shifted = jnp.exp(raw - top)
                inv_sum = 1.0 / jnp.sum(shifted, 1, keepdims=True)
                probs = shifted * inv_sum
                product = jnp.concatenate([grad_prob[part], own_products[p, part]], 1)
                delta = jnp.sum(probs * product, 1, keepdims=True)
                weights.append(probs.astype(BF16))
                grad_scores.append((probs * (product - delta)).astype(BF16))
                for k, column in enumerate((top, inv_sum, delta)):
                    stats[at // CHUNK] = jnp.where(lane == k * pairs + p, column, stats[at // CHUNK])
            weights = jnp.concatenate(weights, 0)
            grad_scores = jnp.concatenate(grad_scores, 0)
            weights_out[p] = weights[:, 2 * m :]
            scores_out[p] = grad_scores[:, 2 * m :]
            keys, values = (
                jnp.concatenate([block, own_qkv[:, at + p * pair : at + (p + 1) * pair]], 0)
                for block, at in zip(near_of(p), (channels, 2 * channels))
            )
            cols = slice(p * pair, (p + 1) * pair)
            attention[:, cols] = merge(mm(weights, values)).astype(BF16)
            grad_query[:, cols] = (merge(mm(grad_scores, keys)) * scale).astype(BF16)
        stats_out[...] = jnp.transpose(jnp.concatenate(stats, 0))[: 3 * pairs]

    for copy in fetch:
        copy.wait()


def product_kernel(
    scale,
    pair,
    weights,
    grad_scores,
    attention,
    grad_query,
    own_qkv,
    own_grad,
    latent,
    w_out,
    w_qkv,
    mesh_out_hbm,
    grad_normed,
    grad_key,
    grad_value,
    mesh_out,
    sems,
):
    m, channels = latent.shape
    mesh_out[...] = (latent[...].astype(F32) + mm(attention[...], w_out[...])).astype(BF16)
    out = pltpu.make_async_copy(mesh_out, mesh_out_hbm, sems.at[0])
    out.start()

    @pl.when(everywhere())
    def _():
        for p in range(channels // pair):
            cols = slice(p * pair, (p + 1) * pair)
            grad_key[:, cols] = mm_tn(grad_scores[p], halves(own_qkv[:, cols], scale))
            grad_value[:, cols] = mm_tn(weights[p], halves(own_grad[:, cols]))
        grad_normed[...] = mm_nt(grad_query[...], w_qkv[:, :channels])

    out.wait()


def finish_kernel(
    pair,
    chip_stats,
    off_stats,
    bias,
    near_q,
    chip_grad,
    off_grad,
    own_qkv,
    grad_key,
    grad_value,
    grad_normed,
    w_qkv,
    normal,
    inv_std,
    cot,
    grad_out,
):
    m, channels = normal.shape
    pairs = channels // pair

    stats = []
    for h in range(2):
        lanes = slice(h * m, (h + 1) * m)
        stats.append(jnp.concatenate([chip_stats[:, lanes], off_stats[:, lanes]], 1))

    def multiply(p):
        cols = slice(p * pair, (p + 1) * pair)
        key2 = halves(own_qkv[:, channels + p * pair : channels + (p + 1) * pair])
        value2 = halves(own_qkv[:, 2 * channels + p * pair : 2 * channels + (p + 1) * pair])
        query = near_q[:, cols]
        grad = jnp.concatenate([chip_grad[:, cols], off_grad[:, cols]], 0)
        return query, grad, mm_nt(key2, query), mm_nt(value2, grad)

    total = grad_normed[...]
    group = 2
    gks, gvs = [], []
    ahead = multiply(0)
    for p in range(pairs):
        cols = slice(p * pair, (p + 1) * pair)
        query, grad, scores, grad_prob = ahead
        if p + 1 < pairs:
            ahead = multiply(p + 1)
        weights, grad_scores = [], []
        for at in range(0, 2 * m, CHUNK):
            part = slice(at, at + CHUNK)
            place = slice(at % m, at % m + CHUNK)
            top, inv_sum, delta = (
                stats[at // m][k * pairs + p : k * pairs + p + 1] for k in range(3)
            )
            probs = jnp.exp(scores[part] + bias[place] - top) * inv_sum
            weights.append(probs.astype(BF16))
            grad_scores.append((probs * (grad_prob[part] - delta)).astype(BF16))
        gk = grad_key[:, cols] + merge(mm(jnp.concatenate(grad_scores, 0), query))
        gv = grad_value[:, cols] + merge(mm(jnp.concatenate(weights, 0), grad))
        gks.append(gk.astype(BF16))
        gvs.append(gv.astype(BF16))
        if len(gks) == group:
            at = channels + (p + 1 - group) * pair
            width = group * pair
            for blocks, start in ((gks, at), (gvs, at + channels)):
                total = total + mm_nt(
                    jnp.concatenate(blocks, 1), w_qkv[:, start : start + width]
                )
            gks, gvs = [], []
    centred = (
        total
        - jnp.mean(total, -1, keepdims=True)
        - normal[...] * jnp.mean(total * normal[...], -1, keepdims=True)
    )
    grad_out[...] = (cot[...].astype(F32) + inv_std[:, :1] * centred).astype(BF16)


def body(
    grid_in,
    mesh_in,
    own_src,
    own_dst,
    side_src,
    side_dst,
    side_count,
    far_src,
    far_dst,
    far_count,
    window,
    cotangent,
    w_edge,
    w_qkv,
    w_out,
):
    devices = lax.axis_size("node")
    grid_rows, channels = grid_in.shape
    m = mesh_in.shape[0]
    far_slots = far_src.shape[0]
    far_depth = far_slots // devices
    head_dim = channels // HEADS
    pair = 2 * head_dim
    pairs = channels // pair
    scale = head_dim ** (-0.5)
    meta_rows = side_src.shape[0] // (2 * LANES)

    side_src, side_dst = side_src.reshape(-1, LANES), side_dst.reshape(-1, LANES)
    own_src, own_dst = own_src.reshape(-1, LANES), own_dst.reshape(-1, LANES)
    far_src, far_dst = far_src.reshape(1, -1), far_dst.reshape(1, -1)
    side_count, far_count = side_count.reshape(1, -1), far_count.reshape(1, -1)
    message = ((BAND + meta_rows, channels), BF16)
    far_block = (2 * far_slots, channels // 2 + LANES)
    far_message, chip_message, off_message, w_edge = call(
        pack_kernel,
        [(far_block, BF16), message, message, (w_edge.shape, BF16)],
        [grid_in, window, side_src, side_dst, side_count, far_src, far_dst, far_count, w_edge],
        hbm=range(9),
        hbm_outs=range(3),
        scratch=like(grid_in, window, side_src, side_dst, side_count, far_src, far_dst, far_count)
        + [
            pltpu.VMEM(far_block, BF16),
            pltpu.VMEM((2, meta_rows, channels), BF16),
            dma(9),
            dma(5),
        ],
        name="pack",
    )
    from_chip, from_off = exchange(chip_message, off_message, "node")
    got_far = lax.all_to_all(
        far_message.reshape(devices, 2 * far_depth, far_block[1]),
        "node",
        split_axis=0,
        concat_axis=0,
        tiled=True,
    ).reshape(far_block)

    rows = ((m, channels), BF16)
    partial, own_grad = call(
        own_kernel,
        [((m, channels), F32), rows],
        [grid_in, mesh_in, own_src, own_dst, cotangent, w_out, w_edge],
        hbm=range(6),
        hbm_outs=(1,),
        scratch=like(grid_in, mesh_in, own_src, own_dst, cotangent, w_out, cotangent) + [dma(7)],
        name="own",
    )
    (partial,) = call(
        functools.partial(side_kernel, meta_rows),
        [((m, channels), F32)],
        [from_chip, from_off, w_edge, partial],
        name="side",
        flops=8 * 10**9,
    )
    latent, normed, normal, inv_std = call(
        functools.partial(latent_kernel, far_depth),
        [rows, rows, ((m, channels), F32), ((m, LANES), F32)],
        [got_far, partial],
        name="latent",
    )
    chip_normed, off_normed = exchange(normed, normed, "node")
    own_block = ((pairs, 2 * m, m), F32)
    own_qkv, w_qkv, own_grad, own_scores, own_products, bias, near_bias = call(
        functools.partial(project_kernel, scale, pair, meta_rows),
        [((m, 3 * channels), BF16), (w_qkv.shape, BF16), rows, own_block, own_block]
        + [((m, 3 * m), F32), ((m, 2 * m), F32)],
        [normed, from_chip, from_off, window, own_grad, w_qkv],
        hbm=(3, 4, 5),
        scratch=like(window) + [dma(3 * PIECES + 2)],
        name="project",
    )
    chip_grad, off_grad = exchange(own_grad, own_grad, "node")
    probs = ((pairs, 2 * m, m), BF16)
    stats, attention, grad_query, weights, grad_scores, near_q, w_out, cotangent = call(
        functools.partial(attend_kernel, scale, pair),
        [
            ((3 * pairs, 2 * m), F32),
            rows,
            rows,
            probs,
            probs,
            ((2 * m, channels), BF16),
            (w_out.shape, BF16),
            rows,
        ],
        [chip_normed, off_normed, w_qkv, own_qkv, own_grad, own_scores, own_products]
        + [bias, w_out, cotangent],
        hbm=(8, 9),
        scratch=[dma(2)],
        name="attend",
    )
    chip_stats, off_stats = exchange(stats, stats, "node")
    mesh_out, grad_normed, grad_key, grad_value = call(
        functools.partial(product_kernel, scale, pair),
        [
            rows,
            ((m, channels), F32),
            ((m, channels), F32),
            ((m, channels), F32),
        ],
        [
            weights,
            grad_scores,
            attention,
            grad_query,
            own_qkv,
            own_grad,
            latent,
            w_out,
            w_qkv,
        ],
        hbm_outs=(0,),
        scratch=[pltpu.VMEM((m, channels), BF16), dma(1)],
        name="product",
    )
    (mesh_grad,) = call(
        functools.partial(finish_kernel, pair),
        [rows],
        [
            chip_stats,
            off_stats,
            near_bias,
            near_q,
            chip_grad,
            off_grad,
            own_qkv,
            grad_key,
            grad_value,
            grad_normed,
            w_qkv,
            normal,
            inv_std,
            cotangent,
        ],
        name="finish",
    )
    return (mesh_out, mesh_grad)


def solution(mesh):
    rows = P(("groups", "node"), None)
    flat = P(("groups", "node"))
    placed = (rows, rows) + (flat,) * 8 + (P(None, ("groups", "node")), rows, P(), P(), P())
    return jax.shard_map(
        body, mesh=mesh, in_specs=placed, out_specs=(rows, rows), check_vma=False
    )
```

```python
import functools

import jax
import jax.numpy as jnp
from jax import lax
from jax.experimental import pallas as pl
from jax.experimental.pallas import tpu as pltpu
from jax.sharding import PartitionSpec as P

HEADS = 16
BAND = 128
LANES = 128
F32 = jnp.float32
BF16 = jnp.bfloat16
I32 = jnp.int32
VMEM_LIMIT = 28 * 2**20
PIECES = 2
CHUNK = 64


def mm(a, b):
    return lax.dot_general(a, b, (((1,), (0,)), ((), ())), preferred_element_type=F32)


def mm_nt(a, b):
    return lax.dot_general(a, b, (((1,), (1,)), ((), ())), preferred_element_type=F32)


def mm_tn(a, b):
    return lax.dot_general(a, b, (((0,), (0,)), ((), ())), preferred_element_type=F32)


def iota(shape, dim):
    return lax.broadcasted_iota(I32, shape, dim)


def call(kernel, outs, args, hbm=(), hbm_outs=(), scratch=(), name=None, flops=None):
    args = [
        pltpu.with_memory_space_constraint(a, pltpu.HBM) if i in hbm else a
        for i, a in enumerate(args)
    ]

    def specs(count, far):
        return [
            pl.BlockSpec(memory_space=pltpu.HBM if i in far else pltpu.VMEM) for i in range(count)
        ]

    return pl.pallas_call(
        kernel,
        out_shape=[
            (pltpu.HBM if i in hbm_outs else jax.ShapeDtypeStruct)(shape, dtype)
            for i, (shape, dtype) in enumerate(outs)
        ],
        in_specs=specs(len(args), hbm),
        out_specs=specs(len(outs), hbm_outs),
        scratch_shapes=list(scratch),
        compiler_params=pltpu.CompilerParams(vmem_limit_bytes=VMEM_LIMIT),
        cost_estimate=flops and pl.CostEstimate(flops=flops, transcendentals=0, bytes_accessed=0),
        name=name,
    )(*args)


def dma(count):
    return pltpu.SemaphoreType.DMA((count,))


def start_all(pairs, sems):
    copies = [pltpu.make_async_copy(src, dst, sems.at[i]) for i, (src, dst) in enumerate(pairs)]
    for copy in copies:
        copy.start()
    return copies


def like(*arrays):
    return [pltpu.VMEM(a.shape, a.dtype) for a in arrays]


def exchange(chip_message, off_message, axis):
    n = lax.axis_size(axis)
    from_off = lax.ppermute(
        off_message, axis, [p for i in range(1, n - 1, 2) for p in ((i, i + 1), (i + 1, i))]
    )
    from_chip = lax.ppermute(
        chip_message, axis, [p for i in range(0, n, 2) for p in ((i, i + 1), (i + 1, i))]
    )
    return from_chip, from_off


def is_odd():
    return lax.axis_index("node") % 2


def everywhere():
    return lax.axis_index("node") >= 0


def gelu(projected):
    x = projected.astype(BF16).astype(F32)
    inner = (2.0 / jnp.pi) ** 0.5 * (x + 0.044715 * (x * x * x))
    return (0.5 * x * (1.0 + jnp.tanh(inner))).astype(BF16)


def onehot_rows(index_rows, count):
    parts = [
        jnp.where(iota((count, row.shape[1]), 0) == row, 1.0, 0.0).astype(BF16)
        for row in index_rows
    ]
    return parts[0] if len(parts) == 1 else jnp.concatenate(parts, 1)


def norm_stats(latent):
    values = latent.astype(F32)
    row_mean = jnp.mean(values, -1, keepdims=True)
    centred = values - row_mean
    variance = jnp.mean(centred * centred, -1, keepdims=True)
    inv_std = lax.rsqrt(variance + 1e-05)
    return centred * inv_std, inv_std


def pack_kernel(
    grid_hbm,
    window_hbm,
    side_src_hbm,
    side_dst_hbm,
    side_count_hbm,
    far_src_hbm,
    far_dst_hbm,
    far_count_hbm,
    w_edge_hbm,
    far_out,
    chip_out,
    off_out,
    w_edge,
    grid,
    window,
    side_src,
    side_dst,
    side_count,
    far_src,
    far_dst,
    far_count,
    far,
    meta,
    sems,
    out_sems,
):
    grid_rows, channels = grid.shape
    mesh_rows = window.shape[1]
    slots = far_src.shape[1]
    devices = far_count.shape[1]
    depth = slots // devices
    first = grid_rows - BAND
    count = side_src.shape[0] // 2
    copies = start_all(
        [
            (side_src_hbm, side_src),
            (side_dst_hbm, side_dst),
            (side_count_hbm, side_count),
            (window_hbm, window),
            (grid_hbm, grid),
            (far_src_hbm, far_src),
            (far_dst_hbm, far_dst),
            (far_count_hbm, far_count),
            (w_edge_hbm, w_edge),
        ],
        sems,
    )
    for copy in copies[:4]:
        copy.wait()
    for k in range(2):
        rank = iota((count, LANES), 0) * LANES + iota((count, LANES), 1)
        src = side_src[k * count : (k + 1) * count] - k * first
        live = rank < side_count[:, k : k + 1]
        dst = jnp.where(live, side_dst[k * count : (k + 1) * count], mesh_rows)
        reach = jnp.concatenate([window[...], jnp.zeros((count - 2, mesh_rows), I32)], 0)
        blank = jnp.zeros((count, channels - 2 * LANES - mesh_rows), I32)
        meta[k] = jnp.concatenate([src, dst, reach, blank], 1).astype(F32).astype(BF16)
    copies[4].wait()
    odd = is_odd()
    outs = start_all(
        [
            pair
            for k, out in ((1 - odd, chip_out), (odd, off_out))
            for pair in (
                (grid.at[pl.ds(pl.multiple_of(k * first, BAND), BAND)], out.at[pl.ds(0, BAND)]),
                (meta.at[k], out.at[pl.ds(BAND, count)]),
            )
        ],
        out_sems,
    )
    for copy in copies[5:8]:
        copy.wait()
    slot = iota((1, slots), 1)
    receiver = jnp.where(iota((devices, slots), 0) == iota((devices, slots), 1) // depth, 1.0, 0.0)
    live = mm(far_count[...].astype(F32).astype(BF16), receiver.astype(BF16))
    target = jnp.where((slot % depth).astype(F32) < live, far_dst[...].astype(F32), 1.0 * mesh_rows)
    row = iota((2 * slots, slots), 0)
    mine = slot == row // (2 * depth) * depth + row % depth
    source = jnp.sum(jnp.where(mine, far_src[...].astype(F32), 0.0), 1, keepdims=True)
    column = jnp.sum(jnp.where(mine, target, 0.0), 1, keepdims=True)
    pick = jnp.where(iota((2 * slots, grid_rows), 1).astype(F32) == source, 1.0, 0.0).astype(BF16)
    rows = mm(pick, grid[...]).astype(BF16)
    copies[8].wait()
    rows = gelu(mm(rows, w_edge[...]))
    half = channels // 2
    is_first = iota((2 * slots, half), 0) % (2 * depth) < depth
    far[:, :half] = jnp.where(is_first, rows[:, :half], rows[:, half:])
    far[:, half:] = jnp.broadcast_to(column, (2 * slots, LANES)).astype(BF16)
    last = pltpu.make_async_copy(far, far_out, out_sems.at[4])
    last.start()
    for copy in outs + [last]:
        copy.wait()


def own_kernel(
    grid_hbm,
    mesh_in_hbm,
    own_src_hbm,
    own_dst_hbm,
    cot_hbm,
    w_out_hbm,
    w_edge,
    partial_out,
    grad_hbm,
    grid,
    mesh_in,
    own_src,
    own_dst,
    cot,
    w_out,
    grad,
    sems,
):
    grid_rows = grid.shape[0]
    mesh_rows = mesh_in.shape[0]
    copies = start_all(
        [
            (own_src_hbm, own_src),
            (own_dst_hbm, own_dst),
            (cot_hbm, cot),
            (w_out_hbm, w_out),
            (grid_hbm, grid),
            (mesh_in_hbm, mesh_in),
        ],
        sems,
    )
    for copy in copies[:2]:
        copy.wait()
    rows = own_src.shape[0]
    src = onehot_rows([own_src[r : r + 1] for r in range(rows)], grid_rows)
    dst = onehot_rows([own_dst[r : r + 1] for r in range(rows)], mesh_rows)
    counts = mm_nt(dst, src).astype(BF16)
    for copy in copies[2:4]:
        copy.wait()
    grad[...] = mm_nt(cot[...], w_out[...]).astype(BF16)
    out = pltpu.make_async_copy(grad, grad_hbm, sems.at[6])
    out.start()
    for copy in copies[4:]:
        copy.wait()
    active = gelu(mm(grid[...], w_edge[...]))
    partial_out[...] = mesh_in[...].astype(F32) + mm(counts, active)
    out.wait()


def meta_of(message, count):
    return message[BAND : BAND + count].astype(F32).astype(I32)


def side_kernel(count, chip, off, w_edge, partial, partial_out):
    mesh_rows = partial.shape[0]
    uppers, lowers = [], []
    for side in (chip, off):
        meta = meta_of(side, count)
        src = onehot_rows([meta[r : r + 1, :LANES] for r in range(count)], BAND)
        dst = onehot_rows([meta[r : r + 1, LANES : 2 * LANES] for r in range(count)], mesh_rows)
        counts = mm_nt(dst, src)
        upper = counts.astype(BF16)
        uppers.append(upper)
        lowers.append((counts - upper.astype(F32)).astype(BF16))
    active = gelu(mm(jnp.concatenate([chip[:BAND], off[:BAND]], 0), w_edge[...]))
    landing = jnp.concatenate(uppers + lowers, 1)
    partial_out[...] = partial[...] + mm(landing, jnp.concatenate([active, active], 0))


def latent_kernel(depth, far, partial, latent_out, normed_out, normal_out, inv_std_out):
    mesh_rows, channels = partial.shape
    slots = far.shape[0]
    half = channels // 2
    first = far[:, :half]
    second = pltpu.roll(first.astype(F32), slots - depth, 0).astype(BF16)
    target = jnp.transpose(far[:, half:].astype(F32))
    if mesh_rows != LANES:
        target = jnp.broadcast_to(target[:1], (mesh_rows, slots))
    is_row = iota((mesh_rows, slots), 1) % (2 * depth) < depth
    hit = (target == iota((mesh_rows, slots), 0).astype(F32)) & is_row
    landing = jnp.where(hit, 1.0, 0.0).astype(BF16)
    total = partial[...] + mm(landing, jnp.concatenate([first, second], 1))
    latent = total.astype(BF16)
    latent_out[...] = latent
    normal, inv_std = norm_stats(latent)
    normed_out[...] = normal.astype(BF16)
    normal_out[...] = normal
    inv_std_out[...] = jnp.broadcast_to(inv_std, inv_std_out.shape)


def halves(rows, scale=None):
    first = iota(rows.shape, 1) < rows.shape[1] // 2
    if scale is not None:
        rows = rows * jnp.asarray(scale, rows.dtype)
    zero = jnp.zeros_like(rows)
    return jnp.concatenate([jnp.where(first, rows, zero), jnp.where(first, zero, rows)], 0)


def merge(stacked):
    m = stacked.shape[0] // 2
    first = iota((m, stacked.shape[1]), 1) < stacked.shape[1] // 2
    return jnp.where(first, stacked[:m], stacked[m:])


def near_places(m):
    odd = is_odd()
    return (1 - odd) * 2 * m, odd * 2 * m


def project_kernel(
    scale,
    pair,
    count,
    normed,
    chip_first,
    off_first,
    window_hbm,
    grad_hbm,
    w_qkv_hbm,
    qkv_out,
    w_qkv,
    grad_out,
    scores_out,
    products_out,
    bias_out,
    near_bias_out,
    window,
    sems,
):
    m, channels = normed.shape
    width = channels // PIECES
    starts = [part * channels + c * width for c in range(PIECES) for part in range(3)]
    copies = start_all(
        [(window_hbm, window), (grad_hbm, grad_out)]
        + [(w_qkv_hbm.at[:, pl.ds(at, width)], w_qkv.at[:, pl.ds(at, width)]) for at in starts],
        sems,
    )
    copies[0].wait()
    def masks():
        chip_at, off_at = near_places(m)
        reach = [meta_of(side, count)[:8, 2 * LANES : 2 * LANES + m] for side in (chip_first, off_first)]
        reach = jnp.concatenate(reach, 1)
        key_at = iota((m, 2 * m), 0) + m
        lane = iota((m, 2 * m), 1)
        query_at = jnp.where(lane < m, lane + chip_at, lane - m + off_at)
        keep = (key_at >= query_at - reach[0:1, :]) & (key_at <= query_at + reach[1:2, :])
        near_bias_out[...] = jnp.where(keep, 0.0, -jnp.inf).astype(F32)
        me = lax.axis_index("node")
        row = iota((3 * m, m), 0)
        key_at = jnp.where(row < m, row + chip_at, jnp.where(row < 2 * m, row - m + off_at, row - m))
        query_at = iota((3 * m, m), 1) + m
        at_end = (me == 0) | (me == lax.axis_size("node") - 1)
        missing = (row >= m) & (row < 2 * m) & at_end
        keep = (key_at >= query_at - window[0:1, :]) & (key_at <= query_at + window[1:2, :])
        bias = jnp.where(keep & jnp.logical_not(missing), 0.0, -jnp.inf).astype(F32)
        bias_out[...] = jnp.transpose(bias)

    masks()
    copies[1].wait()
    for i, at in enumerate(starts):
        copies[2 + i].wait()
        cols = slice(at, at + width)
        qkv_out[:, cols] = mm(normed[...], w_qkv[:, cols]).astype(BF16)
        for p in range(i // 3 * width // pair, (i // 3 + 1) * width // pair):
            q, k, v = (
                slice(part * channels + p * pair, part * channels + (p + 1) * pair)
                for part in range(3)
            )
            if i % 3 == 1:
                scores_out[p] = mm_nt(halves(qkv_out[:, q], scale), qkv_out[:, k])
            if i % 3 == 2:
                products_out[p] = mm_nt(halves(grad_out[:, q]), qkv_out[:, v])


def attend_kernel(
    scale,
    pair,
    chip_normed,
    off_normed,
    w_qkv,
    own_qkv,
    own_grad,
    own_scores,
    own_products,
    bias,
    w_out_hbm,
    cot_hbm,
    stats_out,
    attention,
    grad_query,
    weights_out,
    scores_out,
    near_q,
    w_out,
    cot,
    sems,
):
    fetch = start_all([(w_out_hbm, w_out), (cot_hbm, cot)], sems)
    m, channels = chip_normed.shape
    pairs = channels // pair

    @pl.when(everywhere())
    def _():
        near = jnp.concatenate([chip_normed[...], off_normed[...]], 0)

        def bring(group):
            cols = slice(group * 2 * pair, (group + 1) * 2 * pair)
            near_q[:, cols] = mm(near, w_qkv[:, cols]).astype(BF16) * jnp.asarray(scale, BF16)
            blocks = []
            for part in range(1, 3):
                at = part * channels + group * 2 * pair
                blocks.append(mm(near, w_qkv[:, at : at + 2 * pair]).astype(BF16))
            return blocks

        brought = {0: bring(0)}
        lane = iota((CHUNK, LANES), 1)
        stats = [jnp.zeros((CHUNK, LANES), F32) for _ in range(2 * m // CHUNK)]

        def near_of(p):
            return [b[:, p % 2 * pair : (p % 2 + 1) * pair] for b in brought[p // 2]]

        def multiply(p):
            cols = slice(p * pair, (p + 1) * pair)
            keys, values = near_of(p)
            return (
                mm_nt(halves(own_qkv[:, cols], scale), keys),
                mm_nt(halves(own_grad[:, cols]), values),
            )

        ahead = multiply(0)
        for p in range(pairs):
            scores, grad_prob = ahead
            if p + 1 < pairs:
                if p % 2 == 0 and p + 2 < pairs:
                    brought[p // 2 + 1] = bring(p // 2 + 1)
                ahead = multiply(p + 1)
            weights, grad_scores = [], []
            for at in range(0, 2 * m, CHUNK):
                part = slice(at, at + CHUNK)
                place = slice(at % m, at % m + CHUNK)
                raw = jnp.concatenate([scores[part], own_scores[p, part]], 1) + bias[place]
                top = jnp.max(raw, 1, keepdims=True)
                shifted = jnp.exp(raw - top)
                inv_sum = 1.0 / jnp.sum(shifted, 1, keepdims=True)
                probs = shifted * inv_sum
                product = jnp.concatenate([grad_prob[part], own_products[p, part]], 1)
                delta = jnp.sum(probs * product, 1, keepdims=True)
                weights.append(probs.astype(BF16))
                grad_scores.append((probs * (product - delta)).astype(BF16))
                for k, column in enumerate((top, inv_sum, delta)):
                    stats[at // CHUNK] = jnp.where(lane == k * pairs + p, column, stats[at // CHUNK])
            weights = jnp.concatenate(weights, 0)
            grad_scores = jnp.concatenate(grad_scores, 0)
            weights_out[p] = weights[:, 2 * m :]
            scores_out[p] = grad_scores[:, 2 * m :]
            keys, values = (
                jnp.concatenate([block, own_qkv[:, at + p * pair : at + (p + 1) * pair]], 0)
                for block, at in zip(near_of(p), (channels, 2 * channels))
            )
            cols = slice(p * pair, (p + 1) * pair)
            attention[:, cols] = merge(mm(weights, values)).astype(BF16)
            grad_query[:, cols] = (merge(mm(grad_scores, keys)) * scale).astype(BF16)
        stats_out[...] = jnp.transpose(jnp.concatenate(stats, 0))[: 3 * pairs]

    for copy in fetch:
        copy.wait()


def product_kernel(
    scale,
    pair,
    weights,
    grad_scores,
    attention,
    grad_query,
    own_qkv,
    own_grad,
    latent,
    w_out,
    w_qkv,
    mesh_out_hbm,
    grad_normed,
    grad_key,
    grad_value,
    mesh_out,
    sems,
):
    m, channels = latent.shape
    mesh_out[...] = (latent[...].astype(F32) + mm(attention[...], w_out[...])).astype(BF16)
    out = pltpu.make_async_copy(mesh_out, mesh_out_hbm, sems.at[0])
    out.start()

    @pl.when(everywhere())
    def _():
        for p in range(channels // pair):
            cols = slice(p * pair, (p + 1) * pair)
            grad_key[:, cols] = mm_tn(grad_scores[p], halves(own_qkv[:, cols], scale))
            grad_value[:, cols] = mm_tn(weights[p], halves(own_grad[:, cols]))
        grad_normed[...] = mm_nt(grad_query[...], w_qkv[:, :channels])

    out.wait()


def finish_kernel(
    pair,
    chip_stats,
    off_stats,
    bias,
    near_q,
    chip_grad,
    off_grad,
    own_qkv,
    grad_key,
    grad_value,
    grad_normed,
    w_qkv,
    normal,
    inv_std,
    cot,
    grad_out,
):
    m, channels = normal.shape
    pairs = channels // pair

    stats = []
    for h in range(2):
        lanes = slice(h * m, (h + 1) * m)
        stats.append(jnp.concatenate([chip_stats[:, lanes], off_stats[:, lanes]], 1))

    def multiply(p):
        cols = slice(p * pair, (p + 1) * pair)
        key2 = halves(own_qkv[:, channels + p * pair : channels + (p + 1) * pair])
        value2 = halves(own_qkv[:, 2 * channels + p * pair : 2 * channels + (p + 1) * pair])
        query = near_q[:, cols]
        grad = jnp.concatenate([chip_grad[:, cols], off_grad[:, cols]], 0)
        return query, grad, mm_nt(key2, query), mm_nt(value2, grad)

    total = grad_normed[...]
    group = 2
    gks, gvs = [], []
    ahead = multiply(0)
    for p in range(pairs):
        cols = slice(p * pair, (p + 1) * pair)
        query, grad, scores, grad_prob = ahead
        if p + 1 < pairs:
            ahead = multiply(p + 1)
        weights, grad_scores = [], []
        for at in range(0, 2 * m, CHUNK):
            part = slice(at, at + CHUNK)
            place = slice(at % m, at % m + CHUNK)
            top, inv_sum, delta = (
                stats[at // m][k * pairs + p : k * pairs + p + 1] for k in range(3)
            )
            probs = jnp.exp(scores[part] + bias[place] - top) * inv_sum
            weights.append(probs.astype(BF16))
            grad_scores.append((probs * (grad_prob[part] - delta)).astype(BF16))
        gk = grad_key[:, cols] + merge(mm(jnp.concatenate(grad_scores, 0), query))
        gv = grad_value[:, cols] + merge(mm(jnp.concatenate(weights, 0), grad))
        gks.append(gk.astype(BF16))
        gvs.append(gv.astype(BF16))
        if len(gks) == group:
            at = channels + (p + 1 - group) * pair
            width = group * pair
            for blocks, start in ((gks, at), (gvs, at + channels)):
                total = total + mm_nt(
                    jnp.concatenate(blocks, 1), w_qkv[:, start : start + width]
                )
            gks, gvs = [], []
    centred = (
        total
        - jnp.mean(total, -1, keepdims=True)
        - normal[...] * jnp.mean(total * normal[...], -1, keepdims=True)
    )
    grad_out[...] = (cot[...].astype(F32) + inv_std[:, :1] * centred).astype(BF16)


def body(
    grid_in,
    mesh_in,
    own_src,
    own_dst,
    side_src,
    side_dst,
    side_count,
    far_src,
    far_dst,
    far_count,
    window,
    cotangent,
    w_edge,
    w_qkv,
    w_out,
):
    devices = lax.axis_size("node")
    grid_rows, channels = grid_in.shape
    m = mesh_in.shape[0]
    far_slots = far_src.shape[0]
    far_depth = far_slots // devices
    head_dim = channels // HEADS
    pair = 2 * head_dim
    pairs = channels // pair
    scale = head_dim ** (-0.5)
    meta_rows = side_src.shape[0] // (2 * LANES)

    side_src, side_dst = side_src.reshape(-1, LANES), side_dst.reshape(-1, LANES)
    own_src, own_dst = own_src.reshape(-1, LANES), own_dst.reshape(-1, LANES)
    far_src, far_dst = far_src.reshape(1, -1), far_dst.reshape(1, -1)
    side_count, far_count = side_count.reshape(1, -1), far_count.reshape(1, -1)
    message = ((BAND + meta_rows, channels), BF16)
    far_block = (2 * far_slots, channels // 2 + LANES)
    far_message, chip_message, off_message, w_edge = call(
        pack_kernel,
        [(far_block, BF16), message, message, (w_edge.shape, BF16)],
        [grid_in, window, side_src, side_dst, side_count, far_src, far_dst, far_count, w_edge],
        hbm=range(9),
        hbm_outs=range(3),
        scratch=like(grid_in, window, side_src, side_dst, side_count, far_src, far_dst, far_count)
        + [
            pltpu.VMEM(far_block, BF16),
            pltpu.VMEM((2, meta_rows, channels), BF16),
            dma(9),
            dma(5),
        ],
        name="pack",
    )
    from_chip, from_off = exchange(chip_message, off_message, "node")
    got_far = lax.all_to_all(
        far_message.reshape(devices, 2 * far_depth, far_block[1]),
        "node",
        split_axis=0,
        concat_axis=0,
        tiled=True,
    ).reshape(far_block)

    rows = ((m, channels), BF16)
    partial, own_grad = call(
        own_kernel,
        [((m, channels), F32), rows],
        [grid_in, mesh_in, own_src, own_dst, cotangent, w_out, w_edge],
        hbm=range(6),
        hbm_outs=(1,),
        scratch=like(grid_in, mesh_in, own_src, own_dst, cotangent, w_out, cotangent) + [dma(7)],
        name="own",
    )
    (partial,) = call(
        functools.partial(side_kernel, meta_rows),
        [((m, channels), F32)],
        [from_chip, from_off, w_edge, partial],
        name="side",
        flops=8 * 10**9,
    )
    latent, normed, normal, inv_std = call(
        functools.partial(latent_kernel, far_depth),
        [rows, rows, ((m, channels), F32), ((m, LANES), F32)],
        [got_far, partial],
        name="latent",
    )
    chip_normed, off_normed = exchange(normed, normed, "node")
    own_block = ((pairs, 2 * m, m), F32)
    own_qkv, w_qkv, own_grad, own_scores, own_products, bias, near_bias = call(
        functools.partial(project_kernel, scale, pair, meta_rows),
        [((m, 3 * channels), BF16), (w_qkv.shape, BF16), rows, own_block, own_block]
        + [((m, 3 * m), F32), ((m, 2 * m), F32)],
        [normed, from_chip, from_off, window, own_grad, w_qkv],
        hbm=(3, 4, 5),
        scratch=like(window) + [dma(3 * PIECES + 2)],
        name="project",
    )
    chip_grad, off_grad = exchange(own_grad, own_grad, "node")
    probs = ((pairs, 2 * m, m), BF16)
    stats, attention, grad_query, weights, grad_scores, near_q, w_out, cotangent = call(
        functools.partial(attend_kernel, scale, pair),
        [
            ((3 * pairs, 2 * m), F32),
            rows,
            rows,
            probs,
            probs,
            ((2 * m, channels), BF16),
            (w_out.shape, BF16),
            rows,
        ],
        [chip_normed, off_normed, w_qkv, own_qkv, own_grad, own_scores, own_products]
        + [bias, w_out, cotangent],
        hbm=(8, 9),
        scratch=[dma(2)],
        name="attend",
    )
    chip_stats, off_stats = exchange(stats, stats, "node")
    mesh_out, grad_normed, grad_key, grad_value = call(
        functools.partial(product_kernel, scale, pair),
        [
            rows,
            ((m, channels), F32),
            ((m, channels), F32),
            ((m, channels), F32),
        ],
        [
            weights,
            grad_scores,
            attention,
            grad_query,
            own_qkv,
            own_grad,
            latent,
            w_out,
            w_qkv,
        ],
        hbm_outs=(0,),
        scratch=[pltpu.VMEM((m, channels), BF16), dma(1)],
        name="product",
    )
    (mesh_grad,) = call(
        functools.partial(finish_kernel, pair),
        [rows],
        [
            chip_stats,
            off_stats,
            near_bias,
            near_q,
            chip_grad,
            off_grad,
            own_qkv,
            grad_key,
            grad_value,
            grad_normed,
            w_qkv,
            normal,
            inv_std,
            cotangent,
        ],
        name="finish",
    )
    return (mesh_out, mesh_grad)


def solution(mesh):
    rows = P(("groups", "node"), None)
    flat = P(("groups", "node"))
    placed = (rows, rows) + (flat,) * 8 + (P(None, ("groups", "node")), rows, P(), P(), P())
    return jax.shard_map(
        body, mesh=mesh, in_specs=placed, out_specs=(rows, rows), check_vma=False
    )
```

```python
import functools

import jax
import jax.numpy as jnp
from jax import lax
from jax.experimental import pallas as pl
from jax.experimental.pallas import tpu as pltpu
from jax.sharding import PartitionSpec as P

HEADS = 16
BAND = 128
LANES = 128
F32 = jnp.float32
BF16 = jnp.bfloat16
I32 = jnp.int32
VMEM_LIMIT = 28 * 2**20
PIECES = 2
CHUNK = 64


def mm(a, b):
    return lax.dot_general(a, b, (((1,), (0,)), ((), ())), preferred_element_type=F32)


def mm_nt(a, b):
    return lax.dot_general(a, b, (((1,), (1,)), ((), ())), preferred_element_type=F32)


def mm_tn(a, b):
    return lax.dot_general(a, b, (((0,), (0,)), ((), ())), preferred_element_type=F32)


def iota(shape, dim):
    return lax.broadcasted_iota(I32, shape, dim)


def call(kernel, outs, args, hbm=(), hbm_outs=(), scratch=(), name=None, flops=None):
    args = [
        pltpu.with_memory_space_constraint(a, pltpu.HBM) if i in hbm else a
        for i, a in enumerate(args)
    ]

    def specs(count, far):
        return [
            pl.BlockSpec(memory_space=pltpu.HBM if i in far else pltpu.VMEM) for i in range(count)
        ]

    return pl.pallas_call(
        kernel,
        out_shape=[
            (pltpu.HBM if i in hbm_outs else jax.ShapeDtypeStruct)(shape, dtype)
            for i, (shape, dtype) in enumerate(outs)
        ],
        in_specs=specs(len(args), hbm),
        out_specs=specs(len(outs), hbm_outs),
        scratch_shapes=list(scratch),
        compiler_params=pltpu.CompilerParams(vmem_limit_bytes=VMEM_LIMIT),
        cost_estimate=flops and pl.CostEstimate(flops=flops, transcendentals=0, bytes_accessed=0),
        name=name,
    )(*args)


def dma(count):
    return pltpu.SemaphoreType.DMA((count,))


def start_all(pairs, sems):
    copies = [pltpu.make_async_copy(src, dst, sems.at[i]) for i, (src, dst) in enumerate(pairs)]
    for copy in copies:
        copy.start()
    return copies


def like(*arrays):
    return [pltpu.VMEM(a.shape, a.dtype) for a in arrays]


def swap_off(rows, axis):
    n = lax.axis_size(axis)
    pairs = [p for i in range(1, n - 1, 2) for p in ((i, i + 1), (i + 1, i))]
    return lax.ppermute(rows, axis, pairs)


def swap_chip(rows, axis):
    n = lax.axis_size(axis)
    return lax.ppermute(rows, axis, [p for i in range(0, n, 2) for p in ((i, i + 1), (i + 1, i))])


def exchange(chip_message, off_message, axis):
    from_off = swap_off(off_message, axis)
    return swap_chip(chip_message, axis), from_off


def is_odd():
    return lax.axis_index("node") % 2


def everywhere():
    return lax.axis_index("node") >= 0


def gelu(projected):
    x = projected.astype(BF16).astype(F32)
    inner = (2.0 / jnp.pi) ** 0.5 * (x + 0.044715 * (x * x * x))
    return (0.5 * x * (1.0 + jnp.tanh(inner))).astype(BF16)


def onehot_rows(index_rows, count):
    parts = [
        jnp.where(iota((count, row.shape[1]), 0) == row, 1.0, 0.0).astype(BF16)
        for row in index_rows
    ]
    return parts[0] if len(parts) == 1 else jnp.concatenate(parts, 1)


def norm_stats(latent):
    values = latent.astype(F32)
    row_mean = jnp.mean(values, -1, keepdims=True)
    centred = values - row_mean
    variance = jnp.mean(centred * centred, -1, keepdims=True)
    inv_std = lax.rsqrt(variance + 1e-05)
    return centred * inv_std, inv_std


def pack_kernel(
    grid_hbm,
    window_hbm,
    side_src_hbm,
    side_dst_hbm,
    side_count_hbm,
    far_src_hbm,
    far_dst_hbm,
    far_count_hbm,
    w_edge_hbm,
    far_out,
    chip_out,
    off_out,
    w_edge,
    grid,
    window,
    side_src,
    side_dst,
    side_count,
    far_src,
    far_dst,
    far_count,
    far,
    meta,
    sems,
    out_sems,
):
    grid_rows, channels = grid.shape
    mesh_rows = window.shape[1]
    slots = far_src.shape[1]
    devices = far_count.shape[1]
    depth = slots // devices
    first = grid_rows - BAND
    count = side_src.shape[0] // 2
    copies = start_all(
        [
            (side_src_hbm, side_src),
            (side_dst_hbm, side_dst),
            (side_count_hbm, side_count),
            (window_hbm, window),
            (grid_hbm, grid),
            (far_src_hbm, far_src),
            (far_dst_hbm, far_dst),
            (far_count_hbm, far_count),
            (w_edge_hbm, w_edge),
        ],
        sems,
    )
    for copy in copies[:4]:
        copy.wait()
    for k in range(2):
        rank = iota((count, LANES), 0) * LANES + iota((count, LANES), 1)
        src = side_src[k * count : (k + 1) * count] - k * first
        live = rank < side_count[:, k : k + 1]
        dst = jnp.where(live, side_dst[k * count : (k + 1) * count], mesh_rows)
        reach = jnp.concatenate([window[...], jnp.zeros((count - 2, mesh_rows), I32)], 0)
        blank = jnp.zeros((count, channels - 2 * LANES - mesh_rows), I32)
        meta[k] = jnp.concatenate([src, dst, reach, blank], 1).astype(F32).astype(BF16)
    copies[4].wait()
    odd = is_odd()
    outs = start_all(
        [
            pair
            for k, out in ((1 - odd, chip_out), (odd, off_out))
            for pair in (
                (grid.at[pl.ds(pl.multiple_of(k * first, BAND), BAND)], out.at[pl.ds(0, BAND)]),
                (meta.at[k], out.at[pl.ds(BAND, count)]),
            )
        ],
        out_sems,
    )
    for copy in copies[5:8]:
        copy.wait()
    slot = iota((1, slots), 1)
    receiver = jnp.where(iota((devices, slots), 0) == iota((devices, slots), 1) // depth, 1.0, 0.0)
    live = mm(far_count[...].astype(F32).astype(BF16), receiver.astype(BF16))
    target = jnp.where((slot % depth).astype(F32) < live, far_dst[...].astype(F32), 1.0 * mesh_rows)
    row = iota((2 * slots, slots), 0)
    mine = slot == row // (2 * depth) * depth + row % depth
    source = jnp.sum(jnp.where(mine, far_src[...].astype(F32), 0.0), 1, keepdims=True)
    column = jnp.sum(jnp.where(mine, target, 0.0), 1, keepdims=True)
    pick = jnp.where(iota((2 * slots, grid_rows), 1).astype(F32) == source, 1.0, 0.0).astype(BF16)
    rows = mm(pick, grid[...]).astype(BF16)
    copies[8].wait()
    rows = gelu(mm(rows, w_edge[...]))
    half = channels // 2
    is_first = iota((2 * slots, half), 0) % (2 * depth) < depth
    far[:, :half] = jnp.where(is_first, rows[:, :half], rows[:, half:])
    far[:, half:] = jnp.broadcast_to(column, (2 * slots, LANES)).astype(BF16)
    last = pltpu.make_async_copy(far, far_out, out_sems.at[4])
    last.start()
    for copy in outs + [last]:
        copy.wait()


def own_kernel(
    grid_hbm,
    mesh_in_hbm,
    own_src_hbm,
    own_dst_hbm,
    cot_hbm,
    w_out_hbm,
    w_edge,
    partial_out,
    grad_hbm,
    grid,
    mesh_in,
    own_src,
    own_dst,
    cot,
    w_out,
    grad,
    sems,
):
    grid_rows = grid.shape[0]
    mesh_rows = mesh_in.shape[0]
    copies = start_all(
        [
            (own_src_hbm, own_src),
            (own_dst_hbm, own_dst),
            (cot_hbm, cot),
            (w_out_hbm, w_out),
            (grid_hbm, grid),
            (mesh_in_hbm, mesh_in),
        ],
        sems,
    )
    for copy in copies[:2]:
        copy.wait()
    rows = own_src.shape[0]
    src = onehot_rows([own_src[r : r + 1] for r in range(rows)], grid_rows)
    dst = onehot_rows([own_dst[r : r + 1] for r in range(rows)], mesh_rows)
    counts = mm_nt(dst, src).astype(BF16)
    for copy in copies[2:4]:
        copy.wait()
    grad[...] = mm_nt(cot[...], w_out[...]).astype(BF16)
    out = pltpu.make_async_copy(grad, grad_hbm, sems.at[6])
    out.start()
    for copy in copies[4:]:
        copy.wait()
    active = gelu(mm(grid[...], w_edge[...]))
    partial_out[...] = mesh_in[...].astype(F32) + mm(counts, active)
    out.wait()


def meta_of(message, count):
    return message[BAND : BAND + count].astype(F32).astype(I32)


def side_kernel(count, chip, off, w_edge, partial, partial_out):
    mesh_rows = partial.shape[0]
    uppers, lowers = [], []
    for side in (chip, off):
        meta = meta_of(side, count)
        src = onehot_rows([meta[r : r + 1, :LANES] for r in range(count)], BAND)
        dst = onehot_rows([meta[r : r + 1, LANES : 2 * LANES] for r in range(count)], mesh_rows)
        counts = mm_nt(dst, src)
        upper = counts.astype(BF16)
        uppers.append(upper)
        lowers.append((counts - upper.astype(F32)).astype(BF16))
    active = gelu(mm(jnp.concatenate([chip[:BAND], off[:BAND]], 0), w_edge[...]))
    landing = jnp.concatenate(uppers + lowers, 1)
    partial_out[...] = partial[...] + mm(landing, jnp.concatenate([active, active], 0))


def latent_kernel(depth, far, partial, latent_out, normed_out, normal_out, inv_std_out):
    mesh_rows, channels = partial.shape
    slots = far.shape[0]
    half = channels // 2
    first = far[:, :half]
    second = pltpu.roll(first.astype(F32), slots - depth, 0).astype(BF16)
    target = jnp.transpose(far[:, half:].astype(F32))
    if mesh_rows != LANES:
        target = jnp.broadcast_to(target[:1], (mesh_rows, slots))
    is_row = iota((mesh_rows, slots), 1) % (2 * depth) < depth
    hit = (target == iota((mesh_rows, slots), 0).astype(F32)) & is_row
    landing = jnp.where(hit, 1.0, 0.0).astype(BF16)
    total = partial[...] + mm(landing, jnp.concatenate([first, second], 1))
    latent = total.astype(BF16)
    latent_out[...] = latent
    normal, inv_std = norm_stats(latent)
    normed_out[...] = normal.astype(BF16)
    normal_out[...] = normal
    inv_std_out[...] = jnp.broadcast_to(inv_std, inv_std_out.shape)


def halves(rows, scale=None):
    first = iota(rows.shape, 1) < rows.shape[1] // 2
    if scale is not None:
        rows = rows * jnp.asarray(scale, rows.dtype)
    zero = jnp.zeros_like(rows)
    return jnp.concatenate([jnp.where(first, rows, zero), jnp.where(first, zero, rows)], 0)


def merge(stacked):
    m = stacked.shape[0] // 2
    first = iota((m, stacked.shape[1]), 1) < stacked.shape[1] // 2
    return jnp.where(first, stacked[:m], stacked[m:])


def near_places(m):
    odd = is_odd()
    return (1 - odd) * 2 * m, odd * 2 * m


def project_kernel(
    scale,
    pair,
    count,
    normed,
    chip_first,
    off_first,
    window_hbm,
    grad_hbm,
    w_qkv_hbm,
    qkv_out,
    w_qkv,
    grad_out,
    scores_out,
    products_out,
    bias_out,
    near_bias_out,
    normed_out,
    window,
    sems,
):
    normed_out[...] = normed[...]
    m, channels = normed.shape
    width = channels // PIECES
    starts = [part * channels + c * width for c in range(PIECES) for part in range(3)]
    copies = start_all(
        [(window_hbm, window), (grad_hbm, grad_out)]
        + [(w_qkv_hbm.at[:, pl.ds(at, width)], w_qkv.at[:, pl.ds(at, width)]) for at in starts],
        sems,
    )
    copies[0].wait()
    def masks():
        chip_at, off_at = near_places(m)
        reach = [meta_of(side, count)[:8, 2 * LANES : 2 * LANES + m] for side in (chip_first, off_first)]
        reach = jnp.concatenate(reach, 1)
        key_at = iota((m, 2 * m), 0) + m
        lane = iota((m, 2 * m), 1)
        query_at = jnp.where(lane < m, lane + chip_at, lane - m + off_at)
        keep = (key_at >= query_at - reach[0:1, :]) & (key_at <= query_at + reach[1:2, :])
        near_bias_out[...] = jnp.where(keep, 0.0, -jnp.inf).astype(F32)
        me = lax.axis_index("node")
        row = iota((3 * m, m), 0)
        key_at = jnp.where(row < m, row + chip_at, jnp.where(row < 2 * m, row - m + off_at, row - m))
        query_at = iota((3 * m, m), 1) + m
        at_end = (me == 0) | (me == lax.axis_size("node") - 1)
        missing = (row >= m) & (row < 2 * m) & at_end
        keep = (key_at >= query_at - window[0:1, :]) & (key_at <= query_at + window[1:2, :])
        bias = jnp.where(keep & jnp.logical_not(missing), 0.0, -jnp.inf).astype(F32)
        bias_out[...] = jnp.transpose(bias)

    masks()
    copies[1].wait()
    for i, at in enumerate(starts):
        copies[2 + i].wait()
        cols = slice(at, at + width)
        qkv_out[:, cols] = mm(normed[...], w_qkv[:, cols]).astype(BF16)
        for p in range(i // 3 * width // pair, (i // 3 + 1) * width // pair):
            q, k, v = (
                slice(part * channels + p * pair, part * channels + (p + 1) * pair)
                for part in range(3)
            )
            if i % 3 == 1:
                scores_out[p] = mm_nt(halves(qkv_out[:, q], scale), qkv_out[:, k])
            if i % 3 == 2:
                products_out[p] = mm_nt(halves(grad_out[:, q]), qkv_out[:, v])


def attend_kernel(
    scale,
    pair,
    chip_normed,
    off_normed,
    w_qkv,
    own_qkv,
    own_grad,
    own_scores,
    own_products,
    bias,
    w_out_hbm,
    cot_hbm,
    stats_out,
    kv,
    weights_out,
    scores_out,
    near_q,
    w_out,
    cot,
    sems,
):
    fetch = start_all([(w_out_hbm, w_out), (cot_hbm, cot)], sems)
    m, channels = chip_normed.shape
    pairs = channels // pair

    @pl.when(everywhere())
    def _():
        near = jnp.concatenate([chip_normed[...], off_normed[...]], 0)

        def bring(group):
            cols = slice(group * 2 * pair, (group + 1) * 2 * pair)
            near_q[:, cols] = mm(near, w_qkv[:, cols]).astype(BF16) * jnp.asarray(scale, BF16)
            blocks = []
            for part in range(1, 3):
                at = part * channels + group * 2 * pair
                block = mm(near, w_qkv[:, at : at + 2 * pair]).astype(BF16)
                kv[: 2 * m, at - channels : at - channels + 2 * pair] = block
                blocks.append(block)
            return blocks

        brought = {0: bring(0)}
        kv[2 * m :] = own_qkv[:, channels:]
        lane = iota((CHUNK, LANES), 1)
        stats = [jnp.zeros((CHUNK, LANES), F32) for _ in range(2 * m // CHUNK)]

        def near_of(p):
            return [b[:, p % 2 * pair : (p % 2 + 1) * pair] for b in brought[p // 2]]

        def multiply(p):
            cols = slice(p * pair, (p + 1) * pair)
            keys, values = near_of(p)
            return (
                mm_nt(halves(own_qkv[:, cols], scale), keys),
                mm_nt(halves(own_grad[:, cols]), values),
            )

        ahead = multiply(0)
        for p in range(pairs):
            scores, grad_prob = ahead
            if p + 1 < pairs:
                if p % 2 == 0 and p + 2 < pairs:
                    brought[p // 2 + 1] = bring(p // 2 + 1)
                ahead = multiply(p + 1)
            weights, grad_scores = [], []
            for at in range(0, 2 * m, CHUNK):
                part = slice(at, at + CHUNK)
                place = slice(at % m, at % m + CHUNK)
                raw = jnp.concatenate([scores[part], own_scores[p, part]], 1) + bias[place]
                top = jnp.max(raw, 1, keepdims=True)
                shifted = jnp.exp(raw - top)
                inv_sum = 1.0 / jnp.sum(shifted, 1, keepdims=True)
                probs = shifted * inv_sum
                product = jnp.concatenate([grad_prob[part], own_products[p, part]], 1)
                delta = jnp.sum(probs * product, 1, keepdims=True)
                weights.append(probs.astype(BF16))
                grad_scores.append((probs * (product - delta)).astype(BF16))
                for k, column in enumerate((top, inv_sum, delta)):
                    stats[at // CHUNK] = jnp.where(lane == k * pairs + p, column, stats[at // CHUNK])
            weights_out[p] = jnp.concatenate(weights, 0)
            scores_out[p] = jnp.concatenate(grad_scores, 0)
        stats_out[...] = jnp.transpose(jnp.concatenate(stats, 0))[: 3 * pairs]

    for copy in fetch:
        copy.wait()


def product_kernel(
    scale,
    pair,
    weights,
    grad_scores,
    kv,
    own_qkv,
    own_grad,
    latent,
    w_out,
    w_qkv,
    mesh_out_hbm,
    grad_normed,
    grad_key,
    grad_value,
    attention,
    grad_query,
    mesh_out,
    sems,
):
    m, channels = latent.shape
    pairs = channels // pair
    for p in range(pairs):
        cols = slice(p * pair, (p + 1) * pair)
        value = kv[:, channels + p * pair : channels + (p + 1) * pair]
        attention[:, cols] = merge(mm(weights[p], value)).astype(BF16)
    mesh_out[...] = (latent[...].astype(F32) + mm(attention[...], w_out[...])).astype(BF16)
    out = pltpu.make_async_copy(mesh_out, mesh_out_hbm, sems.at[0])
    out.start()

    @pl.when(everywhere())
    def _():
        for p in range(pairs):
            cols = slice(p * pair, (p + 1) * pair)
            grad_query[:, cols] = (merge(mm(grad_scores[p], kv[:, cols])) * scale).astype(BF16)
        for p in range(pairs):
            cols = slice(p * pair, (p + 1) * pair)
            grad_key[:, cols] = mm_tn(grad_scores[p, :, 2 * m :], halves(own_qkv[:, cols], scale))
            grad_value[:, cols] = mm_tn(weights[p, :, 2 * m :], halves(own_grad[:, cols]))
        grad_normed[...] = mm_nt(grad_query[...], w_qkv[:, :channels])

    out.wait()


def finish_kernel(
    pair,
    chip_stats,
    off_stats,
    bias,
    near_q,
    chip_grad,
    off_grad,
    own_qkv,
    grad_key,
    grad_value,
    grad_normed,
    w_qkv,
    normal,
    inv_std,
    cot,
    grad_out,
):
    m, channels = normal.shape
    pairs = channels // pair

    stats = []
    for h in range(2):
        lanes = slice(h * m, (h + 1) * m)
        stats.append(jnp.concatenate([chip_stats[:, lanes], off_stats[:, lanes]], 1))

    def multiply(p):
        cols = slice(p * pair, (p + 1) * pair)
        key2 = halves(own_qkv[:, channels + p * pair : channels + (p + 1) * pair])
        value2 = halves(own_qkv[:, 2 * channels + p * pair : 2 * channels + (p + 1) * pair])
        query = near_q[:, cols]
        grad = jnp.concatenate([chip_grad[:, cols], off_grad[:, cols]], 0)
        return query, grad, mm_nt(key2, query), mm_nt(value2, grad)

    total = grad_normed[...]
    group = 2
    gks, gvs = [], []
    ahead = multiply(0)
    for p in range(pairs):
        cols = slice(p * pair, (p + 1) * pair)
        query, grad, scores, grad_prob = ahead
        if p + 1 < pairs:
            ahead = multiply(p + 1)
        weights, grad_scores = [], []
        for at in range(0, 2 * m, CHUNK):
            part = slice(at, at + CHUNK)
            place = slice(at % m, at % m + CHUNK)
            top, inv_sum, delta = (
                stats[at // m][k * pairs + p : k * pairs + p + 1] for k in range(3)
            )
            probs = jnp.exp(scores[part] + bias[place] - top) * inv_sum
            weights.append(probs.astype(BF16))
            grad_scores.append((probs * (grad_prob[part] - delta)).astype(BF16))
        gk = grad_key[:, cols] + merge(mm(jnp.concatenate(grad_scores, 0), query))
        gv = grad_value[:, cols] + merge(mm(jnp.concatenate(weights, 0), grad))
        gks.append(gk.astype(BF16))
        gvs.append(gv.astype(BF16))
        if len(gks) == group:
            at = channels + (p + 1 - group) * pair
            width = group * pair
            for blocks, start in ((gks, at), (gvs, at + channels)):
                total = total + mm_nt(
                    jnp.concatenate(blocks, 1), w_qkv[:, start : start + width]
                )
            gks, gvs = [], []
    centred = (
        total
        - jnp.mean(total, -1, keepdims=True)
        - normal[...] * jnp.mean(total * normal[...], -1, keepdims=True)
    )
    grad_out[...] = (cot[...].astype(F32) + inv_std[:, :1] * centred).astype(BF16)


def body(
    grid_in,
    mesh_in,
    own_src,
    own_dst,
    side_src,
    side_dst,
    side_count,
    far_src,
    far_dst,
    far_count,
    window,
    cotangent,
    w_edge,
    w_qkv,
    w_out,
):
    devices = lax.axis_size("node")
    grid_rows, channels = grid_in.shape
    m = mesh_in.shape[0]
    far_slots = far_src.shape[0]
    far_depth = far_slots // devices
    head_dim = channels // HEADS
    pair = 2 * head_dim
    pairs = channels // pair
    scale = head_dim ** (-0.5)
    meta_rows = side_src.shape[0] // (2 * LANES)

    side_src, side_dst = side_src.reshape(-1, LANES), side_dst.reshape(-1, LANES)
    own_src, own_dst = own_src.reshape(-1, LANES), own_dst.reshape(-1, LANES)
    far_src, far_dst = far_src.reshape(1, -1), far_dst.reshape(1, -1)
    side_count, far_count = side_count.reshape(1, -1), far_count.reshape(1, -1)
    message = ((BAND + meta_rows, channels), BF16)
    far_block = (2 * far_slots, channels // 2 + LANES)
    far_message, chip_message, off_message, w_edge = call(
        pack_kernel,
        [(far_block, BF16), message, message, (w_edge.shape, BF16)],
        [grid_in, window, side_src, side_dst, side_count, far_src, far_dst, far_count, w_edge],
        hbm=range(9),
        hbm_outs=range(3),
        scratch=like(grid_in, window, side_src, side_dst, side_count, far_src, far_dst, far_count)
        + [
            pltpu.VMEM(far_block, BF16),
            pltpu.VMEM((2, meta_rows, channels), BF16),
            dma(9),
            dma(5),
        ],
        name="pack",
    )
    from_chip, from_off = exchange(chip_message, off_message, "node")
    got_far = lax.all_to_all(
        far_message.reshape(devices, 2 * far_depth, far_block[1]),
        "node",
        split_axis=0,
        concat_axis=0,
        tiled=True,
    ).reshape(far_block)

    rows = ((m, channels), BF16)
    partial, own_grad = call(
        own_kernel,
        [((m, channels), F32), rows],
        [grid_in, mesh_in, own_src, own_dst, cotangent, w_out, w_edge],
        hbm=range(6),
        hbm_outs=(1,),
        scratch=like(grid_in, mesh_in, own_src, own_dst, cotangent, w_out, cotangent) + [dma(7)],
        name="own",
    )
    (partial,) = call(
        functools.partial(side_kernel, meta_rows),
        [((m, channels), F32)],
        [from_chip, from_off, w_edge, partial],
        name="side",
        flops=8 * 10**9,
    )
    latent, normed, normal, inv_std = call(
        functools.partial(latent_kernel, far_depth),
        [rows, rows, ((m, channels), F32), ((m, LANES), F32)],
        [got_far, partial],
        name="latent",
    )
    off_normed = swap_off(normed, "node")
    own_block = ((pairs, 2 * m, m), F32)
    own_qkv, w_qkv, own_grad, own_scores, own_products, bias, near_bias, normed = call(
        functools.partial(project_kernel, scale, pair, meta_rows),
        [((m, 3 * channels), BF16), (w_qkv.shape, BF16), rows, own_block, own_block]
        + [((m, 3 * m), F32), ((m, 2 * m), F32), rows],
        [normed, from_chip, from_off, window, own_grad, w_qkv],
        hbm=(3, 4, 5),
        scratch=like(window) + [dma(3 * PIECES + 2)],
        name="project",
    )
    chip_normed = swap_chip(normed, "node")
    chip_grad, off_grad = exchange(own_grad, own_grad, "node")
    probs = ((pairs, 2 * m, 3 * m), BF16)
    stats, kv, weights, grad_scores, near_q, w_out, cotangent = call(
        functools.partial(attend_kernel, scale, pair),
        [
            ((3 * pairs, 2 * m), F32),
            ((3 * m, 2 * channels), BF16),
            probs,
            probs,
            ((2 * m, channels), BF16),
            (w_out.shape, BF16),
            rows,
        ],
        [chip_normed, off_normed, w_qkv, own_qkv, own_grad, own_scores, own_products]
        + [bias, w_out, cotangent],
        hbm=(8, 9),
        scratch=[dma(2)],
        name="attend",
    )
    chip_stats, off_stats = exchange(stats, stats, "node")
    mesh_out, grad_normed, grad_key, grad_value = call(
        functools.partial(product_kernel, scale, pair),
        [
            rows,
            ((m, channels), F32),
            ((m, channels), F32),
            ((m, channels), F32),
        ],
        [
            weights,
            grad_scores,
            kv,
            own_qkv,
            own_grad,
            latent,
            w_out,
            w_qkv,
        ],
        hbm_outs=(0,),
        scratch=[pltpu.VMEM((m, channels), BF16)] * 3 + [dma(1)],
        name="product",
    )
    (mesh_grad,) = call(
        functools.partial(finish_kernel, pair),
        [rows],
        [
            chip_stats,
            off_stats,
            near_bias,
            near_q,
            chip_grad,
            off_grad,
            own_qkv,
            grad_key,
            grad_value,
            grad_normed,
            w_qkv,
            normal,
            inv_std,
            cotangent,
        ],
        name="finish",
    )
    return (mesh_out, mesh_grad)


def solution(mesh):
    rows = P(("groups", "node"), None)
    flat = P(("groups", "node"))
    placed = (rows, rows) + (flat,) * 8 + (P(None, ("groups", "node")), rows, P(), P(), P())
    return jax.shard_map(
        body, mesh=mesh, in_specs=placed, out_specs=(rows, rows), check_vma=False
    )
```

```python
import functools

import jax
import jax.numpy as jnp
from jax import lax
from jax.experimental import pallas as pl
from jax.experimental.pallas import tpu as pltpu
from jax.sharding import PartitionSpec as P

HEADS = 16
BAND = 128
LANES = 128
F32 = jnp.float32
BF16 = jnp.bfloat16
I32 = jnp.int32
VMEM_LIMIT = 28 * 2**20
PIECES = 2
CHUNK = 64


def mm(a, b):
    return lax.dot_general(a, b, (((1,), (0,)), ((), ())), preferred_element_type=F32)


def mm_nt(a, b):
    return lax.dot_general(a, b, (((1,), (1,)), ((), ())), preferred_element_type=F32)


def mm_tn(a, b):
    return lax.dot_general(a, b, (((0,), (0,)), ((), ())), preferred_element_type=F32)


def iota(shape, dim):
    return lax.broadcasted_iota(I32, shape, dim)


def call(kernel, outs, args, hbm=(), hbm_outs=(), scratch=(), name=None, flops=None):
    args = [
        pltpu.with_memory_space_constraint(a, pltpu.HBM) if i in hbm else a
        for i, a in enumerate(args)
    ]

    def specs(count, far):
        return [
            pl.BlockSpec(memory_space=pltpu.HBM if i in far else pltpu.VMEM) for i in range(count)
        ]

    return pl.pallas_call(
        kernel,
        out_shape=[
            (pltpu.HBM if i in hbm_outs else jax.ShapeDtypeStruct)(shape, dtype)
            for i, (shape, dtype) in enumerate(outs)
        ],
        in_specs=specs(len(args), hbm),
        out_specs=specs(len(outs), hbm_outs),
        scratch_shapes=list(scratch),
        compiler_params=pltpu.CompilerParams(vmem_limit_bytes=VMEM_LIMIT),
        cost_estimate=flops and pl.CostEstimate(flops=flops, transcendentals=0, bytes_accessed=0),
        name=name,
    )(*args)


def dma(count):
    return pltpu.SemaphoreType.DMA((count,))


def start_all(pairs, sems):
    copies = [pltpu.make_async_copy(src, dst, sems.at[i]) for i, (src, dst) in enumerate(pairs)]
    for copy in copies:
        copy.start()
    return copies


def like(*arrays):
    return [pltpu.VMEM(a.shape, a.dtype) for a in arrays]


def swap_off(rows, axis):
    n = lax.axis_size(axis)
    pairs = [p for i in range(1, n - 1, 2) for p in ((i, i + 1), (i + 1, i))]
    return lax.ppermute(rows, axis, pairs)


def swap_chip(rows, axis):
    n = lax.axis_size(axis)
    return lax.ppermute(rows, axis, [p for i in range(0, n, 2) for p in ((i, i + 1), (i + 1, i))])


def exchange(chip_message, off_message, axis):
    from_chip = swap_chip(chip_message, axis)
    return from_chip, swap_off(off_message, axis)


def is_odd():
    return lax.axis_index("node") % 2


def everywhere():
    return lax.axis_index("node") >= 0


def gelu(projected):
    x = projected.astype(BF16).astype(F32)
    inner = (2.0 / jnp.pi) ** 0.5 * (x + 0.044715 * (x * x * x))
    return (0.5 * x * (1.0 + jnp.tanh(inner))).astype(BF16)


def onehot_rows(index_rows, count):
    parts = [
        jnp.where(iota((count, row.shape[1]), 0) == row, 1.0, 0.0).astype(BF16)
        for row in index_rows
    ]
    return parts[0] if len(parts) == 1 else jnp.concatenate(parts, 1)


def norm_stats(latent):
    values = latent.astype(F32)
    row_mean = jnp.mean(values, -1, keepdims=True)
    centred = values - row_mean
    variance = jnp.mean(centred * centred, -1, keepdims=True)
    inv_std = lax.rsqrt(variance + 1e-05)
    return centred * inv_std, inv_std


def pack_kernel(
    grid_hbm,
    window_hbm,
    side_src_hbm,
    side_dst_hbm,
    side_count_hbm,
    far_src_hbm,
    far_dst_hbm,
    far_count_hbm,
    w_edge_hbm,
    far_out,
    chip_out,
    off_out,
    w_edge,
    grid,
    window,
    side_src,
    side_dst,
    side_count,
    far_src,
    far_dst,
    far_count,
    far,
    meta,
    sems,
    out_sems,
):
    grid_rows, channels = grid.shape
    mesh_rows = window.shape[1]
    slots = far_src.shape[1]
    devices = far_count.shape[1]
    depth = slots // devices
    first = grid_rows - BAND
    count = side_src.shape[0] // 2
    copies = start_all(
        [
            (side_src_hbm, side_src),
            (side_dst_hbm, side_dst),
            (side_count_hbm, side_count),
            (window_hbm, window),
            (grid_hbm, grid),
            (far_src_hbm, far_src),
            (far_dst_hbm, far_dst),
            (far_count_hbm, far_count),
            (w_edge_hbm, w_edge),
        ],
        sems,
    )
    for copy in copies[:4]:
        copy.wait()
    for k in range(2):
        rank = iota((count, LANES), 0) * LANES + iota((count, LANES), 1)
        src = side_src[k * count : (k + 1) * count] - k * first
        live = rank < side_count[:, k : k + 1]
        dst = jnp.where(live, side_dst[k * count : (k + 1) * count], mesh_rows)
        reach = jnp.concatenate([window[...], jnp.zeros((count - 2, mesh_rows), I32)], 0)
        blank = jnp.zeros((count, channels - 2 * LANES - mesh_rows), I32)
        meta[k] = jnp.concatenate([src, dst, reach, blank], 1).astype(F32).astype(BF16)
    copies[4].wait()
    odd = is_odd()
    outs = start_all(
        [
            pair
            for k, out in ((1 - odd, chip_out), (odd, off_out))
            for pair in (
                (grid.at[pl.ds(pl.multiple_of(k * first, BAND), BAND)], out.at[pl.ds(0, BAND)]),
                (meta.at[k], out.at[pl.ds(BAND, count)]),
            )
        ],
        out_sems,
    )
    for copy in copies[5:8]:
        copy.wait()
    slot = iota((1, slots), 1)
    receiver = jnp.where(iota((devices, slots), 0) == iota((devices, slots), 1) // depth, 1.0, 0.0)
    live = mm(far_count[...].astype(F32).astype(BF16), receiver.astype(BF16))
    target = jnp.where((slot % depth).astype(F32) < live, far_dst[...].astype(F32), 1.0 * mesh_rows)
    row = iota((2 * slots, slots), 0)
    mine = slot == row // (2 * depth) * depth + row % depth
    source = jnp.sum(jnp.where(mine, far_src[...].astype(F32), 0.0), 1, keepdims=True)
    column = jnp.sum(jnp.where(mine, target, 0.0), 1, keepdims=True)
    pick = jnp.where(iota((2 * slots, grid_rows), 1).astype(F32) == source, 1.0, 0.0).astype(BF16)
    rows = mm(pick, grid[...]).astype(BF16)
    copies[8].wait()
    rows = gelu(mm(rows, w_edge[...]))
    half = channels // 2
    is_first = iota((2 * slots, half), 0) % (2 * depth) < depth
    far[:, :half] = jnp.where(is_first, rows[:, :half], rows[:, half:])
    far[:, half:] = jnp.broadcast_to(column, (2 * slots, LANES)).astype(BF16)
    last = pltpu.make_async_copy(far, far_out, out_sems.at[4])
    last.start()
    for copy in outs + [last]:
        copy.wait()


def own_kernel(
    grid_hbm,
    mesh_in_hbm,
    own_src_hbm,
    own_dst_hbm,
    cot_hbm,
    w_out_hbm,
    w_edge,
    partial_out,
    grad_hbm,
    grid,
    mesh_in,
    own_src,
    own_dst,
    cot,
    w_out,
    grad,
    sems,
):
    grid_rows = grid.shape[0]
    mesh_rows = mesh_in.shape[0]
    copies = start_all(
        [
            (own_src_hbm, own_src),
            (own_dst_hbm, own_dst),
            (cot_hbm, cot),
            (w_out_hbm, w_out),
            (grid_hbm, grid),
            (mesh_in_hbm, mesh_in),
        ],
        sems,
    )
    for copy in copies[:2]:
        copy.wait()
    rows = own_src.shape[0]
    src = onehot_rows([own_src[r : r + 1] for r in range(rows)], grid_rows)
    dst = onehot_rows([own_dst[r : r + 1] for r in range(rows)], mesh_rows)
    counts = mm_nt(dst, src).astype(BF16)
    for copy in copies[2:4]:
        copy.wait()
    grad[...] = mm_nt(cot[...], w_out[...]).astype(BF16)
    out = pltpu.make_async_copy(grad, grad_hbm, sems.at[6])
    out.start()
    for copy in copies[4:]:
        copy.wait()
    active = gelu(mm(grid[...], w_edge[...]))
    partial_out[...] = mesh_in[...].astype(F32) + mm(counts, active)
    out.wait()


def meta_of(message, count):
    return message[BAND : BAND + count].astype(F32).astype(I32)


def side_kernel(count, chip, off, w_edge, partial, partial_out):
    mesh_rows = partial.shape[0]
    uppers, lowers = [], []
    for side in (chip, off):
        meta = meta_of(side, count)
        src = onehot_rows([meta[r : r + 1, :LANES] for r in range(count)], BAND)
        dst = onehot_rows([meta[r : r + 1, LANES : 2 * LANES] for r in range(count)], mesh_rows)
        counts = mm_nt(dst, src)
        upper = counts.astype(BF16)
        uppers.append(upper)
        lowers.append((counts - upper.astype(F32)).astype(BF16))
    active = gelu(mm(jnp.concatenate([chip[:BAND], off[:BAND]], 0), w_edge[...]))
    landing = jnp.concatenate(uppers + lowers, 1)
    partial_out[...] = partial[...] + mm(landing, jnp.concatenate([active, active], 0))


def latent_kernel(depth, far, partial, latent_out, normed_out, normal_out, inv_std_out):
    mesh_rows, channels = partial.shape
    slots = far.shape[0]
    half = channels // 2
    first = far[:, :half]
    second = pltpu.roll(first.astype(F32), slots - depth, 0).astype(BF16)
    target = jnp.transpose(far[:, half:].astype(F32))
    if mesh_rows != LANES:
        target = jnp.broadcast_to(target[:1], (mesh_rows, slots))
    is_row = iota((mesh_rows, slots), 1) % (2 * depth) < depth
    hit = (target == iota((mesh_rows, slots), 0).astype(F32)) & is_row
    landing = jnp.where(hit, 1.0, 0.0).astype(BF16)
    total = partial[...] + mm(landing, jnp.concatenate([first, second], 1))
    latent = total.astype(BF16)
    latent_out[...] = latent
    normal, inv_std = norm_stats(latent)
    normed_out[...] = normal.astype(BF16)
    normal_out[...] = normal
    inv_std_out[...] = jnp.broadcast_to(inv_std, inv_std_out.shape)


def halves(rows, scale=None):
    first = iota(rows.shape, 1) < rows.shape[1] // 2
    if scale is not None:
        rows = rows * jnp.asarray(scale, rows.dtype)
    zero = jnp.zeros_like(rows)
    return jnp.concatenate([jnp.where(first, rows, zero), jnp.where(first, zero, rows)], 0)


def merge(stacked):
    m = stacked.shape[0] // 2
    first = iota((m, stacked.shape[1]), 1) < stacked.shape[1] // 2
    return jnp.where(first, stacked[:m], stacked[m:])


def near_places(m):
    odd = is_odd()
    return (1 - odd) * 2 * m, odd * 2 * m


def project_kernel(
    scale,
    pair,
    count,
    normed,
    chip_first,
    off_first,
    window_hbm,
    grad_hbm,
    w_qkv_hbm,
    qkv_out,
    w_qkv,
    grad_out,
    scores_out,
    products_out,
    bias_out,
    near_bias_out,
    window,
    sems,
):
    m, channels = normed.shape
    width = channels // PIECES
    starts = [part * channels + c * width for c in range(PIECES) for part in range(3)]
    copies = start_all(
        [(window_hbm, window), (grad_hbm, grad_out)]
        + [(w_qkv_hbm.at[:, pl.ds(at, width)], w_qkv.at[:, pl.ds(at, width)]) for at in starts],
        sems,
    )
    copies[0].wait()
    def masks():
        chip_at, off_at = near_places(m)
        reach = [meta_of(side, count)[:8, 2 * LANES : 2 * LANES + m] for side in (chip_first, off_first)]
        reach = jnp.concatenate(reach, 1)
        key_at = iota((m, 2 * m), 0) + m
        lane = iota((m, 2 * m), 1)
        query_at = jnp.where(lane < m, lane + chip_at, lane - m + off_at)
        keep = (key_at >= query_at - reach[0:1, :]) & (key_at <= query_at + reach[1:2, :])
        near_bias_out[...] = jnp.where(keep, 0.0, -jnp.inf).astype(F32)
        me = lax.axis_index("node")
        row = iota((3 * m, m), 0)
        key_at = jnp.where(row < m, row + chip_at, jnp.where(row < 2 * m, row - m + off_at, row - m))
        query_at = iota((3 * m, m), 1) + m
        at_end = (me == 0) | (me == lax.axis_size("node") - 1)
        missing = (row >= m) & (row < 2 * m) & at_end
        keep = (key_at >= query_at - window[0:1, :]) & (key_at <= query_at + window[1:2, :])
        bias = jnp.where(keep & jnp.logical_not(missing), 0.0, -jnp.inf).astype(F32)
        bias_out[...] = jnp.transpose(bias)

    masks()
    copies[1].wait()
    for i, at in enumerate(starts):
        copies[2 + i].wait()
        cols = slice(at, at + width)
        qkv_out[:, cols] = mm(normed[...], w_qkv[:, cols]).astype(BF16)
        for p in range(i // 3 * width // pair, (i // 3 + 1) * width // pair):
            q, k, v = (
                slice(part * channels + p * pair, part * channels + (p + 1) * pair)
                for part in range(3)
            )
            if i % 3 == 1:
                scores_out[p] = mm_nt(halves(qkv_out[:, q], scale), qkv_out[:, k])
            if i % 3 == 2:
                products_out[p] = mm_nt(halves(grad_out[:, q]), qkv_out[:, v])


def attend_kernel(
    scale,
    pair,
    chip_normed,
    off_normed,
    w_qkv,
    own_qkv,
    own_grad,
    own_scores,
    own_products,
    bias,
    w_out_hbm,
    cot_hbm,
    stats_out,
    kv,
    weights_out,
    scores_out,
    near_q,
    w_out,
    cot,
    sems,
):
    fetch = start_all([(w_out_hbm, w_out), (cot_hbm, cot)], sems)
    m, channels = chip_normed.shape
    pairs = channels // pair

    @pl.when(everywhere())
    def _():
        near = jnp.concatenate([chip_normed[...], off_normed[...]], 0)

        def bring(group):
            cols = slice(group * 2 * pair, (group + 1) * 2 * pair)
            near_q[:, cols] = mm(near, w_qkv[:, cols]).astype(BF16) * jnp.asarray(scale, BF16)
            blocks = []
            for part in range(1, 3):
                at = part * channels + group * 2 * pair
                block = mm(near, w_qkv[:, at : at + 2 * pair]).astype(BF16)
                kv[: 2 * m, at - channels : at - channels + 2 * pair] = block
                blocks.append(block)
            return blocks

        brought = {0: bring(0)}
        kv[2 * m :] = own_qkv[:, channels:]
        lane = iota((CHUNK, LANES), 1)
        stats = [jnp.zeros((CHUNK, LANES), F32) for _ in range(2 * m // CHUNK)]

        def near_of(p):
            return [b[:, p % 2 * pair : (p % 2 + 1) * pair] for b in brought[p // 2]]

        def multiply(p):
            cols = slice(p * pair, (p + 1) * pair)
            keys, values = near_of(p)
            return (
                mm_nt(halves(own_qkv[:, cols], scale), keys),
                mm_nt(halves(own_grad[:, cols]), values),
            )

        ahead = multiply(0)
        for p in range(pairs):
            scores, grad_prob = ahead
            if p + 1 < pairs:
                if p % 2 == 0 and p + 2 < pairs:
                    brought[p // 2 + 1] = bring(p // 2 + 1)
                ahead = multiply(p + 1)
            weights, grad_scores = [], []
            for at in range(0, 2 * m, CHUNK):
                part = slice(at, at + CHUNK)
                place = slice(at % m, at % m + CHUNK)
                raw = jnp.concatenate([scores[part], own_scores[p, part]], 1) + bias[place]
                top = jnp.max(raw, 1, keepdims=True)
                shifted = jnp.exp(raw - top)
                inv_sum = 1.0 / jnp.sum(shifted, 1, keepdims=True)
                probs = shifted * inv_sum
                product = jnp.concatenate([grad_prob[part], own_products[p, part]], 1)
                delta = jnp.sum(probs * product, 1, keepdims=True)
                weights.append(probs.astype(BF16))
                grad_scores.append((probs * (product - delta)).astype(BF16))
                for k, column in enumerate((top, inv_sum, delta)):
                    stats[at // CHUNK] = jnp.where(lane == k * pairs + p, column, stats[at // CHUNK])
            weights_out[p] = jnp.concatenate(weights, 0)
            scores_out[p] = jnp.concatenate(grad_scores, 0)
        stats_out[...] = jnp.transpose(jnp.concatenate(stats, 0))[: 3 * pairs]

    for copy in fetch:
        copy.wait()


def product_kernel(
    scale,
    pair,
    weights,
    grad_scores,
    kv,
    own_qkv,
    own_grad,
    latent,
    w_out,
    w_qkv,
    mesh_out_hbm,
    grad_normed,
    grad_key,
    grad_value,
    attention,
    grad_query,
    mesh_out,
    sems,
):
    m, channels = latent.shape
    pairs = channels // pair
    for p in range(pairs):
        cols = slice(p * pair, (p + 1) * pair)
        value = kv[:, channels + p * pair : channels + (p + 1) * pair]
        attention[:, cols] = merge(mm(weights[p], value)).astype(BF16)
    mesh_out[...] = (latent[...].astype(F32) + mm(attention[...], w_out[...])).astype(BF16)
    out = pltpu.make_async_copy(mesh_out, mesh_out_hbm, sems.at[0])
    out.start()

    @pl.when(everywhere())
    def _():
        for p in range(pairs):
            cols = slice(p * pair, (p + 1) * pair)
            grad_query[:, cols] = (merge(mm(grad_scores[p], kv[:, cols])) * scale).astype(BF16)
        for p in range(pairs):
            cols = slice(p * pair, (p + 1) * pair)
            grad_key[:, cols] = mm_tn(grad_scores[p, :, 2 * m :], halves(own_qkv[:, cols], scale))
            grad_value[:, cols] = mm_tn(weights[p, :, 2 * m :], halves(own_grad[:, cols]))
        grad_normed[...] = mm_nt(grad_query[...], w_qkv[:, :channels])

    out.wait()


def finish_kernel(
    pair,
    chip_stats,
    off_stats,
    bias,
    near_q,
    chip_grad,
    off_grad,
    own_qkv,
    grad_key,
    grad_value,
    grad_normed,
    w_qkv,
    normal,
    inv_std,
    cot,
    grad_out,
):
    m, channels = normal.shape
    pairs = channels // pair

    stats = []
    for h in range(2):
        lanes = slice(h * m, (h + 1) * m)
        stats.append(jnp.concatenate([chip_stats[:, lanes], off_stats[:, lanes]], 1))

    def multiply(p):
        cols = slice(p * pair, (p + 1) * pair)
        key2 = halves(own_qkv[:, channels + p * pair : channels + (p + 1) * pair])
        value2 = halves(own_qkv[:, 2 * channels + p * pair : 2 * channels + (p + 1) * pair])
        query = near_q[:, cols]
        grad = jnp.concatenate([chip_grad[:, cols], off_grad[:, cols]], 0)
        return query, grad, mm_nt(key2, query), mm_nt(value2, grad)

    total = grad_normed[...]
    group = 2
    gks, gvs = [], []
    ahead = multiply(0)
    for p in range(pairs):
        cols = slice(p * pair, (p + 1) * pair)
        query, grad, scores, grad_prob = ahead
        if p + 1 < pairs:
            ahead = multiply(p + 1)
        weights, grad_scores = [], []
        for at in range(0, 2 * m, CHUNK):
            part = slice(at, at + CHUNK)
            place = slice(at % m, at % m + CHUNK)
            top, inv_sum, delta = (
                stats[at // m][k * pairs + p : k * pairs + p + 1] for k in range(3)
            )
            probs = jnp.exp(scores[part] + bias[place] - top) * inv_sum
            weights.append(probs.astype(BF16))
            grad_scores.append((probs * (grad_prob[part] - delta)).astype(BF16))
        gk = grad_key[:, cols] + merge(mm(jnp.concatenate(grad_scores, 0), query))
        gv = grad_value[:, cols] + merge(mm(jnp.concatenate(weights, 0), grad))
        gks.append(gk.astype(BF16))
        gvs.append(gv.astype(BF16))
        if len(gks) == group:
            at = channels + (p + 1 - group) * pair
            width = group * pair
            for blocks, start in ((gks, at), (gvs, at + channels)):
                total = total + mm_nt(
                    jnp.concatenate(blocks, 1), w_qkv[:, start : start + width]
                )
            gks, gvs = [], []
    centred = (
        total
        - jnp.mean(total, -1, keepdims=True)
        - normal[...] * jnp.mean(total * normal[...], -1, keepdims=True)
    )
    grad_out[...] = (cot[...].astype(F32) + inv_std[:, :1] * centred).astype(BF16)


def body(
    grid_in,
    mesh_in,
    own_src,
    own_dst,
    side_src,
    side_dst,
    side_count,
    far_src,
    far_dst,
    far_count,
    window,
    cotangent,
    w_edge,
    w_qkv,
    w_out,
):
    devices = lax.axis_size("node")
    grid_rows, channels = grid_in.shape
    m = mesh_in.shape[0]
    far_slots = far_src.shape[0]
    far_depth = far_slots // devices
    head_dim = channels // HEADS
    pair = 2 * head_dim
    pairs = channels // pair
    scale = head_dim ** (-0.5)
    meta_rows = side_src.shape[0] // (2 * LANES)

    side_src, side_dst = side_src.reshape(-1, LANES), side_dst.reshape(-1, LANES)
    own_src, own_dst = own_src.reshape(-1, LANES), own_dst.reshape(-1, LANES)
    far_src, far_dst = far_src.reshape(1, -1), far_dst.reshape(1, -1)
    side_count, far_count = side_count.reshape(1, -1), far_count.reshape(1, -1)
    message = ((BAND + meta_rows, channels), BF16)
    far_block = (2 * far_slots, channels // 2 + LANES)
    far_message, chip_message, off_message, w_edge = call(
        pack_kernel,
        [(far_block, BF16), message, message, (w_edge.shape, BF16)],
        [grid_in, window, side_src, side_dst, side_count, far_src, far_dst, far_count, w_edge],
        hbm=range(9),
        hbm_outs=range(3),
        scratch=like(grid_in, window, side_src, side_dst, side_count, far_src, far_dst, far_count)
        + [
            pltpu.VMEM(far_block, BF16),
            pltpu.VMEM((2, meta_rows, channels), BF16),
            dma(9),
            dma(5),
        ],
        name="pack",
    )
    from_chip, from_off = exchange(chip_message, off_message, "node")
    got_far = lax.all_to_all(
        far_message.reshape(devices, 2 * far_depth, far_block[1]),
        "node",
        split_axis=0,
        concat_axis=0,
        tiled=True,
    ).reshape(far_block)

    rows = ((m, channels), BF16)
    partial, own_grad = call(
        own_kernel,
        [((m, channels), F32), rows],
        [grid_in, mesh_in, own_src, own_dst, cotangent, w_out, w_edge],
        hbm=range(6),
        hbm_outs=(1,),
        scratch=like(grid_in, mesh_in, own_src, own_dst, cotangent, w_out, cotangent) + [dma(7)],
        name="own",
    )
    (partial,) = call(
        functools.partial(side_kernel, meta_rows),
        [((m, channels), F32)],
        [from_chip, from_off, w_edge, partial],
        name="side",
        flops=8 * 10**9,
    )
    latent, normed, normal, inv_std = call(
        functools.partial(latent_kernel, far_depth),
        [rows, rows, ((m, channels), F32), ((m, LANES), F32)],
        [got_far, partial],
        name="latent",
    )
    chip_normed, off_normed = exchange(normed, normed, "node")
    own_block = ((pairs, 2 * m, m), F32)
    own_qkv, w_qkv, own_grad, own_scores, own_products, bias, near_bias = call(
        functools.partial(project_kernel, scale, pair, meta_rows),
        [((m, 3 * channels), BF16), (w_qkv.shape, BF16), rows, own_block, own_block]
        + [((m, 3 * m), F32), ((m, 2 * m), F32)],
        [normed, from_chip, from_off, window, own_grad, w_qkv],
        hbm=(3, 4, 5),
        scratch=like(window) + [dma(3 * PIECES + 2)],
        name="project",
    )
    chip_grad, off_grad = exchange(own_grad, own_grad, "node")
    probs = ((pairs, 2 * m, 3 * m), BF16)
    stats, kv, weights, grad_scores, near_q, w_out, cotangent = call(
        functools.partial(attend_kernel, scale, pair),
        [
            ((3 * pairs, 2 * m), F32),
            ((3 * m, 2 * channels), BF16),
            probs,
            probs,
            ((2 * m, channels), BF16),
            (w_out.shape, BF16),
            rows,
        ],
        [chip_normed, off_normed, w_qkv, own_qkv, own_grad, own_scores, own_products]
        + [bias, w_out, cotangent],
        hbm=(8, 9),
        scratch=[dma(2)],
        name="attend",
    )
    chip_stats, off_stats = exchange(stats, stats, "node")
    mesh_out, grad_normed, grad_key, grad_value = call(
        functools.partial(product_kernel, scale, pair),
        [
            rows,
            ((m, channels), F32),
            ((m, channels), F32),
            ((m, channels), F32),
        ],
        [
            weights,
            grad_scores,
            kv,
            own_qkv,
            own_grad,
            latent,
            w_out,
            w_qkv,
        ],
        hbm_outs=(0,),
        scratch=[pltpu.VMEM((m, channels), BF16)] * 3 + [dma(1)],
        name="product",
    )
    (mesh_grad,) = call(
        functools.partial(finish_kernel, pair),
        [rows],
        [
            chip_stats,
            off_stats,
            near_bias,
            near_q,
            chip_grad,
            off_grad,
            own_qkv,
            grad_key,
            grad_value,
            grad_normed,
            w_qkv,
            normal,
            inv_std,
            cotangent,
        ],
        name="finish",
    )
    return (mesh_out, mesh_grad)


def solution(mesh):
    rows = P(("groups", "node"), None)
    flat = P(("groups", "node"))
    placed = (rows, rows) + (flat,) * 8 + (P(None, ("groups", "node")), rows, P(), P(), P())
    return jax.shard_map(
        body, mesh=mesh, in_specs=placed, out_specs=(rows, rows), check_vma=False
    )
```

```python
import functools

import jax
import jax.numpy as jnp
from jax import lax
from jax.experimental import pallas as pl
from jax.experimental.pallas import tpu as pltpu
from jax.sharding import PartitionSpec as P

HEADS = 16
BAND = 128
LANES = 128
F32 = jnp.float32
BF16 = jnp.bfloat16
I32 = jnp.int32
VMEM_LIMIT = 28 * 2**20
PIECES = 2
PAD = 8
CHUNK = 64


def mm(a, b):
    return lax.dot_general(a, b, (((1,), (0,)), ((), ())), preferred_element_type=F32)


def mm_nt(a, b):
    return lax.dot_general(a, b, (((1,), (1,)), ((), ())), preferred_element_type=F32)


def mm_tn(a, b):
    return lax.dot_general(a, b, (((0,), (0,)), ((), ())), preferred_element_type=F32)


def iota(shape, dim):
    return lax.broadcasted_iota(I32, shape, dim)


def call(kernel, outs, args, hbm=(), hbm_outs=(), scratch=(), name=None, flops=None):
    args = [
        pltpu.with_memory_space_constraint(a, pltpu.HBM) if i in hbm else a
        for i, a in enumerate(args)
    ]

    def specs(count, far):
        return [
            pl.BlockSpec(memory_space=pltpu.HBM if i in far else pltpu.VMEM) for i in range(count)
        ]

    return pl.pallas_call(
        kernel,
        out_shape=[
            (pltpu.HBM if i in hbm_outs else jax.ShapeDtypeStruct)(shape, dtype)
            for i, (shape, dtype) in enumerate(outs)
        ],
        in_specs=specs(len(args), hbm),
        out_specs=specs(len(outs), hbm_outs),
        scratch_shapes=list(scratch),
        compiler_params=pltpu.CompilerParams(vmem_limit_bytes=VMEM_LIMIT),
        cost_estimate=flops and pl.CostEstimate(flops=flops, transcendentals=0, bytes_accessed=0),
        name=name,
    )(*args)


def dma(count):
    return pltpu.SemaphoreType.DMA((count,))


def start_all(pairs, sems):
    copies = [pltpu.make_async_copy(src, dst, sems.at[i]) for i, (src, dst) in enumerate(pairs)]
    for copy in copies:
        copy.start()
    return copies


def like(*arrays):
    return [pltpu.VMEM(a.shape, a.dtype) for a in arrays]


def swap_off(rows, axis):
    n = lax.axis_size(axis)
    pairs = [p for i in range(1, n - 1, 2) for p in ((i, i + 1), (i + 1, i))]
    return lax.ppermute(rows, axis, pairs)


def swap_chip(rows, axis):
    n = lax.axis_size(axis)
    return lax.ppermute(rows, axis, [p for i in range(0, n, 2) for p in ((i, i + 1), (i + 1, i))])


def exchange(chip_message, off_message, axis):
    from_chip = swap_chip(chip_message, axis)
    return from_chip, swap_off(off_message, axis)


def is_odd():
    return lax.axis_index("node") % 2


def everywhere():
    return lax.axis_index("node") >= 0


def gelu(projected):
    x = projected.astype(BF16).astype(F32)
    inner = (2.0 / jnp.pi) ** 0.5 * (x + 0.044715 * (x * x * x))
    return (0.5 * x * (1.0 + jnp.tanh(inner))).astype(BF16)


def onehot_rows(index_rows, count):
    parts = [
        jnp.where(iota((count, row.shape[1]), 0) == row, 1.0, 0.0).astype(BF16)
        for row in index_rows
    ]
    return parts[0] if len(parts) == 1 else jnp.concatenate(parts, 1)


def norm_stats(latent):
    values = latent.astype(F32)
    row_mean = jnp.mean(values, -1, keepdims=True)
    centred = values - row_mean
    variance = jnp.mean(centred * centred, -1, keepdims=True)
    inv_std = lax.rsqrt(variance + 1e-05)
    return centred * inv_std, inv_std


def pack_kernel(
    grid_hbm,
    window_hbm,
    side_src_hbm,
    side_dst_hbm,
    side_count_hbm,
    far_src_hbm,
    far_dst_hbm,
    far_count_hbm,
    w_edge_hbm,
    far_out,
    chip_out,
    off_out,
    w_edge,
    grid,
    window,
    side_src,
    side_dst,
    side_count,
    far_src,
    far_dst,
    far_count,
    far,
    meta,
    sems,
    out_sems,
):
    grid_rows, channels = grid.shape
    mesh_rows = window.shape[1]
    slots = far_src.shape[1]
    devices = far_count.shape[1]
    depth = slots // devices
    first = grid_rows - BAND
    count = side_src.shape[0] // 2
    copies = start_all(
        [
            (side_src_hbm, side_src),
            (side_dst_hbm, side_dst),
            (side_count_hbm, side_count),
            (window_hbm, window),
            (grid_hbm, grid),
            (far_src_hbm, far_src),
            (far_dst_hbm, far_dst),
            (far_count_hbm, far_count),
            (w_edge_hbm, w_edge),
        ],
        sems,
    )
    for copy in copies[:4]:
        copy.wait()
    for k in range(2):
        rank = iota((count, LANES), 0) * LANES + iota((count, LANES), 1)
        src = side_src[k * count : (k + 1) * count] - k * first
        live = rank < side_count[:, k : k + 1]
        dst = jnp.where(live, side_dst[k * count : (k + 1) * count], mesh_rows)
        reach = jnp.concatenate([window[...], jnp.zeros((count - 2, mesh_rows), I32)], 0)
        blank = jnp.zeros((count, channels - 2 * LANES - mesh_rows), I32)
        meta[k] = jnp.concatenate([src, dst, reach, blank], 1).astype(F32).astype(BF16)
    copies[4].wait()
    odd = is_odd()
    outs = start_all(
        [
            pair
            for k, out in ((1 - odd, chip_out), (odd, off_out))
            for pair in (
                (grid.at[pl.ds(pl.multiple_of(k * first, BAND), BAND)], out.at[pl.ds(0, BAND)]),
                (meta.at[k], out.at[pl.ds(BAND, count)]),
            )
        ],
        out_sems,
    )
    for copy in copies[5:8]:
        copy.wait()
    slot = iota((1, slots), 1)
    receiver = jnp.where(iota((devices, slots), 0) == iota((devices, slots), 1) // depth, 1.0, 0.0)
    live = mm(far_count[...].astype(F32).astype(BF16), receiver.astype(BF16))
    target = jnp.where((slot % depth).astype(F32) < live, far_dst[...].astype(F32), 1.0 * mesh_rows)
    row = iota((2 * slots, slots), 0)
    mine = slot == row // (2 * depth) * depth + row % depth
    source = jnp.sum(jnp.where(mine, far_src[...].astype(F32), 0.0), 1, keepdims=True)
    column = jnp.sum(jnp.where(mine, target, 0.0), 1, keepdims=True)
    pick = jnp.where(iota((2 * slots, grid_rows), 1).astype(F32) == source, 1.0, 0.0).astype(BF16)
    rows = mm(pick, grid[...]).astype(BF16)
    copies[8].wait()
    rows = gelu(mm(rows, w_edge[...]))
    half = channels // 2
    is_first = iota((2 * slots, half), 0) % (2 * depth) < depth
    far[:, :half] = jnp.where(is_first, rows[:, :half], rows[:, half:])
    far[:, half:] = jnp.broadcast_to(column, (2 * slots, LANES)).astype(BF16)
    last = pltpu.make_async_copy(far, far_out, out_sems.at[4])
    last.start()
    for copy in outs + [last]:
        copy.wait()


def own_kernel(
    grid_hbm,
    mesh_in_hbm,
    own_src_hbm,
    own_dst_hbm,
    cot_hbm,
    w_out_hbm,
    w_edge,
    partial_out,
    grad_hbm,
    grid,
    mesh_in,
    own_src,
    own_dst,
    cot,
    w_out,
    grad,
    sems,
):
    grid_rows = grid.shape[0]
    mesh_rows = mesh_in.shape[0]
    copies = start_all(
        [
            (own_src_hbm, own_src),
            (own_dst_hbm, own_dst),
            (cot_hbm, cot),
            (w_out_hbm, w_out),
            (grid_hbm, grid),
            (mesh_in_hbm, mesh_in),
        ],
        sems,
    )
    for copy in copies[:2]:
        copy.wait()
    rows = own_src.shape[0]
    src = onehot_rows([own_src[r : r + 1] for r in range(rows)], grid_rows)
    dst = onehot_rows([own_dst[r : r + 1] for r in range(rows)], mesh_rows)
    counts = mm_nt(dst, src).astype(BF16)
    for copy in copies[2:4]:
        copy.wait()
    grad[...] = mm_nt(cot[...], w_out[...]).astype(BF16)
    out = pltpu.make_async_copy(grad, grad_hbm, sems.at[6])
    out.start()
    for copy in copies[4:]:
        copy.wait()
    active = gelu(mm(grid[...], w_edge[...]))
    partial_out[...] = mesh_in[...].astype(F32) + mm(counts, active)
    out.wait()


def meta_of(message, count):
    return message[BAND : BAND + count].astype(F32).astype(I32)


def side_kernel(count, chip, off, w_edge, partial, partial_out):
    mesh_rows = partial.shape[0]
    uppers, lowers = [], []
    for side in (chip, off):
        meta = meta_of(side, count)
        src = onehot_rows([meta[r : r + 1, :LANES] for r in range(count)], BAND)
        dst = onehot_rows([meta[r : r + 1, LANES : 2 * LANES] for r in range(count)], mesh_rows)
        counts = mm_nt(dst, src)
        upper = counts.astype(BF16)
        uppers.append(upper)
        lowers.append((counts - upper.astype(F32)).astype(BF16))
    active = gelu(mm(jnp.concatenate([chip[:BAND], off[:BAND]], 0), w_edge[...]))
    landing = jnp.concatenate(uppers + lowers, 1)
    partial_out[...] = partial[...] + mm(landing, jnp.concatenate([active, active], 0))


def latent_kernel(
    depth, far, partial, latent_out, normed_out, off_out, normal_out, inv_std_out
):
    mesh_rows, channels = partial.shape
    slots = far.shape[0]
    half = channels // 2
    first = far[:, :half]
    second = pltpu.roll(first.astype(F32), slots - depth, 0).astype(BF16)
    target = jnp.transpose(far[:, half:].astype(F32))
    if mesh_rows != LANES:
        target = jnp.broadcast_to(target[:1], (mesh_rows, slots))
    is_row = iota((mesh_rows, slots), 1) % (2 * depth) < depth
    hit = (target == iota((mesh_rows, slots), 0).astype(F32)) & is_row
    landing = jnp.where(hit, 1.0, 0.0).astype(BF16)
    total = partial[...] + mm(landing, jnp.concatenate([first, second], 1))
    latent = total.astype(BF16)
    latent_out[...] = latent
    normal, inv_std = norm_stats(latent)
    normed = normal.astype(BF16)
    normed_out[...] = normed
    off_out[...] = jnp.concatenate([normed, jnp.zeros((PAD, channels), BF16)], 0)
    normal_out[...] = normal
    inv_std_out[...] = jnp.broadcast_to(inv_std, inv_std_out.shape)


def halves(rows, scale=None):
    first = iota(rows.shape, 1) < rows.shape[1] // 2
    if scale is not None:
        rows = rows * jnp.asarray(scale, rows.dtype)
    zero = jnp.zeros_like(rows)
    return jnp.concatenate([jnp.where(first, rows, zero), jnp.where(first, zero, rows)], 0)


def merge(stacked):
    m = stacked.shape[0] // 2
    first = iota((m, stacked.shape[1]), 1) < stacked.shape[1] // 2
    return jnp.where(first, stacked[:m], stacked[m:])


def near_places(m):
    odd = is_odd()
    return (1 - odd) * 2 * m, odd * 2 * m


def project_kernel(
    scale,
    pair,
    count,
    normed,
    chip_first,
    off_first,
    window_hbm,
    grad_hbm,
    w_qkv_hbm,
    qkv_out,
    w_qkv,
    grad_out,
    scores_out,
    products_out,
    bias_out,
    near_bias_out,
    normed_out,
    window,
    sems,
):
    m, channels = normed.shape
    normed_out[...] = normed[...]
    width = channels // PIECES
    starts = [part * channels + c * width for c in range(PIECES) for part in range(3)]
    copies = start_all(
        [(window_hbm, window), (grad_hbm, grad_out)]
        + [(w_qkv_hbm.at[:, pl.ds(at, width)], w_qkv.at[:, pl.ds(at, width)]) for at in starts],
        sems,
    )
    copies[0].wait()
    def masks():
        chip_at, off_at = near_places(m)
        reach = [meta_of(side, count)[:8, 2 * LANES : 2 * LANES + m] for side in (chip_first, off_first)]
        reach = jnp.concatenate(reach, 1)
        key_at = iota((m, 2 * m), 0) + m
        lane = iota((m, 2 * m), 1)
        query_at = jnp.where(lane < m, lane + chip_at, lane - m + off_at)
        keep = (key_at >= query_at - reach[0:1, :]) & (key_at <= query_at + reach[1:2, :])
        near_bias_out[...] = jnp.where(keep, 0.0, -jnp.inf).astype(F32)
        me = lax.axis_index("node")
        row = iota((3 * m, m), 0)
        key_at = jnp.where(row < m, row + chip_at, jnp.where(row < 2 * m, row - m + off_at, row - m))
        query_at = iota((3 * m, m), 1) + m
        at_end = (me == 0) | (me == lax.axis_size("node") - 1)
        missing = (row >= m) & (row < 2 * m) & at_end
        keep = (key_at >= query_at - window[0:1, :]) & (key_at <= query_at + window[1:2, :])
        bias = jnp.where(keep & jnp.logical_not(missing), 0.0, -jnp.inf).astype(F32)
        bias_out[...] = jnp.transpose(bias)

    masks()
    copies[1].wait()
    for i, at in enumerate(starts):
        copies[2 + i].wait()
        cols = slice(at, at + width)
        qkv_out[:, cols] = mm(normed[...], w_qkv[:, cols]).astype(BF16)
        for p in range(i // 3 * width // pair, (i // 3 + 1) * width // pair):
            q, k, v = (
                slice(part * channels + p * pair, part * channels + (p + 1) * pair)
                for part in range(3)
            )
            if i % 3 == 1:
                scores_out[p] = mm_nt(halves(qkv_out[:, q], scale), qkv_out[:, k])
            if i % 3 == 2:
                products_out[p] = mm_nt(halves(grad_out[:, q]), qkv_out[:, v])


def attend_kernel(
    scale,
    pair,
    chip_normed,
    off_normed,
    w_qkv,
    own_qkv,
    own_grad,
    own_scores,
    own_products,
    bias,
    w_out_hbm,
    cot_hbm,
    stats_out,
    kv,
    weights_out,
    scores_out,
    near_q,
    w_out,
    cot,
    sems,
):
    fetch = start_all([(w_out_hbm, w_out), (cot_hbm, cot)], sems)
    m, channels = chip_normed.shape
    pairs = channels // pair

    @pl.when(everywhere())
    def _():
        near = jnp.concatenate([chip_normed[...], off_normed[:m]], 0)

        def bring(group):
            cols = slice(group * 2 * pair, (group + 1) * 2 * pair)
            near_q[:, cols] = mm(near, w_qkv[:, cols]).astype(BF16) * jnp.asarray(scale, BF16)
            blocks = []
            for part in range(1, 3):
                at = part * channels + group * 2 * pair
                block = mm(near, w_qkv[:, at : at + 2 * pair]).astype(BF16)
                kv[: 2 * m, at - channels : at - channels + 2 * pair] = block
                blocks.append(block)
            return blocks

        brought = {0: bring(0)}
        kv[2 * m :] = own_qkv[:, channels:]
        lane = iota((CHUNK, LANES), 1)
        stats = [jnp.zeros((CHUNK, LANES), F32) for _ in range(2 * m // CHUNK)]

        def near_of(p):
            return [b[:, p % 2 * pair : (p % 2 + 1) * pair] for b in brought[p // 2]]

        def multiply(p):
            cols = slice(p * pair, (p + 1) * pair)
            keys, values = near_of(p)
            return (
                mm_nt(halves(own_qkv[:, cols], scale), keys),
                mm_nt(halves(own_grad[:, cols]), values),
            )

        ahead = multiply(0)
        for p in range(pairs):
            scores, grad_prob = ahead
            if p + 1 < pairs:
                if p % 2 == 0 and p + 2 < pairs:
                    brought[p // 2 + 1] = bring(p // 2 + 1)
                ahead = multiply(p + 1)
            weights, grad_scores = [], []
            for at in range(0, 2 * m, CHUNK):
                part = slice(at, at + CHUNK)
                place = slice(at % m, at % m + CHUNK)
                raw = jnp.concatenate([scores[part], own_scores[p, part]], 1) + bias[place]
                top = jnp.max(raw, 1, keepdims=True)
                shifted = jnp.exp(raw - top)
                inv_sum = 1.0 / jnp.sum(shifted, 1, keepdims=True)
                probs = shifted * inv_sum
                product = jnp.concatenate([grad_prob[part], own_products[p, part]], 1)
                delta = jnp.sum(probs * product, 1, keepdims=True)
                weights.append(probs.astype(BF16))
                grad_scores.append((probs * (product - delta)).astype(BF16))
                for k, column in enumerate((top, inv_sum, delta)):
                    stats[at // CHUNK] = jnp.where(lane == k * pairs + p, column, stats[at // CHUNK])
            weights_out[p] = jnp.concatenate(weights, 0)
            scores_out[p] = jnp.concatenate(grad_scores, 0)
        stats_out[...] = jnp.transpose(jnp.concatenate(stats, 0))[: 3 * pairs]

    for copy in fetch:
        copy.wait()


def product_kernel(
    scale,
    pair,
    weights,
    grad_scores,
    kv,
    own_qkv,
    own_grad,
    latent,
    w_out,
    w_qkv,
    mesh_out_hbm,
    grad_normed,
    grad_key,
    grad_value,
    attention,
    grad_query,
    mesh_out,
    sems,
):
    m, channels = latent.shape
    pairs = channels // pair
    for p in range(pairs):
        cols = slice(p * pair, (p + 1) * pair)
        value = kv[:, channels + p * pair : channels + (p + 1) * pair]
        attention[:, cols] = merge(mm(weights[p], value)).astype(BF16)
    mesh_out[...] = (latent[...].astype(F32) + mm(attention[...], w_out[...])).astype(BF16)
    out = pltpu.make_async_copy(mesh_out, mesh_out_hbm, sems.at[0])
    out.start()

    @pl.when(everywhere())
    def _():
        for p in range(pairs):
            cols = slice(p * pair, (p + 1) * pair)
            grad_query[:, cols] = (merge(mm(grad_scores[p], kv[:, cols])) * scale).astype(BF16)
        for p in range(pairs):
            cols = slice(p * pair, (p + 1) * pair)
            grad_key[:, cols] = mm_tn(grad_scores[p, :, 2 * m :], halves(own_qkv[:, cols], scale))
            grad_value[:, cols] = mm_tn(weights[p, :, 2 * m :], halves(own_grad[:, cols]))
        grad_normed[...] = mm_nt(grad_query[...], w_qkv[:, :channels])

    out.wait()


def finish_kernel(
    pair,
    chip_stats,
    off_stats,
    bias,
    near_q,
    chip_grad,
    off_grad,
    own_qkv,
    grad_key,
    grad_value,
    grad_normed,
    w_qkv,
    normal,
    inv_std,
    cot,
    grad_out,
):
    m, channels = normal.shape
    pairs = channels // pair

    stats = []
    for h in range(2):
        lanes = slice(h * m, (h + 1) * m)
        stats.append(jnp.concatenate([chip_stats[:, lanes], off_stats[:, lanes]], 1))

    def multiply(p):
        cols = slice(p * pair, (p + 1) * pair)
        key2 = halves(own_qkv[:, channels + p * pair : channels + (p + 1) * pair])
        value2 = halves(own_qkv[:, 2 * channels + p * pair : 2 * channels + (p + 1) * pair])
        query = near_q[:, cols]
        grad = jnp.concatenate([chip_grad[:, cols], off_grad[:, cols]], 0)
        return query, grad, mm_nt(key2, query), mm_nt(value2, grad)

    total = grad_normed[...]
    group = 2
    gks, gvs = [], []
    ahead = multiply(0)
    for p in range(pairs):
        cols = slice(p * pair, (p + 1) * pair)
        query, grad, scores, grad_prob = ahead
        if p + 1 < pairs:
            ahead = multiply(p + 1)
        weights, grad_scores = [], []
        for at in range(0, 2 * m, CHUNK):
            part = slice(at, at + CHUNK)
            place = slice(at % m, at % m + CHUNK)
            top, inv_sum, delta = (
                stats[at // m][k * pairs + p : k * pairs + p + 1] for k in range(3)
            )
            probs = jnp.exp(scores[part] + bias[place] - top) * inv_sum
            weights.append(probs.astype(BF16))
            grad_scores.append((probs * (grad_prob[part] - delta)).astype(BF16))
        gk = grad_key[:, cols] + merge(mm(jnp.concatenate(grad_scores, 0), query))
        gv = grad_value[:, cols] + merge(mm(jnp.concatenate(weights, 0), grad))
        gks.append(gk.astype(BF16))
        gvs.append(gv.astype(BF16))
        if len(gks) == group:
            at = channels + (p + 1 - group) * pair
            width = group * pair
            for blocks, start in ((gks, at), (gvs, at + channels)):
                total = total + mm_nt(
                    jnp.concatenate(blocks, 1), w_qkv[:, start : start + width]
                )
            gks, gvs = [], []
    centred = (
        total
        - jnp.mean(total, -1, keepdims=True)
        - normal[...] * jnp.mean(total * normal[...], -1, keepdims=True)
    )
    grad_out[...] = (cot[...].astype(F32) + inv_std[:, :1] * centred).astype(BF16)


def body(
    grid_in,
    mesh_in,
    own_src,
    own_dst,
    side_src,
    side_dst,
    side_count,
    far_src,
    far_dst,
    far_count,
    window,
    cotangent,
    w_edge,
    w_qkv,
    w_out,
):
    devices = lax.axis_size("node")
    grid_rows, channels = grid_in.shape
    m = mesh_in.shape[0]
    far_slots = far_src.shape[0]
    far_depth = far_slots // devices
    head_dim = channels // HEADS
    pair = 2 * head_dim
    pairs = channels // pair
    scale = head_dim ** (-0.5)
    meta_rows = side_src.shape[0] // (2 * LANES)

    side_src, side_dst = side_src.reshape(-1, LANES), side_dst.reshape(-1, LANES)
    own_src, own_dst = own_src.reshape(-1, LANES), own_dst.reshape(-1, LANES)
    far_src, far_dst = far_src.reshape(1, -1), far_dst.reshape(1, -1)
    side_count, far_count = side_count.reshape(1, -1), far_count.reshape(1, -1)
    message = ((BAND + meta_rows, channels), BF16)
    far_block = (2 * far_slots, channels // 2 + LANES)
    far_message, chip_message, off_message, w_edge = call(
        pack_kernel,
        [(far_block, BF16), message, message, (w_edge.shape, BF16)],
        [grid_in, window, side_src, side_dst, side_count, far_src, far_dst, far_count, w_edge],
        hbm=range(9),
        hbm_outs=range(3),
        scratch=like(grid_in, window, side_src, side_dst, side_count, far_src, far_dst, far_count)
        + [
            pltpu.VMEM(far_block, BF16),
            pltpu.VMEM((2, meta_rows, channels), BF16),
            dma(9),
            dma(5),
        ],
        name="pack",
    )
    from_chip, from_off = exchange(chip_message, off_message, "node")
    got_far = lax.all_to_all(
        far_message.reshape(devices, 2 * far_depth, far_block[1]),
        "node",
        split_axis=0,
        concat_axis=0,
        tiled=True,
    ).reshape(far_block)

    rows = ((m, channels), BF16)
    partial, own_grad = call(
        own_kernel,
        [((m, channels), F32), rows],
        [grid_in, mesh_in, own_src, own_dst, cotangent, w_out, w_edge],
        hbm=range(6),
        hbm_outs=(1,),
        scratch=like(grid_in, mesh_in, own_src, own_dst, cotangent, w_out, cotangent) + [dma(7)],
        name="own",
    )
    (partial,) = call(
        functools.partial(side_kernel, meta_rows),
        [((m, channels), F32)],
        [from_chip, from_off, w_edge, partial],
        name="side",
        flops=8 * 10**9,
    )
    latent, normed, off_message, normal, inv_std = call(
        functools.partial(latent_kernel, far_depth),
        [rows, rows, ((m + PAD, channels), BF16), ((m, channels), F32), ((m, LANES), F32)],
        [got_far, partial],
        name="latent",
    )
    off_normed = swap_off(off_message, "node")
    own_block = ((pairs, 2 * m, m), F32)
    own_qkv, w_qkv, own_grad, own_scores, own_products, bias, near_bias, normed = call(
        functools.partial(project_kernel, scale, pair, meta_rows),
        [((m, 3 * channels), BF16), (w_qkv.shape, BF16), rows, own_block, own_block]
        + [((m, 3 * m), F32), ((m, 2 * m), F32), rows],
        [normed, from_chip, from_off, window, own_grad, w_qkv],
        hbm=(3, 4, 5),
        scratch=like(window) + [dma(3 * PIECES + 2)],
        name="project",
    )
    chip_normed = swap_chip(normed, "node")
    chip_grad, off_grad = exchange(own_grad, own_grad, "node")
    probs = ((pairs, 2 * m, 3 * m), BF16)
    stats, kv, weights, grad_scores, near_q, w_out, cotangent = call(
        functools.partial(attend_kernel, scale, pair),
        [
            ((3 * pairs, 2 * m), F32),
            ((3 * m, 2 * channels), BF16),
            probs,
            probs,
            ((2 * m, channels), BF16),
            (w_out.shape, BF16),
            rows,
        ],
        [chip_normed, off_normed, w_qkv, own_qkv, own_grad, own_scores, own_products]
        + [bias, w_out, cotangent],
        hbm=(8, 9),
        scratch=[dma(2)],
        name="attend",
    )
    chip_stats, off_stats = exchange(stats, stats, "node")
    mesh_out, grad_normed, grad_key, grad_value = call(
        functools.partial(product_kernel, scale, pair),
        [
            rows,
            ((m, channels), F32),
            ((m, channels), F32),
            ((m, channels), F32),
        ],
        [
            weights,
            grad_scores,
            kv,
            own_qkv,
            own_grad,
            latent,
            w_out,
            w_qkv,
        ],
        hbm_outs=(0,),
        scratch=[pltpu.VMEM((m, channels), BF16)] * 3 + [dma(1)],
        name="product",
    )
    (mesh_grad,) = call(
        functools.partial(finish_kernel, pair),
        [rows],
        [
            chip_stats,
            off_stats,
            near_bias,
            near_q,
            chip_grad,
            off_grad,
            own_qkv,
            grad_key,
            grad_value,
            grad_normed,
            w_qkv,
            normal,
            inv_std,
            cotangent,
        ],
        name="finish",
    )
    return (mesh_out, mesh_grad)


def solution(mesh):
    rows = P(("groups", "node"), None)
    flat = P(("groups", "node"))
    placed = (rows, rows) + (flat,) * 8 + (P(None, ("groups", "node")), rows, P(), P(), P())
    return jax.shard_map(
        body, mesh=mesh, in_specs=placed, out_specs=(rows, rows), check_vma=False
    )
```

```python
import functools

import jax
import jax.numpy as jnp
from jax import lax
from jax.experimental import pallas as pl
from jax.experimental.pallas import tpu as pltpu
from jax.sharding import PartitionSpec as P

HEADS = 16
BAND = 128
LANES = 128
F32 = jnp.float32
BF16 = jnp.bfloat16
I32 = jnp.int32
VMEM_LIMIT = 28 * 2**20
PIECES = 2
PAD = 8
CHUNK = 64


def mm(a, b):
    return lax.dot_general(a, b, (((1,), (0,)), ((), ())), preferred_element_type=F32)


def mm_nt(a, b):
    return lax.dot_general(a, b, (((1,), (1,)), ((), ())), preferred_element_type=F32)


def mm_tn(a, b):
    return lax.dot_general(a, b, (((0,), (0,)), ((), ())), preferred_element_type=F32)


def iota(shape, dim):
    return lax.broadcasted_iota(I32, shape, dim)


def call(
    kernel, outs, args, hbm=(), hbm_outs=(), anywhere=(), scratch=(), name=None, flops=None
):
    args = [
        pltpu.with_memory_space_constraint(a, pltpu.HBM) if i in hbm else a
        for i, a in enumerate(args)
    ]

    def specs(count, far, free=()):
        return [
            pl.BlockSpec(
                memory_space=pltpu.HBM if i in far else pl.ANY if i in free else pltpu.VMEM
            )
            for i in range(count)
        ]

    return pl.pallas_call(
        kernel,
        out_shape=[
            (pltpu.HBM if i in hbm_outs else jax.ShapeDtypeStruct)(shape, dtype)
            for i, (shape, dtype) in enumerate(outs)
        ],
        in_specs=specs(len(args), hbm, anywhere),
        out_specs=specs(len(outs), hbm_outs),
        scratch_shapes=list(scratch),
        compiler_params=pltpu.CompilerParams(vmem_limit_bytes=VMEM_LIMIT),
        cost_estimate=flops and pl.CostEstimate(flops=flops, transcendentals=0, bytes_accessed=0),
        name=name,
    )(*args)


def dma(count):
    return pltpu.SemaphoreType.DMA((count,))


def start_all(pairs, sems):
    copies = [pltpu.make_async_copy(src, dst, sems.at[i]) for i, (src, dst) in enumerate(pairs)]
    for copy in copies:
        copy.start()
    return copies


def like(*arrays):
    return [pltpu.VMEM(a.shape, a.dtype) for a in arrays]


def swap_off(rows, axis):
    n = lax.axis_size(axis)
    pairs = [p for i in range(1, n - 1, 2) for p in ((i, i + 1), (i + 1, i))]
    return lax.ppermute(rows, axis, pairs)


def swap_chip(rows, axis):
    n = lax.axis_size(axis)
    return lax.ppermute(rows, axis, [p for i in range(0, n, 2) for p in ((i, i + 1), (i + 1, i))])


def exchange(chip_message, off_message, axis):
    from_chip = swap_chip(chip_message, axis)
    return from_chip, swap_off(off_message, axis)


def is_odd():
    return lax.axis_index("node") % 2


def everywhere():
    return lax.axis_index("node") >= 0


def gelu(projected):
    x = projected.astype(BF16).astype(F32)
    inner = (2.0 / jnp.pi) ** 0.5 * (x + 0.044715 * (x * x * x))
    return (0.5 * x * (1.0 + jnp.tanh(inner))).astype(BF16)


def onehot_rows(index_rows, count):
    parts = [
        jnp.where(iota((count, row.shape[1]), 0) == row, 1.0, 0.0).astype(BF16)
        for row in index_rows
    ]
    return parts[0] if len(parts) == 1 else jnp.concatenate(parts, 1)


def norm_stats(latent):
    values = latent.astype(F32)
    row_mean = jnp.mean(values, -1, keepdims=True)
    centred = values - row_mean
    variance = jnp.mean(centred * centred, -1, keepdims=True)
    inv_std = lax.rsqrt(variance + 1e-05)
    return centred * inv_std, inv_std


def pack_kernel(
    grid_hbm,
    window_hbm,
    side_src_hbm,
    side_dst_hbm,
    side_count_hbm,
    far_src_hbm,
    far_dst_hbm,
    far_count_hbm,
    w_edge_hbm,
    far_out,
    chip_out,
    off_out,
    w_edge,
    grid,
    window,
    side_src,
    side_dst,
    side_count,
    far_src,
    far_dst,
    far_count,
    far,
    meta,
    sems,
    out_sems,
):
    grid_rows, channels = grid.shape
    mesh_rows = window.shape[1]
    slots = far_src.shape[1]
    devices = far_count.shape[1]
    depth = slots // devices
    first = grid_rows - BAND
    count = side_src.shape[0] // 2
    copies = start_all(
        [
            (side_src_hbm, side_src),
            (side_dst_hbm, side_dst),
            (side_count_hbm, side_count),
            (window_hbm, window),
            (grid_hbm, grid),
            (far_src_hbm, far_src),
            (far_dst_hbm, far_dst),
            (far_count_hbm, far_count),
            (w_edge_hbm, w_edge),
        ],
        sems,
    )
    for copy in copies[:4]:
        copy.wait()
    for k in range(2):
        rank = iota((count, LANES), 0) * LANES + iota((count, LANES), 1)
        src = side_src[k * count : (k + 1) * count] - k * first
        live = rank < side_count[:, k : k + 1]
        dst = jnp.where(live, side_dst[k * count : (k + 1) * count], mesh_rows)
        reach = jnp.concatenate([window[...], jnp.zeros((count - 2, mesh_rows), I32)], 0)
        blank = jnp.zeros((count, channels - 2 * LANES - mesh_rows), I32)
        meta[k] = jnp.concatenate([src, dst, reach, blank], 1).astype(F32).astype(BF16)
    copies[4].wait()
    odd = is_odd()
    outs = start_all(
        [
            pair
            for k, out in ((1 - odd, chip_out), (odd, off_out))
            for pair in (
                (grid.at[pl.ds(pl.multiple_of(k * first, BAND), BAND)], out.at[pl.ds(0, BAND)]),
                (meta.at[k], out.at[pl.ds(BAND, count)]),
            )
        ],
        out_sems,
    )
    for copy in copies[5:8]:
        copy.wait()
    slot = iota((1, slots), 1)
    receiver = jnp.where(iota((devices, slots), 0) == iota((devices, slots), 1) // depth, 1.0, 0.0)
    live = mm(far_count[...].astype(F32).astype(BF16), receiver.astype(BF16))
    target = jnp.where((slot % depth).astype(F32) < live, far_dst[...].astype(F32), 1.0 * mesh_rows)
    row = iota((2 * slots, slots), 0)
    mine = slot == row // (2 * depth) * depth + row % depth
    source = jnp.sum(jnp.where(mine, far_src[...].astype(F32), 0.0), 1, keepdims=True)
    column = jnp.sum(jnp.where(mine, target, 0.0), 1, keepdims=True)
    pick = jnp.where(iota((2 * slots, grid_rows), 1).astype(F32) == source, 1.0, 0.0).astype(BF16)
    rows = mm(pick, grid[...]).astype(BF16)
    copies[8].wait()
    rows = gelu(mm(rows, w_edge[...]))
    half = channels // 2
    is_first = iota((2 * slots, half), 0) % (2 * depth) < depth
    far[:, :half] = jnp.where(is_first, rows[:, :half], rows[:, half:])
    far[:, half:] = jnp.broadcast_to(column, (2 * slots, LANES)).astype(BF16)
    last = pltpu.make_async_copy(far, far_out, out_sems.at[4])
    last.start()
    for copy in outs + [last]:
        copy.wait()


def own_kernel(
    grid_hbm,
    mesh_in_hbm,
    own_src_hbm,
    own_dst_hbm,
    cot_hbm,
    w_out_hbm,
    w_edge,
    chip_message,
    partial_out,
    grad_hbm,
    grid,
    mesh_in,
    own_src,
    own_dst,
    cot,
    w_out,
    grad,
    sems,
):
    grid_rows = grid.shape[0]
    mesh_rows = mesh_in.shape[0]
    copies = start_all(
        [
            (own_src_hbm, own_src),
            (own_dst_hbm, own_dst),
            (cot_hbm, cot),
            (w_out_hbm, w_out),
            (grid_hbm, grid),
            (mesh_in_hbm, mesh_in),
        ],
        sems,
    )
    for copy in copies[:2]:
        copy.wait()
    rows = own_src.shape[0]
    src = onehot_rows([own_src[r : r + 1] for r in range(rows)], grid_rows)
    dst = onehot_rows([own_dst[r : r + 1] for r in range(rows)], mesh_rows)
    counts = mm_nt(dst, src).astype(BF16)
    for copy in copies[2:4]:
        copy.wait()
    grad[...] = mm_nt(cot[...], w_out[...]).astype(BF16)
    out = pltpu.make_async_copy(grad, grad_hbm, sems.at[6])
    out.start()
    for copy in copies[4:]:
        copy.wait()
    active = gelu(mm(grid[...], w_edge[...]))
    partial_out[...] = mesh_in[...].astype(F32) + mm(counts, active)
    out.wait()


def meta_of(message, count):
    return message[BAND : BAND + count].astype(F32).astype(I32)


def side_kernel(count, chip, off, w_edge, partial, partial_out):
    mesh_rows = partial.shape[0]
    uppers, lowers = [], []
    for side in (chip, off):
        meta = meta_of(side, count)
        src = onehot_rows([meta[r : r + 1, :LANES] for r in range(count)], BAND)
        dst = onehot_rows([meta[r : r + 1, LANES : 2 * LANES] for r in range(count)], mesh_rows)
        counts = mm_nt(dst, src)
        upper = counts.astype(BF16)
        uppers.append(upper)
        lowers.append((counts - upper.astype(F32)).astype(BF16))
    active = gelu(mm(jnp.concatenate([chip[:BAND], off[:BAND]], 0), w_edge[...]))
    landing = jnp.concatenate(uppers + lowers, 1)
    partial_out[...] = partial[...] + mm(landing, jnp.concatenate([active, active], 0))


def latent_kernel(
    depth, far, partial, latent_out, normed_out, off_out, normal_out, inv_std_out
):
    mesh_rows, channels = partial.shape
    slots = far.shape[0]
    half = channels // 2
    first = far[:, :half]
    second = pltpu.roll(first.astype(F32), slots - depth, 0).astype(BF16)
    target = jnp.transpose(far[:, half:].astype(F32))
    if mesh_rows != LANES:
        target = jnp.broadcast_to(target[:1], (mesh_rows, slots))
    is_row = iota((mesh_rows, slots), 1) % (2 * depth) < depth
    hit = (target == iota((mesh_rows, slots), 0).astype(F32)) & is_row
    landing = jnp.where(hit, 1.0, 0.0).astype(BF16)
    total = partial[...] + mm(landing, jnp.concatenate([first, second], 1))
    latent = total.astype(BF16)
    latent_out[...] = latent
    normal, inv_std = norm_stats(latent)
    normed = normal.astype(BF16)
    normed_out[...] = normed
    off_out[...] = jnp.concatenate([normed, jnp.zeros((PAD, channels), BF16)], 0)
    normal_out[...] = normal
    inv_std_out[...] = jnp.broadcast_to(inv_std, inv_std_out.shape)


def halves(rows, scale=None):
    first = iota(rows.shape, 1) < rows.shape[1] // 2
    if scale is not None:
        rows = rows * jnp.asarray(scale, rows.dtype)
    zero = jnp.zeros_like(rows)
    return jnp.concatenate([jnp.where(first, rows, zero), jnp.where(first, zero, rows)], 0)


def merge(stacked):
    m = stacked.shape[0] // 2
    first = iota((m, stacked.shape[1]), 1) < stacked.shape[1] // 2
    return jnp.where(first, stacked[:m], stacked[m:])


def near_places(m):
    odd = is_odd()
    return (1 - odd) * 2 * m, odd * 2 * m


def project_kernel(
    scale,
    pair,
    count,
    normed,
    chip_first,
    off_first,
    window_hbm,
    grad_hbm,
    w_qkv_hbm,
    chip_grad,
    off_grad,
    qkv_out,
    w_qkv,
    grad_out,
    near_grad,
    scores_out,
    products_out,
    bias_out,
    near_bias_out,
    normed_out,
    window,
    sems,
):
    m, channels = normed.shape
    normed_out[...] = normed[...]
    width = channels // PIECES
    starts = [part * channels + c * width for c in range(PIECES) for part in range(3)]
    copies = start_all(
        [(window_hbm, window), (grad_hbm, grad_out)]
        + [(w_qkv_hbm.at[:, pl.ds(at, width)], w_qkv.at[:, pl.ds(at, width)]) for at in starts]
        + [(chip_grad, near_grad.at[pl.ds(0, m)]), (off_grad, near_grad.at[pl.ds(m, m)])],
        sems,
    )
    copies[0].wait()
    def masks():
        chip_at, off_at = near_places(m)
        reach = [meta_of(side, count)[:8, 2 * LANES : 2 * LANES + m] for side in (chip_first, off_first)]
        reach = jnp.concatenate(reach, 1)
        key_at = iota((m, 2 * m), 0) + m
        lane = iota((m, 2 * m), 1)
        query_at = jnp.where(lane < m, lane + chip_at, lane - m + off_at)
        keep = (key_at >= query_at - reach[0:1, :]) & (key_at <= query_at + reach[1:2, :])
        near_bias_out[...] = jnp.where(keep, 0.0, -jnp.inf).astype(F32)
        me = lax.axis_index("node")
        row = iota((3 * m, m), 0)
        key_at = jnp.where(row < m, row + chip_at, jnp.where(row < 2 * m, row - m + off_at, row - m))
        query_at = iota((3 * m, m), 1) + m
        at_end = (me == 0) | (me == lax.axis_size("node") - 1)
        missing = (row >= m) & (row < 2 * m) & at_end
        keep = (key_at >= query_at - window[0:1, :]) & (key_at <= query_at + window[1:2, :])
        bias = jnp.where(keep & jnp.logical_not(missing), 0.0, -jnp.inf).astype(F32)
        bias_out[...] = jnp.transpose(bias)

    masks()
    copies[1].wait()
    for i, at in enumerate(starts):
        copies[2 + i].wait()
        cols = slice(at, at + width)
        qkv_out[:, cols] = mm(normed[...], w_qkv[:, cols]).astype(BF16)
        for p in range(i // 3 * width // pair, (i // 3 + 1) * width // pair):
            q, k, v = (
                slice(part * channels + p * pair, part * channels + (p + 1) * pair)
                for part in range(3)
            )
            if i % 3 == 1:
                scores_out[p] = mm_nt(halves(qkv_out[:, q], scale), qkv_out[:, k])
            if i % 3 == 2:
                products_out[p] = mm_nt(halves(grad_out[:, q]), qkv_out[:, v])
    for copy in copies[-2:]:
        copy.wait()


def attend_kernel(
    scale,
    pair,
    chip_normed,
    off_normed,
    w_qkv,
    own_qkv,
    own_grad,
    own_scores,
    own_products,
    bias,
    w_out_hbm,
    cot_hbm,
    stats_out,
    kv,
    weights_out,
    scores_out,
    near_q,
    w_out,
    cot,
    sems,
):
    fetch = start_all([(w_out_hbm, w_out), (cot_hbm, cot)], sems)
    m, channels = chip_normed.shape
    pairs = channels // pair

    @pl.when(everywhere())
    def _():
        near = jnp.concatenate([chip_normed[...], off_normed[:m]], 0)

        def bring(group):
            cols = slice(group * 2 * pair, (group + 1) * 2 * pair)
            near_q[:, cols] = mm(near, w_qkv[:, cols]).astype(BF16) * jnp.asarray(scale, BF16)
            blocks = []
            for part in range(1, 3):
                at = part * channels + group * 2 * pair
                block = mm(near, w_qkv[:, at : at + 2 * pair]).astype(BF16)
                kv[: 2 * m, at - channels : at - channels + 2 * pair] = block
                blocks.append(block)
            return blocks

        brought = {0: bring(0)}
        kv[2 * m :] = own_qkv[:, channels:]
        lane = iota((CHUNK, LANES), 1)
        stats = [jnp.zeros((CHUNK, LANES), F32) for _ in range(2 * m // CHUNK)]

        def near_of(p):
            return [b[:, p % 2 * pair : (p % 2 + 1) * pair] for b in brought[p // 2]]

        def multiply(p):
            cols = slice(p * pair, (p + 1) * pair)
            keys, values = near_of(p)
            return (
                mm_nt(halves(own_qkv[:, cols], scale), keys),
                mm_nt(halves(own_grad[:, cols]), values),
            )

        ahead = multiply(0)
        for p in range(pairs):
            scores, grad_prob = ahead
            if p + 1 < pairs:
                if p % 2 == 0 and p + 2 < pairs:
                    brought[p // 2 + 1] = bring(p // 2 + 1)
                ahead = multiply(p + 1)
            weights, grad_scores = [], []
            for at in range(0, 2 * m, CHUNK):
                part = slice(at, at + CHUNK)
                place = slice(at % m, at % m + CHUNK)
                raw = jnp.concatenate([scores[part], own_scores[p, part]], 1) + bias[place]
                top = jnp.max(raw, 1, keepdims=True)
                shifted = jnp.exp(raw - top)
                inv_sum = 1.0 / jnp.sum(shifted, 1, keepdims=True)
                probs = shifted * inv_sum
                product = jnp.concatenate([grad_prob[part], own_products[p, part]], 1)
                delta = jnp.sum(probs * product, 1, keepdims=True)
                weights.append(probs.astype(BF16))
                grad_scores.append((probs * (product - delta)).astype(BF16))
                for k, column in enumerate((top, inv_sum, delta)):
                    stats[at // CHUNK] = jnp.where(lane == k * pairs + p, column, stats[at // CHUNK])
            weights_out[p] = jnp.concatenate(weights, 0)
            scores_out[p] = jnp.concatenate(grad_scores, 0)
        stats_out[...] = jnp.transpose(jnp.concatenate(stats, 0))[: 3 * pairs]

    for copy in fetch:
        copy.wait()


def product_kernel(
    scale,
    pair,
    weights,
    grad_scores,
    kv,
    own_qkv,
    own_grad,
    latent,
    w_out,
    w_qkv,
    mesh_out_hbm,
    grad_normed,
    grad_key,
    grad_value,
    attention,
    grad_query,
    mesh_out,
    sems,
):
    m, channels = latent.shape
    pairs = channels // pair
    for p in range(pairs):
        cols = slice(p * pair, (p + 1) * pair)
        value = kv[:, channels + p * pair : channels + (p + 1) * pair]
        attention[:, cols] = merge(mm(weights[p], value)).astype(BF16)
    mesh_out[...] = (latent[...].astype(F32) + mm(attention[...], w_out[...])).astype(BF16)
    out = pltpu.make_async_copy(mesh_out, mesh_out_hbm, sems.at[0])
    out.start()

    @pl.when(everywhere())
    def _():
        for p in range(pairs):
            cols = slice(p * pair, (p + 1) * pair)
            grad_query[:, cols] = (merge(mm(grad_scores[p], kv[:, cols])) * scale).astype(BF16)
        for p in range(pairs):
            cols = slice(p * pair, (p + 1) * pair)
            grad_key[:, cols] = mm_tn(grad_scores[p, :, 2 * m :], halves(own_qkv[:, cols], scale))
            grad_value[:, cols] = mm_tn(weights[p, :, 2 * m :], halves(own_grad[:, cols]))
        grad_normed[...] = mm_nt(grad_query[...], w_qkv[:, :channels])

    out.wait()


def finish_kernel(
    pair,
    chip_stats,
    off_stats,
    bias,
    near_q,
    near_grad,
    own_qkv,
    grad_key,
    grad_value,
    grad_normed,
    w_qkv,
    normal,
    inv_std,
    cot,
    grad_out,
):
    m, channels = normal.shape
    pairs = channels // pair

    stats = []
    for h in range(2):
        lanes = slice(h * m, (h + 1) * m)
        stats.append(jnp.concatenate([chip_stats[:, lanes], off_stats[:, lanes]], 1))

    def multiply(p):
        cols = slice(p * pair, (p + 1) * pair)
        key2 = halves(own_qkv[:, channels + p * pair : channels + (p + 1) * pair])
        value2 = halves(own_qkv[:, 2 * channels + p * pair : 2 * channels + (p + 1) * pair])
        query = near_q[:, cols]
        grad = near_grad[:, cols]
        return query, grad, mm_nt(key2, query), mm_nt(value2, grad)

    total = grad_normed[...]
    group = 2
    gks, gvs = [], []
    ahead = multiply(0)
    for p in range(pairs):
        cols = slice(p * pair, (p + 1) * pair)
        query, grad, scores, grad_prob = ahead
        if p + 1 < pairs:
            ahead = multiply(p + 1)
        weights, grad_scores = [], []
        for at in range(0, 2 * m, CHUNK):
            part = slice(at, at + CHUNK)
            place = slice(at % m, at % m + CHUNK)
            top, inv_sum, delta = (
                stats[at // m][k * pairs + p : k * pairs + p + 1] for k in range(3)
            )
            probs = jnp.exp(scores[part] + bias[place] - top) * inv_sum
            weights.append(probs.astype(BF16))
            grad_scores.append((probs * (grad_prob[part] - delta)).astype(BF16))
        gk = grad_key[:, cols] + merge(mm(jnp.concatenate(grad_scores, 0), query))
        gv = grad_value[:, cols] + merge(mm(jnp.concatenate(weights, 0), grad))
        gks.append(gk.astype(BF16))
        gvs.append(gv.astype(BF16))
        if len(gks) == group:
            at = channels + (p + 1 - group) * pair
            width = group * pair
            for blocks, start in ((gks, at), (gvs, at + channels)):
                total = total + mm_nt(
                    jnp.concatenate(blocks, 1), w_qkv[:, start : start + width]
                )
            gks, gvs = [], []
    centred = (
        total
        - jnp.mean(total, -1, keepdims=True)
        - normal[...] * jnp.mean(total * normal[...], -1, keepdims=True)
    )
    grad_out[...] = (cot[...].astype(F32) + inv_std[:, :1] * centred).astype(BF16)


def body(
    grid_in,
    mesh_in,
    own_src,
    own_dst,
    side_src,
    side_dst,
    side_count,
    far_src,
    far_dst,
    far_count,
    window,
    cotangent,
    w_edge,
    w_qkv,
    w_out,
):
    devices = lax.axis_size("node")
    grid_rows, channels = grid_in.shape
    m = mesh_in.shape[0]
    far_slots = far_src.shape[0]
    far_depth = far_slots // devices
    head_dim = channels // HEADS
    pair = 2 * head_dim
    pairs = channels // pair
    scale = head_dim ** (-0.5)
    meta_rows = side_src.shape[0] // (2 * LANES)

    side_src, side_dst = side_src.reshape(-1, LANES), side_dst.reshape(-1, LANES)
    own_src, own_dst = own_src.reshape(-1, LANES), own_dst.reshape(-1, LANES)
    far_src, far_dst = far_src.reshape(1, -1), far_dst.reshape(1, -1)
    side_count, far_count = side_count.reshape(1, -1), far_count.reshape(1, -1)
    message = ((BAND + meta_rows, channels), BF16)
    far_block = (2 * far_slots, channels // 2 + LANES)
    far_message, chip_message, off_message, w_edge = call(
        pack_kernel,
        [(far_block, BF16), message, message, (w_edge.shape, BF16)],
        [grid_in, window, side_src, side_dst, side_count, far_src, far_dst, far_count, w_edge],
        hbm=range(9),
        hbm_outs=range(3),
        scratch=like(grid_in, window, side_src, side_dst, side_count, far_src, far_dst, far_count)
        + [
            pltpu.VMEM(far_block, BF16),
            pltpu.VMEM((2, meta_rows, channels), BF16),
            dma(9),
            dma(5),
        ],
        name="pack",
    )
    from_chip, from_off = exchange(chip_message, off_message, "node")
    got_far = lax.all_to_all(
        far_message.reshape(devices, 2 * far_depth, far_block[1]),
        "node",
        split_axis=0,
        concat_axis=0,
        tiled=True,
    ).reshape(far_block)

    rows = ((m, channels), BF16)
    partial, own_grad = call(
        own_kernel,
        [((m, channels), F32), rows],
        [grid_in, mesh_in, own_src, own_dst, cotangent, w_out, w_edge, from_chip],
        hbm=range(6),
        anywhere=(7,),
        hbm_outs=(1,),
        scratch=like(grid_in, mesh_in, own_src, own_dst, cotangent, w_out, cotangent) + [dma(7)],
        name="own",
    )
    chip_grad, off_grad = exchange(own_grad, own_grad, "node")
    (partial,) = call(
        functools.partial(side_kernel, meta_rows),
        [((m, channels), F32)],
        [from_chip, from_off, w_edge, partial],
        name="side",
        flops=8 * 10**9,
    )
    latent, normed, off_message, normal, inv_std = call(
        functools.partial(latent_kernel, far_depth),
        [rows, rows, ((m + PAD, channels), BF16), ((m, channels), F32), ((m, LANES), F32)],
        [got_far, partial],
        name="latent",
    )
    off_normed = swap_off(off_message, "node")
    own_block = ((pairs, 2 * m, m), F32)
    own_qkv, w_qkv, own_grad, near_grad, own_scores, own_products, bias, near_bias, normed = call(
        functools.partial(project_kernel, scale, pair, meta_rows),
        [((m, 3 * channels), BF16), (w_qkv.shape, BF16), rows, ((2 * m, channels), BF16)]
        + [own_block, own_block]
        + [((m, 3 * m), F32), ((m, 2 * m), F32), rows],
        [normed, from_chip, from_off, window, own_grad, w_qkv, chip_grad, off_grad],
        hbm=(3, 4, 5),
        anywhere=(6, 7),
        scratch=like(window) + [dma(3 * PIECES + 4)],
        name="project",
    )
    chip_normed = swap_chip(normed, "node")
    probs = ((pairs, 2 * m, 3 * m), BF16)
    stats, kv, weights, grad_scores, near_q, w_out, cotangent = call(
        functools.partial(attend_kernel, scale, pair),
        [
            ((3 * pairs, 2 * m), F32),
            ((3 * m, 2 * channels), BF16),
            probs,
            probs,
            ((2 * m, channels), BF16),
            (w_out.shape, BF16),
            rows,
        ],
        [chip_normed, off_normed, w_qkv, own_qkv, own_grad, own_scores, own_products]
        + [bias, w_out, cotangent],
        hbm=(8, 9),
        scratch=[dma(2)],
        name="attend",
    )
    chip_stats, off_stats = exchange(stats, stats, "node")
    mesh_out, grad_normed, grad_key, grad_value = call(
        functools.partial(product_kernel, scale, pair),
        [
            rows,
            ((m, channels), F32),
            ((m, channels), F32),
            ((m, channels), F32),
        ],
        [
            weights,
            grad_scores,
            kv,
            own_qkv,
            own_grad,
            latent,
            w_out,
            w_qkv,
        ],
        hbm_outs=(0,),
        scratch=[pltpu.VMEM((m, channels), BF16)] * 3 + [dma(1)],
        name="product",
    )
    (mesh_grad,) = call(
        functools.partial(finish_kernel, pair),
        [rows],
        [
            chip_stats,
            off_stats,
            near_bias,
            near_q,
            near_grad,
            own_qkv,
            grad_key,
            grad_value,
            grad_normed,
            w_qkv,
            normal,
            inv_std,
            cotangent,
        ],
        name="finish",
    )
    return (mesh_out, mesh_grad)


def solution(mesh):
    rows = P(("groups", "node"), None)
    flat = P(("groups", "node"))
    placed = (rows, rows) + (flat,) * 8 + (P(None, ("groups", "node")), rows, P(), P(), P())
    return jax.shard_map(
        body, mesh=mesh, in_specs=placed, out_specs=(rows, rows), check_vma=False
    )
```

```python
import functools

import jax
import jax.numpy as jnp
from jax import lax
from jax.experimental import pallas as pl
from jax.experimental.pallas import tpu as pltpu
from jax.sharding import PartitionSpec as P

HEADS = 16
BAND = 128
LANES = 128
F32 = jnp.float32
BF16 = jnp.bfloat16
I32 = jnp.int32
VMEM_LIMIT = 28 * 2**20
PIECES = 2
PAD = 8
CHUNK = 64


def mm(a, b):
    return lax.dot_general(a, b, (((1,), (0,)), ((), ())), preferred_element_type=F32)


def mm_nt(a, b):
    return lax.dot_general(a, b, (((1,), (1,)), ((), ())), preferred_element_type=F32)


def mm_tn(a, b):
    return lax.dot_general(a, b, (((0,), (0,)), ((), ())), preferred_element_type=F32)


def iota(shape, dim):
    return lax.broadcasted_iota(I32, shape, dim)


def call(kernel, outs, args, hbm=(), hbm_outs=(), scratch=(), name=None, flops=None):
    args = [
        pltpu.with_memory_space_constraint(a, pltpu.HBM) if i in hbm else a
        for i, a in enumerate(args)
    ]

    def specs(count, far):
        return [
            pl.BlockSpec(memory_space=pltpu.HBM if i in far else pltpu.VMEM) for i in range(count)
        ]

    return pl.pallas_call(
        kernel,
        out_shape=[
            (pltpu.HBM if i in hbm_outs else jax.ShapeDtypeStruct)(shape, dtype)
            for i, (shape, dtype) in enumerate(outs)
        ],
        in_specs=specs(len(args), hbm),
        out_specs=specs(len(outs), hbm_outs),
        scratch_shapes=list(scratch),
        compiler_params=pltpu.CompilerParams(vmem_limit_bytes=VMEM_LIMIT),
        cost_estimate=flops and pl.CostEstimate(flops=flops, transcendentals=0, bytes_accessed=0),
        name=name,
    )(*args)


def dma(count):
    return pltpu.SemaphoreType.DMA((count,))


def start_all(pairs, sems):
    copies = [pltpu.make_async_copy(src, dst, sems.at[i]) for i, (src, dst) in enumerate(pairs)]
    for copy in copies:
        copy.start()
    return copies


def like(*arrays):
    return [pltpu.VMEM(a.shape, a.dtype) for a in arrays]


def swap_off(rows, axis):
    n = lax.axis_size(axis)
    pairs = [p for i in range(1, n - 1, 2) for p in ((i, i + 1), (i + 1, i))]
    return lax.ppermute(rows, axis, pairs)


def swap_chip(rows, axis):
    n = lax.axis_size(axis)
    return lax.ppermute(rows, axis, [p for i in range(0, n, 2) for p in ((i, i + 1), (i + 1, i))])


def exchange(chip_message, off_message, axis):
    from_chip = swap_chip(chip_message, axis)
    return from_chip, swap_off(off_message, axis)


def is_odd():
    return lax.axis_index("node") % 2


def everywhere():
    return lax.axis_index("node") >= 0


def gelu(projected):
    x = projected.astype(BF16).astype(F32)
    inner = (2.0 / jnp.pi) ** 0.5 * (x + 0.044715 * (x * x * x))
    return (0.5 * x * (1.0 + jnp.tanh(inner))).astype(BF16)


def onehot_rows(index_rows, count):
    parts = [
        jnp.where(iota((count, row.shape[1]), 0) == row, 1.0, 0.0).astype(BF16)
        for row in index_rows
    ]
    return parts[0] if len(parts) == 1 else jnp.concatenate(parts, 1)


def norm_stats(latent):
    values = latent.astype(F32)
    row_mean = jnp.mean(values, -1, keepdims=True)
    centred = values - row_mean
    variance = jnp.mean(centred * centred, -1, keepdims=True)
    inv_std = lax.rsqrt(variance + 1e-05)
    return centred * inv_std, inv_std


def pack_kernel(
    grid_hbm,
    window_hbm,
    side_src_hbm,
    side_dst_hbm,
    side_count_hbm,
    far_src_hbm,
    far_dst_hbm,
    far_count_hbm,
    far_out,
    chip_out,
    off_out,
    grid,
    window,
    side_src,
    side_dst,
    side_count,
    far_src,
    far_dst,
    far_count,
    far,
    meta,
    sems,
    out_sems,
):
    grid_rows, channels = grid.shape
    mesh_rows = window.shape[1]
    slots = far_src.shape[1]
    devices = far_count.shape[1]
    depth = slots // devices
    first = grid_rows - BAND
    count = side_src.shape[0] // 2
    copies = start_all(
        [
            (side_src_hbm, side_src),
            (side_dst_hbm, side_dst),
            (side_count_hbm, side_count),
            (window_hbm, window),
            (grid_hbm, grid),
            (far_src_hbm, far_src),
            (far_dst_hbm, far_dst),
            (far_count_hbm, far_count),
        ],
        sems,
    )
    for copy in copies[:4]:
        copy.wait()
    for k in range(2):
        rank = iota((count, LANES), 0) * LANES + iota((count, LANES), 1)
        src = side_src[k * count : (k + 1) * count] - k * first
        live = rank < side_count[:, k : k + 1]
        dst = jnp.where(live, side_dst[k * count : (k + 1) * count], mesh_rows)
        reach = jnp.concatenate([window[...], jnp.zeros((count - 2, mesh_rows), I32)], 0)
        blank = jnp.zeros((count, channels - 2 * LANES - mesh_rows), I32)
        meta[k] = jnp.concatenate([src, dst, reach, blank], 1).astype(F32).astype(BF16)
    copies[4].wait()
    odd = is_odd()
    outs = start_all(
        [
            pair
            for k, out in ((1 - odd, chip_out), (odd, off_out))
            for pair in (
                (grid.at[pl.ds(pl.multiple_of(k * first, BAND), BAND)], out.at[pl.ds(0, BAND)]),
                (meta.at[k], out.at[pl.ds(BAND, count)]),
            )
        ],
        out_sems,
    )
    for copy in copies[5:8]:
        copy.wait()
    slot = iota((1, slots), 1)
    receiver = jnp.where(iota((devices, slots), 0) == iota((devices, slots), 1) // depth, 1.0, 0.0)
    live = mm(far_count[...].astype(F32).astype(BF16), receiver.astype(BF16))
    target = jnp.where((slot % depth).astype(F32) < live, far_dst[...].astype(F32), 1.0 * mesh_rows)
    row = iota((2 * slots, slots), 0)
    mine = slot == row // (2 * depth) * depth + row % depth
    source = jnp.sum(jnp.where(mine, far_src[...].astype(F32), 0.0), 1, keepdims=True)
    column = jnp.sum(jnp.where(mine, target, 0.0), 1, keepdims=True)
    pick = jnp.where(iota((2 * slots, grid_rows), 1).astype(F32) == source, 1.0, 0.0).astype(BF16)
    rows = mm(pick, grid[...]).astype(BF16)
    half = channels // 2
    is_first = iota((2 * slots, half), 0) % (2 * depth) < depth
    far[:, :half] = jnp.where(is_first, rows[:, :half], rows[:, half:])
    far[:, half:] = jnp.broadcast_to(column, (2 * slots, LANES)).astype(BF16)
    last = pltpu.make_async_copy(far, far_out, out_sems.at[4])
    last.start()
    for copy in outs + [last]:
        copy.wait()


def own_kernel(
    grid_hbm,
    mesh_in_hbm,
    own_src_hbm,
    own_dst_hbm,
    cot_hbm,
    w_out_hbm,
    w_edge_hbm,
    partial_out,
    grad_hbm,
    w_edge,
    grid,
    mesh_in,
    own_src,
    own_dst,
    cot,
    w_out,
    grad,
    sems,
):
    grid_rows = grid.shape[0]
    mesh_rows = mesh_in.shape[0]
    copies = start_all(
        [
            (own_src_hbm, own_src),
            (own_dst_hbm, own_dst),
            (cot_hbm, cot),
            (w_out_hbm, w_out),
            (grid_hbm, grid),
            (w_edge_hbm, w_edge),
            (mesh_in_hbm, mesh_in),
        ],
        sems,
    )
    for copy in copies[:2]:
        copy.wait()
    rows = own_src.shape[0]
    src = onehot_rows([own_src[r : r + 1] for r in range(rows)], grid_rows)
    dst = onehot_rows([own_dst[r : r + 1] for r in range(rows)], mesh_rows)
    counts = mm_nt(dst, src).astype(BF16)
    for copy in copies[2:4]:
        copy.wait()
    grad[...] = mm_nt(cot[...], w_out[...]).astype(BF16)
    out = pltpu.make_async_copy(grad, grad_hbm, sems.at[7])
    out.start()
    for copy in copies[4:]:
        copy.wait()
    active = gelu(mm(grid[...], w_edge[...]))
    partial_out[...] = mesh_in[...].astype(F32) + mm(counts, active)
    out.wait()


def meta_of(message, count):
    return message[BAND : BAND + count].astype(F32).astype(I32)


def side_kernel(count, chip, off, w_edge, partial, partial_out):
    mesh_rows = partial.shape[0]
    uppers, lowers = [], []
    for side in (chip, off):
        meta = meta_of(side, count)
        src = onehot_rows([meta[r : r + 1, :LANES] for r in range(count)], BAND)
        dst = onehot_rows([meta[r : r + 1, LANES : 2 * LANES] for r in range(count)], mesh_rows)
        counts = mm_nt(dst, src)
        upper = counts.astype(BF16)
        uppers.append(upper)
        lowers.append((counts - upper.astype(F32)).astype(BF16))
    active = gelu(mm(jnp.concatenate([chip[:BAND], off[:BAND]], 0), w_edge[...]))
    landing = jnp.concatenate(uppers + lowers, 1)
    partial_out[...] = partial[...] + mm(landing, jnp.concatenate([active, active], 0))


def latent_kernel(
    depth, far, w_edge, partial, latent_out, normed_out, off_out, normal_out, inv_std_out
):
    mesh_rows, channels = partial.shape
    slots = far.shape[0]
    half = channels // 2
    first = far[:, :half]
    second = pltpu.roll(first.astype(F32), slots - depth, 0).astype(BF16)
    target = jnp.transpose(far[:, half:].astype(F32))
    if mesh_rows != LANES:
        target = jnp.broadcast_to(target[:1], (mesh_rows, slots))
    is_row = iota((mesh_rows, slots), 1) % (2 * depth) < depth
    hit = (target == iota((mesh_rows, slots), 0).astype(F32)) & is_row
    landing = jnp.where(hit, 1.0, 0.0).astype(BF16)
    active = gelu(mm(jnp.concatenate([first, second], 1), w_edge[...]))
    total = partial[...] + mm(landing, active)
    latent = total.astype(BF16)
    latent_out[...] = latent
    normal, inv_std = norm_stats(latent)
    normed = normal.astype(BF16)
    normed_out[...] = normed
    off_out[...] = jnp.concatenate([normed, jnp.zeros((PAD, channels), BF16)], 0)
    normal_out[...] = normal
    inv_std_out[...] = jnp.broadcast_to(inv_std, inv_std_out.shape)


def halves(rows, scale=None):
    first = iota(rows.shape, 1) < rows.shape[1] // 2
    if scale is not None:
        rows = rows * jnp.asarray(scale, rows.dtype)
    zero = jnp.zeros_like(rows)
    return jnp.concatenate([jnp.where(first, rows, zero), jnp.where(first, zero, rows)], 0)


def merge(stacked):
    m = stacked.shape[0] // 2
    first = iota((m, stacked.shape[1]), 1) < stacked.shape[1] // 2
    return jnp.where(first, stacked[:m], stacked[m:])


def near_places(m):
    odd = is_odd()
    return (1 - odd) * 2 * m, odd * 2 * m


def project_kernel(
    scale,
    pair,
    count,
    normed,
    chip_first,
    off_first,
    window_hbm,
    grad_hbm,
    w_qkv_hbm,
    qkv_out,
    w_qkv,
    grad_out,
    scores_out,
    products_out,
    bias_out,
    near_bias_out,
    normed_out,
    window,
    sems,
):
    m, channels = normed.shape
    normed_out[...] = normed[...]
    width = channels // PIECES
    starts = [part * channels + c * width for c in range(PIECES) for part in range(3)]
    copies = start_all(
        [(window_hbm, window), (grad_hbm, grad_out)]
        + [(w_qkv_hbm.at[:, pl.ds(at, width)], w_qkv.at[:, pl.ds(at, width)]) for at in starts],
        sems,
    )
    copies[0].wait()
    def masks():
        chip_at, off_at = near_places(m)
        reach = [meta_of(side, count)[:8, 2 * LANES : 2 * LANES + m] for side in (chip_first, off_first)]
        reach = jnp.concatenate(reach, 1)
        key_at = iota((m, 2 * m), 0) + m
        lane = iota((m, 2 * m), 1)
        query_at = jnp.where(lane < m, lane + chip_at, lane - m + off_at)
        keep = (key_at >= query_at - reach[0:1, :]) & (key_at <= query_at + reach[1:2, :])
        near_bias_out[...] = jnp.where(keep, 0.0, -jnp.inf).astype(F32)
        me = lax.axis_index("node")
        row = iota((3 * m, m), 0)
        key_at = jnp.where(row < m, row + chip_at, jnp.where(row < 2 * m, row - m + off_at, row - m))
        query_at = iota((3 * m, m), 1) + m
        at_end = (me == 0) | (me == lax.axis_size("node") - 1)
        missing = (row >= m) & (row < 2 * m) & at_end
        keep = (key_at >= query_at - window[0:1, :]) & (key_at <= query_at + window[1:2, :])
        bias = jnp.where(keep & jnp.logical_not(missing), 0.0, -jnp.inf).astype(F32)
        bias_out[...] = jnp.transpose(bias)

    masks()
    copies[1].wait()
    for i, at in enumerate(starts):
        copies[2 + i].wait()
        cols = slice(at, at + width)
        qkv_out[:, cols] = mm(normed[...], w_qkv[:, cols]).astype(BF16)
        for p in range(i // 3 * width // pair, (i // 3 + 1) * width // pair):
            q, k, v = (
                slice(part * channels + p * pair, part * channels + (p + 1) * pair)
                for part in range(3)
            )
            if i % 3 == 1:
                scores_out[p] = mm_nt(halves(qkv_out[:, q], scale), qkv_out[:, k])
            if i % 3 == 2:
                products_out[p] = mm_nt(halves(grad_out[:, q]), qkv_out[:, v])


def attend_kernel(
    scale,
    pair,
    chip_normed,
    off_normed,
    w_qkv,
    own_qkv,
    own_grad,
    own_scores,
    own_products,
    bias,
    w_out_hbm,
    cot_hbm,
    stats_out,
    kv,
    weights_out,
    scores_out,
    near_q,
    w_out,
    cot,
    sems,
):
    fetch = start_all([(w_out_hbm, w_out), (cot_hbm, cot)], sems)
    m, channels = chip_normed.shape
    pairs = channels // pair

    @pl.when(everywhere())
    def _():
        near = jnp.concatenate([chip_normed[...], off_normed[:m]], 0)

        def bring(group):
            cols = slice(group * 2 * pair, (group + 1) * 2 * pair)
            near_q[:, cols] = mm(near, w_qkv[:, cols]).astype(BF16) * jnp.asarray(scale, BF16)
            blocks = []
            for part in range(1, 3):
                at = part * channels + group * 2 * pair
                block = mm(near, w_qkv[:, at : at + 2 * pair]).astype(BF16)
                kv[: 2 * m, at - channels : at - channels + 2 * pair] = block
                blocks.append(block)
            return blocks

        brought = {0: bring(0)}
        kv[2 * m :] = own_qkv[:, channels:]
        lane = iota((CHUNK, LANES), 1)
        stats = [jnp.zeros((CHUNK, LANES), F32) for _ in range(2 * m // CHUNK)]

        def near_of(p):
            return [b[:, p % 2 * pair : (p % 2 + 1) * pair] for b in brought[p // 2]]

        def multiply(p):
            cols = slice(p * pair, (p + 1) * pair)
            keys, values = near_of(p)
            return (
                mm_nt(halves(own_qkv[:, cols], scale), keys),
                mm_nt(halves(own_grad[:, cols]), values),
            )

        ahead = multiply(0)
        for p in range(pairs):
            scores, grad_prob = ahead
            if p + 1 < pairs:
                if p % 2 == 0 and p + 2 < pairs:
                    brought[p // 2 + 1] = bring(p // 2 + 1)
                ahead = multiply(p + 1)
            weights, grad_scores = [], []
            for at in range(0, 2 * m, CHUNK):
                part = slice(at, at + CHUNK)
                place = slice(at % m, at % m + CHUNK)
                raw = jnp.concatenate([scores[part], own_scores[p, part]], 1) + bias[place]
                top = jnp.max(raw, 1, keepdims=True)
                shifted = jnp.exp(raw - top)
                inv_sum = 1.0 / jnp.sum(shifted, 1, keepdims=True)
                probs = shifted * inv_sum
                product = jnp.concatenate([grad_prob[part], own_products[p, part]], 1)
                delta = jnp.sum(probs * product, 1, keepdims=True)
                weights.append(probs.astype(BF16))
                grad_scores.append((probs * (product - delta)).astype(BF16))
                for k, column in enumerate((top, inv_sum, delta)):
                    stats[at // CHUNK] = jnp.where(lane == k * pairs + p, column, stats[at // CHUNK])
            weights_out[p] = jnp.concatenate(weights, 0)
            scores_out[p] = jnp.concatenate(grad_scores, 0)
        stats_out[...] = jnp.transpose(jnp.concatenate(stats, 0))[: 3 * pairs]

    for copy in fetch:
        copy.wait()


def product_kernel(
    scale,
    pair,
    weights,
    grad_scores,
    kv,
    own_qkv,
    own_grad,
    latent,
    w_out,
    w_qkv,
    mesh_out_hbm,
    grad_normed,
    grad_key,
    grad_value,
    attention,
    grad_query,
    mesh_out,
    sems,
):
    m, channels = latent.shape
    pairs = channels // pair
    for p in range(pairs):
        cols = slice(p * pair, (p + 1) * pair)
        value = kv[:, channels + p * pair : channels + (p + 1) * pair]
        attention[:, cols] = merge(mm(weights[p], value)).astype(BF16)
    mesh_out[...] = (latent[...].astype(F32) + mm(attention[...], w_out[...])).astype(BF16)
    out = pltpu.make_async_copy(mesh_out, mesh_out_hbm, sems.at[0])
    out.start()

    @pl.when(everywhere())
    def _():
        for p in range(pairs):
            cols = slice(p * pair, (p + 1) * pair)
            grad_query[:, cols] = (merge(mm(grad_scores[p], kv[:, cols])) * scale).astype(BF16)
        for p in range(pairs):
            cols = slice(p * pair, (p + 1) * pair)
            grad_key[:, cols] = mm_tn(grad_scores[p, :, 2 * m :], halves(own_qkv[:, cols], scale))
            grad_value[:, cols] = mm_tn(weights[p, :, 2 * m :], halves(own_grad[:, cols]))
        grad_normed[...] = mm_nt(grad_query[...], w_qkv[:, :channels])

    out.wait()


def finish_kernel(
    pair,
    chip_stats,
    off_stats,
    bias,
    near_q,
    chip_grad,
    off_grad,
    own_qkv,
    grad_key,
    grad_value,
    grad_normed,
    w_qkv,
    normal,
    inv_std,
    cot,
    grad_out,
):
    m, channels = normal.shape
    pairs = channels // pair

    stats = []
    for h in range(2):
        lanes = slice(h * m, (h + 1) * m)
        stats.append(jnp.concatenate([chip_stats[:, lanes], off_stats[:, lanes]], 1))

    def multiply(p):
        cols = slice(p * pair, (p + 1) * pair)
        key2 = halves(own_qkv[:, channels + p * pair : channels + (p + 1) * pair])
        value2 = halves(own_qkv[:, 2 * channels + p * pair : 2 * channels + (p + 1) * pair])
        query = near_q[:, cols]
        grad = jnp.concatenate([chip_grad[:, cols], off_grad[:, cols]], 0)
        return query, grad, mm_nt(key2, query), mm_nt(value2, grad)

    total = grad_normed[...]
    group = 2
    gks, gvs = [], []
    ahead = multiply(0)
    for p in range(pairs):
        cols = slice(p * pair, (p + 1) * pair)
        query, grad, scores, grad_prob = ahead
        if p + 1 < pairs:
            ahead = multiply(p + 1)
        weights, grad_scores = [], []
        for at in range(0, 2 * m, CHUNK):
            part = slice(at, at + CHUNK)
            place = slice(at % m, at % m + CHUNK)
            top, inv_sum, delta = (
                stats[at // m][k * pairs + p : k * pairs + p + 1] for k in range(3)
            )
            probs = jnp.exp(scores[part] + bias[place] - top) * inv_sum
            weights.append(probs.astype(BF16))
            grad_scores.append((probs * (grad_prob[part] - delta)).astype(BF16))
        gk = grad_key[:, cols] + merge(mm(jnp.concatenate(grad_scores, 0), query))
        gv = grad_value[:, cols] + merge(mm(jnp.concatenate(weights, 0), grad))
        gks.append(gk.astype(BF16))
        gvs.append(gv.astype(BF16))
        if len(gks) == group:
            at = channels + (p + 1 - group) * pair
            width = group * pair
            for blocks, start in ((gks, at), (gvs, at + channels)):
                total = total + mm_nt(
                    jnp.concatenate(blocks, 1), w_qkv[:, start : start + width]
                )
            gks, gvs = [], []
    centred = (
        total
        - jnp.mean(total, -1, keepdims=True)
        - normal[...] * jnp.mean(total * normal[...], -1, keepdims=True)
    )
    grad_out[...] = (cot[...].astype(F32) + inv_std[:, :1] * centred).astype(BF16)


def body(
    grid_in,
    mesh_in,
    own_src,
    own_dst,
    side_src,
    side_dst,
    side_count,
    far_src,
    far_dst,
    far_count,
    window,
    cotangent,
    w_edge,
    w_qkv,
    w_out,
):
    devices = lax.axis_size("node")
    grid_rows, channels = grid_in.shape
    m = mesh_in.shape[0]
    far_slots = far_src.shape[0]
    far_depth = far_slots // devices
    head_dim = channels // HEADS
    pair = 2 * head_dim
    pairs = channels // pair
    scale = head_dim ** (-0.5)
    meta_rows = side_src.shape[0] // (2 * LANES)

    side_src, side_dst = side_src.reshape(-1, LANES), side_dst.reshape(-1, LANES)
    own_src, own_dst = own_src.reshape(-1, LANES), own_dst.reshape(-1, LANES)
    far_src, far_dst = far_src.reshape(1, -1), far_dst.reshape(1, -1)
    side_count, far_count = side_count.reshape(1, -1), far_count.reshape(1, -1)
    message = ((BAND + meta_rows, channels), BF16)
    far_block = (2 * far_slots, channels // 2 + LANES)
    far_message, chip_message, off_message = call(
        pack_kernel,
        [(far_block, BF16), message, message],
        [grid_in, window, side_src, side_dst, side_count, far_src, far_dst, far_count],
        hbm=range(8),
        hbm_outs=range(3),
        scratch=like(grid_in, window, side_src, side_dst, side_count, far_src, far_dst, far_count)
        + [
            pltpu.VMEM(far_block, BF16),
            pltpu.VMEM((2, meta_rows, channels), BF16),
            dma(8),
            dma(5),
        ],
        name="pack",
    )
    from_chip, from_off = exchange(chip_message, off_message, "node")
    got_far = lax.all_to_all(
        far_message.reshape(devices, 2 * far_depth, far_block[1]),
        "node",
        split_axis=0,
        concat_axis=0,
        tiled=True,
    ).reshape(far_block)

    rows = ((m, channels), BF16)
    partial, own_grad, w_edge = call(
        own_kernel,
        [((m, channels), F32), rows, (w_edge.shape, BF16)],
        [grid_in, mesh_in, own_src, own_dst, cotangent, w_out, w_edge],
        hbm=range(7),
        hbm_outs=(1,),
        scratch=like(grid_in, mesh_in, own_src, own_dst, cotangent, w_out, cotangent) + [dma(8)],
        name="own",
    )
    (partial,) = call(
        functools.partial(side_kernel, meta_rows),
        [((m, channels), F32)],
        [from_chip, from_off, w_edge, partial],
        name="side",
        flops=8 * 10**9,
    )
    latent, normed, off_message, normal, inv_std = call(
        functools.partial(latent_kernel, far_depth),
        [rows, rows, ((m + PAD, channels), BF16), ((m, channels), F32), ((m, LANES), F32)],
        [got_far, w_edge, partial],
        name="latent",
    )
    off_normed = swap_off(off_message, "node")
    own_block = ((pairs, 2 * m, m), F32)
    own_qkv, w_qkv, own_grad, own_scores, own_products, bias, near_bias, normed = call(
        functools.partial(project_kernel, scale, pair, meta_rows),
        [((m, 3 * channels), BF16), (w_qkv.shape, BF16), rows, own_block, own_block]
        + [((m, 3 * m), F32), ((m, 2 * m), F32), rows],
        [normed, from_chip, from_off, window, own_grad, w_qkv],
        hbm=(3, 4, 5),
        scratch=like(window) + [dma(3 * PIECES + 2)],
        name="project",
    )
    chip_normed = swap_chip(normed, "node")
    chip_grad, off_grad = exchange(own_grad, own_grad, "node")
    probs = ((pairs, 2 * m, 3 * m), BF16)
    stats, kv, weights, grad_scores, near_q, w_out, cotangent = call(
        functools.partial(attend_kernel, scale, pair),
        [
            ((3 * pairs, 2 * m), F32),
            ((3 * m, 2 * channels), BF16),
            probs,
            probs,
            ((2 * m, channels), BF16),
            (w_out.shape, BF16),
            rows,
        ],
        [chip_normed, off_normed, w_qkv, own_qkv, own_grad, own_scores, own_products]
        + [bias, w_out, cotangent],
        hbm=(8, 9),
        scratch=[dma(2)],
        name="attend",
    )
    chip_stats, off_stats = exchange(stats, stats, "node")
    mesh_out, grad_normed, grad_key, grad_value = call(
        functools.partial(product_kernel, scale, pair),
        [
            rows,
            ((m, channels), F32),
            ((m, channels), F32),
            ((m, channels), F32),
        ],
        [
            weights,
            grad_scores,
            kv,
            own_qkv,
            own_grad,
            latent,
            w_out,
            w_qkv,
        ],
        hbm_outs=(0,),
        scratch=[pltpu.VMEM((m, channels), BF16)] * 3 + [dma(1)],
        name="product",
    )
    (mesh_grad,) = call(
        functools.partial(finish_kernel, pair),
        [rows],
        [
            chip_stats,
            off_stats,
            near_bias,
            near_q,
            chip_grad,
            off_grad,
            own_qkv,
            grad_key,
            grad_value,
            grad_normed,
            w_qkv,
            normal,
            inv_std,
            cotangent,
        ],
        name="finish",
    )
    return (mesh_out, mesh_grad)


def solution(mesh):
    rows = P(("groups", "node"), None)
    flat = P(("groups", "node"))
    placed = (rows, rows) + (flat,) * 8 + (P(None, ("groups", "node")), rows, P(), P(), P())
    return jax.shard_map(
        body, mesh=mesh, in_specs=placed, out_specs=(rows, rows), check_vma=False
    )
```

```python
import functools

import jax
import jax.numpy as jnp
from jax import lax
from jax.experimental import pallas as pl
from jax.experimental.pallas import tpu as pltpu
from jax.sharding import PartitionSpec as P

HEADS = 16
BAND = 128
LANES = 128
F32 = jnp.float32
BF16 = jnp.bfloat16
I32 = jnp.int32
VMEM_LIMIT = 28 * 2**20
PIECES = 2
EARLY = 32
PAD = 8
CHUNK = 64


def mm(a, b):
    return lax.dot_general(a, b, (((1,), (0,)), ((), ())), preferred_element_type=F32)


def mm_nt(a, b):
    return lax.dot_general(a, b, (((1,), (1,)), ((), ())), preferred_element_type=F32)


def mm_tn(a, b):
    return lax.dot_general(a, b, (((0,), (0,)), ((), ())), preferred_element_type=F32)


def iota(shape, dim):
    return lax.broadcasted_iota(I32, shape, dim)


def call(kernel, outs, args, hbm=(), hbm_outs=(), scratch=(), name=None, flops=None):
    args = [
        pltpu.with_memory_space_constraint(a, pltpu.HBM) if i in hbm else a
        for i, a in enumerate(args)
    ]

    def specs(count, far):
        return [
            pl.BlockSpec(memory_space=pltpu.HBM if i in far else pltpu.VMEM) for i in range(count)
        ]

    return pl.pallas_call(
        kernel,
        out_shape=[
            (pltpu.HBM if i in hbm_outs else jax.ShapeDtypeStruct)(shape, dtype)
            for i, (shape, dtype) in enumerate(outs)
        ],
        in_specs=specs(len(args), hbm),
        out_specs=specs(len(outs), hbm_outs),
        scratch_shapes=list(scratch),
        compiler_params=pltpu.CompilerParams(vmem_limit_bytes=VMEM_LIMIT),
        cost_estimate=flops and pl.CostEstimate(flops=flops, transcendentals=0, bytes_accessed=0),
        name=name,
    )(*args)


def dma(count):
    return pltpu.SemaphoreType.DMA((count,))


def start_all(pairs, sems):
    copies = [pltpu.make_async_copy(src, dst, sems.at[i]) for i, (src, dst) in enumerate(pairs)]
    for copy in copies:
        copy.start()
    return copies


def like(*arrays):
    return [pltpu.VMEM(a.shape, a.dtype) for a in arrays]


def swap_off(rows, axis):
    n = lax.axis_size(axis)
    pairs = [p for i in range(1, n - 1, 2) for p in ((i, i + 1), (i + 1, i))]
    return lax.ppermute(rows, axis, pairs)


def swap_chip(rows, axis):
    n = lax.axis_size(axis)
    return lax.ppermute(rows, axis, [p for i in range(0, n, 2) for p in ((i, i + 1), (i + 1, i))])


def exchange(chip_message, off_message, axis):
    from_chip = swap_chip(chip_message, axis)
    return from_chip, swap_off(off_message, axis)


def is_odd():
    return lax.axis_index("node") % 2


def everywhere():
    return lax.axis_index("node") >= 0


def gelu(projected):
    x = projected.astype(BF16).astype(F32)
    inner = (2.0 / jnp.pi) ** 0.5 * (x + 0.044715 * (x * x * x))
    return (0.5 * x * (1.0 + jnp.tanh(inner))).astype(BF16)


def onehot_rows(index_rows, count):
    parts = [
        jnp.where(iota((count, row.shape[1]), 0) == row, 1.0, 0.0).astype(BF16)
        for row in index_rows
    ]
    return parts[0] if len(parts) == 1 else jnp.concatenate(parts, 1)


def norm_stats(latent):
    values = latent.astype(F32)
    row_mean = jnp.mean(values, -1, keepdims=True)
    centred = values - row_mean
    variance = jnp.mean(centred * centred, -1, keepdims=True)
    inv_std = lax.rsqrt(variance + 1e-05)
    return centred * inv_std, inv_std


def pack_kernel(
    grid_hbm,
    cot_hbm,
    window_hbm,
    side_src_hbm,
    side_dst_hbm,
    side_count_hbm,
    far_src_hbm,
    far_dst_hbm,
    far_count_hbm,
    far_out,
    chip_out,
    off_out,
    grid,
    cot,
    window,
    side_src,
    side_dst,
    side_count,
    far_src,
    far_dst,
    far_count,
    far,
    meta,
    sems,
    out_sems,
):
    grid_rows, channels = grid.shape
    mesh_rows = window.shape[1]
    slots = far_src.shape[1]
    devices = far_count.shape[1]
    depth = slots // devices
    first = grid_rows - BAND
    count = side_src.shape[0] // 2
    copies = start_all(
        [
            (side_src_hbm, side_src),
            (side_dst_hbm, side_dst),
            (side_count_hbm, side_count),
            (window_hbm, window),
            (grid_hbm, grid),
            (cot_hbm.at[pl.ds(0, EARLY)], cot),
            (far_src_hbm, far_src),
            (far_dst_hbm, far_dst),
            (far_count_hbm, far_count),
        ],
        sems,
    )
    for copy in copies[:4]:
        copy.wait()
    for k in range(2):
        rank = iota((count, LANES), 0) * LANES + iota((count, LANES), 1)
        src = side_src[k * count : (k + 1) * count] - k * first
        live = rank < side_count[:, k : k + 1]
        dst = jnp.where(live, side_dst[k * count : (k + 1) * count], mesh_rows)
        reach = jnp.concatenate([window[...], jnp.zeros((count - 2, mesh_rows), I32)], 0)
        blank = jnp.zeros((count, channels - 2 * LANES - mesh_rows), I32)
        meta[k] = jnp.concatenate([src, dst, reach, blank], 1).astype(F32).astype(BF16)
    for copy in copies[4:6]:
        copy.wait()
    odd = is_odd()
    outs = start_all(
        [
            pair
            for k, out in ((1 - odd, chip_out), (odd, off_out))
            for pair in (
                (grid.at[pl.ds(pl.multiple_of(k * first, BAND), BAND)], out.at[pl.ds(0, BAND)]),
                (meta.at[k], out.at[pl.ds(BAND, count)]),
                (cot, out.at[pl.ds(BAND + count, EARLY)]),
            )
        ],
        out_sems,
    )
    for copy in copies[6:9]:
        copy.wait()
    slot = iota((1, slots), 1)
    receiver = jnp.where(iota((devices, slots), 0) == iota((devices, slots), 1) // depth, 1.0, 0.0)
    live = mm(far_count[...].astype(F32).astype(BF16), receiver.astype(BF16))
    target = jnp.where((slot % depth).astype(F32) < live, far_dst[...].astype(F32), 1.0 * mesh_rows)
    row = iota((2 * slots, slots), 0)
    mine = slot == row // (2 * depth) * depth + row % depth
    source = jnp.sum(jnp.where(mine, far_src[...].astype(F32), 0.0), 1, keepdims=True)
    column = jnp.sum(jnp.where(mine, target, 0.0), 1, keepdims=True)
    pick = jnp.where(iota((2 * slots, grid_rows), 1).astype(F32) == source, 1.0, 0.0).astype(BF16)
    rows = mm(pick, grid[...]).astype(BF16)
    half = channels // 2
    is_first = iota((2 * slots, half), 0) % (2 * depth) < depth
    far[:, :half] = jnp.where(is_first, rows[:, :half], rows[:, half:])
    far[:, half:] = jnp.broadcast_to(column, (2 * slots, LANES)).astype(BF16)
    last = pltpu.make_async_copy(far, far_out, out_sems.at[6])
    last.start()
    for copy in outs + [last]:
        copy.wait()


def own_kernel(
    grid_hbm,
    mesh_in_hbm,
    own_src_hbm,
    own_dst_hbm,
    cot_hbm,
    w_out_hbm,
    w_edge_hbm,
    partial_out,
    grad_hbm,
    w_edge,
    grid,
    mesh_in,
    own_src,
    own_dst,
    cot,
    w_out,
    grad,
    sems,
):
    grid_rows = grid.shape[0]
    mesh_rows = mesh_in.shape[0]
    copies = start_all(
        [
            (own_src_hbm, own_src),
            (own_dst_hbm, own_dst),
            (cot_hbm, cot),
            (w_out_hbm, w_out),
            (grid_hbm, grid),
            (w_edge_hbm, w_edge),
            (mesh_in_hbm, mesh_in),
        ],
        sems,
    )
    for copy in copies[:2]:
        copy.wait()
    rows = own_src.shape[0]
    src = onehot_rows([own_src[r : r + 1] for r in range(rows)], grid_rows)
    dst = onehot_rows([own_dst[r : r + 1] for r in range(rows)], mesh_rows)
    counts = mm_nt(dst, src).astype(BF16)
    for copy in copies[2:4]:
        copy.wait()
    grad[...] = mm_nt(cot[...], w_out[...]).astype(BF16)
    out = pltpu.make_async_copy(grad, grad_hbm, sems.at[7])
    out.start()
    for copy in copies[4:]:
        copy.wait()
    active = gelu(mm(grid[...], w_edge[...]))
    partial_out[...] = mesh_in[...].astype(F32) + mm(counts, active)
    out.wait()


def meta_of(message, count):
    return message[BAND : BAND + count].astype(F32).astype(I32)


def side_kernel(count, chip, off, w_edge, partial, partial_out):
    mesh_rows = partial.shape[0]
    uppers, lowers = [], []
    for side in (chip, off):
        meta = meta_of(side, count)
        src = onehot_rows([meta[r : r + 1, :LANES] for r in range(count)], BAND)
        dst = onehot_rows([meta[r : r + 1, LANES : 2 * LANES] for r in range(count)], mesh_rows)
        counts = mm_nt(dst, src)
        upper = counts.astype(BF16)
        uppers.append(upper)
        lowers.append((counts - upper.astype(F32)).astype(BF16))
    active = gelu(mm(jnp.concatenate([chip[:BAND], off[:BAND]], 0), w_edge[...]))
    landing = jnp.concatenate(uppers + lowers, 1)
    partial_out[...] = partial[...] + mm(landing, jnp.concatenate([active, active], 0))


def latent_kernel(
    depth, far, w_edge, partial, latent_out, normed_out, off_out, normal_out, inv_std_out
):
    mesh_rows, channels = partial.shape
    slots = far.shape[0]
    half = channels // 2
    first = far[:, :half]
    second = pltpu.roll(first.astype(F32), slots - depth, 0).astype(BF16)
    target = jnp.transpose(far[:, half:].astype(F32))
    if mesh_rows != LANES:
        target = jnp.broadcast_to(target[:1], (mesh_rows, slots))
    is_row = iota((mesh_rows, slots), 1) % (2 * depth) < depth
    hit = (target == iota((mesh_rows, slots), 0).astype(F32)) & is_row
    landing = jnp.where(hit, 1.0, 0.0).astype(BF16)
    active = gelu(mm(jnp.concatenate([first, second], 1), w_edge[...]))
    total = partial[...] + mm(landing, active)
    latent = total.astype(BF16)
    latent_out[...] = latent
    normal, inv_std = norm_stats(latent)
    normed = normal.astype(BF16)
    normed_out[...] = normed
    off_out[...] = jnp.concatenate([normed, jnp.zeros((PAD, channels), BF16)], 0)
    normal_out[...] = normal
    inv_std_out[...] = jnp.broadcast_to(inv_std, inv_std_out.shape)


def halves(rows, scale=None):
    first = iota(rows.shape, 1) < rows.shape[1] // 2
    if scale is not None:
        rows = rows * jnp.asarray(scale, rows.dtype)
    zero = jnp.zeros_like(rows)
    return jnp.concatenate([jnp.where(first, rows, zero), jnp.where(first, zero, rows)], 0)


def merge(stacked):
    m = stacked.shape[0] // 2
    first = iota((m, stacked.shape[1]), 1) < stacked.shape[1] // 2
    return jnp.where(first, stacked[:m], stacked[m:])


def near_places(m):
    odd = is_odd()
    return (1 - odd) * 2 * m, odd * 2 * m


def project_kernel(
    scale,
    pair,
    count,
    normed,
    chip_first,
    off_first,
    window_hbm,
    grad_hbm,
    w_qkv_hbm,
    qkv_out,
    w_qkv,
    grad_out,
    late_out,
    scores_out,
    products_out,
    bias_out,
    near_bias_out,
    normed_out,
    window,
    sems,
):
    m, channels = normed.shape
    normed_out[...] = normed[...]
    width = channels // PIECES
    starts = [part * channels + c * width for c in range(PIECES) for part in range(3)]
    copies = start_all(
        [(window_hbm, window), (grad_hbm, grad_out)]
        + [(w_qkv_hbm.at[:, pl.ds(at, width)], w_qkv.at[:, pl.ds(at, width)]) for at in starts],
        sems,
    )
    copies[0].wait()
    def masks():
        chip_at, off_at = near_places(m)
        reach = [meta_of(side, count)[:8, 2 * LANES : 2 * LANES + m] for side in (chip_first, off_first)]
        reach = jnp.concatenate(reach, 1)
        key_at = iota((m, 2 * m), 0) + m
        lane = iota((m, 2 * m), 1)
        query_at = jnp.where(lane < m, lane + chip_at, lane - m + off_at)
        keep = (key_at >= query_at - reach[0:1, :]) & (key_at <= query_at + reach[1:2, :])
        near_bias_out[...] = jnp.where(keep, 0.0, -jnp.inf).astype(F32)
        me = lax.axis_index("node")
        row = iota((3 * m, m), 0)
        key_at = jnp.where(row < m, row + chip_at, jnp.where(row < 2 * m, row - m + off_at, row - m))
        query_at = iota((3 * m, m), 1) + m
        at_end = (me == 0) | (me == lax.axis_size("node") - 1)
        missing = (row >= m) & (row < 2 * m) & at_end
        keep = (key_at >= query_at - window[0:1, :]) & (key_at <= query_at + window[1:2, :])
        bias = jnp.where(keep & jnp.logical_not(missing), 0.0, -jnp.inf).astype(F32)
        bias_out[...] = jnp.transpose(bias)

    masks()
    copies[1].wait()
    late_out[...] = grad_out[EARLY:]
    for i, at in enumerate(starts):
        copies[2 + i].wait()
        cols = slice(at, at + width)
        qkv_out[:, cols] = mm(normed[...], w_qkv[:, cols]).astype(BF16)
        for p in range(i // 3 * width // pair, (i // 3 + 1) * width // pair):
            q, k, v = (
                slice(part * channels + p * pair, part * channels + (p + 1) * pair)
                for part in range(3)
            )
            if i % 3 == 1:
                scores_out[p] = mm_nt(halves(qkv_out[:, q], scale), qkv_out[:, k])
            if i % 3 == 2:
                products_out[p] = mm_nt(halves(grad_out[:, q]), qkv_out[:, v])


def attend_kernel(
    scale,
    pair,
    chip_normed,
    off_normed,
    w_qkv,
    own_qkv,
    own_grad,
    own_scores,
    own_products,
    bias,
    w_out_hbm,
    cot_hbm,
    stats_out,
    kv,
    weights_out,
    scores_out,
    near_q,
    w_out,
    cot,
    sems,
):
    fetch = start_all([(w_out_hbm, w_out), (cot_hbm, cot)], sems)
    m, channels = chip_normed.shape
    pairs = channels // pair

    @pl.when(everywhere())
    def _():
        near = jnp.concatenate([chip_normed[...], off_normed[:m]], 0)

        def bring(group):
            cols = slice(group * 2 * pair, (group + 1) * 2 * pair)
            near_q[:, cols] = mm(near, w_qkv[:, cols]).astype(BF16) * jnp.asarray(scale, BF16)
            blocks = []
            for part in range(1, 3):
                at = part * channels + group * 2 * pair
                block = mm(near, w_qkv[:, at : at + 2 * pair]).astype(BF16)
                kv[: 2 * m, at - channels : at - channels + 2 * pair] = block
                blocks.append(block)
            return blocks

        brought = {0: bring(0)}
        kv[2 * m :] = own_qkv[:, channels:]
        lane = iota((CHUNK, LANES), 1)
        stats = [jnp.zeros((CHUNK, LANES), F32) for _ in range(2 * m // CHUNK)]

        def near_of(p):
            return [b[:, p % 2 * pair : (p % 2 + 1) * pair] for b in brought[p // 2]]

        def multiply(p):
            cols = slice(p * pair, (p + 1) * pair)
            keys, values = near_of(p)
            return (
                mm_nt(halves(own_qkv[:, cols], scale), keys),
                mm_nt(halves(own_grad[:, cols]), values),
            )

        ahead = multiply(0)
        for p in range(pairs):
            scores, grad_prob = ahead
            if p + 1 < pairs:
                if p % 2 == 0 and p + 2 < pairs:
                    brought[p // 2 + 1] = bring(p // 2 + 1)
                ahead = multiply(p + 1)
            weights, grad_scores = [], []
            for at in range(0, 2 * m, CHUNK):
                part = slice(at, at + CHUNK)
                place = slice(at % m, at % m + CHUNK)
                raw = jnp.concatenate([scores[part], own_scores[p, part]], 1) + bias[place]
                top = jnp.max(raw, 1, keepdims=True)
                shifted = jnp.exp(raw - top)
                inv_sum = 1.0 / jnp.sum(shifted, 1, keepdims=True)
                probs = shifted * inv_sum
                product = jnp.concatenate([grad_prob[part], own_products[p, part]], 1)
                delta = jnp.sum(probs * product, 1, keepdims=True)
                weights.append(probs.astype(BF16))
                grad_scores.append((probs * (product - delta)).astype(BF16))
                for k, column in enumerate((top, inv_sum, delta)):
                    stats[at // CHUNK] = jnp.where(lane == k * pairs + p, column, stats[at // CHUNK])
            weights_out[p] = jnp.concatenate(weights, 0)
            scores_out[p] = jnp.concatenate(grad_scores, 0)
        stats_out[...] = jnp.transpose(jnp.concatenate(stats, 0))[: 3 * pairs]

    for copy in fetch:
        copy.wait()


def product_kernel(
    scale,
    pair,
    weights,
    grad_scores,
    kv,
    own_qkv,
    own_grad,
    latent,
    w_out,
    w_qkv,
    chip_first,
    off_first,
    mesh_out_hbm,
    grad_normed,
    grad_key,
    grad_value,
    early_grad,
    attention,
    grad_query,
    mesh_out,
    sems,
):
    m, channels = latent.shape
    pairs = channels // pair
    for p in range(pairs):
        cols = slice(p * pair, (p + 1) * pair)
        value = kv[:, channels + p * pair : channels + (p + 1) * pair]
        attention[:, cols] = merge(mm(weights[p], value)).astype(BF16)
    mesh_out[...] = (latent[...].astype(F32) + mm(attention[...], w_out[...])).astype(BF16)
    out = pltpu.make_async_copy(mesh_out, mesh_out_hbm, sems.at[0])
    out.start()

    @pl.when(everywhere())
    def _():
        for p in range(pairs):
            cols = slice(p * pair, (p + 1) * pair)
            grad_query[:, cols] = (merge(mm(grad_scores[p], kv[:, cols])) * scale).astype(BF16)
        for p in range(pairs):
            cols = slice(p * pair, (p + 1) * pair)
            grad_key[:, cols] = mm_tn(grad_scores[p, :, 2 * m :], halves(own_qkv[:, cols], scale))
            grad_value[:, cols] = mm_tn(weights[p, :, 2 * m :], halves(own_grad[:, cols]))
        grad_normed[...] = mm_nt(grad_query[...], w_qkv[:, :channels])
        cots = jnp.concatenate([chip_first[-EARLY:], off_first[-EARLY:]], 0)
        early_grad[...] = mm_nt(cots, w_out[...]).astype(BF16)

    out.wait()


def finish_kernel(
    pair,
    chip_stats,
    off_stats,
    bias,
    near_q,
    early_grad,
    chip_grad,
    off_grad,
    own_qkv,
    grad_key,
    grad_value,
    grad_normed,
    w_qkv,
    normal,
    inv_std,
    cot,
    grad_out,
):
    m, channels = normal.shape
    pairs = channels // pair

    stats = []
    for h in range(2):
        lanes = slice(h * m, (h + 1) * m)
        stats.append(jnp.concatenate([chip_stats[:, lanes], off_stats[:, lanes]], 1))

    def multiply(p):
        cols = slice(p * pair, (p + 1) * pair)
        key2 = halves(own_qkv[:, channels + p * pair : channels + (p + 1) * pair])
        value2 = halves(own_qkv[:, 2 * channels + p * pair : 2 * channels + (p + 1) * pair])
        query = near_q[:, cols]
        grad = jnp.concatenate(
            [early_grad[:EARLY, cols], chip_grad[:, cols], early_grad[EARLY:, cols], off_grad[:, cols]],
            0,
        )
        return query, grad, mm_nt(key2, query), mm_nt(value2, grad)

    total = grad_normed[...]
    group = 2
    gks, gvs = [], []
    ahead = multiply(0)
    for p in range(pairs):
        cols = slice(p * pair, (p + 1) * pair)
        query, grad, scores, grad_prob = ahead
        if p + 1 < pairs:
            ahead = multiply(p + 1)
        weights, grad_scores = [], []
        for at in range(0, 2 * m, CHUNK):
            part = slice(at, at + CHUNK)
            place = slice(at % m, at % m + CHUNK)
            top, inv_sum, delta = (
                stats[at // m][k * pairs + p : k * pairs + p + 1] for k in range(3)
            )
            probs = jnp.exp(scores[part] + bias[place] - top) * inv_sum
            weights.append(probs.astype(BF16))
            grad_scores.append((probs * (grad_prob[part] - delta)).astype(BF16))
        gk = grad_key[:, cols] + merge(mm(jnp.concatenate(grad_scores, 0), query))
        gv = grad_value[:, cols] + merge(mm(jnp.concatenate(weights, 0), grad))
        gks.append(gk.astype(BF16))
        gvs.append(gv.astype(BF16))
        if len(gks) == group:
            at = channels + (p + 1 - group) * pair
            width = group * pair
            for blocks, start in ((gks, at), (gvs, at + channels)):
                total = total + mm_nt(
                    jnp.concatenate(blocks, 1), w_qkv[:, start : start + width]
                )
            gks, gvs = [], []
    centred = (
        total
        - jnp.mean(total, -1, keepdims=True)
        - normal[...] * jnp.mean(total * normal[...], -1, keepdims=True)
    )
    grad_out[...] = (cot[...].astype(F32) + inv_std[:, :1] * centred).astype(BF16)


def body(
    grid_in,
    mesh_in,
    own_src,
    own_dst,
    side_src,
    side_dst,
    side_count,
    far_src,
    far_dst,
    far_count,
    window,
    cotangent,
    w_edge,
    w_qkv,
    w_out,
):
    devices = lax.axis_size("node")
    grid_rows, channels = grid_in.shape
    m = mesh_in.shape[0]
    far_slots = far_src.shape[0]
    far_depth = far_slots // devices
    head_dim = channels // HEADS
    pair = 2 * head_dim
    pairs = channels // pair
    scale = head_dim ** (-0.5)
    meta_rows = side_src.shape[0] // (2 * LANES)

    side_src, side_dst = side_src.reshape(-1, LANES), side_dst.reshape(-1, LANES)
    own_src, own_dst = own_src.reshape(-1, LANES), own_dst.reshape(-1, LANES)
    far_src, far_dst = far_src.reshape(1, -1), far_dst.reshape(1, -1)
    side_count, far_count = side_count.reshape(1, -1), far_count.reshape(1, -1)
    message = ((BAND + meta_rows + EARLY, channels), BF16)
    far_block = (2 * far_slots, channels // 2 + LANES)
    far_message, chip_message, off_message = call(
        pack_kernel,
        [(far_block, BF16), message, message],
        [grid_in, cotangent, window, side_src, side_dst, side_count, far_src, far_dst, far_count],
        hbm=range(9),
        hbm_outs=range(3),
        scratch=like(grid_in)
        + [pltpu.VMEM((EARLY, channels), BF16)]
        + like(window, side_src, side_dst, side_count, far_src, far_dst, far_count)
        + [
            pltpu.VMEM(far_block, BF16),
            pltpu.VMEM((2, meta_rows, channels), BF16),
            dma(9),
            dma(7),
        ],
        name="pack",
    )
    from_chip, from_off = exchange(chip_message, off_message, "node")
    got_far = lax.all_to_all(
        far_message.reshape(devices, 2 * far_depth, far_block[1]),
        "node",
        split_axis=0,
        concat_axis=0,
        tiled=True,
    ).reshape(far_block)

    rows = ((m, channels), BF16)
    partial, own_grad, w_edge = call(
        own_kernel,
        [((m, channels), F32), rows, (w_edge.shape, BF16)],
        [grid_in, mesh_in, own_src, own_dst, cotangent, w_out, w_edge],
        hbm=range(7),
        hbm_outs=(1,),
        scratch=like(grid_in, mesh_in, own_src, own_dst, cotangent, w_out, cotangent) + [dma(8)],
        name="own",
    )
    (partial,) = call(
        functools.partial(side_kernel, meta_rows),
        [((m, channels), F32)],
        [from_chip, from_off, w_edge, partial],
        name="side",
        flops=8 * 10**9,
    )
    latent, normed, off_message, normal, inv_std = call(
        functools.partial(latent_kernel, far_depth),
        [rows, rows, ((m + PAD, channels), BF16), ((m, channels), F32), ((m, LANES), F32)],
        [got_far, w_edge, partial],
        name="latent",
    )
    off_normed = swap_off(off_message, "node")
    own_block = ((pairs, 2 * m, m), F32)
    own_qkv, w_qkv, own_grad, late_grad, own_scores, own_products, bias, near_bias, normed = call(
        functools.partial(project_kernel, scale, pair, meta_rows),
        [((m, 3 * channels), BF16), (w_qkv.shape, BF16), rows]
        + [((m - EARLY, channels), BF16), own_block, own_block]
        + [((m, 3 * m), F32), ((m, 2 * m), F32), rows],
        [normed, from_chip, from_off, window, own_grad, w_qkv],
        hbm=(3, 4, 5),
        scratch=like(window) + [dma(3 * PIECES + 2)],
        name="project",
    )
    chip_normed = swap_chip(normed, "node")
    chip_grad, off_grad = exchange(late_grad, late_grad, "node")
    probs = ((pairs, 2 * m, 3 * m), BF16)
    stats, kv, weights, grad_scores, near_q, w_out, cotangent = call(
        functools.partial(attend_kernel, scale, pair),
        [
            ((3 * pairs, 2 * m), F32),
            ((3 * m, 2 * channels), BF16),
            probs,
            probs,
            ((2 * m, channels), BF16),
            (w_out.shape, BF16),
            rows,
        ],
        [chip_normed, off_normed, w_qkv, own_qkv, own_grad, own_scores, own_products]
        + [bias, w_out, cotangent],
        hbm=(8, 9),
        scratch=[dma(2)],
        name="attend",
    )
    chip_stats, off_stats = exchange(stats, stats, "node")
    mesh_out, grad_normed, grad_key, grad_value, early_grad = call(
        functools.partial(product_kernel, scale, pair),
        [
            rows,
            ((m, channels), F32),
            ((m, channels), F32),
            ((m, channels), F32),
            ((2 * EARLY, channels), BF16),
        ],
        [
            weights,
            grad_scores,
            kv,
            own_qkv,
            own_grad,
            latent,
            w_out,
            w_qkv,
            from_chip,
            from_off,
        ],
        hbm_outs=(0,),
        scratch=[pltpu.VMEM((m, channels), BF16)] * 3 + [dma(1)],
        name="product",
    )
    (mesh_grad,) = call(
        functools.partial(finish_kernel, pair),
        [rows],
        [
            chip_stats,
            off_stats,
            near_bias,
            near_q,
            early_grad,
            chip_grad,
            off_grad,
            own_qkv,
            grad_key,
            grad_value,
            grad_normed,
            w_qkv,
            normal,
            inv_std,
            cotangent,
        ],
        name="finish",
    )
    return (mesh_out, mesh_grad)


def solution(mesh):
    rows = P(("groups", "node"), None)
    flat = P(("groups", "node"))
    placed = (rows, rows) + (flat,) * 8 + (P(None, ("groups", "node")), rows, P(), P(), P())
    return jax.shard_map(
        body, mesh=mesh, in_specs=placed, out_specs=(rows, rows), check_vma=False
    )
```

```python
import functools

import jax
import jax.numpy as jnp
from jax import lax
from jax.experimental import pallas as pl
from jax.experimental.pallas import tpu as pltpu
from jax.sharding import PartitionSpec as P

HEADS = 16
BAND = 128
LANES = 128
F32 = jnp.float32
BF16 = jnp.bfloat16
I32 = jnp.int32
VMEM_LIMIT = 28 * 2**20
PIECES = 2
PAD = 8
CHUNK = 64


def mm(a, b):
    return lax.dot_general(a, b, (((1,), (0,)), ((), ())), preferred_element_type=F32)


def mm_nt(a, b):
    return lax.dot_general(a, b, (((1,), (1,)), ((), ())), preferred_element_type=F32)


def mm_tn(a, b):
    return lax.dot_general(a, b, (((0,), (0,)), ((), ())), preferred_element_type=F32)


def iota(shape, dim):
    return lax.broadcasted_iota(I32, shape, dim)


def call(kernel, outs, args, hbm=(), hbm_outs=(), scratch=(), name=None, flops=None):
    args = [
        pltpu.with_memory_space_constraint(a, pltpu.HBM) if i in hbm else a
        for i, a in enumerate(args)
    ]

    def specs(count, far):
        return [
            pl.BlockSpec(memory_space=pltpu.HBM if i in far else pltpu.VMEM) for i in range(count)
        ]

    return pl.pallas_call(
        kernel,
        out_shape=[
            (pltpu.HBM if i in hbm_outs else jax.ShapeDtypeStruct)(shape, dtype)
            for i, (shape, dtype) in enumerate(outs)
        ],
        in_specs=specs(len(args), hbm),
        out_specs=specs(len(outs), hbm_outs),
        scratch_shapes=list(scratch),
        compiler_params=pltpu.CompilerParams(vmem_limit_bytes=VMEM_LIMIT),
        cost_estimate=flops and pl.CostEstimate(flops=flops, transcendentals=0, bytes_accessed=0),
        name=name,
    )(*args)


def dma(count):
    return pltpu.SemaphoreType.DMA((count,))


def start_all(pairs, sems):
    copies = [pltpu.make_async_copy(src, dst, sems.at[i]) for i, (src, dst) in enumerate(pairs)]
    for copy in copies:
        copy.start()
    return copies


def like(*arrays):
    return [pltpu.VMEM(a.shape, a.dtype) for a in arrays]


def swap_off(rows, axis):
    n = lax.axis_size(axis)
    pairs = [p for i in range(1, n - 1, 2) for p in ((i, i + 1), (i + 1, i))]
    return lax.ppermute(rows, axis, pairs)


def swap_chip(rows, axis):
    n = lax.axis_size(axis)
    return lax.ppermute(rows, axis, [p for i in range(0, n, 2) for p in ((i, i + 1), (i + 1, i))])


def exchange(chip_message, off_message, axis):
    from_chip = swap_chip(chip_message, axis)
    return from_chip, swap_off(off_message, axis)


def is_odd():
    return lax.axis_index("node") % 2


def everywhere():
    return lax.axis_index("node") >= 0


def gelu(projected):
    x = projected.astype(BF16).astype(F32)
    inner = (2.0 / jnp.pi) ** 0.5 * (x + 0.044715 * (x * x * x))
    return (0.5 * x * (1.0 + jnp.tanh(inner))).astype(BF16)


def onehot_rows(index_rows, count):
    parts = [
        jnp.where(iota((count, row.shape[1]), 0) == row, 1.0, 0.0).astype(BF16)
        for row in index_rows
    ]
    return parts[0] if len(parts) == 1 else jnp.concatenate(parts, 1)


def norm_stats(latent):
    values = latent.astype(F32)
    row_mean = jnp.mean(values, -1, keepdims=True)
    centred = values - row_mean
    variance = jnp.mean(centred * centred, -1, keepdims=True)
    inv_std = lax.rsqrt(variance + 1e-05)
    return centred * inv_std, inv_std


def pack_kernel(
    grid_hbm,
    window_hbm,
    side_src_hbm,
    side_dst_hbm,
    side_count_hbm,
    far_src_hbm,
    far_dst_hbm,
    far_count_hbm,
    far_out,
    chip_out,
    off_out,
    grid,
    window,
    side_src,
    side_dst,
    side_count,
    far_src,
    far_dst,
    far_count,
    far,
    meta,
    sems,
    out_sems,
):
    grid_rows, channels = grid.shape
    mesh_rows = window.shape[1]
    slots = far_src.shape[1]
    devices = far_count.shape[1]
    depth = slots // devices
    first = grid_rows - BAND
    count = side_src.shape[0] // 2
    copies = start_all(
        [
            (side_src_hbm, side_src),
            (side_dst_hbm, side_dst),
            (side_count_hbm, side_count),
            (window_hbm, window),
            (grid_hbm, grid),
            (far_src_hbm, far_src),
            (far_dst_hbm, far_dst),
            (far_count_hbm, far_count),
        ],
        sems,
    )
    for copy in copies[:4]:
        copy.wait()
    for k in range(2):
        rank = iota((count, LANES), 0) * LANES + iota((count, LANES), 1)
        src = side_src[k * count : (k + 1) * count] - k * first
        live = rank < side_count[:, k : k + 1]
        dst = jnp.where(live, side_dst[k * count : (k + 1) * count], mesh_rows)
        reach = jnp.concatenate([window[...], jnp.zeros((count - 2, mesh_rows), I32)], 0)
        blank = jnp.zeros((count, channels - 2 * LANES - mesh_rows), I32)
        meta[k] = jnp.concatenate([src, dst, reach, blank], 1).astype(F32).astype(BF16)
    copies[4].wait()
    odd = is_odd()
    outs = start_all(
        [
            pair
            for k, out in ((1 - odd, chip_out), (odd, off_out))
            for pair in (
                (grid.at[pl.ds(pl.multiple_of(k * first, BAND), BAND)], out.at[pl.ds(0, BAND)]),
                (meta.at[k], out.at[pl.ds(BAND, count)]),
            )
        ],
        out_sems,
    )
    for copy in copies[5:8]:
        copy.wait()
    slot = iota((1, slots), 1)
    receiver = jnp.where(iota((devices, slots), 0) == iota((devices, slots), 1) // depth, 1.0, 0.0)
    live = mm(far_count[...].astype(F32).astype(BF16), receiver.astype(BF16))
    target = jnp.where((slot % depth).astype(F32) < live, far_dst[...].astype(F32), 1.0 * mesh_rows)
    row = iota((2 * slots, slots), 0)
    mine = slot == row // (2 * depth) * depth + row % depth
    source = jnp.sum(jnp.where(mine, far_src[...].astype(F32), 0.0), 1, keepdims=True)
    column = jnp.sum(jnp.where(mine, target, 0.0), 1, keepdims=True)
    pick = jnp.where(iota((2 * slots, grid_rows), 1).astype(F32) == source, 1.0, 0.0).astype(BF16)
    rows = mm(pick, grid[...]).astype(BF16)
    half = channels // 2
    is_first = iota((2 * slots, half), 0) % (2 * depth) < depth
    far[:, :half] = jnp.where(is_first, rows[:, :half], rows[:, half:])
    far[:, half:] = jnp.broadcast_to(column, (2 * slots, LANES)).astype(BF16)
    last = pltpu.make_async_copy(far, far_out, out_sems.at[4])
    last.start()
    for copy in outs + [last]:
        copy.wait()


def own_kernel(
    grid_hbm,
    mesh_in_hbm,
    own_src_hbm,
    own_dst_hbm,
    cot_hbm,
    w_out_hbm,
    w_edge_hbm,
    partial_out,
    grad_hbm,
    w_edge,
    grid,
    mesh_in,
    own_src,
    own_dst,
    cot,
    w_out,
    grad,
    sems,
):
    grid_rows = grid.shape[0]
    mesh_rows = mesh_in.shape[0]
    copies = start_all(
        [
            (own_src_hbm, own_src),
            (own_dst_hbm, own_dst),
            (cot_hbm, cot),
            (w_out_hbm, w_out),
            (grid_hbm, grid),
            (w_edge_hbm, w_edge),
            (mesh_in_hbm, mesh_in),
        ],
        sems,
    )
    for copy in copies[:2]:
        copy.wait()
    rows = own_src.shape[0]
    src = onehot_rows([own_src[r : r + 1] for r in range(rows)], grid_rows)
    dst = onehot_rows([own_dst[r : r + 1] for r in range(rows)], mesh_rows)
    counts = mm_nt(dst, src).astype(BF16)
    for copy in copies[2:4]:
        copy.wait()
    grad[...] = mm_nt(cot[...], w_out[...]).astype(BF16)
    out = pltpu.make_async_copy(grad, grad_hbm, sems.at[7])
    out.start()
    for copy in copies[4:]:
        copy.wait()
    active = gelu(mm(grid[...], w_edge[...]))
    partial_out[...] = mesh_in[...].astype(F32) + mm(counts, active)
    out.wait()


def meta_of(message, count):
    return message[BAND : BAND + count].astype(F32).astype(I32)


def side_kernel(count, chip, off, w_edge, partial, partial_out):
    mesh_rows = partial.shape[0]
    uppers, lowers = [], []
    for side in (chip, off):
        meta = meta_of(side, count)
        src = onehot_rows([meta[r : r + 1, :LANES] for r in range(count)], BAND)
        dst = onehot_rows([meta[r : r + 1, LANES : 2 * LANES] for r in range(count)], mesh_rows)
        counts = mm_nt(dst, src)
        upper = counts.astype(BF16)
        uppers.append(upper)
        lowers.append((counts - upper.astype(F32)).astype(BF16))
    active = gelu(mm(jnp.concatenate([chip[:BAND], off[:BAND]], 0), w_edge[...]))
    landing = jnp.concatenate(uppers + lowers, 1)
    partial_out[...] = partial[...] + mm(landing, jnp.concatenate([active, active], 0))


def latent_kernel(
    depth, far, w_edge, partial, latent_out, normed_out, off_out, normal_out, inv_std_out
):
    mesh_rows, channels = partial.shape
    slots = far.shape[0]
    half = channels // 2
    first = far[:, :half]
    second = pltpu.roll(first.astype(F32), slots - depth, 0).astype(BF16)
    target = jnp.transpose(far[:, half:].astype(F32))
    if mesh_rows != LANES:
        target = jnp.broadcast_to(target[:1], (mesh_rows, slots))
    is_row = iota((mesh_rows, slots), 1) % (2 * depth) < depth
    hit = (target == iota((mesh_rows, slots), 0).astype(F32)) & is_row
    landing = jnp.where(hit, 1.0, 0.0).astype(BF16)
    active = gelu(mm(jnp.concatenate([first, second], 1), w_edge[...]))
    total = partial[...] + mm(landing, active)
    latent = total.astype(BF16)
    latent_out[...] = latent
    normal, inv_std = norm_stats(latent)
    normed = normal.astype(BF16)
    normed_out[...] = normed
    off_out[...] = jnp.concatenate([normed, jnp.zeros((PAD, channels), BF16)], 0)
    normal_out[...] = normal
    inv_std_out[...] = jnp.broadcast_to(inv_std, inv_std_out.shape)


def halves(rows, scale=None):
    first = iota(rows.shape, 1) < rows.shape[1] // 2
    if scale is not None:
        rows = rows * jnp.asarray(scale, rows.dtype)
    zero = jnp.zeros_like(rows)
    return jnp.concatenate([jnp.where(first, rows, zero), jnp.where(first, zero, rows)], 0)


def merge(stacked):
    m = stacked.shape[0] // 2
    first = iota((m, stacked.shape[1]), 1) < stacked.shape[1] // 2
    return jnp.where(first, stacked[:m], stacked[m:])


def near_places(m):
    odd = is_odd()
    return (1 - odd) * 2 * m, odd * 2 * m


def project_kernel(
    scale,
    pair,
    count,
    normed,
    chip_first,
    off_first,
    window_hbm,
    grad_hbm,
    w_qkv_hbm,
    qkv_out,
    w_qkv,
    grad_out,
    scores_out,
    products_out,
    bias_out,
    near_bias_out,
    normed_out,
    window,
    sems,
):
    m, channels = normed.shape
    normed_out[...] = normed[...]
    width = channels // PIECES
    starts = [part * channels + c * width for c in range(PIECES) for part in range(3)]
    copies = start_all(
        [(window_hbm, window), (grad_hbm, grad_out)]
        + [(w_qkv_hbm.at[:, pl.ds(at, width)], w_qkv.at[:, pl.ds(at, width)]) for at in starts],
        sems,
    )
    copies[0].wait()
    def masks():
        chip_at, off_at = near_places(m)
        reach = [meta_of(side, count)[:8, 2 * LANES : 2 * LANES + m] for side in (chip_first, off_first)]
        reach = jnp.concatenate(reach, 1)
        key_at = iota((m, 2 * m), 0) + m
        lane = iota((m, 2 * m), 1)
        query_at = jnp.where(lane < m, lane + chip_at, lane - m + off_at)
        keep = (key_at >= query_at - reach[0:1, :]) & (key_at <= query_at + reach[1:2, :])
        near_bias_out[...] = jnp.where(keep, 0.0, -jnp.inf).astype(F32)
        me = lax.axis_index("node")
        row = iota((3 * m, m), 0)
        key_at = jnp.where(row < m, row + chip_at, jnp.where(row < 2 * m, row - m + off_at, row - m))
        query_at = iota((3 * m, m), 1) + m
        at_end = (me == 0) | (me == lax.axis_size("node") - 1)
        missing = (row >= m) & (row < 2 * m) & at_end
        keep = (key_at >= query_at - window[0:1, :]) & (key_at <= query_at + window[1:2, :])
        bias = jnp.where(keep & jnp.logical_not(missing), 0.0, -jnp.inf).astype(F32)
        bias_out[...] = jnp.transpose(bias)

    masks()
    copies[1].wait()
    for i, at in enumerate(starts):
        copies[2 + i].wait()
        cols = slice(at, at + width)
        qkv_out[:, cols] = mm(normed[...], w_qkv[:, cols]).astype(BF16)
        for p in range(i // 3 * width // pair, (i // 3 + 1) * width // pair):
            q, k, v = (
                slice(part * channels + p * pair, part * channels + (p + 1) * pair)
                for part in range(3)
            )
            if i % 3 == 1:
                scores_out[p] = mm_nt(halves(qkv_out[:, q], scale), qkv_out[:, k])
            if i % 3 == 2:
                products_out[p] = mm_nt(halves(grad_out[:, q]), qkv_out[:, v])


def attend_kernel(
    scale,
    pair,
    chip_normed,
    off_normed,
    w_qkv,
    own_qkv,
    own_grad,
    own_scores,
    own_products,
    bias,
    w_out_hbm,
    cot_hbm,
    stats_out,
    kv,
    weights_out,
    scores_out,
    near_q,
    w_out,
    cot,
    sems,
):
    fetch = start_all([(w_out_hbm, w_out), (cot_hbm, cot)], sems)
    m, channels = chip_normed.shape
    pairs = channels // pair

    @pl.when(everywhere())
    def _():
        near = jnp.concatenate([chip_normed[...], off_normed[:m]], 0)

        def bring(group):
            cols = slice(group * 2 * pair, (group + 1) * 2 * pair)
            near_q[:, cols] = mm(near, w_qkv[:, cols]).astype(BF16) * jnp.asarray(scale, BF16)
            blocks = []
            for part in range(1, 3):
                at = part * channels + group * 2 * pair
                block = mm(near, w_qkv[:, at : at + 2 * pair]).astype(BF16)
                kv[: 2 * m, at - channels : at - channels + 2 * pair] = block
                blocks.append(block)
            return blocks

        brought = {0: bring(0)}
        kv[2 * m :] = own_qkv[:, channels:]
        lane = iota((CHUNK, LANES), 1)
        stats = [jnp.zeros((CHUNK, LANES), F32) for _ in range(2 * m // CHUNK)]

        def near_of(p):
            return [b[:, p % 2 * pair : (p % 2 + 1) * pair] for b in brought[p // 2]]

        def multiply(p):
            cols = slice(p * pair, (p + 1) * pair)
            keys, values = near_of(p)
            return (
                mm_nt(halves(own_qkv[:, cols], scale), keys),
                mm_nt(halves(own_grad[:, cols]), values),
            )

        ahead = multiply(0)
        for p in range(pairs):
            scores, grad_prob = ahead
            if p + 1 < pairs:
                if p % 2 == 0 and p + 2 < pairs:
                    brought[p // 2 + 1] = bring(p // 2 + 1)
                ahead = multiply(p + 1)
            weights, grad_scores = [], []
            for at in range(0, 2 * m, CHUNK):
                part = slice(at, at + CHUNK)
                place = slice(at % m, at % m + CHUNK)
                raw = jnp.concatenate([scores[part], own_scores[p, part]], 1) + bias[place]
                top = jnp.max(raw, 1, keepdims=True)
                shifted = jnp.exp(raw - top)
                inv_sum = 1.0 / jnp.sum(shifted, 1, keepdims=True)
                probs = shifted * inv_sum
                product = jnp.concatenate([grad_prob[part], own_products[p, part]], 1)
                delta = jnp.sum(probs * product, 1, keepdims=True)
                weights.append(probs.astype(BF16))
                grad_scores.append((probs * (product - delta)).astype(BF16))
                for k, column in enumerate((top, inv_sum, delta)):
                    stats[at // CHUNK] = jnp.where(lane == k * pairs + p, column, stats[at // CHUNK])
            weights_out[p] = jnp.concatenate(weights, 0)
            scores_out[p] = jnp.concatenate(grad_scores, 0)
        stats_out[...] = jnp.transpose(jnp.concatenate(stats, 0))[: 3 * pairs]

    for copy in fetch:
        copy.wait()


def product_kernel(
    scale,
    pair,
    weights,
    grad_scores,
    kv,
    own_qkv,
    own_grad,
    latent,
    w_out,
    w_qkv,
    mesh_out_hbm,
    grad_normed,
    grad_key,
    grad_value,
    attention,
    grad_query,
    mesh_out,
    sems,
):
    m, channels = latent.shape
    pairs = channels // pair
    for p in range(pairs):
        cols = slice(p * pair, (p + 1) * pair)
        value = kv[:, channels + p * pair : channels + (p + 1) * pair]
        attention[:, cols] = merge(mm(weights[p], value)).astype(BF16)
    mesh_out[...] = (latent[...].astype(F32) + mm(attention[...], w_out[...])).astype(BF16)
    out = pltpu.make_async_copy(mesh_out, mesh_out_hbm, sems.at[0])
    out.start()

    @pl.when(everywhere())
    def _():
        for p in range(pairs):
            cols = slice(p * pair, (p + 1) * pair)
            grad_query[:, cols] = (merge(mm(grad_scores[p], kv[:, cols])) * scale).astype(BF16)
        for p in range(pairs):
            cols = slice(p * pair, (p + 1) * pair)
            grad_key[:, cols] = mm_tn(grad_scores[p, :, 2 * m :], halves(own_qkv[:, cols], scale))
            grad_value[:, cols] = mm_tn(weights[p, :, 2 * m :], halves(own_grad[:, cols]))
        grad_normed[...] = mm_nt(grad_query[...], w_qkv[:, :channels])

    out.wait()


def finish_kernel(
    pair,
    chip_stats,
    off_stats,
    bias,
    near_q,
    chip_grad,
    off_grad,
    own_qkv,
    grad_key,
    grad_value,
    grad_normed,
    w_qkv,
    normal,
    inv_std,
    cot,
    grad_out,
):
    m, channels = normal.shape
    pairs = channels // pair

    stats = []
    for h in range(2):
        lanes = slice(h * m, (h + 1) * m)
        stats.append(jnp.concatenate([chip_stats[:, lanes], off_stats[:, lanes]], 1))

    def multiply(p):
        cols = slice(p * pair, (p + 1) * pair)
        key2 = halves(own_qkv[:, channels + p * pair : channels + (p + 1) * pair])
        value2 = halves(own_qkv[:, 2 * channels + p * pair : 2 * channels + (p + 1) * pair])
        query = near_q[:, cols]
        grad = jnp.concatenate([chip_grad[:, cols], off_grad[:, cols]], 0)
        return query, grad, mm_nt(key2, query), mm_nt(value2, grad)

    total = grad_normed[...]
    group = pairs // 2
    gks, gvs = [], []
    ahead = multiply(0)
    for p in range(pairs):
        cols = slice(p * pair, (p + 1) * pair)
        query, grad, scores, grad_prob = ahead
        if p + 1 < pairs:
            ahead = multiply(p + 1)
        weights, grad_scores = [], []
        for at in range(0, 2 * m, CHUNK):
            part = slice(at, at + CHUNK)
            place = slice(at % m, at % m + CHUNK)
            top, inv_sum, delta = (
                stats[at // m][k * pairs + p : k * pairs + p + 1] for k in range(3)
            )
            probs = jnp.exp(scores[part] + bias[place] - top) * inv_sum
            weights.append(probs.astype(BF16))
            grad_scores.append((probs * (grad_prob[part] - delta)).astype(BF16))
        gk = grad_key[:, cols] + merge(mm(jnp.concatenate(grad_scores, 0), query))
        gv = grad_value[:, cols] + merge(mm(jnp.concatenate(weights, 0), grad))
        gks.append(gk.astype(BF16))
        gvs.append(gv.astype(BF16))
        if len(gks) == group:
            at = channels + (p + 1 - group) * pair
            width = group * pair
            for blocks, start in ((gks, at), (gvs, at + channels)):
                total = total + mm_nt(
                    jnp.concatenate(blocks, 1), w_qkv[:, start : start + width]
                )
            gks, gvs = [], []
    centred = (
        total
        - jnp.mean(total, -1, keepdims=True)
        - normal[...] * jnp.mean(total * normal[...], -1, keepdims=True)
    )
    grad_out[...] = (cot[...].astype(F32) + inv_std[:, :1] * centred).astype(BF16)


def body(
    grid_in,
    mesh_in,
    own_src,
    own_dst,
    side_src,
    side_dst,
    side_count,
    far_src,
    far_dst,
    far_count,
    window,
    cotangent,
    w_edge,
    w_qkv,
    w_out,
):
    devices = lax.axis_size("node")
    grid_rows, channels = grid_in.shape
    m = mesh_in.shape[0]
    far_slots = far_src.shape[0]
    far_depth = far_slots // devices
    head_dim = channels // HEADS
    pair = 2 * head_dim
    pairs = channels // pair
    scale = head_dim ** (-0.5)
    meta_rows = side_src.shape[0] // (2 * LANES)

    side_src, side_dst = side_src.reshape(-1, LANES), side_dst.reshape(-1, LANES)
    own_src, own_dst = own_src.reshape(-1, LANES), own_dst.reshape(-1, LANES)
    far_src, far_dst = far_src.reshape(1, -1), far_dst.reshape(1, -1)
    side_count, far_count = side_count.reshape(1, -1), far_count.reshape(1, -1)
    message = ((BAND + meta_rows, channels), BF16)
    far_block = (2 * far_slots, channels // 2 + LANES)
    far_message, chip_message, off_message = call(
        pack_kernel,
        [(far_block, BF16), message, message],
        [grid_in, window, side_src, side_dst, side_count, far_src, far_dst, far_count],
        hbm=range(8),
        hbm_outs=range(3),
        scratch=like(grid_in, window, side_src, side_dst, side_count, far_src, far_dst, far_count)
        + [
            pltpu.VMEM(far_block, BF16),
            pltpu.VMEM((2, meta_rows, channels), BF16),
            dma(8),
            dma(5),
        ],
        name="pack",
    )
    from_chip, from_off = exchange(chip_message, off_message, "node")
    got_far = lax.all_to_all(
        far_message.reshape(devices, 2 * far_depth, far_block[1]),
        "node",
        split_axis=0,
        concat_axis=0,
        tiled=True,
    ).reshape(far_block)

    rows = ((m, channels), BF16)
    partial, own_grad, w_edge = call(
        own_kernel,
        [((m, channels), F32), rows, (w_edge.shape, BF16)],
        [grid_in, mesh_in, own_src, own_dst, cotangent, w_out, w_edge],
        hbm=range(7),
        hbm_outs=(1,),
        scratch=like(grid_in, mesh_in, own_src, own_dst, cotangent, w_out, cotangent) + [dma(8)],
        name="own",
    )
    (partial,) = call(
        functools.partial(side_kernel, meta_rows),
        [((m, channels), F32)],
        [from_chip, from_off, w_edge, partial],
        name="side",
        flops=8 * 10**9,
    )
    latent, normed, off_message, normal, inv_std = call(
        functools.partial(latent_kernel, far_depth),
        [rows, rows, ((m + PAD, channels), BF16), ((m, channels), F32), ((m, LANES), F32)],
        [got_far, w_edge, partial],
        name="latent",
    )
    off_normed = swap_off(off_message, "node")
    own_block = ((pairs, 2 * m, m), F32)
    own_qkv, w_qkv, own_grad, own_scores, own_products, bias, near_bias, normed = call(
        functools.partial(project_kernel, scale, pair, meta_rows),
        [((m, 3 * channels), BF16), (w_qkv.shape, BF16), rows, own_block, own_block]
        + [((m, 3 * m), F32), ((m, 2 * m), F32), rows],
        [normed, from_chip, from_off, window, own_grad, w_qkv],
        hbm=(3, 4, 5),
        scratch=like(window) + [dma(3 * PIECES + 2)],
        name="project",
    )
    chip_normed = swap_chip(normed, "node")
    chip_grad, off_grad = exchange(own_grad, own_grad, "node")
    probs = ((pairs, 2 * m, 3 * m), BF16)
    stats, kv, weights, grad_scores, near_q, w_out, cotangent = call(
        functools.partial(attend_kernel, scale, pair),
        [
            ((3 * pairs, 2 * m), F32),
            ((3 * m, 2 * channels), BF16),
            probs,
            probs,
            ((2 * m, channels), BF16),
            (w_out.shape, BF16),
            rows,
        ],
        [chip_normed, off_normed, w_qkv, own_qkv, own_grad, own_scores, own_products]
        + [bias, w_out, cotangent],
        hbm=(8, 9),
        scratch=[dma(2)],
        name="attend",
    )
    chip_stats, off_stats = exchange(stats, stats, "node")
    mesh_out, grad_normed, grad_key, grad_value = call(
        functools.partial(product_kernel, scale, pair),
        [
            rows,
            ((m, channels), F32),
            ((m, channels), F32),
            ((m, channels), F32),
        ],
        [
            weights,
            grad_scores,
            kv,
            own_qkv,
            own_grad,
            latent,
            w_out,
            w_qkv,
        ],
        hbm_outs=(0,),
        scratch=[pltpu.VMEM((m, channels), BF16)] * 3 + [dma(1)],
        name="product",
    )
    (mesh_grad,) = call(
        functools.partial(finish_kernel, pair),
        [rows],
        [
            chip_stats,
            off_stats,
            near_bias,
            near_q,
            chip_grad,
            off_grad,
            own_qkv,
            grad_key,
            grad_value,
            grad_normed,
            w_qkv,
            normal,
            inv_std,
            cotangent,
        ],
        name="finish",
    )
    return (mesh_out, mesh_grad)


def solution(mesh):
    rows = P(("groups", "node"), None)
    flat = P(("groups", "node"))
    placed = (rows, rows) + (flat,) * 8 + (P(None, ("groups", "node")), rows, P(), P(), P())
    return jax.shard_map(
        body, mesh=mesh, in_specs=placed, out_specs=(rows, rows), check_vma=False
    )
```

```python
import functools

import jax
import jax.numpy as jnp
from jax import lax
from jax.experimental import pallas as pl
from jax.experimental.pallas import tpu as pltpu
from jax.sharding import PartitionSpec as P

HEADS = 16
BAND = 128
LANES = 128
F32 = jnp.float32
BF16 = jnp.bfloat16
I32 = jnp.int32
VMEM_LIMIT = 28 * 2**20
PIECES = 2
PAD = 8
CHUNK = 64


def mm(a, b):
    return lax.dot_general(a, b, (((1,), (0,)), ((), ())), preferred_element_type=F32)


def mm_nt(a, b):
    return lax.dot_general(a, b, (((1,), (1,)), ((), ())), preferred_element_type=F32)


def mm_tn(a, b):
    return lax.dot_general(a, b, (((0,), (0,)), ((), ())), preferred_element_type=F32)


def iota(shape, dim):
    return lax.broadcasted_iota(I32, shape, dim)


def call(kernel, outs, args, hbm=(), hbm_outs=(), scratch=(), name=None, flops=None):
    args = [
        pltpu.with_memory_space_constraint(a, pltpu.HBM) if i in hbm else a
        for i, a in enumerate(args)
    ]

    def specs(count, far):
        return [
            pl.BlockSpec(memory_space=pltpu.HBM if i in far else pltpu.VMEM) for i in range(count)
        ]

    return pl.pallas_call(
        kernel,
        out_shape=[
            (pltpu.HBM if i in hbm_outs else jax.ShapeDtypeStruct)(shape, dtype)
            for i, (shape, dtype) in enumerate(outs)
        ],
        in_specs=specs(len(args), hbm),
        out_specs=specs(len(outs), hbm_outs),
        scratch_shapes=list(scratch),
        compiler_params=pltpu.CompilerParams(vmem_limit_bytes=VMEM_LIMIT),
        cost_estimate=flops and pl.CostEstimate(flops=flops, transcendentals=0, bytes_accessed=0),
        name=name,
    )(*args)


def dma(count):
    return pltpu.SemaphoreType.DMA((count,))


def start_all(pairs, sems):
    copies = [pltpu.make_async_copy(src, dst, sems.at[i]) for i, (src, dst) in enumerate(pairs)]
    for copy in copies:
        copy.start()
    return copies


def like(*arrays):
    return [pltpu.VMEM(a.shape, a.dtype) for a in arrays]


def swap_off(rows, axis):
    n = lax.axis_size(axis)
    pairs = [p for i in range(1, n - 1, 2) for p in ((i, i + 1), (i + 1, i))]
    return lax.ppermute(rows, axis, pairs)


def swap_chip(rows, axis):
    n = lax.axis_size(axis)
    return lax.ppermute(rows, axis, [p for i in range(0, n, 2) for p in ((i, i + 1), (i + 1, i))])


def exchange(chip_message, off_message, axis):
    from_chip = swap_chip(chip_message, axis)
    return from_chip, swap_off(off_message, axis)


def is_odd():
    return lax.axis_index("node") % 2


def everywhere():
    return lax.axis_index("node") >= 0


def gelu(projected):
    x = projected.astype(BF16).astype(F32)
    inner = (2.0 / jnp.pi) ** 0.5 * (x + 0.044715 * (x * x * x))
    return (0.5 * x * (1.0 + jnp.tanh(inner))).astype(BF16)


def onehot_rows(index_rows, count):
    parts = [
        jnp.where(iota((count, row.shape[1]), 0) == row, 1.0, 0.0).astype(BF16)
        for row in index_rows
    ]
    return parts[0] if len(parts) == 1 else jnp.concatenate(parts, 1)


def norm_stats(latent):
    values = latent.astype(F32)
    row_mean = jnp.mean(values, -1, keepdims=True)
    centred = values - row_mean
    variance = jnp.mean(centred * centred, -1, keepdims=True)
    inv_std = lax.rsqrt(variance + 1e-05)
    return centred * inv_std, inv_std


def pack_kernel(
    grid_hbm,
    window_hbm,
    side_src_hbm,
    side_dst_hbm,
    side_count_hbm,
    far_src_hbm,
    far_dst_hbm,
    far_count_hbm,
    far_out,
    chip_out,
    off_out,
    grid,
    window,
    side_src,
    side_dst,
    side_count,
    far_src,
    far_dst,
    far_count,
    far,
    meta,
    sems,
    out_sems,
):
    grid_rows, channels = grid.shape
    mesh_rows = window.shape[1]
    slots = far_src.shape[1]
    devices = far_count.shape[1]
    depth = slots // devices
    first = grid_rows - BAND
    count = side_src.shape[0] // 2
    copies = start_all(
        [
            (side_src_hbm, side_src),
            (side_dst_hbm, side_dst),
            (side_count_hbm, side_count),
            (window_hbm, window),
            (grid_hbm, grid),
            (far_src_hbm, far_src),
            (far_dst_hbm, far_dst),
            (far_count_hbm, far_count),
        ],
        sems,
    )
    for copy in copies[:4]:
        copy.wait()
    for k in range(2):
        rank = iota((count, LANES), 0) * LANES + iota((count, LANES), 1)
        src = side_src[k * count : (k + 1) * count] - k * first
        live = rank < side_count[:, k : k + 1]
        dst = jnp.where(live, side_dst[k * count : (k + 1) * count], mesh_rows)
        reach = jnp.concatenate([window[...], jnp.zeros((count - 2, mesh_rows), I32)], 0)
        blank = jnp.zeros((count, channels - 2 * LANES - mesh_rows), I32)
        meta[k] = jnp.concatenate([src, dst, reach, blank], 1).astype(F32).astype(BF16)
    copies[4].wait()
    odd = is_odd()
    outs = start_all(
        [
            pair
            for k, out in ((1 - odd, chip_out), (odd, off_out))
            for pair in (
                (grid.at[pl.ds(pl.multiple_of(k * first, BAND), BAND)], out.at[pl.ds(0, BAND)]),
                (meta.at[k], out.at[pl.ds(BAND, count)]),
            )
        ],
        out_sems,
    )
    for copy in copies[5:8]:
        copy.wait()
    slot = iota((1, slots), 1)
    receiver = jnp.where(iota((devices, slots), 0) == iota((devices, slots), 1) // depth, 1.0, 0.0)
    live = mm(far_count[...].astype(F32).astype(BF16), receiver.astype(BF16))
    target = jnp.where((slot % depth).astype(F32) < live, far_dst[...].astype(F32), 1.0 * mesh_rows)
    row = iota((2 * slots, slots), 0)
    mine = slot == row // (2 * depth) * depth + row % depth
    source = jnp.sum(jnp.where(mine, far_src[...].astype(F32), 0.0), 1, keepdims=True)
    column = jnp.sum(jnp.where(mine, target, 0.0), 1, keepdims=True)
    pick = jnp.where(iota((2 * slots, grid_rows), 1).astype(F32) == source, 1.0, 0.0).astype(BF16)
    rows = mm(pick, grid[...]).astype(BF16)
    half = channels // 2
    is_first = iota((2 * slots, half), 0) % (2 * depth) < depth
    far[:, :half] = jnp.where(is_first, rows[:, :half], rows[:, half:])
    far[:, half:] = jnp.broadcast_to(column, (2 * slots, LANES)).astype(BF16)
    last = pltpu.make_async_copy(far, far_out, out_sems.at[4])
    last.start()
    for copy in outs + [last]:
        copy.wait()


def own_kernel(
    grid_hbm,
    mesh_in_hbm,
    own_src_hbm,
    own_dst_hbm,
    cot_hbm,
    w_out_hbm,
    w_edge_hbm,
    partial_out,
    grad_hbm,
    w_edge,
    grid,
    mesh_in,
    own_src,
    own_dst,
    cot,
    w_out,
    grad,
    sems,
):
    grid_rows = grid.shape[0]
    mesh_rows = mesh_in.shape[0]
    copies = start_all(
        [
            (own_src_hbm, own_src),
            (own_dst_hbm, own_dst),
            (cot_hbm, cot),
            (w_out_hbm, w_out),
            (grid_hbm, grid),
            (w_edge_hbm, w_edge),
            (mesh_in_hbm, mesh_in),
        ],
        sems,
    )
    for copy in copies[:2]:
        copy.wait()
    rows = own_src.shape[0]
    src = onehot_rows([own_src[r : r + 1] for r in range(rows)], grid_rows)
    dst = onehot_rows([own_dst[r : r + 1] for r in range(rows)], mesh_rows)
    counts = mm_nt(dst, src).astype(BF16)
    for copy in copies[2:4]:
        copy.wait()
    grad[...] = mm_nt(cot[...], w_out[...]).astype(BF16)
    out = pltpu.make_async_copy(grad, grad_hbm, sems.at[7])
    out.start()
    for copy in copies[4:]:
        copy.wait()
    active = gelu(mm(grid[...], w_edge[...]))
    partial_out[...] = mesh_in[...].astype(F32) + mm(counts, active)
    out.wait()


def meta_of(message, count):
    return message[BAND : BAND + count].astype(F32).astype(I32)


def side_kernel(count, chip, off, w_edge, partial, partial_out):
    mesh_rows = partial.shape[0]
    uppers, lowers = [], []
    for side in (chip, off):
        meta = meta_of(side, count)
        src = onehot_rows([meta[r : r + 1, :LANES] for r in range(count)], BAND)
        dst = onehot_rows([meta[r : r + 1, LANES : 2 * LANES] for r in range(count)], mesh_rows)
        counts = mm_nt(dst, src)
        upper = counts.astype(BF16)
        uppers.append(upper)
        lowers.append((counts - upper.astype(F32)).astype(BF16))
    active = gelu(mm(jnp.concatenate([chip[:BAND], off[:BAND]], 0), w_edge[...]))
    landing = jnp.concatenate(uppers + lowers, 1)
    partial_out[...] = partial[...] + mm(landing, jnp.concatenate([active, active], 0))


def latent_kernel(
    depth, far, w_edge, partial, latent_out, normed_out, off_out, normal_out, inv_std_out
):
    mesh_rows, channels = partial.shape
    slots = far.shape[0]
    half = channels // 2
    first = far[:, :half]
    second = pltpu.roll(first.astype(F32), slots - depth, 0).astype(BF16)
    target = jnp.transpose(far[:, half:].astype(F32))
    if mesh_rows != LANES:
        target = jnp.broadcast_to(target[:1], (mesh_rows, slots))
    is_row = iota((mesh_rows, slots), 1) % (2 * depth) < depth
    hit = (target == iota((mesh_rows, slots), 0).astype(F32)) & is_row
    landing = jnp.where(hit, 1.0, 0.0).astype(BF16)
    active = gelu(mm(jnp.concatenate([first, second], 1), w_edge[...]))
    total = partial[...] + mm(landing, active)
    latent = total.astype(BF16)
    latent_out[...] = latent
    normal, inv_std = norm_stats(latent)
    normed = normal.astype(BF16)
    normed_out[...] = normed
    off_out[...] = jnp.concatenate([normed, jnp.zeros((PAD, channels), BF16)], 0)
    normal_out[...] = normal
    inv_std_out[...] = jnp.broadcast_to(inv_std, inv_std_out.shape)


def halves(rows, scale=None):
    first = iota(rows.shape, 1) < rows.shape[1] // 2
    if scale is not None:
        rows = rows * jnp.asarray(scale, rows.dtype)
    zero = jnp.zeros_like(rows)
    return jnp.concatenate([jnp.where(first, rows, zero), jnp.where(first, zero, rows)], 0)


def merge(stacked):
    m = stacked.shape[0] // 2
    first = iota((m, stacked.shape[1]), 1) < stacked.shape[1] // 2
    return jnp.where(first, stacked[:m], stacked[m:])


def near_places(m):
    odd = is_odd()
    return (1 - odd) * 2 * m, odd * 2 * m


def project_kernel(
    scale,
    pair,
    count,
    normed,
    chip_first,
    off_first,
    window_hbm,
    grad_hbm,
    w_qkv_hbm,
    qkv_out,
    w_qkv,
    grad_out,
    scores_out,
    products_out,
    bias_out,
    near_bias_out,
    normed_out,
    window,
    sems,
):
    m, channels = normed.shape
    normed_out[...] = normed[...]
    width = channels // PIECES
    starts = [part * channels + c * width for c in range(PIECES) for part in range(3)]
    copies = start_all(
        [(window_hbm, window), (grad_hbm, grad_out)]
        + [(w_qkv_hbm.at[:, pl.ds(at, width)], w_qkv.at[:, pl.ds(at, width)]) for at in starts],
        sems,
    )
    copies[0].wait()
    def masks():
        chip_at, off_at = near_places(m)
        reach = [meta_of(side, count)[:8, 2 * LANES : 2 * LANES + m] for side in (chip_first, off_first)]
        reach = jnp.concatenate(reach, 1)
        key_at = iota((m, 2 * m), 0) + m
        lane = iota((m, 2 * m), 1)
        query_at = jnp.where(lane < m, lane + chip_at, lane - m + off_at)
        keep = (key_at >= query_at - reach[0:1, :]) & (key_at <= query_at + reach[1:2, :])
        near_bias_out[...] = jnp.where(keep, 0.0, -jnp.inf).astype(F32)
        me = lax.axis_index("node")
        row = iota((3 * m, m), 0)
        key_at = jnp.where(row < m, row + chip_at, jnp.where(row < 2 * m, row - m + off_at, row - m))
        query_at = iota((3 * m, m), 1) + m
        at_end = (me == 0) | (me == lax.axis_size("node") - 1)
        missing = (row >= m) & (row < 2 * m) & at_end
        keep = (key_at >= query_at - window[0:1, :]) & (key_at <= query_at + window[1:2, :])
        bias = jnp.where(keep & jnp.logical_not(missing), 0.0, -jnp.inf).astype(F32)
        bias_out[...] = jnp.transpose(bias)

    masks()
    copies[1].wait()
    for i, at in enumerate(starts):
        copies[2 + i].wait()
        cols = slice(at, at + width)
        qkv_out[:, cols] = mm(normed[...], w_qkv[:, cols]).astype(BF16)
        for p in range(i // 3 * width // pair, (i // 3 + 1) * width // pair):
            q, k, v = (
                slice(part * channels + p * pair, part * channels + (p + 1) * pair)
                for part in range(3)
            )
            if i % 3 == 1:
                scores_out[p] = mm_nt(halves(qkv_out[:, q], scale), qkv_out[:, k])
            if i % 3 == 2:
                products_out[p] = mm_nt(halves(grad_out[:, q]), qkv_out[:, v])


def attend_kernel(
    scale,
    pair,
    chip_normed,
    off_normed,
    w_qkv,
    own_qkv,
    own_grad,
    own_scores,
    own_products,
    bias,
    w_out_hbm,
    cot_hbm,
    stats_out,
    kv,
    weights_out,
    scores_out,
    near_q,
    w_out,
    cot,
    sems,
):
    fetch = start_all([(w_out_hbm, w_out), (cot_hbm, cot)], sems)
    m, channels = chip_normed.shape
    pairs = channels // pair

    @pl.when(everywhere())
    def _():
        near = jnp.concatenate([chip_normed[...], off_normed[:m]], 0)

        def bring(group):
            cols = slice(group * 2 * pair, (group + 1) * 2 * pair)
            near_q[:, cols] = mm(near, w_qkv[:, cols]).astype(BF16) * jnp.asarray(scale, BF16)
            blocks = []
            for part in range(1, 3):
                at = part * channels + group * 2 * pair
                block = mm(near, w_qkv[:, at : at + 2 * pair]).astype(BF16)
                kv[: 2 * m, at - channels : at - channels + 2 * pair] = block
                blocks.append(block)
            return blocks

        brought = {0: bring(0)}
        kv[2 * m :] = own_qkv[:, channels:]
        lane = iota((CHUNK, LANES), 1)
        stats = [jnp.zeros((CHUNK, LANES), F32) for _ in range(2 * m // CHUNK)]

        def near_of(p):
            return [b[:, p % 2 * pair : (p % 2 + 1) * pair] for b in brought[p // 2]]

        def multiply(p):
            cols = slice(p * pair, (p + 1) * pair)
            keys, values = near_of(p)
            return (
                mm_nt(halves(own_qkv[:, cols], scale), keys),
                mm_nt(halves(own_grad[:, cols]), values),
            )

        ahead = multiply(0)
        for p in range(pairs):
            scores, grad_prob = ahead
            if p + 1 < pairs:
                if p % 2 == 0 and p + 2 < pairs:
                    brought[p // 2 + 1] = bring(p // 2 + 1)
                ahead = multiply(p + 1)
            weights, grad_scores = [], []
            for at in range(0, 2 * m, CHUNK):
                part = slice(at, at + CHUNK)
                place = slice(at % m, at % m + CHUNK)
                raw = jnp.concatenate([scores[part], own_scores[p, part]], 1) + bias[place]
                top = jnp.max(raw, 1, keepdims=True)
                shifted = jnp.exp(raw - top)
                inv_sum = 1.0 / jnp.sum(shifted, 1, keepdims=True)
                probs = shifted * inv_sum
                product = jnp.concatenate([grad_prob[part], own_products[p, part]], 1)
                delta = jnp.sum(probs * product, 1, keepdims=True)
                weights.append(probs.astype(BF16))
                grad_scores.append((probs * (product - delta)).astype(BF16))
                for k, column in enumerate((top, inv_sum, delta)):
                    stats[at // CHUNK] = jnp.where(lane == k * pairs + p, column, stats[at // CHUNK])
            weights_out[p] = jnp.concatenate(weights, 0)
            scores_out[p] = jnp.concatenate(grad_scores, 0)
        stats_out[...] = jnp.transpose(jnp.concatenate(stats, 0))[: 3 * pairs]

    for copy in fetch:
        copy.wait()


def product_kernel(
    scale,
    pair,
    weights,
    grad_scores,
    kv,
    own_qkv,
    own_grad,
    latent,
    w_out,
    w_qkv,
    mesh_out_hbm,
    grad_normed,
    grad_key,
    grad_value,
    attention,
    grad_query,
    mesh_out,
    sems,
):
    m, channels = latent.shape
    pairs = channels // pair
    for p in range(pairs):
        cols = slice(p * pair, (p + 1) * pair)
        value = kv[:, channels + p * pair : channels + (p + 1) * pair]
        attention[:, cols] = merge(mm(weights[p], value)).astype(BF16)
    mesh_out[...] = (latent[...].astype(F32) + mm(attention[...], w_out[...])).astype(BF16)
    out = pltpu.make_async_copy(mesh_out, mesh_out_hbm, sems.at[0])
    out.start()

    @pl.when(everywhere())
    def _():
        for p in range(pairs):
            cols = slice(p * pair, (p + 1) * pair)
            grad_query[:, cols] = (merge(mm(grad_scores[p], kv[:, cols])) * scale).astype(BF16)
        for p in range(pairs):
            cols = slice(p * pair, (p + 1) * pair)
            grad_key[:, cols] = mm_tn(grad_scores[p, :, 2 * m :], halves(own_qkv[:, cols], scale))
            grad_value[:, cols] = mm_tn(weights[p, :, 2 * m :], halves(own_grad[:, cols]))
        grad_normed[...] = mm_nt(grad_query[...], w_qkv[:, :channels])

    out.wait()


def finish_kernel(
    pair,
    chip_stats,
    off_stats,
    bias,
    near_q,
    chip_grad,
    off_grad,
    own_qkv,
    grad_key,
    grad_value,
    grad_normed,
    w_qkv,
    normal,
    inv_std,
    cot,
    grad_out,
):
    m, channels = normal.shape
    pairs = channels // pair

    stats = []
    for h in range(2):
        lanes = slice(h * m, (h + 1) * m)
        stats.append(jnp.concatenate([chip_stats[:, lanes], off_stats[:, lanes]], 1))

    def multiply(p):
        cols = slice(p * pair, (p + 1) * pair)
        key2 = halves(own_qkv[:, channels + p * pair : channels + (p + 1) * pair])
        value2 = halves(own_qkv[:, 2 * channels + p * pair : 2 * channels + (p + 1) * pair])
        query = near_q[:, cols]
        grad = jnp.concatenate([chip_grad[:, cols], off_grad[:, cols]], 0)
        return query, grad, mm_nt(key2, query), mm_nt(value2, grad)

    total = grad_normed[...]
    group_ends = (pairs * 3 // 4, pairs)
    gks, gvs = [], []
    ahead = multiply(0)
    for p in range(pairs):
        cols = slice(p * pair, (p + 1) * pair)
        query, grad, scores, grad_prob = ahead
        if p + 1 < pairs:
            ahead = multiply(p + 1)
        weights, grad_scores = [], []
        for at in range(0, 2 * m, CHUNK):
            part = slice(at, at + CHUNK)
            place = slice(at % m, at % m + CHUNK)
            top, inv_sum, delta = (
                stats[at // m][k * pairs + p : k * pairs + p + 1] for k in range(3)
            )
            probs = jnp.exp(scores[part] + bias[place] - top) * inv_sum
            weights.append(probs.astype(BF16))
            grad_scores.append((probs * (grad_prob[part] - delta)).astype(BF16))
        gk = grad_key[:, cols] + merge(mm(jnp.concatenate(grad_scores, 0), query))
        gv = grad_value[:, cols] + merge(mm(jnp.concatenate(weights, 0), grad))
        gks.append(gk.astype(BF16))
        gvs.append(gv.astype(BF16))
        if p + 1 in group_ends:
            at = channels + (p + 1 - len(gks)) * pair
            width = len(gks) * pair
            for blocks, start in ((gks, at), (gvs, at + channels)):
                total = total + mm_nt(
                    jnp.concatenate(blocks, 1), w_qkv[:, start : start + width]
                )
            gks, gvs = [], []
    centred = (
        total
        - jnp.mean(total, -1, keepdims=True)
        - normal[...] * jnp.mean(total * normal[...], -1, keepdims=True)
    )
    grad_out[...] = (cot[...].astype(F32) + inv_std[:, :1] * centred).astype(BF16)


def body(
    grid_in,
    mesh_in,
    own_src,
    own_dst,
    side_src,
    side_dst,
    side_count,
    far_src,
    far_dst,
    far_count,
    window,
    cotangent,
    w_edge,
    w_qkv,
    w_out,
):
    devices = lax.axis_size("node")
    grid_rows, channels = grid_in.shape
    m = mesh_in.shape[0]
    far_slots = far_src.shape[0]
    far_depth = far_slots // devices
    head_dim = channels // HEADS
    pair = 2 * head_dim
    pairs = channels // pair
    scale = head_dim ** (-0.5)
    meta_rows = side_src.shape[0] // (2 * LANES)

    side_src, side_dst = side_src.reshape(-1, LANES), side_dst.reshape(-1, LANES)
    own_src, own_dst = own_src.reshape(-1, LANES), own_dst.reshape(-1, LANES)
    far_src, far_dst = far_src.reshape(1, -1), far_dst.reshape(1, -1)
    side_count, far_count = side_count.reshape(1, -1), far_count.reshape(1, -1)
    message = ((BAND + meta_rows, channels), BF16)
    far_block = (2 * far_slots, channels // 2 + LANES)
    far_message, chip_message, off_message = call(
        pack_kernel,
        [(far_block, BF16), message, message],
        [grid_in, window, side_src, side_dst, side_count, far_src, far_dst, far_count],
        hbm=range(8),
        hbm_outs=range(3),
        scratch=like(grid_in, window, side_src, side_dst, side_count, far_src, far_dst, far_count)
        + [
            pltpu.VMEM(far_block, BF16),
            pltpu.VMEM((2, meta_rows, channels), BF16),
            dma(8),
            dma(5),
        ],
        name="pack",
    )
    from_chip, from_off = exchange(chip_message, off_message, "node")
    got_far = lax.all_to_all(
        far_message.reshape(devices, 2 * far_depth, far_block[1]),
        "node",
        split_axis=0,
        concat_axis=0,
        tiled=True,
    ).reshape(far_block)

    rows = ((m, channels), BF16)
    partial, own_grad, w_edge = call(
        own_kernel,
        [((m, channels), F32), rows, (w_edge.shape, BF16)],
        [grid_in, mesh_in, own_src, own_dst, cotangent, w_out, w_edge],
        hbm=range(7),
        hbm_outs=(1,),
        scratch=like(grid_in, mesh_in, own_src, own_dst, cotangent, w_out, cotangent) + [dma(8)],
        name="own",
    )
    (partial,) = call(
        functools.partial(side_kernel, meta_rows),
        [((m, channels), F32)],
        [from_chip, from_off, w_edge, partial],
        name="side",
        flops=8 * 10**9,
    )
    latent, normed, off_message, normal, inv_std = call(
        functools.partial(latent_kernel, far_depth),
        [rows, rows, ((m + PAD, channels), BF16), ((m, channels), F32), ((m, LANES), F32)],
        [got_far, w_edge, partial],
        name="latent",
    )
    off_normed = swap_off(off_message, "node")
    own_block = ((pairs, 2 * m, m), F32)
    own_qkv, w_qkv, own_grad, own_scores, own_products, bias, near_bias, normed = call(
        functools.partial(project_kernel, scale, pair, meta_rows),
        [((m, 3 * channels), BF16), (w_qkv.shape, BF16), rows, own_block, own_block]
        + [((m, 3 * m), F32), ((m, 2 * m), F32), rows],
        [normed, from_chip, from_off, window, own_grad, w_qkv],
        hbm=(3, 4, 5),
        scratch=like(window) + [dma(3 * PIECES + 2)],
        name="project",
    )
    chip_normed = swap_chip(normed, "node")
    chip_grad, off_grad = exchange(own_grad, own_grad, "node")
    probs = ((pairs, 2 * m, 3 * m), BF16)
    stats, kv, weights, grad_scores, near_q, w_out, cotangent = call(
        functools.partial(attend_kernel, scale, pair),
        [
            ((3 * pairs, 2 * m), F32),
            ((3 * m, 2 * channels), BF16),
            probs,
            probs,
            ((2 * m, channels), BF16),
            (w_out.shape, BF16),
            rows,
        ],
        [chip_normed, off_normed, w_qkv, own_qkv, own_grad, own_scores, own_products]
        + [bias, w_out, cotangent],
        hbm=(8, 9),
        scratch=[dma(2)],
        name="attend",
    )
    chip_stats, off_stats = exchange(stats, stats, "node")
    mesh_out, grad_normed, grad_key, grad_value = call(
        functools.partial(product_kernel, scale, pair),
        [
            rows,
            ((m, channels), F32),
            ((m, channels), F32),
            ((m, channels), F32),
        ],
        [
            weights,
            grad_scores,
            kv,
            own_qkv,
            own_grad,
            latent,
            w_out,
            w_qkv,
        ],
        hbm_outs=(0,),
        scratch=[pltpu.VMEM((m, channels), BF16)] * 3 + [dma(1)],
        name="product",
    )
    (mesh_grad,) = call(
        functools.partial(finish_kernel, pair),
        [rows],
        [
            chip_stats,
            off_stats,
            near_bias,
            near_q,
            chip_grad,
            off_grad,
            own_qkv,
            grad_key,
            grad_value,
            grad_normed,
            w_qkv,
            normal,
            inv_std,
            cotangent,
        ],
        name="finish",
    )
    return (mesh_out, mesh_grad)


def solution(mesh):
    rows = P(("groups", "node"), None)
    flat = P(("groups", "node"))
    placed = (rows, rows) + (flat,) * 8 + (P(None, ("groups", "node")), rows, P(), P(), P())
    return jax.shard_map(
        body, mesh=mesh, in_specs=placed, out_specs=(rows, rows), check_vma=False
    )
```
